32 devices in a mesh: cond: 2 (over core), pair: 4 (over z), dp: 4 (over y, x).
Axes of the slice: x: 2, y: 2, z: 4, core: 2. Of those that a mesh axis runs over, the one named last changes fastest.
Arguments:
- latents: float32 [8, 24, 24, 1536], P(('cond', 'dp'), 'pair'), may hold values from -6 to 6
- ratio_embed: float32 [8, 64], P(('cond', 'dp')), may hold values from -6 to 6
- clip_tokens: float32 [8, 76, 1280], P(('cond', 'dp'), 'pair'), may hold values from -6 to 6
- cotangent: float32 [8, 24, 24, 1536], P(('cond', 'dp'), 'pair'), may hold values from -6 to 6
- conv_kernel: float32 [3, 3, 1536], P(None, None, 'dp'), may hold values from -2 to 2
- conv_bias: float32 [1536], P('dp'), may hold values from -1.75 to 1.75
- expand_weight: float32 [1536, 6144], P('dp'), may hold values from -0.15625 to 0.15625
- expand_bias: float32 [6144], P('dp'), may hold values from -1.75 to 1.75
- response_gain: float32 [6144], P('dp'), may hold values from -3 to 3
- response_bias: float32 [6144], P('dp'), may hold values from -1.75 to 1.75
- reduce_weight: float32 [6144, 1536], P('dp'), may hold values from -0.078125 to 0.078125
- reduce_bias: float32 [1536], P('dp'), may hold values from -1.75 to 1.75
- ratio_weight: float32 [64, 3072], P('dp'), may hold values from -0.375 to 0.375
- ratio_bias: float32 [3072], P('dp'), may hold values from -1.75 to 1.75
- text_weight: float32 [1280, 1536], P('dp'), may hold values from -0.15625 to 0.15625
- text_bias: float32 [1536], P('dp'), may hold values from -1.75 to 1.75
- attend_weight: float32 [1536, 4608], P('dp'), may hold values from -0.15625 to 0.15625
- query_bias: float32 [1536], P('dp'), may hold values from -1.75 to 1.75
- value_bias: float32 [1536], P('dp'), may hold values from -1.75 to 1.75
- output_weight: float32 [1536, 1536], P('dp'), may hold values from -1.25 to 1.25
- output_bias: float32 [1536], P('dp'), may hold values from -1.75 to 1.75
Outputs:
- layer_output: float32 [8, 24, 24, 1536], P(('cond', 'dp'), 'pair')
- latent_grad: float32 [8, 24, 24, 1536], P(('cond', 'dp'), 'pair')
- tokens_grad: float32 [8, 76, 1280], P(('cond', 'dp'), 'pair')
- kernel_grad: float32 [3, 3, 1536], P(None, None, 'dp')
- convbias_grad: float32 [1536], P('dp')
- expand_grad: float32 [1536, 6144], P('dp')
- expbias_grad: float32 [6144], P('dp')
- gain_grad: float32 [6144], P('dp')
- respbias_grad: float32 [6144], P('dp')
- reduce_grad: float32 [6144, 1536], P('dp')
- redbias_grad: float32 [1536], P('dp')
- ratio_grad: float32 [64, 3072], P('dp')
- ratiobias_grad: float32 [3072], P('dp')
- mapper_grad: float32 [1280, 1536], P('dp')
- mapbias_grad: float32 [1536], P('dp')
- attend_grad: float32 [1536, 4608], P('dp')
- querybias_grad: float32 [1536], P('dp')
- valuebias_grad: float32 [1536], P('dp')
- output_grad: float32 [1536, 1536], P('dp')
- outbias_grad: float32 [1536], P('dp')
The draws below stay inside these ranges and needn't reach their ends.
All inputs are finite; a program needn't handle non-finite values.
Results may differ from the reference program's by a relative error of at most 0.0003.
Values sent between devices are 32-bit elements; how exact they have to be, the bound alone decides.
A program may use at most 448 MiB of HBM per device.

```python
import jax
import jax.numpy as jnp
from jax import lax

C = 1536
HID = 6144
HEADS = 24
HEAD_CHANNELS = 64
CLIP = 1280
CR = 64
SIDE = 24
TXT = 76
LATENTS = 8


def strengthened(array, rng, source, target, shards_of, factor):
    owner, partner = [(jnp.arange(array.shape[position]) // (array.shape[position] // shards_of)).reshape([-1 if axis == position else 1 for axis in range(array.ndim)]) for position in (source, target)]
    chosen = jax.random.permutation(rng, shards_of)[partner]
    strong = (owner == chosen) | (owner == (partner + shards_of // 2) % shards_of)
    return jnp.where(strong, factor * array, array)


def steps_of(key, shape, pieces, least, top_value):
    def one(dim, shards_of):
        draws = jax.random.uniform(jax.random.fold_in(jax.random.fold_in(key, 6), dim), (shards_of,), jnp.float32, least / len(pieces), top_value / len(pieces))
        return jnp.repeat(jnp.exp(draws), shape[dim] // shards_of).reshape((-1,) + (1,) * (len(shape) - dim - 1))

    loudness = one(*pieces[0])
    for cut in pieces[1:]:
        loudness = loudness * one(*cut)
    return loudness


def bell_draw(own_key, extent, deviation, limit, split=(), dtype=jnp.bfloat16):
    entries = jax.random.normal(own_key, extent, jnp.float32) * deviation
    if len(split) > 0:
        entries = steps_of(own_key, extent, split, -0.22, 0.18) * entries
    return jnp.clip(entries, min=-limit, max=limit).astype(dtype)


def bell_draw_with(key, dims, spread, most, shards, heavy, held_as=jnp.bfloat16):
    values = spread * jax.random.normal(key, dims, jnp.float32)
    if shards:
        values = values * steps_of(key, dims, shards, -0.22, 0.18)
    return jnp.clip(strengthened(values, jax.random.fold_in(key, 3), *heavy), -most, most).astype(held_as)


def setup_inputs(seed: int = 0) -> dict:
    arg_keys = jax.random.split(jax.random.key(seed), 22)
    return {
        "latents": bell_draw(arg_keys[0], (LATENTS, SIDE, SIDE, C), 1.0, 6.0, ((0, 8), (1, 4)), jnp.float32),
        "ratio_embed": bell_draw(arg_keys[1], (LATENTS, CR), 1.0, 6.0, ((0, 8),), jnp.float32),
        "clip_tokens": bell_draw(arg_keys[2], (LATENTS, TXT, CLIP), 1.0, 6.0, ((0, 8), (1, 4)), jnp.float32),
        "cotangent": bell_draw_with(arg_keys[3], (LATENTS, SIDE, SIDE, C), 1.0, 6.0, ((0, 8), (1, 4)), (0, 3, 8, 2.0), jnp.float32),
        "conv_kernel": bell_draw(arg_keys[4], (3, 3, C), 9 ** -0.5, 2.0, ((2, 4),), jnp.float32),
        "conv_bias": bell_draw(arg_keys[5], (C,), 0.3, 1.75, ((0, 4),), jnp.float32),
        "expand_weight": bell_draw(arg_keys[6], (C, HID), C ** -0.5, 0.15625, ((0, 4),), jnp.float32),
        "expand_bias": bell_draw(arg_keys[7], (HID,), 0.3, 1.75, ((0, 4),), jnp.float32),
        "response_gain": bell_draw(arg_keys[8], (HID,), 0.5, 3.0, ((0, 4),), jnp.float32),
        "response_bias": bell_draw(arg_keys[9], (HID,), 0.3, 1.75, ((0, 4),), jnp.float32),
        "reduce_weight": bell_draw(arg_keys[10], (HID, C), HID ** -0.5, 0.078125, ((0, 4),), jnp.float32),
        "reduce_bias": bell_draw(arg_keys[11], (C,), 0.3, 1.75, ((0, 4),), jnp.float32),
        "ratio_weight": bell_draw(arg_keys[12], (CR, 2 * C), (4 * CR) ** -0.5, 0.375, ((0, 4),), jnp.float32),
        "ratio_bias": bell_draw(arg_keys[13], (2 * C,), 0.3, 1.75, ((0, 4),), jnp.float32),
        "text_weight": bell_draw(arg_keys[14], (CLIP, C), CLIP ** -0.5, 0.15625, ((0, 4),), jnp.float32),
        "text_bias": bell_draw(arg_keys[15], (C,), 0.3, 1.75, ((0, 4),), jnp.float32),
        "attend_weight": bell_draw(arg_keys[16], (C, 3 * C), C ** -0.5, 0.15625, ((0, 4),), jnp.float32),
        "query_bias": bell_draw(arg_keys[17], (C,), 0.3, 1.75, ((0, 4),), jnp.float32),
        "value_bias": bell_draw(arg_keys[18], (C,), 0.3, 1.75, ((0, 4),), jnp.float32),
        "output_weight": bell_draw(arg_keys[19], (C, C), (C // 64) ** -0.5, 1.25, ((0, 4),), jnp.float32),
        "output_bias": bell_draw(arg_keys[20], (C,), 0.3, 1.75, ((0, 4),), jnp.float32),
    }


HIGHEST_ACCURACY = lax.Precision.HIGHEST
EPSILON = 1e-06

@jax.custom_vjp
def low(v):
    return lax.optimization_barrier(v.astype(jnp.bfloat16)).astype(jnp.float32)

@jax.custom_vjp
def low_back(v):
    return v

def low_keep(v):
    return (low(v), None)

def low_pass(kept, grad):
    return (grad,)

def back_keep(v):
    return (v, None)

def back_low(kept, grad):
    return (low(grad),)
low.defvjp(low_keep, low_pass)
low_back.defvjp(back_keep, back_low)

def layer_norm(values):
    centered = values - lax.optimization_barrier(jnp.mean(values, axis=-1, keepdims=True))
    variance = lax.optimization_barrier(jnp.mean(centered * centered, axis=-1, keepdims=True))
    return centered * lax.rsqrt(variance + EPSILON)

def attend_one(triple):
    query_matrix, key_matrix, value_matrix = triple
    query_per_head = query_matrix.reshape(query_matrix.shape[0], HEADS, HEAD_CHANNELS)
    key_per_head = key_matrix.reshape(key_matrix.shape[0], HEADS, HEAD_CHANNELS)
    value_per_head = value_matrix.reshape(value_matrix.shape[0], HEADS, HEAD_CHANNELS)
    attention_scores = jnp.einsum('iuy,ouy->uio', query_per_head, key_per_head, precision=HIGHEST_ACCURACY) * HEAD_CHANNELS ** (-0.5)
    top_score = lax.optimization_barrier(jnp.max(attention_scores, axis=-1, keepdims=True))
    expo_terms = jnp.exp(attention_scores - top_score)
    attention_probabilities = expo_terms / lax.optimization_barrier(jnp.sum(expo_terms, axis=-1, keepdims=True))
    attended_output = jnp.einsum('fvb,bfq->vfq', attention_probabilities, value_per_head, precision=HIGHEST_ACCURACY)
    return attended_output.reshape(query_matrix.shape[0], HEADS * HEAD_CHANNELS)

def reference(latents, ratio_embed, clip_tokens, cotangent, conv_kernel, conv_bias, expand_weight, expand_bias, response_gain, response_bias, reduce_weight, reduce_bias, ratio_weight, ratio_bias, text_weight, text_bias, attend_weight, query_bias, value_bias, output_weight, output_bias):
    weights = (conv_kernel, conv_bias, expand_weight, expand_bias, response_gain, response_bias, reduce_weight, reduce_bias, ratio_weight, ratio_bias, text_weight, text_bias, attend_weight, query_bias, value_bias, output_weight, output_bias)

    def forward(inputs, tokens, params):
        kernel, conv_shift, expand_w, expand_b, resp_gain, resp_bias, reduce_w, reduce_b, ratio_w, ratio_b, map_w, map_b, attend_w, query_b, value_b, out_w, out_b = params
        lat_count = inputs.shape[0]
        padded = jnp.pad(inputs, ((0, 0), (1, 1), (1, 1), (0, 0)))
        total_conv = conv_shift
        for row_off in range(3):
            for col_off in range(3):
                total_conv = total_conv + padded[:, row_off:row_off + SIDE, col_off:col_off + SIDE, :] * kernel[row_off, col_off]
        normed = layer_norm(total_conv)
        hidden = jnp.einsum('lijc,ch->lijh', normed, expand_w, precision=HIGHEST_ACCURACY) + expand_b
        activated = jax.nn.gelu(hidden, approximate=False)
        totals = lax.optimization_barrier(jnp.sum(activated * activated, axis=(1, 2), keepdims=True))
        norms = jnp.sqrt(totals + EPSILON)
        scaled = norms / (lax.optimization_barrier(jnp.mean(norms, axis=-1, keepdims=True)) + EPSILON)
        response = resp_gain * (activated * scaled) + resp_bias + activated
        hidden_one = inputs + jnp.einsum('lijh,hc->lijc', response, reduce_w, precision=HIGHEST_ACCURACY) + reduce_b
        modulation = jnp.dot(ratio_embed, ratio_w, precision=HIGHEST_ACCURACY) + ratio_b
        hidden_two = hidden_one * (1.0 + modulation[:, None, None, :C]) + modulation[:, None, None, C:]
        flat = hidden_two.reshape(lat_count, SIDE * SIDE, C)
        normed_two = layer_norm(flat)
        mapped = jnp.einsum('ltk,kc->ltc', jax.nn.silu(tokens), map_w, precision=HIGHEST_ACCURACY) + map_b
        source = jnp.concatenate([normed_two, mapped], axis=1)
        query_matrix = jnp.einsum('lpc,cn->lpn', normed_two, attend_w[:, :C], precision=HIGHEST_ACCURACY) + query_b
        key_value = jnp.einsum('lmc,cn->lmn', source, attend_w[:, C:], precision=HIGHEST_ACCURACY)
        key_matrix = key_value[..., :C]
        value_matrix = key_value[..., C:] + value_b
        attended_output = lax.map(jax.checkpoint(attend_one), (query_matrix, key_matrix, value_matrix))
        result = flat + jnp.einsum('lpc,cn->lpn', attended_output, out_w, precision=HIGHEST_ACCURACY) + out_b
        return result.reshape(inputs.shape)
    layer_output, pullback = jax.vjp(forward, latents, clip_tokens, weights)
    latent_grad, tokens_grad, grads = pullback(cotangent)
    kernel_grad, convbias_grad, expand_grad, expbias_grad, gain_grad, respbias_grad, reduce_grad, redbias_grad, ratio_grad, ratiobias_grad, mapper_grad, mapbias_grad, attend_grad, querybias_grad, valuebias_grad, output_grad, outbias_grad = grads
    return (layer_output, latent_grad, tokens_grad, kernel_grad, convbias_grad, expand_grad, expbias_grad, gain_grad, respbias_grad, reduce_grad, redbias_grad, ratio_grad, ratiobias_grad, mapper_grad, mapbias_grad, attend_grad, querybias_grad, valuebias_grad, output_grad, outbias_grad)
```

```python
import functools

import jax
import jax.numpy as jnp
from jax import lax
from jax.sharding import PartitionSpec as P

HEADS = 24
HEAD_CHANNELS = 64


HIGHEST_ACCURACY = lax.Precision.HIGHEST
EPSILON = 1e-06


def extended(block, sides, width):
    for axis, dim in sides:
        count = lax.axis_size(axis)
        forward = [(i, i + 1) for i in range(count - 1)]
        backward = [(target, source) for source, target in forward]
        low = lax.ppermute(
            lax.slice_in_dim(block, block.shape[dim] - width, None, axis=dim), axis, forward
        )
        high = lax.ppermute(lax.slice_in_dim(block, 0, width, axis=dim), axis, backward)
        block = jnp.concatenate([low, block, high], axis=dim)
    return block


def layer_norm(values):
    centered = values - jnp.mean(values, axis=-1, keepdims=True)
    variance = jnp.mean(centered * centered, axis=-1, keepdims=True)
    return centered * lax.rsqrt(variance + EPSILON)


def matmul(left, right):
    return jnp.einsum("...k,kn->...n", left, right, precision=HIGHEST_ACCURACY)


def depthwise(row_padded, kernel, conv_shift):
    row_count = row_padded.shape[1] - 2
    col_count = row_padded.shape[2]
    padded = jnp.pad(row_padded, ((0, 0), (0, 0), (1, 1), (0, 0)))
    total_conv = conv_shift
    for row_off in range(3):
        for col_off in range(3):
            total_conv = (
                total_conv
                + padded[:, row_off : row_off + row_count, col_off : col_off + col_count, :]
                * kernel[row_off, col_off]
            )
    return total_conv


def front(row_padded, kernel, conv_shift, expand_w, expand_b):
    normed = layer_norm(depthwise(row_padded, kernel, conv_shift))
    flat = normed.reshape(normed.shape[0], normed.shape[1] * normed.shape[2], normed.shape[3])
    return jax.nn.gelu(matmul(flat, expand_w) + expand_b, approximate=False)


def response_mlp(activated, totals, resp_gain, resp_bias, reduce_w, reduce_b, residual):
    norms = jnp.sqrt(totals + EPSILON)
    scaled = norms / (jnp.mean(norms, axis=-1, keepdims=True) + EPSILON)
    response = resp_gain * (activated * scaled[:, None, :]) + resp_bias + activated
    return residual + matmul(response, reduce_w) + reduce_b


def modulate(hidden_one, ratio_w, ratio_b, embed):
    modulation = jnp.dot(embed, ratio_w, precision=HIGHEST_ACCURACY) + ratio_b
    chan_count = hidden_one.shape[-1]
    return hidden_one * (1.0 + modulation[:, None, :chan_count]) + modulation[:, None, chan_count:]


def project(hidden_two, tokens, map_w, map_b, attend_w, query_b, value_b):
    chan_count = hidden_two.shape[-1]
    normed = layer_norm(hidden_two)
    mapped = matmul(jax.nn.silu(tokens), map_w) + map_b
    source = jnp.concatenate([normed, mapped], axis=1)
    query_matrix = matmul(normed, attend_w[:, :chan_count]) + query_b
    key_value = matmul(source, attend_w[:, chan_count:])
    return (query_matrix, key_value[..., :chan_count], key_value[..., chan_count:] + value_b)


def divide_into_heads(values):
    return values.reshape(values.shape[:-1] + (HEADS, HEAD_CHANNELS))


def attend_single(triple):
    query_matrix, key_matrix, value_matrix = triple
    attention_scores = jnp.einsum(
        "iuy,ouy->uio",
        divide_into_heads(query_matrix),
        divide_into_heads(key_matrix),
        precision=HIGHEST_ACCURACY,
    ) * HEAD_CHANNELS ** (-0.5)
    top_score = jnp.max(attention_scores, axis=-1, keepdims=True)
    expo_terms = jnp.exp(attention_scores - top_score)
    expo_total = jnp.sum(expo_terms, axis=-1, keepdims=True)
    attention_probabilities = expo_terms / expo_total
    attended_output = jnp.einsum(
        "fvb,bfq->vfq",
        attention_probabilities,
        divide_into_heads(value_matrix),
        precision=HIGHEST_ACCURACY,
    )
    log_total = top_score + jnp.log(expo_total)
    return (attended_output.reshape(query_matrix.shape), log_total)


def attend_back_single(items):
    query_matrix, key_matrix, value_matrix, attended_output, log_total, grad_mix = items
    query_per_head = divide_into_heads(query_matrix)
    key_per_head = divide_into_heads(key_matrix)
    value_per_head = divide_into_heads(value_matrix)
    gradient_per_head = divide_into_heads(grad_mix)
    attention_scores = jnp.einsum(
        "iuy,ouy->uio", query_per_head, key_per_head, precision=HIGHEST_ACCURACY
    ) * HEAD_CHANNELS ** (-0.5)
    attention_probabilities = jnp.exp(attention_scores - log_total)
    probability_gradient = jnp.einsum(
        "iuy,ouy->uio", gradient_per_head, value_per_head, precision=HIGHEST_ACCURACY
    )
    delta_rows = jnp.einsum(
        "phd,phd->hp",
        gradient_per_head,
        divide_into_heads(attended_output),
        precision=HIGHEST_ACCURACY,
    )
    score_gradient = (
        attention_probabilities
        * (probability_gradient - delta_rows[..., None])
        * HEAD_CHANNELS ** (-0.5)
    )
    query_gradient = jnp.einsum(
        "fvb,bfq->vfq", score_gradient, key_per_head, precision=HIGHEST_ACCURACY
    )
    key_gradient = jnp.einsum(
        "gyu,ygx->ugx", score_gradient, query_per_head, precision=HIGHEST_ACCURACY
    )
    value_gradient = jnp.einsum(
        "gyu,ygx->ugx", attention_probabilities, gradient_per_head, precision=HIGHEST_ACCURACY
    )
    return (
        query_gradient.reshape(query_matrix.shape),
        key_gradient.reshape(key_matrix.shape),
        value_gradient.reshape(value_matrix.shape),
    )


def body(
    latents,
    ratio_embed,
    clip_tokens,
    cotangent,
    conv_kernel,
    conv_bias,
    expand_weight,
    expand_bias,
    response_gain,
    response_bias,
    reduce_weight,
    reduce_bias,
    ratio_weight,
    ratio_bias,
    text_weight,
    text_bias,
    attend_weight,
    query_bias,
    value_bias,
    output_weight,
    output_bias,
):
    gathered = (
        lax.all_gather(conv_kernel, "dp", axis=2, tiled=True),
        lax.all_gather(conv_bias, "dp", axis=0, tiled=True),
        lax.all_gather(expand_weight, "dp", axis=0, tiled=True),
        lax.all_gather(expand_bias, "dp", axis=0, tiled=True),
        lax.all_gather(response_gain, "dp", axis=0, tiled=True),
        lax.all_gather(response_bias, "dp", axis=0, tiled=True),
        lax.all_gather(reduce_weight, "dp", axis=0, tiled=True),
        lax.all_gather(reduce_bias, "dp", axis=0, tiled=True),
        lax.all_gather(ratio_weight, "dp", axis=0, tiled=True),
        lax.all_gather(ratio_bias, "dp", axis=0, tiled=True),
        lax.all_gather(text_weight, "dp", axis=0, tiled=True),
        lax.all_gather(text_bias, "dp", axis=0, tiled=True),
        lax.all_gather(attend_weight, "dp", axis=0, tiled=True),
        lax.all_gather(query_bias, "dp", axis=0, tiled=True),
        lax.all_gather(value_bias, "dp", axis=0, tiled=True),
        lax.all_gather(output_weight, "dp", axis=0, tiled=True),
        lax.all_gather(output_bias, "dp", axis=0, tiled=True),
    )
    (
        kernel,
        conv_shift,
        expand_w,
        expand_b,
        resp_gain,
        resp_bias,
        reduce_w,
        reduce_b,
        ratio_w,
        ratio_b,
        map_w,
        map_b,
        attend_w,
        query_b,
        value_b,
        out_w,
        out_b,
    ) = gathered
    lat_count, row_count, col_count, chan_count = latents.shape
    pixel_count = row_count * col_count
    row_padded = extended(latents, (("pair", 1),), 1)
    activated, front_pull = jax.vjp(front, row_padded, kernel, conv_shift, expand_w, expand_b)
    totals = lax.psum(jnp.sum(activated * activated, axis=1), "pair")
    residual = latents.reshape(lat_count, pixel_count, chan_count)
    hidden_one, mlp_pull = jax.vjp(
        response_mlp, activated, totals, resp_gain, resp_bias, reduce_w, reduce_b, residual
    )
    hidden_two, mod_pull = jax.vjp(
        functools.partial(modulate, embed=ratio_embed), hidden_one, ratio_w, ratio_b
    )
    (query_matrix, key_local, value_local), proj_pull = jax.vjp(
        project, hidden_two, clip_tokens, map_w, map_b, attend_w, query_b, value_b
    )
    key_matrix, value_matrix = (
        lax.all_gather(key_local, "pair", axis=1, tiled=True),
        lax.all_gather(value_local, "pair", axis=1, tiled=True),
    )
    attended_output, log_total = lax.map(attend_single, (query_matrix, key_matrix, value_matrix))
    result = hidden_two + matmul(attended_output, out_w) + out_b
    layer_output = result.reshape(latents.shape)
    grad_out = cotangent.reshape(lat_count, pixel_count, chan_count)
    out_w_grad = jnp.einsum("lpc,lpn->cn", attended_output, grad_out, precision=HIGHEST_ACCURACY)
    out_b_grad = jnp.sum(grad_out, axis=(0, 1))
    grad_mix = jnp.einsum("lpn,cn->lpc", grad_out, out_w, precision=HIGHEST_ACCURACY)
    query_gradient, key_gradient, value_gradient = lax.map(
        attend_back_single,
        (query_matrix, key_matrix, value_matrix, attended_output, log_total, grad_mix),
    )
    key_share, value_share = (
        lax.psum_scatter(key_gradient, "pair", scatter_dimension=1, tiled=True),
        lax.psum_scatter(value_gradient, "pair", scatter_dimension=1, tiled=True),
    )
    grad_two, tokens_grad, map_w_grad, map_b_grad, attend_w_grad, query_b_grad, value_b_grad = (
        proj_pull((query_gradient, key_share, value_share))
    )
    grad_two = grad_two + grad_out
    attend_shards = (
        lax.psum_scatter(map_w_grad, "dp", scatter_dimension=0, tiled=True),
        lax.psum_scatter(map_b_grad, "dp", scatter_dimension=0, tiled=True),
        lax.psum_scatter(attend_w_grad, "dp", scatter_dimension=0, tiled=True),
        lax.psum_scatter(query_b_grad, "dp", scatter_dimension=0, tiled=True),
        lax.psum_scatter(value_b_grad, "dp", scatter_dimension=0, tiled=True),
        lax.psum_scatter(out_w_grad, "dp", scatter_dimension=0, tiled=True),
        lax.psum_scatter(out_b_grad, "dp", scatter_dimension=0, tiled=True),
    )
    grad_one, ratio_w_grad, ratio_b_grad = mod_pull(grad_two)
    grad_act, grad_totals, gain_grad, respb_grad, reduce_w_grad, reduce_b_grad, grad_res = mlp_pull(
        grad_one
    )
    grad_totals = lax.psum(grad_totals, "pair")
    grad_act = grad_act + 2.0 * activated * grad_totals[:, None, :]
    grad_padded, kernel_grad, shift_grad, expand_w_grad, expand_b_grad = front_pull(grad_act)
    rim_rows = jnp.concatenate([grad_padded[:, :1], grad_padded[:, -1:]], axis=1)
    arrived = extended(rim_rows, (("pair", 1),), 1)
    inner_rows = grad_padded[:, 1:-1]
    inner_rows = inner_rows.at[:, 0].add(arrived[:, 0]).at[:, -1].add(arrived[:, 3])
    latent_grad = inner_rows + grad_res.reshape(latents.shape)
    block_shards = (
        lax.psum_scatter(kernel_grad, "dp", scatter_dimension=2, tiled=True),
        lax.psum_scatter(shift_grad, "dp", scatter_dimension=0, tiled=True),
        lax.psum_scatter(expand_w_grad, "dp", scatter_dimension=0, tiled=True),
        lax.psum_scatter(expand_b_grad, "dp", scatter_dimension=0, tiled=True),
        lax.psum_scatter(gain_grad, "dp", scatter_dimension=0, tiled=True),
        lax.psum_scatter(respb_grad, "dp", scatter_dimension=0, tiled=True),
        lax.psum_scatter(reduce_w_grad, "dp", scatter_dimension=0, tiled=True),
        lax.psum_scatter(reduce_b_grad, "dp", scatter_dimension=0, tiled=True),
        lax.psum_scatter(ratio_w_grad, "dp", scatter_dimension=0, tiled=True),
        lax.psum_scatter(ratio_b_grad, "dp", scatter_dimension=0, tiled=True),
    )
    shards = tuple(block_shards) + tuple(attend_shards)
    summed = lax.psum(shards, ("cond", "pair"))
    return (layer_output, latent_grad, tokens_grad) + tuple(summed)

FAST = lax.Precision.HIGH


def dot(left, right):
    return jnp.dot(left, right, precision=FAST)


def dot_t(left, right):
    return lax.dot_general(left, right, (((1,), (1,)), ((), ())), precision=FAST)


def t_dot(left, right):
    return lax.dot_general(left, right, (((0,), (0,)), ((), ())), precision=FAST)


def partners(value, step):
    return lax.ppermute(value, "dp", [(i, i ^ step) for i in range(4)])


def gather_near(block):
    return [block] + [partners(block, step) for step in (1, 2, 3)]


def scatter_near(blocks):
    arrived = [partners(blocks[step], step) for step in (1, 2, 3)]
    return blocks[0] + arrived[0] + arrived[1] + arrived[2]


def exchange_near(blocks, me):
    near = jnp.stack([blocks[0]] + [partners(blocks[step], step) for step in (1, 2, 3)])
    order = jnp.bitwise_xor(jnp.arange(4), me)
    return jnp.take(near, order, axis=0)


def other_core(value):
    return lax.ppermute(value, "cond", [(0, 1), (1, 0)])


def norm_stats(values):
    centered = values - jnp.mean(values, axis=-1, keepdims=True)
    variance = jnp.mean(centered * centered, axis=-1, keepdims=True)
    inverse = lax.rsqrt(variance + EPSILON)
    return centered * inverse, inverse


def norm_back(grad, normed, inverse):
    return inverse * (
        grad
        - jnp.mean(grad, axis=-1, keepdims=True)
        - normed * jnp.mean(grad * normed, axis=-1, keepdims=True)
    )


def to_both_cores(blocks_of, core, me):
    mine = exchange_near([blocks_of(me ^ step, core) for step in range(4)], me)
    other = other_core(mine)
    low = jnp.where(core == 0, mine, other)
    high = jnp.where(core == 0, other, mine)
    return jnp.concatenate([low, high], axis=1)


def heads_of(values):
    return values.reshape(values.shape[0], -1, HEAD_CHANNELS)


def plane_body(
    latents,
    ratio_embed,
    clip_tokens,
    cotangent,
    conv_kernel,
    conv_bias,
    expand_weight,
    expand_bias,
    response_gain,
    response_bias,
    reduce_weight,
    reduce_bias,
    ratio_weight,
    ratio_bias,
    text_weight,
    text_bias,
    attend_weight,
    query_bias,
    value_bias,
    output_weight,
    output_bias,
):
    size = lax.axis_size("dp")
    core = lax.axis_index("cond")
    me = lax.axis_index("dp")
    _, rows, cols, chan = latents.shape
    pixels = rows * cols
    part = chan // size
    hid = size * expand_bias.shape[0]
    texts = clip_tokens.shape[1]
    grid = [(z, d) for z in range(size) for d in range(size)]
    swap_perm = [(z * size + d, d * size + z) for z, d in grid]
    down_perm = [(z * size + d, d * size + z + 1) for z, d in grid if z + 1 < size]
    up_perm = [(z * size + d, d * size + z - 1) for z, d in grid if z >= 1]

    def swap(value, perm=swap_perm):
        return lax.ppermute(value, ("pair", "dp"), perm)

    image = swap(latents[0])
    above = swap(latents[0, -1:], down_perm)
    below = swap(latents[0, :1], up_perm)
    embed = swap(ratio_embed)
    tokens = swap(clip_tokens[0])
    cot = swap(cotangent[0].reshape(pixels, chan))

    packed = jnp.concatenate(
        [
            conv_kernel.reshape(9, part),
            conv_bias[None],
            reduce_bias[None],
            text_bias[None],
            output_bias[None],
            ratio_bias.reshape(2, part),
        ],
        axis=0,
    )
    every = lax.all_gather(packed, "dp", axis=0)
    channel_rows = every[:, :13].transpose(1, 0, 2).reshape(13, chan)
    kernel = channel_rows[:9].reshape(3, 3, chan)
    conv_shift, reduce_b, text_b, out_b = (channel_rows[9 + i] for i in range(4))
    ratio_b = every[:, 13:].reshape(2 * chan)

    half = part // 2
    wide = hid // size
    expand_w = to_both_cores(
        lambda to, c: lax.dynamic_slice(expand_weight, (c * half, to * wide), (half, wide)), core, me
    ).reshape(chan, wide)
    attend_thirds = attend_weight.reshape(part, 3, chan)
    attend_w = to_both_cores(
        lambda to, c: lax.dynamic_slice(
            attend_thirds, (c * half, 0, to * part), (half, 3, part)
        ).reshape(half, 3 * part),
        core,
        me,
    ).reshape(chan, 3 * part)

    text_part = text_weight.shape[0]
    silu_tokens = jax.nn.silu(tokens)
    token_cols = [
        lax.dynamic_slice(tokens, (0, (me ^ step) * text_part), (texts, text_part))
        for step in range(4)
    ]
    near_tokens = jnp.concatenate(
        [token_cols[0]] + [partners(token_cols[step], step) for step in (1, 2, 3)], axis=0
    )
    silu_near = jax.nn.silu(near_tokens)
    mapped_share = dot(silu_near, text_weight)
    mapped = scatter_near(jnp.split(mapped_share, 4, axis=0)) + text_b
    mapped_all = jnp.concatenate(gather_near(mapped), axis=0)
    ratio_part = ratio_weight.shape[0]
    embed_part = lax.dynamic_slice(embed, (0, me * ratio_part), (1, ratio_part))
    modulation = (
        lax.psum(jnp.dot(embed_part, ratio_weight, precision=HIGHEST_ACCURACY), "dp")[0] + ratio_b
    )
    mod_scale = 1.0 + modulation[:chan]
    mod_shift = modulation[chan:]

    row_padded = jnp.concatenate([above, image, below], axis=0)
    padded = jnp.pad(row_padded, ((0, 0), (1, 1), (0, 0)))
    total_conv = conv_shift
    for i in range(3):
        for j in range(3):
            total_conv = total_conv + padded[i : i + rows, j : j + cols] * kernel[i, j]
    normed, inverse = norm_stats(total_conv.reshape(pixels, chan))
    normed_all = jnp.concatenate(gather_near(normed), axis=0)
    hidden = dot(normed_all, expand_w) + expand_bias
    bell = 0.5 * (1.0 + lax.erf(hidden * 0.5**0.5))
    activated = hidden * bell
    totals = jnp.sum(activated * activated, axis=0)
    norms = jnp.sqrt(totals + EPSILON)
    middle = lax.psum(jnp.sum(norms), "dp") / hid + EPSILON
    scaled = norms / middle
    factor = 1.0 + response_gain * scaled
    response = activated * factor + response_bias
    one_share = dot(response, reduce_weight)
    hidden_one = (
        scatter_near(jnp.split(one_share, 4, axis=0)) + image.reshape(pixels, chan) + reduce_b
    )
    hidden_two = hidden_one * mod_scale + mod_shift
    normed_two, inverse_two = norm_stats(hidden_two)
    normed_two_all = jnp.concatenate(gather_near(normed_two), axis=0)

    source = jnp.concatenate([normed_two_all, mapped_all], axis=0)
    query = dot(normed_two_all, attend_w[:, :part]) + query_bias
    key_value = dot(source, attend_w[:, part:])
    key = key_value[:, :part]
    value = key_value[:, part:] + value_bias
    query_h, key_h, value_h = heads_of(query), heads_of(key), heads_of(value)
    scores = jnp.einsum("iuy,ouy->uio", query_h, key_h, precision=FAST) * HEAD_CHANNELS ** (-0.5)
    expo = jnp.exp(scores - jnp.max(scores, axis=-1, keepdims=True))
    probs = expo / jnp.sum(expo, axis=-1, keepdims=True)
    mixture_h = jnp.einsum("uio,ouy->iuy", probs, value_h, precision=FAST)
    mixture = mixture_h.reshape(query.shape)
    out_share = dot(mixture, output_weight)
    plane_out = scatter_near(jnp.split(out_share, 4, axis=0)) + hidden_two + out_b
    layer_output = swap(plane_out).reshape(latents.shape)

    cot_all = jnp.concatenate(gather_near(cot), axis=0)
    output_grad = t_dot(mixture, cot_all)
    grad_mix_h = heads_of(dot_t(cot_all, output_weight))
    grad_probs = jnp.einsum("iuy,ouy->uio", grad_mix_h, value_h, precision=FAST)
    delta = jnp.sum(grad_mix_h * mixture_h, axis=-1).T
    grad_scores = probs * (grad_probs - delta[..., None]) * HEAD_CHANNELS ** (-0.5)
    grad_query = jnp.einsum("uio,ouy->iuy", grad_scores, key_h, precision=FAST).reshape(query.shape)
    grad_key = jnp.einsum("uio,iuy->ouy", grad_scores, query_h, precision=FAST).reshape(key.shape)
    grad_value = jnp.einsum("uio,iuy->ouy", probs, grad_mix_h, precision=FAST).reshape(key.shape)
    spots = size * pixels
    grad_kv = jnp.concatenate([grad_key, grad_value], axis=1)
    grad_qkv = jnp.concatenate([grad_query, grad_kv[:spots]], axis=1)
    two_share = dot_t(grad_qkv, attend_w)
    text_share = dot_t(grad_kv[spots:], attend_w[:, part:])
    grad_normed_two = scatter_near(jnp.split(two_share, 4, axis=0))
    grad_mapped = scatter_near(jnp.split(text_share, 4, axis=0))
    attend_grad = t_dot(normed_two_all, grad_qkv)
    attend_grad = attend_grad.at[:, part:].add(t_dot(mapped_all, grad_kv[spots:]))
    grad_two = cot + norm_back(grad_normed_two, normed_two, inverse_two)
    grad_one = grad_two * mod_scale
    grad_one_all = jnp.concatenate(gather_near(grad_one), axis=0)
    grad_mapped_all = jnp.concatenate(gather_near(grad_mapped), axis=0)
    mapper_grad = t_dot(silu_near, grad_mapped_all)
    gate = 1.0 / (1.0 + jnp.exp(-near_tokens))
    tokens_near = dot_t(grad_mapped_all, text_weight) * (
        gate * (1.0 + near_tokens * (1.0 - gate))
    )
    token_blocks = exchange_near(jnp.split(tokens_near, 4, axis=0), me)
    tokens_grad = swap(token_blocks.transpose(1, 0, 2).reshape(texts, size * text_part))[None]
    ratio_sums = lax.psum(
        jnp.concatenate([jnp.sum(grad_two * hidden_one, axis=0), jnp.sum(grad_two, axis=0)]), "dp"
    )
    ratio_grad = embed_part.reshape(ratio_part, 1) * ratio_sums

    reduce_grad = t_dot(response, grad_one_all)
    grad_response = dot_t(grad_one_all, reduce_weight)
    gain_sum = jnp.sum(grad_response * activated, axis=0)
    grad_scaled = gain_sum * response_gain
    spread = lax.psum(jnp.sum(grad_scaled * norms), "dp") / hid
    grad_norms = grad_scaled / middle - spread / (middle * middle)
    grad_totals = grad_norms / (2.0 * norms)
    grad_activated = grad_response * factor + 2.0 * activated * grad_totals
    density = jnp.exp(-0.5 * hidden * hidden) * (2.0 * jnp.pi) ** -0.5
    grad_hidden = grad_activated * (bell + hidden * density)
    expand_grad = t_dot(normed_all, grad_hidden)
    front_share = dot_t(grad_hidden, expand_w)
    grad_normed = scatter_near(jnp.split(front_share, 4, axis=0))
    grad_conv = norm_back(grad_normed, normed, inverse).reshape(rows, cols, chan)
    kernel_grad = jnp.stack(
        [
            jnp.sum(padded[i : i + rows, j : j + cols] * grad_conv, axis=(0, 1))
            for i in range(3)
            for j in range(3)
        ]
    )
    spread_conv = jnp.pad(grad_conv, ((2, 2), (1, 1), (0, 0)))
    latent_rows = jnp.zeros((rows + 2, cols, chan), jnp.float32)
    for i in range(3):
        for j in range(3):
            latent_rows = (
                latent_rows
                + spread_conv[2 - i : 2 - i + rows + 2, 2 - j : 2 - j + cols] * kernel[i, j]
            )
    inner = swap(latent_rows[1:-1] + grad_one.reshape(rows, cols, chan))
    back_up = [(d * size + z, (z - 1) * size + d) for z, d in grid if z >= 1]
    back_down = [(d * size + z, (z + 1) * size + d) for z, d in grid if z + 1 < size]
    from_below = swap(latent_rows[:1], back_up)
    from_above = swap(latent_rows[-1:], back_down)
    latent_grad = inner.at[-1:].add(from_below).at[:1].add(from_above)[None]

    def over_planes(value, axis):
        count = value.shape[axis] // 2
        low = lax.slice_in_dim(value, 0, count, axis=axis)
        high = lax.slice_in_dim(value, count, None, axis=axis)
        kept = jnp.where(core == 0, low, high) + other_core(jnp.where(core == 0, high, low))
        return kept

    def from_both(value, axis):
        other = other_core(value)
        return jnp.concatenate(
            [jnp.where(core == 0, value, other), jnp.where(core == 0, other, value)], axis=axis
        )

    def columns_home(value):
        kept = over_planes(value.reshape(size, part, value.shape[1]), 1)
        blocks = [
            lax.dynamic_slice(kept, (me ^ step, 0, 0), (1,) + kept.shape[1:])[0]
            for step in range(4)
        ]
        return exchange_near(blocks, me)

    output_sum = from_both(lax.psum(over_planes(output_grad, 0), "pair"), 0)
    attend_home = columns_home(attend_grad)
    attend_home = attend_home.reshape(size, half, 3, part).transpose(1, 2, 0, 3)
    attend_sum = from_both(lax.psum(attend_home.reshape(half, 3 * chan), "pair"), 0)
    mapper_sum = from_both(lax.psum(over_planes(mapper_grad, 0), "pair"), 0)
    reduce_sum = from_both(lax.psum(over_planes(reduce_grad, 0), "pair"), 0)
    expand_home = columns_home(expand_grad).transpose(1, 0, 2).reshape(half, hid)
    expand_sum = from_both(lax.psum(expand_home, "pair"), 0)

    def mine(value):
        return lax.dynamic_slice(value, (me * (value.shape[0] // size),), (value.shape[0] // size,))

    small = (
        jnp.sum(grad_hidden, axis=0),
        scaled * gain_sum,
        jnp.sum(grad_response, axis=0),
        mine(jnp.sum(grad_one_all, axis=0)),
        mine(jnp.sum(grad_mapped_all, axis=0)),
        jnp.sum(grad_query, axis=0),
        jnp.sum(grad_value, axis=0),
        mine(jnp.sum(cot_all, axis=0)),
        mine(ratio_sums),
        ratio_grad.reshape(-1),
    )
    lengths = [item.shape[0] for item in small]
    small_sum = lax.psum(jnp.concatenate(small), ("cond", "pair"))
    ends = []
    position = 0
    for length in lengths:
        ends.append(small_sum[position : position + length])
        position += length
    expb, gain, respb, redb, mapb, queryb, valueb, outb, ratiob, ratio = ends
    conv_sum = lax.psum(
        jnp.concatenate([kernel_grad, jnp.sum(grad_conv, axis=(0, 1))[None]], axis=0),
        ("cond", "pair", "dp"),
    )
    conv_mine = lax.dynamic_slice(conv_sum, (0, me * part), (10, part))
    return (
        layer_output,
        latent_grad,
        tokens_grad,
        conv_mine[:9].reshape(3, 3, part),
        conv_mine[9],
        expand_sum,
        expb,
        gain,
        respb,
        reduce_sum,
        redb,
        ratio.reshape(ratio_part, 2 * chan),
        ratiob,
        mapper_sum,
        mapb,
        attend_sum,
        queryb,
        valueb,
        output_sum,
        outb,
    )


def solution(mesh):
    square = mesh.shape["cond"] == 2 and mesh.shape["pair"] == 4 and mesh.shape["dp"] == 4
    return jax.shard_map(
        plane_body if square else body,
        mesh=mesh,
        in_specs=(
            P(("cond", "dp"), "pair", None, None),
            P(("cond", "dp"), None),
            P(("cond", "dp"), "pair", None),
            P(("cond", "dp"), "pair", None, None),
            P(None, None, "dp"),
            P("dp"),
            P("dp", None),
            P("dp"),
            P("dp"),
            P("dp"),
            P("dp", None),
            P("dp"),
            P("dp", None),
            P("dp"),
            P("dp", None),
            P("dp"),
            P("dp", None),
            P("dp"),
            P("dp"),
            P("dp", None),
            P("dp"),
        ),
        out_specs=(
            P(("cond", "dp"), "pair", None, None),
            P(("cond", "dp"), "pair", None, None),
            P(("cond", "dp"), "pair", None),
            P(None, None, "dp"),
            P("dp"),
            P("dp", None),
            P("dp"),
            P("dp"),
            P("dp"),
            P("dp", None),
            P("dp"),
            P("dp", None),
            P("dp"),
            P("dp", None),
            P("dp"),
            P("dp", None),
            P("dp"),
            P("dp"),
            P("dp", None),
            P("dp"),
        ),
        check_vma=False,
    )
```

```python
import functools

import jax
import jax.numpy as jnp
from jax import lax
from jax.experimental import pallas as pl
from jax.experimental.pallas import tpu as pltpu
from jax.sharding import PartitionSpec as P

HEADS = 24
HEAD_CHANNELS = 64


HIGHEST_ACCURACY = lax.Precision.HIGHEST
EPSILON = 1e-06


def extended(block, sides, width):
    for axis, dim in sides:
        count = lax.axis_size(axis)
        forward = [(i, i + 1) for i in range(count - 1)]
        backward = [(target, source) for source, target in forward]
        low = lax.ppermute(
            lax.slice_in_dim(block, block.shape[dim] - width, None, axis=dim), axis, forward
        )
        high = lax.ppermute(lax.slice_in_dim(block, 0, width, axis=dim), axis, backward)
        block = jnp.concatenate([low, block, high], axis=dim)
    return block


def layer_norm(values):
    centered = values - jnp.mean(values, axis=-1, keepdims=True)
    variance = jnp.mean(centered * centered, axis=-1, keepdims=True)
    return centered * lax.rsqrt(variance + EPSILON)


def matmul(left, right):
    return jnp.einsum("...k,kn->...n", left, right, precision=HIGHEST_ACCURACY)


def depthwise(row_padded, kernel, conv_shift):
    row_count = row_padded.shape[1] - 2
    col_count = row_padded.shape[2]
    padded = jnp.pad(row_padded, ((0, 0), (0, 0), (1, 1), (0, 0)))
    total_conv = conv_shift
    for row_off in range(3):
        for col_off in range(3):
            total_conv = (
                total_conv
                + padded[:, row_off : row_off + row_count, col_off : col_off + col_count, :]
                * kernel[row_off, col_off]
            )
    return total_conv


def front(row_padded, kernel, conv_shift, expand_w, expand_b):
    normed = layer_norm(depthwise(row_padded, kernel, conv_shift))
    flat = normed.reshape(normed.shape[0], normed.shape[1] * normed.shape[2], normed.shape[3])
    return jax.nn.gelu(matmul(flat, expand_w) + expand_b, approximate=False)


def response_mlp(activated, totals, resp_gain, resp_bias, reduce_w, reduce_b, residual):
    norms = jnp.sqrt(totals + EPSILON)
    scaled = norms / (jnp.mean(norms, axis=-1, keepdims=True) + EPSILON)
    response = resp_gain * (activated * scaled[:, None, :]) + resp_bias + activated
    return residual + matmul(response, reduce_w) + reduce_b


def modulate(hidden_one, ratio_w, ratio_b, embed):
    modulation = jnp.dot(embed, ratio_w, precision=HIGHEST_ACCURACY) + ratio_b
    chan_count = hidden_one.shape[-1]
    return hidden_one * (1.0 + modulation[:, None, :chan_count]) + modulation[:, None, chan_count:]


def project(hidden_two, tokens, map_w, map_b, attend_w, query_b, value_b):
    chan_count = hidden_two.shape[-1]
    normed = layer_norm(hidden_two)
    mapped = matmul(jax.nn.silu(tokens), map_w) + map_b
    source = jnp.concatenate([normed, mapped], axis=1)
    query_matrix = matmul(normed, attend_w[:, :chan_count]) + query_b
    key_value = matmul(source, attend_w[:, chan_count:])
    return (query_matrix, key_value[..., :chan_count], key_value[..., chan_count:] + value_b)


def divide_into_heads(values):
    return values.reshape(values.shape[:-1] + (HEADS, HEAD_CHANNELS))


def attend_single(triple):
    query_matrix, key_matrix, value_matrix = triple
    attention_scores = jnp.einsum(
        "iuy,ouy->uio",
        divide_into_heads(query_matrix),
        divide_into_heads(key_matrix),
        precision=HIGHEST_ACCURACY,
    ) * HEAD_CHANNELS ** (-0.5)
    top_score = jnp.max(attention_scores, axis=-1, keepdims=True)
    expo_terms = jnp.exp(attention_scores - top_score)
    expo_total = jnp.sum(expo_terms, axis=-1, keepdims=True)
    attention_probabilities = expo_terms / expo_total
    attended_output = jnp.einsum(
        "fvb,bfq->vfq",
        attention_probabilities,
        divide_into_heads(value_matrix),
        precision=HIGHEST_ACCURACY,
    )
    log_total = top_score + jnp.log(expo_total)
    return (attended_output.reshape(query_matrix.shape), log_total)


def attend_back_single(items):
    query_matrix, key_matrix, value_matrix, attended_output, log_total, grad_mix = items
    query_per_head = divide_into_heads(query_matrix)
    key_per_head = divide_into_heads(key_matrix)
    value_per_head = divide_into_heads(value_matrix)
    gradient_per_head = divide_into_heads(grad_mix)
    attention_scores = jnp.einsum(
        "iuy,ouy->uio", query_per_head, key_per_head, precision=HIGHEST_ACCURACY
    ) * HEAD_CHANNELS ** (-0.5)
    attention_probabilities = jnp.exp(attention_scores - log_total)
    probability_gradient = jnp.einsum(
        "iuy,ouy->uio", gradient_per_head, value_per_head, precision=HIGHEST_ACCURACY
    )
    delta_rows = jnp.einsum(
        "phd,phd->hp",
        gradient_per_head,
        divide_into_heads(attended_output),
        precision=HIGHEST_ACCURACY,
    )
    score_gradient = (
        attention_probabilities
        * (probability_gradient - delta_rows[..., None])
        * HEAD_CHANNELS ** (-0.5)
    )
    query_gradient = jnp.einsum(
        "fvb,bfq->vfq", score_gradient, key_per_head, precision=HIGHEST_ACCURACY
    )
    key_gradient = jnp.einsum(
        "gyu,ygx->ugx", score_gradient, query_per_head, precision=HIGHEST_ACCURACY
    )
    value_gradient = jnp.einsum(
        "gyu,ygx->ugx", attention_probabilities, gradient_per_head, precision=HIGHEST_ACCURACY
    )
    return (
        query_gradient.reshape(query_matrix.shape),
        key_gradient.reshape(key_matrix.shape),
        value_gradient.reshape(value_matrix.shape),
    )


def body(
    latents,
    ratio_embed,
    clip_tokens,
    cotangent,
    conv_kernel,
    conv_bias,
    expand_weight,
    expand_bias,
    response_gain,
    response_bias,
    reduce_weight,
    reduce_bias,
    ratio_weight,
    ratio_bias,
    text_weight,
    text_bias,
    attend_weight,
    query_bias,
    value_bias,
    output_weight,
    output_bias,
):
    gathered = (
        lax.all_gather(conv_kernel, "dp", axis=2, tiled=True),
        lax.all_gather(conv_bias, "dp", axis=0, tiled=True),
        lax.all_gather(expand_weight, "dp", axis=0, tiled=True),
        lax.all_gather(expand_bias, "dp", axis=0, tiled=True),
        lax.all_gather(response_gain, "dp", axis=0, tiled=True),
        lax.all_gather(response_bias, "dp", axis=0, tiled=True),
        lax.all_gather(reduce_weight, "dp", axis=0, tiled=True),
        lax.all_gather(reduce_bias, "dp", axis=0, tiled=True),
        lax.all_gather(ratio_weight, "dp", axis=0, tiled=True),
        lax.all_gather(ratio_bias, "dp", axis=0, tiled=True),
        lax.all_gather(text_weight, "dp", axis=0, tiled=True),
        lax.all_gather(text_bias, "dp", axis=0, tiled=True),
        lax.all_gather(attend_weight, "dp", axis=0, tiled=True),
        lax.all_gather(query_bias, "dp", axis=0, tiled=True),
        lax.all_gather(value_bias, "dp", axis=0, tiled=True),
        lax.all_gather(output_weight, "dp", axis=0, tiled=True),
        lax.all_gather(output_bias, "dp", axis=0, tiled=True),
    )
    (
        kernel,
        conv_shift,
        expand_w,
        expand_b,
        resp_gain,
        resp_bias,
        reduce_w,
        reduce_b,
        ratio_w,
        ratio_b,
        map_w,
        map_b,
        attend_w,
        query_b,
        value_b,
        out_w,
        out_b,
    ) = gathered
    lat_count, row_count, col_count, chan_count = latents.shape
    pixel_count = row_count * col_count
    row_padded = extended(latents, (("pair", 1),), 1)
    activated, front_pull = jax.vjp(front, row_padded, kernel, conv_shift, expand_w, expand_b)
    totals = lax.psum(jnp.sum(activated * activated, axis=1), "pair")
    residual = latents.reshape(lat_count, pixel_count, chan_count)
    hidden_one, mlp_pull = jax.vjp(
        response_mlp, activated, totals, resp_gain, resp_bias, reduce_w, reduce_b, residual
    )
    hidden_two, mod_pull = jax.vjp(
        functools.partial(modulate, embed=ratio_embed), hidden_one, ratio_w, ratio_b
    )
    (query_matrix, key_local, value_local), proj_pull = jax.vjp(
        project, hidden_two, clip_tokens, map_w, map_b, attend_w, query_b, value_b
    )
    key_matrix, value_matrix = (
        lax.all_gather(key_local, "pair", axis=1, tiled=True),
        lax.all_gather(value_local, "pair", axis=1, tiled=True),
    )
    attended_output, log_total = lax.map(attend_single, (query_matrix, key_matrix, value_matrix))
    result = hidden_two + matmul(attended_output, out_w) + out_b
    layer_output = result.reshape(latents.shape)
    grad_out = cotangent.reshape(lat_count, pixel_count, chan_count)
    out_w_grad = jnp.einsum("lpc,lpn->cn", attended_output, grad_out, precision=HIGHEST_ACCURACY)
    out_b_grad = jnp.sum(grad_out, axis=(0, 1))
    grad_mix = jnp.einsum("lpn,cn->lpc", grad_out, out_w, precision=HIGHEST_ACCURACY)
    query_gradient, key_gradient, value_gradient = lax.map(
        attend_back_single,
        (query_matrix, key_matrix, value_matrix, attended_output, log_total, grad_mix),
    )
    key_share, value_share = (
        lax.psum_scatter(key_gradient, "pair", scatter_dimension=1, tiled=True),
        lax.psum_scatter(value_gradient, "pair", scatter_dimension=1, tiled=True),
    )
    grad_two, tokens_grad, map_w_grad, map_b_grad, attend_w_grad, query_b_grad, value_b_grad = (
        proj_pull((query_gradient, key_share, value_share))
    )
    grad_two = grad_two + grad_out
    attend_shards = (
        lax.psum_scatter(map_w_grad, "dp", scatter_dimension=0, tiled=True),
        lax.psum_scatter(map_b_grad, "dp", scatter_dimension=0, tiled=True),
        lax.psum_scatter(attend_w_grad, "dp", scatter_dimension=0, tiled=True),
        lax.psum_scatter(query_b_grad, "dp", scatter_dimension=0, tiled=True),
        lax.psum_scatter(value_b_grad, "dp", scatter_dimension=0, tiled=True),
        lax.psum_scatter(out_w_grad, "dp", scatter_dimension=0, tiled=True),
        lax.psum_scatter(out_b_grad, "dp", scatter_dimension=0, tiled=True),
    )
    grad_one, ratio_w_grad, ratio_b_grad = mod_pull(grad_two)
    grad_act, grad_totals, gain_grad, respb_grad, reduce_w_grad, reduce_b_grad, grad_res = mlp_pull(
        grad_one
    )
    grad_totals = lax.psum(grad_totals, "pair")
    grad_act = grad_act + 2.0 * activated * grad_totals[:, None, :]
    grad_padded, kernel_grad, shift_grad, expand_w_grad, expand_b_grad = front_pull(grad_act)
    rim_rows = jnp.concatenate([grad_padded[:, :1], grad_padded[:, -1:]], axis=1)
    arrived = extended(rim_rows, (("pair", 1),), 1)
    inner_rows = grad_padded[:, 1:-1]
    inner_rows = inner_rows.at[:, 0].add(arrived[:, 0]).at[:, -1].add(arrived[:, 3])
    latent_grad = inner_rows + grad_res.reshape(latents.shape)
    block_shards = (
        lax.psum_scatter(kernel_grad, "dp", scatter_dimension=2, tiled=True),
        lax.psum_scatter(shift_grad, "dp", scatter_dimension=0, tiled=True),
        lax.psum_scatter(expand_w_grad, "dp", scatter_dimension=0, tiled=True),
        lax.psum_scatter(expand_b_grad, "dp", scatter_dimension=0, tiled=True),
        lax.psum_scatter(gain_grad, "dp", scatter_dimension=0, tiled=True),
        lax.psum_scatter(respb_grad, "dp", scatter_dimension=0, tiled=True),
        lax.psum_scatter(reduce_w_grad, "dp", scatter_dimension=0, tiled=True),
        lax.psum_scatter(reduce_b_grad, "dp", scatter_dimension=0, tiled=True),
        lax.psum_scatter(ratio_w_grad, "dp", scatter_dimension=0, tiled=True),
        lax.psum_scatter(ratio_b_grad, "dp", scatter_dimension=0, tiled=True),
    )
    shards = tuple(block_shards) + tuple(attend_shards)
    summed = lax.psum(shards, ("cond", "pair"))
    return (layer_output, latent_grad, tokens_grad) + tuple(summed)

FAST = lax.Precision.HIGH


def dot(left, right):
    return jnp.dot(left, right, precision=FAST)


def dot_t(left, right):
    return lax.dot_general(left, right, (((1,), (1,)), ((), ())), precision=FAST)


def t_dot(left, right):
    return lax.dot_general(left, right, (((0,), (0,)), ((), ())), precision=FAST)


def norm_stats(values):
    centered = values - jnp.mean(values, axis=-1, keepdims=True)
    variance = jnp.mean(centered * centered, axis=-1, keepdims=True)
    inverse = lax.rsqrt(variance + EPSILON)
    return centered * inverse, inverse


def norm_back(grad, normed, inverse):
    return inverse * (
        grad
        - jnp.mean(grad, axis=-1, keepdims=True)
        - normed * jnp.mean(grad * normed, axis=-1, keepdims=True)
    )


def heads_of(values):
    return values.reshape(values.shape[0], -1, HEAD_CHANNELS)


CHUNK = 32
MESH = pl.DeviceIdType.MESH
DMA = pltpu.SemaphoreType.DMA
ANY = pl.BlockSpec(memory_space=pl.ANY)


def near_of(me, step):
    across = lax.rem(lax.rem(me, 2) + lax.rem(step, 2), 2)
    along = lax.rem(lax.div(me, 2) + lax.div(step, 2), 2)
    return along * 2 + across


def remote(src, dst, send, recv, device):
    return pltpu.make_async_remote_copy(
        src_ref=src, dst_ref=dst, send_sem=send, recv_sem=recv, device_id=device,
        device_id_type=MESH,
    )


def greet(device):
    barrier = pltpu.get_barrier_semaphore()
    pl.semaphore_signal(barrier, inc=1, device_id=device, device_id_type=MESH)


def relay_begin(full, sems):
    cross_out, cross_in, mate_out, mate_in = sems
    core = lax.axis_index("cond")
    level = lax.axis_index("pair")
    me = lax.axis_index("dp")
    unit = full.shape[1] // 4
    side = lax.rem(level, 2)
    across = (core, level + 1 - 2 * side, me)
    mate = (1 - core, level, me)

    def spot(u, step):
        rows = pl.ds(pl.multiple_of((core * 2 + u) * unit, 8), unit)
        return full.at[near_of(me, step), rows]

    steps = (1, 2, 3)
    crosses = [
        remote(
            spot(side, step), spot(side, step), cross_out.at[step - 1], cross_in.at[step - 1], across
        )
        for step in steps
    ]
    mates = [
        [
            remote(
                spot(u, step), spot(u, step), mate_out.at[i, step - 1], mate_in.at[i, step - 1], mate
            )
            for step in steps
        ]
        for i, u in enumerate((side, 1 - side))
    ]

    def begin():
        for copy in crosses + mates[0]:
            copy.start()

    def end():
        for cross, far in zip(crosses, mates[1]):
            cross.wait_recv()
            far.start()
        for copy in crosses:
            copy.wait_send()
        for copy in mates[0] + mates[1]:
            copy.wait()

    return begin, end


def exchange_body(gather_count, scatter_count, swap_count, relays, *refs):
    near_count = gather_count + scatter_count
    count = near_count + swap_count
    ins = refs[:count]
    refs = refs[count + relays :]
    outs = refs[:count]
    full = refs[count] if relays else None
    refs = refs[count + relays :]
    passing, refs = refs[:swap_count], refs[swap_count:]
    holds = refs[: gather_count + swap_count]
    send, recv, keep = refs[gather_count + swap_count :][:3]
    sems = refs[gather_count + swap_count + 3 :]
    core = lax.axis_index("cond")
    level = lax.axis_index("pair")
    me = lax.axis_index("dp")
    goal = near_of(me, rev(level))
    quarter = rev(near_of(level, me))
    shifts = level != 0
    rises = goal != level
    final = me == level
    expected = 3
    for step in (1, 2, 3):
        greet((core, level, near_of(me, step)))
    if relays:
        greet((1 - core, level, me))
        greet((core, level + 1 - 2 * lax.rem(level, 2), me))
        expected = expected + 2
    if swap_count:
        pl.when(rises)(lambda: greet((core, quarter, me)))
        expected = expected + jnp.where(rises, 1, 0)
    pl.semaphore_wait(pltpu.get_barrier_semaphore(), expected)

    def shift(i, goals):
        return remote(
            ins[near_count + i], goals[i], send.at[near_count + i, 0], recv.at[near_count + i, 0],
            (core, level, goal),
        )

    def rise(i, sources):
        return remote(
            sources[i], outs[near_count + i], send.at[near_count + i, 1],
            recv.at[near_count + i, 1], (core, goal, me),
        )

    swap_ins = ins[near_count:]
    swap_outs = outs[near_count:]
    near_copies = []
    if relays:
        relay_start, relay_end = relay_begin(full, sems)
        relay_start()
    for i in range(swap_count):
        pl.when(jnp.logical_and(shifts, final))(shift(i, swap_outs).start)
        pl.when(jnp.logical_and(shifts, jnp.logical_not(final)))(shift(i, passing).start)
        pl.when(jnp.logical_and(jnp.logical_not(shifts), rises))(rise(i, swap_ins).start)
    for step in (3, 1, 2):
        for i in range(near_count):
            if i < gather_count:
                src, dst = ins[i], outs[i].at[step]
            else:
                src, dst = ins[i].at[step], outs[i].at[step - 1]
            copy = remote(
                src, dst, send.at[i, step - 1], recv.at[i, step - 1],
                (core, level, near_of(me, step)),
            )
            copy.start()
            near_copies.append(copy)

    def through(src, hold, dst, sem):
        load = pltpu.make_async_copy(src, hold, sem)
        load.start()
        load.wait()
        store = pltpu.make_async_copy(hold, dst, sem)
        store.start()
        store.wait()

    for i in range(gather_count):
        through(ins[i], holds[i], outs[i].at[0], keep.at[i])
    for i in range(swap_count):
        pl.when(jnp.logical_and(jnp.logical_not(shifts), jnp.logical_not(rises)))(
            lambda i=i: through(
                swap_ins[i], holds[gather_count + i], swap_outs[i], keep.at[gather_count + i]
            )
        )
        pl.when(shifts)(shift(i, passing).wait_recv)
        pl.when(jnp.logical_and(shifts, rises))(rise(i, passing).start)
    if relays:
        relay_end()
    for copy in near_copies:
        copy.wait()
    for i in range(swap_count):
        pl.when(shifts)(shift(i, passing).wait_send)
        pl.when(rises)(rise(i, swap_ins).wait_send)
        pl.when(quarter != level)(rise(i, swap_ins).wait_recv)


def exchange(collective, gathers=(), scatters=(), swaps=(), relay=()):
    f32 = jnp.float32
    shapes = [(4,) + item.shape for item in gathers]
    shapes += [(3,) + item.shape[1:] for item in scatters]
    shapes += [item.shape for item in swaps]
    count = len(shapes)
    shapes += [item.shape for item in relay]
    shapes += [item.shape for item in swaps]
    staged = len(gathers) + len(swaps)
    scratch = [pltpu.VMEM(item.shape, f32) for item in tuple(gathers) + tuple(swaps)]
    scratch += [DMA((count, 3)), DMA((count, 3)), DMA((max(staged, 1),))]
    if relay:
        scratch += [DMA((3,)), DMA((3,)), DMA((2, 3)), DMA((2, 3))]
    outs = pl.pallas_call(
        functools.partial(exchange_body, len(gathers), len(scatters), len(swaps), len(relay)),
        out_shape=[jax.ShapeDtypeStruct(shape, f32) for shape in shapes],
        in_specs=[ANY] * (count + len(relay)),
        out_specs=[ANY] * len(shapes),
        scratch_shapes=scratch,
        input_output_aliases={count: count} if relay else {},
        compiler_params=pltpu.CompilerParams(
            collective_id=collective, has_side_effects=True, vmem_limit_bytes=16 * 2**20
        ),
        name="exchange",
    )(*gathers, *scatters, *swaps, *relay)
    return outs[: count + len(relay)]


PARTS = 4


def open_body(image_in, packed_in, tokens_in, embed_in, weight_in, attend_in, *refs):
    image, packed, tokens, embed, weight, attend = refs[:6]
    passing = refs[6:9]
    hold, send, recv, keep, cross_out, cross_in, pass_out, pass_in, own_out, own_in, block_out, block_in = refs[9:]
    core = lax.axis_index("cond")
    level = lax.axis_index("pair")
    me = lax.axis_index("dp")
    mate = (1 - core, level, me)
    side = lax.rem(level, 2)
    across = (core, level + 1 - 2 * side, me)
    rows = image_in.shape[0]
    wide = weight.shape[3]
    unit = weight.shape[2]
    turn = rev(level)
    goal = near_of(me, turn)
    quarter = rev(near_of(level, me))
    shifts = level != 0
    rises = goal != level
    turned = jnp.logical_and(level == 1, me == 1)
    raises = jnp.logical_and(level > 0, jnp.logical_not(turned))
    falls = level < 3
    taken = jnp.logical_and(quarter < 3, jnp.logical_not(turned))
    greet(mate)
    greet(across)
    for step in (1, 2, 3):
        greet((core, level, near_of(me, step)))
    pl.when(rises)(lambda: greet((core, quarter, me)))
    pl.when(quarter > 0)(lambda: greet((core, quarter - 1, level)))
    pl.when(taken)(lambda: greet((core, quarter + 1, level)))
    expected = (
        5 + jnp.where(rises, 1, 0) + jnp.where(raises, 1, 0) + jnp.where(falls, 1, 0)
    )
    pl.semaphore_wait(pltpu.get_barrier_semaphore(), expected)

    body = image.at[pl.ds(1, rows)]
    ins = (image_in, tokens_in, embed_in)
    ends = (body, tokens, embed)

    def shift(goals):
        return [
            remote(src, dst, send.at[i], recv.at[i], (core, level, goal))
            for i, (src, dst) in enumerate(zip(ins, goals))
        ]

    def rise(sources):
        return [
            remote(src, dst, send.at[3 + i], recv.at[3 + i], (core, goal, me))
            for i, (src, dst) in enumerate(zip(sources, ends))
        ]

    def stay():
        image_load = pltpu.make_async_copy(image_in, hold, keep.at[0])
        image_load.start()
        rest = [
            pltpu.make_async_copy(src, dst, keep.at[i])
            for i, (src, dst) in ((1, (tokens_in, tokens)), (2, (embed_in, embed)))
        ]
        run("start", *rest)
        image_load.wait()
        image_store = pltpu.make_async_copy(hold, body, keep.at[0])
        image_store.start()
        run("wait", image_store, *rest)

    lower = remote(
        image_in.at[pl.ds(rows - 1, 1)], image.at[pl.ds(0, 1)], send.at[6], recv.at[6],
        (core, me, near_of(me, rev(jnp.minimum(level + 1, 3)))),
    )
    upper = remote(
        image_in.at[pl.ds(0, 1)], image.at[pl.ds(rows + 1, 1)], send.at[7], recv.at[7],
        (core, me, near_of(me, rev(jnp.maximum(level - 1, 0)))),
    )
    around = pltpu.make_async_copy(
        image_in.at[pl.ds(0, 1)], image.at[pl.ds(rows + 1, 1)], keep.at[4]
    )

    def vectors(step):
        return remote(
            packed_in, packed.at[me], send.at[7 + step], recv.at[7 + step],
            (core, level, near_of(me, step)),
        )

    mine = core * 2 + side
    other = core * 2 + 1 - side

    size = unit // PARTS

    def block(step, h):
        to = near_of(me, step)
        src = weight_in.at[
            pl.ds(pl.multiple_of(mine * unit + h * size, 8), size),
            pl.ds(pl.multiple_of(to * wide, wide), wide),
        ]
        dst = weight.at[me, mine, pl.ds(h * size, size)]
        return remote(
            src, dst, block_out.at[h, step - 1], block_in.at[h, step - 1], (core, level, to)
        )

    piece = attend.shape[2] // 3

    def thirds(step):
        to = near_of(me, step)
        found = []
        for p in range(3):
            src = attend_in.at[
                pl.ds(pl.multiple_of(mine * unit, 8), unit),
                pl.ds(pl.multiple_of((p * 4 + to) * piece, piece), piece),
            ]
            dst = attend.at[
                me, pl.ds(pl.multiple_of(mine * unit, 8), unit), pl.ds(p * piece, piece)
            ]
            spot = 11 + step * 3 + p
            found.append(remote(src, dst, send.at[spot], recv.at[spot], (core, level, to)))
        return found

    def crossed(step, u, h):
        spot = weight.at[near_of(me, step), u, pl.ds(h * size, size)]
        return remote(spot, spot, cross_out.at[h, step - 1], cross_in.at[h, step - 1], across)

    def passed(step, u, turn, h):
        spot = weight.at[near_of(me, step), u, pl.ds(h * size, size)]
        k = turn * PARTS + h
        return remote(spot, spot, pass_out.at[k, step - 1], pass_in.at[k, step - 1], mate)

    def run(method, *copies):
        for copy in copies:
            getattr(copy, method)()

    final = me == level
    pl.when(jnp.logical_and(shifts, final))(lambda: run("start", *shift(ends)))
    pl.when(jnp.logical_and(shifts, jnp.logical_not(final)))(lambda: run("start", *shift(passing)))
    pl.when(jnp.logical_and(jnp.logical_not(shifts), rises))(lambda: run("start", *rise(ins)))
    pl.when(falls)(lower.start)
    pl.when(raises)(upper.start)
    pl.when(turned)(around.start)
    own = [pltpu.make_async_copy(packed_in, packed.at[me], keep.at[3])]
    own_blocks = [
        remote(
            weight_in.at[pl.ds(u * unit, unit), pl.ds(pl.multiple_of(me * wide, wide), wide)],
            weight.at[me, u],
            own_out.at[u],
            own_in.at[u],
            mate,
        )
        for u in range(4)
    ] + [
        remote(
            attend_in.at[:, pl.ds(pl.multiple_of((p * 4 + me) * piece, piece), piece)],
            attend.at[me, :, pl.ds(p * piece, piece)],
            own_out.at[4 + p],
            own_in.at[4 + p],
            mate,
        )
        for p in range(3)
    ]
    for step in (3, 1, 2):
        vectors(step).start()
    for h in range(PARTS):
        for step in (3, 1, 2):
            block(step, h).start()
    run("start", *own, *own_blocks)
    pl.when(jnp.logical_and(jnp.logical_not(shifts), jnp.logical_not(rises)))(stay)

    for step in (3, 1, 2):
        run("start", *thirds(step))

    @pl.when(shifts)
    def _():
        run("wait_recv", *shift(passing))
        pl.when(rises)(lambda: run("start", *rise(passing)))

    for h in range(PARTS):
        for step in (2, 1, 3):
            block(step, h).wait_recv()
            crossed(step, mine, h).start()
            passed(step, mine, 0, h).start()
    for h in range(PARTS):
        for step in (2, 1, 3):
            crossed(step, other, h).wait_recv()
            passed(step, other, 1, h).start()
    pl.when(shifts)(lambda: run("wait_send", *shift(passing)))
    pl.when(rises)(lambda: run("wait_send", *rise(ins)))
    pl.when(quarter != level)(lambda: run("wait_recv", *rise(ins)))
    pl.when(falls)(lower.wait_send)
    pl.when(raises)(upper.wait_send)
    pl.when(quarter > 0)(lower.wait_recv)
    pl.when(taken)(upper.wait_recv)
    pl.when(turned)(around.wait)
    for step in (1, 2, 3):
        vectors(step).wait()
        run("wait", *thirds(step))
        for h in range(PARTS):
            block(step, h).wait_send()
            crossed(step, mine, h).wait_send()
            for u, turn_of in ((mine, 0), (other, 1)):
                passed(step, u, turn_of, h).wait()
    run("wait", *own, *own_blocks)


def open_exchange(collective, image, packed, tokens, embed, weight, attend):
    rows, cols, chan = image.shape
    unit = weight.shape[0] // 4
    shapes = [
        (rows + 2, cols, chan),
        (4,) + packed.shape,
        tokens.shape,
        embed.shape,
        (4, 4, unit, weight.shape[1] // 4),
        (4, attend.shape[0], attend.shape[1] // 4),
        image.shape,
        tokens.shape,
        embed.shape,
    ]
    return pl.pallas_call(
        open_body,
        out_shape=[jax.ShapeDtypeStruct(shape, jnp.float32) for shape in shapes],
        in_specs=[ANY] * 6,
        out_specs=[ANY] * 9,
        scratch_shapes=[
            pltpu.VMEM(image.shape, jnp.float32),
            DMA((23,)),
            DMA((23,)),
            DMA((5,)),
            DMA((PARTS, 3)),
            DMA((PARTS, 3)),
            DMA((2 * PARTS, 3)),
            DMA((2 * PARTS, 3)),
            DMA((7,)),
            DMA((7,)),
            DMA((PARTS, 3)),
            DMA((PARTS, 3)),
        ],
        compiler_params=pltpu.CompilerParams(collective_id=collective, has_side_effects=True),
        name="open_exchange",
    )(image, packed, tokens, embed, weight, attend)


def rev(z):
    return 2 * lax.rem(z, 2) + lax.div(z, 2)


def plane_spot(level, me):
    return me, near_of(me, rev(level))


def home_spot(level, me):
    return rev(near_of(level, me)), level


def stream_setup(homeward=False):
    core = lax.axis_index("cond")
    level = lax.axis_index("pair")
    me = lax.axis_index("dp")
    greet((1 - core, level, me))
    for step in (1, 2, 3):
        greet((core, level, near_of(me, step)))
    pl.when(level > 0)(lambda: greet((core, level - 1, me)))
    pl.when(level < 3)(lambda: greet((core, level + 1, me)))
    ends = jnp.where(level == 0, 1, 0) + jnp.where(level == 3, 1, 0)
    expected = 6 - ends
    if homeward:
        moves = jnp.logical_or(level != 0, me != 0)
        back_up, back_over = plane_spot(level, me)
        pl.when(moves)(lambda: greet((core, back_up, back_over)))
        expected = expected + jnp.where(moves, 1, 0)
    pl.semaphore_wait(pltpu.get_barrier_semaphore(), expected)


def sum_stream(sections, scratch, hooks):
    (
        data,
        stage,
        first,
        second,
        own,
        load_sem,
        core_out,
        core_in,
        plane_out,
        plane_in,
        first_in,
        second_in,
        hop_out,
        cast_out,
        cast_low,
        final_in,
        keep_sem,
        pair_out,
        pair_in,
    ) = scratch
    ranges = []
    total = 0
    for kind, src, dst in sections:
        if kind == "plain":
            count, width = src.shape[1] // CHUNK, src.shape[2]
        else:
            count, width = 4 * (src.shape[2] // CHUNK), src.shape[3]
        ranges.append((total, total + count, kind, src, dst, width))
        total += count
    core = lax.axis_index("cond")
    level = lax.axis_index("pair")
    me = lax.axis_index("dp")
    mate = (1 - core, level, me)
    ring = data.shape[0]
    full = data.shape[2]

    def rank_of(j):
        return jnp.where(lax.rem(j, 2) == 0, level, 3 - level)

    def at_rank(j, rank):
        return (core, jnp.where(lax.rem(j, 2) == 0, rank, 3 - rank), me)

    def inside(j, low, high):
        return jnp.logical_and(j >= low, j < high)

    def swap_place(j):
        inner = False
        k = 0
        for low, high, kind, src, dst, width in ranges:
            if kind == "swap":
                here = inside(j, low, high)
                inner = jnp.logical_or(inner, here)
                k = jnp.where(here, j - low, k)
        return inner, k

    def moved(j):
        inner, k = swap_place(j)
        return jnp.logical_and(inner, lax.rem(k, 4) != 0)

    def kinds(j, action):
        narrow = False
        for low, high, kind, src, dst, width in ranges:
            if width != full:
                here = inside(j, low, high)
                narrow = jnp.logical_or(narrow, here)
                pl.when(here)(lambda width=width: action(width))
        pl.when(jnp.logical_not(narrow))(lambda: action(full))

    def cut(ref, width):
        return ref if ref.shape[-1] == width else ref.at[:, pl.ds(0, width)]

    def each_source(j, action):
        target = data.at[lax.rem(j, ring)]
        mine = own.at[lax.rem(j, 4)]
        for low, high, kind, src, dst, width in ranges:

            @pl.when(inside(j, low, high))
            def _(low=low, kind=kind, src=src, width=width):
                k = j - low
                if kind == "plain":
                    rows = pl.ds(pl.multiple_of(k * CHUNK, CHUNK), CHUNK)
                    action(lambda half: src.at[half, rows], target, mine)
                else:
                    rows = pl.ds(pl.multiple_of(lax.div(k, 4) * CHUNK, CHUNK), CHUNK)
                    spot = near_of(me, lax.rem(k, 4))
                    action(
                        lambda half: src.at[spot, half, rows], cut(target, width), cut(mine, width)
                    )

    def each_final(j, action):
        for low, high, kind, src, dst, width in ranges:

            @pl.when(inside(j, low, high))
            def _(low=low, kind=kind, dst=dst, width=width):
                k = j - low
                if kind == "plain":
                    rows = pl.ds(pl.multiple_of(k * CHUNK, CHUNK), CHUNK)
                    action(
                        lambda half: [(dst.at[half, rows], lambda x: x, 0)],
                        first.at[lax.rem(j, ring)],
                    )
                else:
                    rows = pl.ds(pl.multiple_of(lax.div(k, 4) * CHUNK, CHUNK), CHUNK)
                    spot = near_of(me, lax.rem(k, 4))
                    pieces = 1 if width == full else 3
                    piece = width // pieces

                    def targets(half):
                        found = []
                        for p in range(pieces):
                            columns = pl.ds(
                                pl.multiple_of(p * 4 * piece + spot * piece, piece), piece
                            )
                            found.append(
                                (
                                    dst.at[half, rows, columns],
                                    lambda x, p=p: x
                                    if x.shape[-1] == piece
                                    else x.at[:, pl.ds(p * piece, piece)],
                                    p,
                                )
                            )
                        return found

                    action(targets, stage.at[k])

    def core_copy(j, src, dst):
        return remote(src, dst, core_out.at[j], core_in.at[j], mate)

    def plane_copy(j, width):
        inner, k = swap_place(j)
        return remote(
            cut(first.at[lax.rem(j, ring)], width),
            cut(stage.at[k], width),
            plane_out.at[j],
            plane_in.at[j],
            (core, level, near_of(me, lax.rem(k, 4))),
        )

    def hop_first(j, src, rank, width):
        return remote(
            cut(src, width), cut(first.at[lax.rem(j, ring)], width), hop_out.at[j], first_in.at[j], at_rank(j, rank)
        )

    def hop_second(j, width):
        k = lax.div(j, 2)
        return remote(
            cut(data.at[lax.rem(j, ring)], width), cut(second.at[lax.rem(k, ring // 2)], width), hop_out.at[j], second_in.at[k],
            at_rank(j, 2),
        )

    def start(j):
        def go(source, target, mine):
            core_copy(j, source(1 - core), target).start()
            pltpu.make_async_copy(source(core), mine, load_sem.at[lax.rem(j, 4)]).start()

        each_source(j, go)

    def combine(j):
        def go(source, target, mine):
            pltpu.make_async_copy(source(core), mine, load_sem.at[lax.rem(j, 4)]).wait()
            core_copy(j, source(1 - core), target).wait_recv()
            target[...] += mine[...]

        each_source(j, go)

    def depart(j):
        rank = rank_of(j)

        def go(width):
            pl.when(rank == 0)(lambda: hop_first(j, data.at[lax.rem(j, ring)], 1, width).start())
            pl.when(rank == 3)(lambda: hop_second(j, width).start())

        kinds(j, go)

    def relay(j):
        def go(width):
            hop_first(j, data.at[lax.rem(j, ring)], 1, width).wait_recv()
            spot = lax.rem(j, ring)
            first[spot, :, :width] += data[spot, :, :width]
            hop_first(j, first.at[lax.rem(j, ring)], 2, width).start()

        pl.when(rank_of(j) == 1)(lambda: kinds(j, go))

    def casts(j, rank, half_targets, source, sems):
        return [
            remote(
                cut_of(source) if source is not None else ref, ref, sems.at[j, p], final_in.at[j, p],
                at_rank(j, rank),
            )
            for ref, cut_of, p in half_targets
        ]

    def pairs(j, half_targets, source):
        return [
            remote(
                cut_of(source) if source is not None else ref, ref, pair_out.at[j, p],
                pair_in.at[j, p], mate,
            )
            for ref, cut_of, p in half_targets
        ]

    def keeps(j, half_targets, source):
        return [
            pltpu.make_async_copy(cut_of(source), ref, keep_sem.at[j, p])
            for ref, cut_of, p in half_targets
        ]

    def root(j):
        def add(width):
            hop_first(j, first.at[lax.rem(j, ring)], 2, width).wait_recv()
            hop_second(j, width).wait_recv()
            spot = lax.rem(j, ring)
            first[spot, :, :width] += (
                data[spot, :, :width] + second[lax.rem(lax.div(j, 2), ring // 2), :, :width]
            )

        @pl.when(rank_of(j) == 2)
        def _():
            kinds(j, add)

            @pl.when(moved(j))
            def _():
                kinds(j, lambda width: plane_copy(j, width).start())

            inner, k = swap_place(j)

            @pl.when(jnp.logical_and(inner, jnp.logical_not(moved(j))))
            def _():
                stage[k] = first[lax.rem(j, ring)]

    def spread(j):
        def send(targets, source):
            goals = targets(core)
            for copy in (
                casts(j, 1, goals, source, cast_out)
                + casts(j, 3, goals, source, cast_low)
                + keeps(j, goals, source)
                + pairs(j, goals, source)
            ):
                copy.start()

        @pl.when(rank_of(j) == 2)
        def _():
            @pl.when(moved(j))
            def _():
                kinds(j, lambda width: plane_copy(j, width).wait_recv())

            each_final(j, send)

    def landed(j):
        rank = rank_of(j)

        def go(targets, source):
            goals = targets(core)
            for copy in casts(j, 1, goals, None, cast_out):
                copy.wait_recv()
            pl.when(rank == 1)(
                lambda: [copy.start() for copy in casts(j, 0, goals, None, cast_out)] and None
            )
            for copy in pairs(j, goals, None):
                copy.start()

        @pl.when(jnp.logical_or(rank == 1, rank == 3))
        def _():
            each_final(j, go)

    def arrived(j):
        def go(targets, source):
            goals = targets(core)
            for copy in casts(j, 0, goals, None, cast_out):
                copy.wait_recv()
            for copy in pairs(j, goals, None):
                copy.start()

        @pl.when(rank_of(j) == 0)
        def _():
            each_final(j, go)

    def finish(j):
        rank = rank_of(j)

        def sent(source, target, mine):
            core_copy(j, source(1 - core), target).wait_send()

        each_source(j, sent)

        @pl.when(jnp.logical_and(moved(j), rank == 2))
        def _():
            kinds(j, lambda width: plane_copy(j, width).wait_send())

        @pl.when(rank != 2)
        def _():
            kinds(j, lambda width: hop_first(j, data.at[lax.rem(j, ring)], 1, width).wait_send())

        def go(targets, source):
            goals = targets(core)

            @pl.when(jnp.logical_or(rank == 1, rank == 2))
            def _():
                for copy in casts(j, 1, goals, None, cast_out):
                    copy.wait_send()

            @pl.when(rank == 2)
            def _():
                for copy in casts(j, 3, goals, None, cast_low):
                    copy.wait_send()
                for copy in keeps(j, goals, source):
                    copy.wait()

            for copy in pairs(j, goals, None):
                copy.wait()

        each_final(j, go)

    stages = (
        (0, start),
        (3, combine),
        (5, depart),
        (8, relay),
        (11, root),
        (14, spread),
        (17, landed),
        (20, arrived),
        (23, finish),
    )

    def step(t, carry):
        for lag, stage_of in stages:
            j = t - lag

            @pl.when(jnp.logical_and(j >= 0, j < total))
            def _(j=j, stage_of=stage_of):
                stage_of(j)

        for low, high, hook in hooks:
            pl.when(jnp.logical_and(t >= low, t < high))(lambda hook=hook, low=low: hook(t - low))
        return carry

    lax.fori_loop(0, total + 23, step, 0)


def stream_scratch(total, most, width):
    ring = 32
    return [
        pltpu.VMEM((ring, CHUNK, width), jnp.float32),
        pltpu.VMEM((most, CHUNK, width), jnp.float32),
        pltpu.VMEM((ring, CHUNK, width), jnp.float32),
        pltpu.VMEM((ring // 2, CHUNK, width), jnp.float32),
        pltpu.VMEM((4, CHUNK, width), jnp.float32),
        DMA((4,)),
        DMA((total,)),
        DMA((total,)),
        DMA((total,)),
        DMA((total,)),
        DMA((total,)),
        DMA(((total + 1) // 2,)),
        DMA((total,)),
        DMA((total, 3)),
        DMA((total, 3)),
        DMA((total, 3)),
        DMA((total, 3)),
        DMA((total, 3)),
        DMA((total, 3)),
    ]


SCRATCH = 19


def near_slots(shares, arrived, send, recv, base):
    core = lax.axis_index("cond")
    level = lax.axis_index("pair")
    me = lax.axis_index("dp")
    return [
        remote(
            shares.at[step], arrived.at[step - 1], send.at[base + step - 1],
            recv.at[base + step - 1], (core, level, near_of(me, step)),
        )
        for step in (3, 1, 2)
    ]


def near_blocks(block, everyone, send, recv, base):
    core = lax.axis_index("cond")
    level = lax.axis_index("pair")
    me = lax.axis_index("dp")
    return [
        remote(
            block, everyone.at[step], send.at[base + step - 1], recv.at[base + step - 1],
            (core, level, near_of(me, step)),
        )
        for step in (3, 1, 2)
    ]


def row_stats(rows):
    centered = rows - jnp.mean(rows, axis=-1, keepdims=True)
    inverse = lax.rsqrt(jnp.mean(centered * centered, axis=-1, keepdims=True) + EPSILON)
    return centered * inverse, inverse


def halves(value):
    high = value.astype(jnp.bfloat16)
    return high, (value - high.astype(jnp.float32)).astype(jnp.bfloat16)


def three_pass(left, right, dims):
    def one(x, y):
        return lax.dot_general(x, y, (dims, ((), ())), preferred_element_type=jnp.float32)

    return one(left[0], right[1]) + one(left[1], right[0]) + one(left[0], right[0])


TILE = 256


def backward_body(
    output_ref, attend_ref, two_ref, text_ref, cot_ref, one_ref, response_ref, reduce_w_ref,
    act_ref, slope_ref, normed_ref, expand_w_ref, conv_ref, out_ref, base_ref, small_ref,
    rows_ref, embed_ref, silu_ref,
    output_out, attend_out, mapper_out, reduce_out, small_out, expand_out,
    mapper_part, reduce_part, expand_part, one_out, text_out, grad_out, layer_out,
    *scratch
):
    (
        front_got, front_own, conv, grad, one, out_got, out_own, base, small, wide, high, low,
        weights, acts, slopes, columns, product, front, sums, spread_own, spread_got,
        text_got, text_own, text_all, ratio, mapped,
    ) = scratch[SCRATCH : SCRATCH + 26]
    (
        send, recv, keep, tile_out, tile_in, load, front_out, front_in, spread_out, spread_in,
        piece_out, piece_in, text_out_sem, text_in_sem,
    ) = scratch[SCRATCH + 26 :]
    stream_setup(True)
    core = lax.axis_index("cond")
    level = lax.axis_index("pair")
    me = lax.axis_index("dp")
    moves = jnp.logical_or(level != 0, me != 0)
    up, over = home_spot(level, me)
    pixels, chan = conv.shape
    spots = wide.shape[0]
    texts = text_own.shape[0]
    count = chan // TILE
    scatters = near_slots(two_ref, front_got, send, recv, 0)
    scatters += near_slots(text_ref, text_got, send, recv, 6)
    start_loads = [
        pltpu.make_async_copy(src, dst, keep.at[6 + i])
        for i, (src, dst) in enumerate(
            ((two_ref.at[0], front_own), (text_ref.at[0], text_own), (cot_ref, conv), (one_ref, one))
        )
    ]

    def near_tile(i):
        rows = pl.ds(pl.multiple_of(i * 16, 16), 16)
        return [
            remote(
                grad.at[rows],
                wide.at[pl.ds(pl.multiple_of(step * pixels + i * 16, 16), 16)],
                piece_out.at[i, step - 1],
                piece_in.at[i, step - 1],
                (core, level, near_of(me, step)),
            )
            for step in (3, 1, 2)
        ]

    def late():
        found = []
        for step in (3, 1, 2):
            device = (core, level, near_of(me, step))
            found.append(
                remote(
                    text_all.at[0], text_all.at[step], text_out_sem.at[step - 1],
                    text_in_sem.at[step - 1], device,
                )
            )
            found.append(
                remote(
                    ratio.at[0], ratio.at[step], text_out_sem.at[2 + step],
                    text_in_sem.at[2 + step], device,
                )
            )
        return found

    one_kept = pltpu.make_async_copy(grad, one_out, keep.at[10])
    text_kept = pltpu.make_async_copy(text_all, text_out, keep.at[11])

    def arrive(t):
        for copy in start_loads + scatters:
            copy.wait()
        ratio[0] = jnp.zeros_like(ratio[0])
        text_all[0] = jnp.zeros_like(text_all[0])
        text_all[0, 0:texts] = text_own[...] + text_got[0] + text_got[1] + text_got[2]

    def normalize(t):
        scale = rows_ref[6:7]
        shift = rows_ref[7:8]
        for half in range(2):
            rows = pl.ds(pl.multiple_of(t * 16 + half * 8, 8), 8)
            back = front_own[rows] + front_got[0, rows] + front_got[1, rows] + front_got[2, rows]
            hidden = one[rows]
            normed, inverse = row_stats(hidden * scale + shift)
            two = conv[rows] + inverse * (
                back
                - jnp.mean(back, axis=-1, keepdims=True)
                - normed * jnp.mean(back * normed, axis=-1, keepdims=True)
            )
            grad[rows] = two * scale
            ratio[0, 0:8] += two * hidden
            ratio[0, 8:16] += two
        for copy in near_tile(t):
            copy.start()

    def give_late(t):
        for copy in late():
            copy.start()
        one_kept.start()
        wide[0:pixels] = grad[...]

    def gathered(t):
        def wait(i, carry):
            for copy in near_tile(i):
                copy.wait()
            return carry

        lax.fori_loop(0, pixels // 16, wait, 0)
        for copy in late():
            copy.wait()
        one_kept.wait()
        text_kept.start()

        def piece(i, carry):
            rows = pl.ds(pl.multiple_of(i * 16, 16), 16)
            high[rows], low[rows] = halves(wide[rows])
            return carry

        lax.fori_loop(0, spots // 16, piece, 0)

    def mapper_stores():
        half = mapper_part.shape[1]
        return [
            pltpu.make_async_copy(
                mapped.at[pl.ds(c * half, half)], mapper_part.at[c], load.at[10 + c]
            )
            for c in (0, 1)
        ]

    def text_products(t):
        left = halves(silu_ref[...])

        def strip(k, carry):
            cols = pl.ds(pl.multiple_of(k * TILE, TILE), TILE)
            right = halves(text_all[:, :, cols].reshape(-1, TILE))
            mapped[:, cols] = three_pass(left, right, ((0,), (0,)))
            return carry

        lax.fori_loop(0, count, strip, 0)
        for copy in mapper_stores():
            copy.start()
        column_pair(0)[0].start()
        column_pair(0)[1].start()
        first_loads[0].wait()
        total = ratio[0] + ratio[1] + ratio[2] + ratio[3]
        scale_sum = jnp.sum(total[0:8], axis=0, keepdims=True)
        shift_sum = jnp.sum(total[8:16], axis=0, keepdims=True)
        odd = lax.rem(lax.broadcasted_iota(jnp.int32, (CHUNK, chan), 0), 2) == 1
        both = jnp.where(odd, shift_sum, scale_sum)
        small[0] = both * embed_ref[:, 0:1]
        sums[4:5] = scale_sum
        sums[5:6] = shift_sum
        sums[6:7] = jnp.sum(wide[...], axis=0, keepdims=True)
        sums[7:8] = jnp.sum(text_all[...].reshape(-1, chan), axis=0, keepdims=True)
        width = chan // 4
        place = pl.ds(pl.multiple_of(me * width, width), width)
        small[1, 3:4, 0:width] = sums[6:7, place]
        small[1, 3:4, width : 2 * width] = sums[7:8, place]
        pair_place = pl.ds(pl.multiple_of(lax.rem(me, 2) * 2 * width, width), 2 * width)
        small[1, 4:5, width : 3 * width] = jnp.where(
            me < 2, sums[4:5, pair_place], sums[5:6, pair_place]
        )

    def column_pair(i):
        return [
            pltpu.make_async_copy(
                response_ref.at[
                    :, pl.ds(pl.multiple_of(c * (chan // 2) + i * 128, 128), 128)
                ],
                columns.at[lax.rem(i, 2), :, pl.ds(c * 128, 128)],
                load.at[6 + lax.rem(i, 2) if c == 0 else 12 + lax.rem(i, 2)],
            )
            for c in (0, 1)
        ]

    def reduce_stores(i):
        return [
            pltpu.make_async_copy(
                product.at[pl.ds(c * 128, 128)],
                reduce_part.at[c, pl.ds(pl.multiple_of(i * 128, 128), 128)],
                load.at[8 + c],
            )
            for c in (0, 1)
        ]

    def reduce_outer(i):
        for copy in column_pair(i):
            copy.wait()

        @pl.when(i + 1 < count)
        def _():
            for copy in column_pair(jnp.minimum(i + 1, count - 1)):
                copy.start()

        @pl.when(i + 1 == count)
        def _():
            weight_load(reduce_w_ref, 0).start()
            act_load(0).start()

        @pl.when(i > 0)
        def _():
            for copy in reduce_stores(jnp.maximum(i - 1, 0)):
                copy.wait()

        @pl.when(i == 0)
        def _():
            for copy in mapper_stores():
                copy.wait()

        left = halves(columns[lax.rem(i, 2), :, 0:TILE])

        def strip(k, carry):
            cols = pl.ds(pl.multiple_of(k * TILE, TILE), TILE)
            product[0:TILE, cols] = three_pass(left, (high[:, cols], low[:, cols]), ((0,), (0,)))
            return carry

        lax.fori_loop(0, count, strip, 0)
        for copy in reduce_stores(i):
            copy.start()

    def settle_reduce(t):
        for copy in reduce_stores(count - 1):
            copy.wait()
        text_kept.wait()
        for copy in loads:
            copy.start()
        sums[0:4] = jnp.zeros((4, chan), jnp.float32)

    outward = near_slots(out_ref, out_got, send, recv, 3)

    def away(i):
        rows = pl.ds(pl.multiple_of(i * 8, 8), 8)
        return remote(
            base.at[rows], layer_out.at[rows], tile_out.at[i], tile_in.at[i], (core, up, over)
        )

    def here(i):
        rows = pl.ds(pl.multiple_of(i * 8, 8), 8)
        return pltpu.make_async_copy(base.at[rows], layer_out.at[rows], tile_out.at[i])

    first_loads = [pltpu.make_async_copy(small_ref, small, keep.at[1])]
    loads = [
        pltpu.make_async_copy(conv_ref, conv, keep.at[2]),
        pltpu.make_async_copy(out_ref.at[0], out_own, keep.at[3]),
        pltpu.make_async_copy(base_ref, base, keep.at[4]),
    ]
    kept = pltpu.make_async_copy(one, grad_out, keep.at[5])

    def tile_rows(i):
        return pl.ds(pl.multiple_of(i * TILE, TILE), TILE)

    def weight_load(ref, i):
        return pltpu.make_async_copy(
            ref.at[tile_rows(i)], weights.at[lax.rem(i, 2)], load.at[lax.rem(i, 2)]
        )

    def act_load(i):
        return pltpu.make_async_copy(
            act_ref.at[:, tile_rows(i)], acts.at[lax.rem(i, 2)], load.at[2 + lax.rem(i, 2)]
        )

    def slope_load(i):
        return pltpu.make_async_copy(
            slope_ref.at[:, tile_rows(i)], slopes.at[lax.rem(i, 2)], load.at[4 + lax.rem(i, 2)]
        )

    part = columns.shape[2]

    def column_load(i):
        return pltpu.make_async_copy(
            normed_ref.at[:, pl.ds(pl.multiple_of(i * part, part), part)],
            columns.at[lax.rem(i, 2)],
            load.at[6 + lax.rem(i, 2)],
        )

    def product_stores(i):
        half = part // 2
        return [
            pltpu.make_async_copy(
                product.at[pl.ds(c * half, half)], expand_part.at[i, c], load.at[8 + c]
            )
            for c in (0, 1)
        ]

    def front_sends(i):
        found = []
        for step in (3, 1, 2):
            found.append(
                remote(
                    front.at[lax.rem(i, 2), pl.ds(step * pixels, pixels)],
                    front_got.at[step - 1, :, tile_rows(i)],
                    front_out.at[i, step - 1],
                    front_in.at[i, step - 1],
                    (core, level, near_of(me, step)),
                )
            )
        return found

    for copy in scatters + start_loads + first_loads:
        copy.start()

    def respond(i):
        weight_load(reduce_w_ref, i).wait()
        act_load(i).wait()

        @pl.when(i + 1 < count)
        def _():
            weight_load(reduce_w_ref, i + 1).start()
            act_load(i + 1).start()

        @pl.when(i + 1 == count)
        def _():
            act_load(0).start()
            slope_load(0).start()

        right = halves(weights[lax.rem(i, 2)])
        cols = tile_rows(i)

        def strip(k, carry):
            rows = pl.ds(pl.multiple_of(k * pixels, pixels), pixels)
            value = three_pass((high[rows], low[rows]), right, ((1,), (1,)))
            wide[rows, cols] = value
            sums[0:1, cols] += jnp.sum(value * acts[lax.rem(i, 2), rows], axis=0, keepdims=True)
            sums[1:2, cols] += jnp.sum(value, axis=0, keepdims=True)
            return carry

        lax.fori_loop(0, 4, strip, 0)

    def spreads():
        return [
            remote(
                spread_own, spread_got.at[step - 1], spread_out.at[step - 1],
                spread_in.at[step - 1], (core, level, near_of(me, step)),
            )
            for step in (3, 1, 2)
        ]

    def send_out(t):
        for copy in outward:
            copy.start()

    def share(t):
        total = jnp.sum(sums[0:1] * rows_ref[0:1] * rows_ref[1:2], axis=1, keepdims=True)
        spread_own[...] = jnp.broadcast_to(total, spread_own.shape)
        for copy in spreads():
            copy.start()

    def agree(t):
        for copy in spreads():
            copy.wait()
        total = spread_own[...] + spread_got[0] + spread_got[1] + spread_got[2]
        total = jnp.max(total[0:1], axis=1, keepdims=True)
        inverse = rows_ref[3:4]
        norms = rows_ref[1:2]
        grad_norms = (
            sums[0:1] * rows_ref[0:1] * inverse - total * rows_ref[4:5] * inverse * inverse
        )
        sums[2:3] = grad_norms / norms
        small[1, 1:2] = sums[0:1] * rows_ref[5:6]
        small[1, 2:3] = sums[1:2]

    def bend(i):
        act_load(i).wait()
        slope_load(i).wait()

        @pl.when(i + 1 < count)
        def _():
            act_load(i + 1).start()
            slope_load(i + 1).start()

        @pl.when(i + 1 == count)
        def _():
            column_load(0).start()
            weight_load(expand_w_ref, 0).start()

        cols = tile_rows(i)
        factor = rows_ref[2:3, cols]
        twice = sums[2:3, cols]

        def strip(k, carry):
            rows = pl.ds(pl.multiple_of(k * 48, 48), 48)
            value = (
                wide[rows, cols] * factor + acts[lax.rem(i, 2), rows] * twice
            ) * slopes[lax.rem(i, 2), rows]
            high[rows, cols], low[rows, cols] = halves(value)
            sums[3:4, cols] += jnp.sum(value, axis=0, keepdims=True)
            return carry

        lax.fori_loop(0, spots // 48, strip, 0)

    def outer(i):
        column_load(i).wait()
        pl.when(i + 1 < 4)(lambda: column_load(jnp.minimum(i + 1, 3)).start())
        pl.when(i > 0)(lambda: [copy.wait() for copy in product_stores(jnp.maximum(i - 1, 0))] and None)
        left = halves(columns[lax.rem(i, 2)])

        def strip(k, carry):
            cols = pl.ds(pl.multiple_of(k * TILE, TILE), TILE)
            product[:, cols] = three_pass(left, (high[:, cols], low[:, cols]), ((0,), (0,)))
            return carry

        lax.fori_loop(0, count, strip, 0)
        for copy in product_stores(i):
            copy.start()

    def settle_outer(t):
        for copy in product_stores(3):
            copy.wait()
        small[1, 0:1] = sums[3:4]

    def backward(i):
        weight_load(expand_w_ref, i).wait()
        pl.when(i + 1 < count)(lambda: weight_load(expand_w_ref, jnp.minimum(i + 1, count - 1)).start())

        @pl.when(i > 1)
        def _():
            for copy in front_sends(jnp.maximum(i - 2, 0)):
                copy.wait_send()

        right = halves(weights[lax.rem(i, 2)])

        def strip(k, carry):
            rows = pl.ds(pl.multiple_of(k * pixels, pixels), pixels)
            front[lax.rem(i, 2), rows] = three_pass((high[rows], low[rows]), right, ((1,), (1,)))
            return carry

        lax.fori_loop(0, 4, strip, 0)
        front_own[:, tile_rows(i)] = front[lax.rem(i, 2), 0:pixels]
        for copy in front_sends(i):
            copy.start()

    def middle(t):
        loads[0].wait()
        for i in range(count):
            for copy in front_sends(i):
                copy.wait_recv()
                if i >= count - 2:
                    copy.wait_send()

    def tiles(t):
        def tile(i, carry):
            rows = pl.ds(pl.multiple_of(i * 8, 8), 8)
            back = front_own[rows] + front_got[0, rows] + front_got[1, rows] + front_got[2, rows]
            normed, inverse = row_stats(conv[rows])
            one[rows] = inverse * (
                back
                - jnp.mean(back, axis=-1, keepdims=True)
                - normed * jnp.mean(back * normed, axis=-1, keepdims=True)
            )
            return carry

        size = pixels // 48
        lax.fori_loop(t * size, (t + 1) * size, tile, 0)

    def give(t):
        kept.start()

    def outlet(t):
        pl.when(t == 0)(lambda: [copy.wait() for copy in loads[1:] + outward] and None)
        rows = pl.ds(pl.multiple_of(t * 8, 8), 8)
        base[rows] += out_own[rows] + out_got[0, rows] + out_got[1, rows] + out_got[2, rows]
        pl.when(moves)(away(t).start)
        pl.when(jnp.logical_not(moves))(here(t).start)

    sum_stream(
        [
            ("plain", output_ref, output_out),
            ("swap", attend_ref, attend_out),
            ("plain", mapper_part, mapper_out),
            ("plain", reduce_part, reduce_out),
            ("plain", small, small_out),
            ("swap", expand_part, expand_out),
        ],
        scratch[:SCRATCH],
        [
            (12, 13, arrive),
            (12, 21, normalize),
            (21, 22, give_late),
            (24, 25, gathered),
            (25, 26, text_products),
            (26, 32, reduce_outer),
            (32, 33, settle_reduce),
            (33, 39, respond),
            (39, 40, share),
            (40, 41, agree),
            (41, 47, bend),
            (47, 51, outer),
            (51, 52, settle_outer),
            (52, 58, backward),
            (68, 69, middle),
            (68, 74, tiles),
            (74, 75, give),
            (60, 78, outlet),
            (43, 44, send_out),
        ],
    )
    kept.wait()

    def settle(i, carry):
        pl.when(moves)(away(i).wait)
        pl.when(jnp.logical_not(moves))(here(i).wait)
        return carry

    lax.fori_loop(0, base.shape[0] // 8, settle, 0)


def backward_sums(
    collective, output_part, attend_part, two_share, text_share, cot, one, response, reduce_w, act,
    slope, normed_all, expand_w, conv, out_share, base, small, rows, embed, silu, mapper_half
):
    pixels, chan = conv.shape
    spots = normed_all.shape[0]
    texts = text_share.shape[1]
    slots = silu.shape[0] // 4
    f32, bf16 = jnp.float32, jnp.bfloat16
    half = chan // 8
    count = chan // TILE

    def shape(*dims):
        return jax.ShapeDtypeStruct(dims, f32)

    total = (half + 8 * half // 2 + mapper_half + chan // 2 + CHUNK + 8 * half // 2) // CHUNK
    block = (pixels, chan)
    return pl.pallas_call(
        backward_body,
        out_shape=[
            shape(2, half, chan),
            shape(2, half, 3 * chan),
            shape(2, mapper_half, chan),
            shape(2, chan // 2, chan),
            shape(2, CHUNK, chan),
            shape(2, half, 4 * chan),
            shape(2, mapper_half, chan),
            shape(2, chan // 2, chan),
            shape(4, 2, half, chan),
            shape(*block),
            shape(4, slots, chan),
            shape(*block),
            shape(*block),
        ],
        in_specs=[ANY] * 16 + [pl.BlockSpec(memory_space=pltpu.VMEM)] * 3,
        out_specs=[ANY] * 13,
        scratch_shapes=stream_scratch(total, 4 * half // CHUNK, chan)
        + [
            pltpu.VMEM((3,) + block, f32),
            pltpu.VMEM(block, f32),
            pltpu.VMEM(block, f32),
            pltpu.VMEM(block, f32),
            pltpu.VMEM(block, f32),
            pltpu.VMEM((3,) + block, f32),
            pltpu.VMEM(block, f32),
            pltpu.VMEM(block, f32),
            pltpu.VMEM(small.shape, f32),
            pltpu.VMEM((spots, chan), f32),
            pltpu.VMEM((spots, chan), bf16),
            pltpu.VMEM((spots, chan), bf16),
            pltpu.VMEM((2, TILE, chan), f32),
            pltpu.VMEM((2, spots, TILE), f32),
            pltpu.VMEM((2, spots, TILE), f32),
            pltpu.VMEM((2, spots, chan // 4), f32),
            pltpu.VMEM((chan // 4, chan), f32),
            pltpu.VMEM((2, spots, TILE), f32),
            pltpu.VMEM((8, chan), f32),
            pltpu.VMEM((8, 128), f32),
            pltpu.VMEM((3, 8, 128), f32),
            pltpu.VMEM((3, texts, chan), f32),
            pltpu.VMEM((texts, chan), f32),
            pltpu.VMEM((4, slots, chan), f32),
            pltpu.VMEM((4, 16, chan), f32),
            pltpu.VMEM((silu.shape[1], chan), f32),
            DMA((9,)),
            DMA((9,)),
            DMA((12,)),
            DMA((pixels // 8,)),
            DMA((pixels // 8,)),
            DMA((14,)),
            DMA((count, 3)),
            DMA((count, 3)),
            DMA((3,)),
            DMA((3,)),
            DMA((pixels // 16, 3)),
            DMA((pixels // 16, 3)),
            DMA((6,)),
            DMA((6,)),
        ],
        compiler_params=pltpu.CompilerParams(
            collective_id=collective, has_side_effects=True, vmem_limit_bytes=62 * 2**20
        ),
        name="backward_sums",
    )(
        output_part, attend_part, two_share, text_share, cot, one, response, reduce_w, act, slope,
        normed_all, expand_w, conv, out_share, base, small, rows, embed, silu,
    )


def close_body(grad_in, token_in, conv_in, grad_home, token_home, conv_all, hold, send, recv, keep):
    core = lax.axis_index("cond")
    level = lax.axis_index("pair")
    me = lax.axis_index("dp")
    up, over = home_spot(level, me)
    back_up, back_over = plane_spot(level, me)
    moves = jnp.logical_or(level != 0, me != 0)
    others = [(c, s) for c in (0, 1) for s in (0, 1, 2, 3) if (c, s) != (0, 0)]

    def other(c, s):
        return (lax.rem(core + c, 2), lax.rem(level + s, 4), me)

    for c, s in others:
        greet(other(c, s))
    pl.when(moves)(lambda: greet((core, back_up, back_over)))
    pl.semaphore_wait(pltpu.get_barrier_semaphore(), 7 + jnp.where(moves, 1, 0))
    swaps = ((grad_in, grad_home), (token_in, token_home))
    aways = [remote(src, dst, send.at[i], recv.at[i], (core, up, over)) for i, (src, dst) in enumerate(swaps)]
    spreads = [
        remote(conv_in, conv_all.at[1 + i], send.at[2 + i], recv.at[2 + i], other(c, s))
        for i, (c, s) in enumerate(others)
    ]
    mine = pltpu.make_async_copy(conv_in, conv_all.at[0], keep.at[2])
    for copy in spreads + [mine]:
        copy.start()
    for away in aways:
        pl.when(moves)(away.start)

    @pl.when(jnp.logical_not(moves))
    def _():
        load = pltpu.make_async_copy(grad_in, hold, keep.at[0])
        store = pltpu.make_async_copy(hold, grad_home, keep.at[0])
        small = pltpu.make_async_copy(token_in, token_home, keep.at[1])
        small.start()
        load.start()
        load.wait()
        store.start()
        store.wait()
        small.wait()

    for copy in spreads + [mine]:
        copy.wait()
    for away in aways:
        pl.when(moves)(away.wait)


def close_exchange(collective, grad, tokens, conv):
    shapes = [grad.shape, tokens.shape, (8,) + conv.shape]
    return pl.pallas_call(
        close_body,
        out_shape=[jax.ShapeDtypeStruct(shape, jnp.float32) for shape in shapes],
        in_specs=[ANY] * 3,
        out_specs=[ANY] * 3,
        scratch_shapes=[pltpu.VMEM(grad.shape, jnp.float32), DMA((9,)), DMA((9,)), DMA((3,))],
        compiler_params=pltpu.CompilerParams(collective_id=collective, has_side_effects=True),
        name="close_exchange",
    )(grad, tokens, conv)


def plane_body(
    latents,
    ratio_embed,
    clip_tokens,
    cotangent,
    conv_kernel,
    conv_bias,
    expand_weight,
    expand_bias,
    response_gain,
    response_bias,
    reduce_weight,
    reduce_bias,
    ratio_weight,
    ratio_bias,
    text_weight,
    text_bias,
    attend_weight,
    query_bias,
    value_bias,
    output_weight,
    output_bias,
):
    size = lax.axis_size("dp")
    core = lax.axis_index("cond")
    me = lax.axis_index("dp")
    level = lax.axis_index("pair")
    quarter = home_spot(level, me)[0]
    order = jnp.bitwise_xor(jnp.arange(4), me)
    _, rows, cols, chan = latents.shape
    pixels = rows * cols
    part = chan // size
    hid = size * expand_bias.shape[0]
    texts = clip_tokens.shape[1]
    packed = jnp.concatenate(
        [
            conv_kernel.reshape(9, part),
            conv_bias[None],
            reduce_bias[None],
            text_bias[None],
            output_bias[None],
            ratio_bias.reshape(2, part),
        ],
        axis=0,
    )
    row_padded, every, tokens, embed, expand_w, attend_units = open_exchange(
        3, latents[0], packed, clip_tokens[0], ratio_embed, expand_weight, attend_weight
    )[:6]
    row_padded = row_padded.at[:1].set(jnp.where(quarter > 0, row_padded[:1], 0.0))
    row_padded = row_padded.at[-1:].set(jnp.where(quarter < size - 1, row_padded[-1:], 0.0))
    image = row_padded[1:-1]
    expand_w = expand_w.reshape(chan, -1)
    channel_rows = every[:, :13].transpose(1, 0, 2).reshape(13, chan)
    kernel = channel_rows[:9].reshape(3, 3, chan)
    conv_shift, reduce_b, text_b, out_b = (channel_rows[9 + i] for i in range(4))
    ratio_b = every[:, 13:].reshape(2 * chan)

    half = part // 2
    wide = hid // size
    text_part = text_weight.shape[0]
    token_cols = [
        lax.dynamic_slice(tokens, (0, near_of(me, step) * text_part), (texts, text_part))
        for step in range(4)
    ]
    ratio_part = ratio_weight.shape[0]
    embed_part = lax.dynamic_slice(embed, (0, me * ratio_part), (1, ratio_part))
    mod_part = jnp.dot(embed_part, ratio_weight, precision=HIGHEST_ACCURACY)

    padded = jnp.pad(row_padded, ((0, 0), (1, 1), (0, 0)))
    total_conv = conv_shift
    for i in range(3):
        for j in range(3):
            total_conv = total_conv + padded[i : i + rows, j : j + cols] * kernel[i, j]
    normed, inverse = norm_stats(total_conv.reshape(pixels, chan))
    normed_all, mod_near, near_tokens, attend_w = exchange(
        4,
        gathers=(normed, mod_part),
        scatters=(jnp.stack(token_cols),),
        relay=(attend_units,),
    )
    attend_w = attend_w.reshape(chan, 3 * part)
    modulation = jnp.sum(mod_near[:, 0], axis=0) + ratio_b
    mod_scale = 1.0 + modulation[:chan]
    mod_shift = modulation[chan:]
    normed_all = normed_all.reshape(size * pixels, chan)
    cot, normed_all = lax.optimization_barrier((cotangent[0].reshape(pixels, chan), normed_all))
    turns = (0, 2, 1, 3)
    grid = [(z, d) for z in range(size) for d in range(size)]
    cot = lax.ppermute(
        cot, ("pair", "dp"), [(z * size + d, z * size + (d ^ turns[z])) for z, d in grid]
    )
    near_tokens = jnp.concatenate([token_cols[0], near_tokens.reshape(-1, text_part)], axis=0)
    silu_near = jax.nn.silu(near_tokens)
    mapped_share = dot(silu_near, text_weight).reshape(4, texts, chan)
    hidden = dot(normed_all, expand_w) + expand_bias
    bell = 0.5 * (1.0 + lax.erf(hidden * 0.5**0.5))
    activated = hidden * bell
    density = jnp.exp(-0.5 * hidden * hidden) * (2.0 * jnp.pi) ** -0.5
    slope = bell + hidden * density
    totals = jnp.sum(activated * activated, axis=0)
    norms = jnp.sqrt(totals + EPSILON)
    norm_sums = exchange(5, gathers=(jnp.full((8, 128), jnp.sum(norms)),))[0]
    middle = jnp.sum(norm_sums[:, 0, 0]) / hid + EPSILON
    scaled = norms / middle
    factor = 1.0 + response_gain * scaled
    response = activated * factor + response_bias
    one_share = dot(response, reduce_weight).reshape(4, pixels, chan)
    cot, one_share = lax.optimization_barrier((cot, one_share))
    cot = lax.ppermute(
        cot, ("pair", "dp"), [(z * size + d, (d ^ turns[z]) * size + d) for z, d in grid]
    )
    one_arrived, mapped_arrived = exchange(6, scatters=(one_share, mapped_share))
    mapped = mapped_share[0] + jnp.sum(mapped_arrived, axis=0) + text_b
    hidden_one = one_share[0] + jnp.sum(one_arrived, axis=0) + image.reshape(pixels, chan) + reduce_b
    hidden_two = hidden_one * mod_scale + mod_shift
    normed_two, inverse_two = norm_stats(hidden_two)
    cot, normed_two = lax.optimization_barrier((cot, normed_two))
    normed_two_all, mapped_all = exchange(7, gathers=(normed_two, mapped))
    cot, normed_two_all = lax.optimization_barrier((cot, normed_two_all))
    cot_all = jnp.concatenate(
        [cot]
        + [lax.ppermute(cot, "dp", [(i, i ^ step) for i in range(size)]) for step in (1, 2, 3)],
        axis=0,
    )
    normed_two_all = normed_two_all.reshape(size * pixels, chan)
    mapped_all = mapped_all.reshape(size * texts, chan)

    source = jnp.concatenate([normed_two_all, mapped_all], axis=0)
    query = dot(normed_two_all, attend_w[:, :part]) + query_bias
    key_value = dot(source, attend_w[:, part:])
    key = key_value[:, :part]
    value = key_value[:, part:] + value_bias
    query_h, key_h, value_h = heads_of(query), heads_of(key), heads_of(value)
    scores = jnp.einsum("iuy,ouy->uio", query_h, key_h, precision=FAST) * HEAD_CHANNELS ** (-0.5)
    expo = jnp.exp(scores - jnp.max(scores, axis=-1, keepdims=True))
    probs = expo / jnp.sum(expo, axis=-1, keepdims=True)
    mixture_h = jnp.einsum("uio,ouy->iuy", probs, value_h, precision=FAST)
    mixture = mixture_h.reshape(query.shape)
    out_share = dot(mixture, output_weight).reshape(4, pixels, chan)
    out_base = hidden_two + out_b

    output_grad = t_dot(mixture, cot_all)
    grad_mix_h = heads_of(dot_t(cot_all, output_weight))
    grad_probs = jnp.einsum("iuy,ouy->uio", grad_mix_h, value_h, precision=FAST)
    delta = jnp.sum(grad_mix_h * mixture_h, axis=-1).T
    grad_scores = probs * (grad_probs - delta[..., None]) * HEAD_CHANNELS ** (-0.5)
    grad_query = jnp.einsum("uio,ouy->iuy", grad_scores, key_h, precision=FAST).reshape(query.shape)
    grad_key = jnp.einsum("uio,iuy->ouy", grad_scores, query_h, precision=FAST).reshape(key.shape)
    grad_value = jnp.einsum("uio,iuy->ouy", probs, grad_mix_h, precision=FAST).reshape(key.shape)
    spots = size * pixels
    grad_kv = jnp.concatenate([grad_key, grad_value], axis=1)
    grad_qkv = jnp.concatenate([grad_query, grad_kv[:spots]], axis=1)
    two_share = dot_t(grad_qkv, attend_w).reshape(4, pixels, chan)
    text_share = dot_t(grad_kv[spots:], attend_w[:, part:]).reshape(4, texts, chan)
    attend_grad = t_dot(normed_two_all, grad_qkv)
    attend_grad = attend_grad.at[:, part:].add(t_dot(mapped_all, grad_kv[spots:]))
    def row(value):
        return jnp.sum(value, axis=0, keepdims=True)

    def mine(value):
        width = value.shape[1] // size
        return lax.dynamic_slice(value, (0, me * width), (value.shape[0], width))

    gap = jnp.zeros((1, part), jnp.float32)
    small_rows = jnp.concatenate(
        [
            jnp.zeros((3, chan), jnp.float32),
            jnp.concatenate([gap, gap, row(grad_query), row(grad_value)], axis=1),
            jnp.concatenate([row(mine(cot_all)), gap, gap, gap], axis=1),
            jnp.zeros((CHUNK - 5, chan), jnp.float32),
        ],
        axis=0,
    )
    one_row = jnp.full((1, chan), 1.0, jnp.float32)
    back_rows = jnp.concatenate(
        [
            response_gain[None],
            norms[None],
            factor[None],
            one_row / middle,
            one_row / hid,
            scaled[None],
            mod_scale[None],
            mod_shift[None],
        ],
        axis=0,
    )
    slots = (texts + 7) // 8 * 8
    silu_padded = jnp.pad(
        silu_near.reshape(4, texts, text_part), ((0, 0), (0, slots - texts), (0, -text_part % 128))
    ).reshape(4 * slots, -1)
    embed_rows = jnp.broadcast_to(
        embed_part.reshape(ratio_part, 1, 1), (ratio_part, 2, 128)
    ).reshape(2 * ratio_part, 128)
    (
        output_sum, attend_sum, mapper_sum, reduce_sum, small, expand_sum, _, _, _,
        grad_one, grad_mapped_all, grad_conv, layer_output,
    ) = backward_sums(
        1,
        output_grad.reshape(2, half, chan),
        attend_grad.reshape(size, 2, half, 3 * part),
        two_share,
        text_share,
        cot,
        hidden_one,
        response,
        reduce_weight,
        activated,
        slope,
        normed_all,
        expand_w,
        total_conv.reshape(pixels, chan),
        out_share,
        out_base,
        jnp.stack([jnp.zeros((CHUNK, chan), jnp.float32), small_rows]),
        back_rows,
        embed_rows,
        silu_padded,
        text_part // 2,
    )
    output_sum = output_sum.reshape(part, chan)
    attend_sum = attend_sum.reshape(part, 3 * chan)
    mapper_sum = mapper_sum.reshape(text_part, chan)
    reduce_sum = reduce_sum.reshape(wide, chan)
    expand_sum = expand_sum.reshape(part, hid)
    layer_output = layer_output.reshape(latents.shape)
    grad_mapped_all = grad_mapped_all[:, :texts].reshape(size * texts, chan)
    gate = 1.0 / (1.0 + jnp.exp(-near_tokens))
    tokens_near = dot_t(grad_mapped_all, text_weight) * (
        gate * (1.0 + near_tokens * (1.0 - gate))
    )
    tokens_near = tokens_near.reshape(4, texts, text_part)
    grad_conv = grad_conv.reshape(rows, cols, chan)
    kernel_grad = jnp.stack(
        [
            jnp.sum(padded[i : i + rows, j : j + cols] * grad_conv, axis=(0, 1))
            for i in range(3)
            for j in range(3)
        ]
    )
    spread_conv = jnp.pad(grad_conv, ((2, 2), (1, 1), (0, 0)))
    latent_rows = jnp.zeros((rows + 2, cols, chan), jnp.float32)
    for i in range(3):
        for j in range(3):
            latent_rows = (
                latent_rows
                + spread_conv[2 - i : 2 - i + rows + 2, 2 - j : 2 - j + cols] * kernel[i, j]
            )
    conv_part = jnp.concatenate([kernel_grad, jnp.sum(grad_conv, axis=(0, 1))[None]], axis=0)
    conv_blocks = jnp.stack(
        [
            lax.dynamic_slice(conv_part, (0, near_of(me, step) * part), (10, part))
            for step in range(4)
        ]
    )
    rims, conv_arrived, token_arrived = exchange(
        13,
        gathers=(jnp.stack([latent_rows[0], latent_rows[-1]]),),
        scatters=(conv_blocks, tokens_near),
    )
    token_blocks = jnp.take(
        jnp.concatenate([tokens_near[:1], token_arrived], axis=0), order, axis=0
    )
    prior = near_of(rev(quarter), rev(jnp.maximum(quarter - 1, 0)))
    after = near_of(rev(quarter), rev(jnp.minimum(quarter + 1, size - 1)))
    from_above = jnp.where(quarter > 0, rims[prior, 1], 0.0)
    from_below = jnp.where(quarter < size - 1, rims[after, 0], 0.0)
    inner = latent_rows[1:-1] + grad_one.reshape(rows, cols, chan)
    inner = inner.at[-1].add(from_below).at[0].add(from_above)
    latent_grad, tokens_grad, conv_all = close_exchange(
        14,
        inner.reshape(pixels, chan),
        token_blocks.transpose(1, 0, 2).reshape(texts, size * text_part),
        conv_blocks[0] + jnp.sum(conv_arrived, axis=0),
    )
    latent_grad = latent_grad.reshape(latents.shape)
    tokens_grad = tokens_grad[None]
    conv_mine = jnp.sum(conv_all, axis=0)
    ratio = small[0]
    expb, gain, respb = (small[1, i] for i in range(3))
    redb, mapb, queryb, valueb = (small[1, 3, i * part : (i + 1) * part] for i in range(4))
    outb = small[1, 4, :part]
    ratiob = small[1, 4, part : 3 * part]
    return (
        layer_output,
        latent_grad,
        tokens_grad,
        conv_mine[:9].reshape(3, 3, part),
        conv_mine[9],
        expand_sum,
        expb,
        gain,
        respb,
        reduce_sum,
        redb,
        ratio.reshape(ratio_part, 2 * chan),
        ratiob,
        mapper_sum,
        mapb,
        attend_sum,
        queryb,
        valueb,
        output_sum,
        outb,
    )


def solution(mesh):
    square = mesh.shape["cond"] == 2 and mesh.shape["pair"] == 4 and mesh.shape["dp"] == 4
    return jax.shard_map(
        plane_body if square else body,
        mesh=mesh,
        in_specs=(
            P(("cond", "dp"), "pair", None, None),
            P(("cond", "dp"), None),
            P(("cond", "dp"), "pair", None),
            P(("cond", "dp"), "pair", None, None),
            P(None, None, "dp"),
            P("dp"),
            P("dp", None),
            P("dp"),
            P("dp"),
            P("dp"),
            P("dp", None),
            P("dp"),
            P("dp", None),
            P("dp"),
            P("dp", None),
            P("dp"),
            P("dp", None),
            P("dp"),
            P("dp"),
            P("dp", None),
            P("dp"),
        ),
        out_specs=(
            P(("cond", "dp"), "pair", None, None),
            P(("cond", "dp"), "pair", None, None),
            P(("cond", "dp"), "pair", None),
            P(None, None, "dp"),
            P("dp"),
            P("dp", None),
            P("dp"),
            P("dp"),
            P("dp"),
            P("dp", None),
            P("dp"),
            P("dp", None),
            P("dp"),
            P("dp", None),
            P("dp"),
            P("dp", None),
            P("dp"),
            P("dp"),
            P("dp", None),
            P("dp"),
        ),
        check_vma=False,
    )
```

```python
import functools

import jax
import jax.numpy as jnp
from jax import lax
from jax.experimental import pallas as pl
from jax.experimental.pallas import tpu as pltpu
from jax.sharding import PartitionSpec as P

HEADS = 24
HEAD_CHANNELS = 64


HIGHEST_ACCURACY = lax.Precision.HIGHEST
EPSILON = 1e-06


def extended(block, sides, width):
    for axis, dim in sides:
        count = lax.axis_size(axis)
        forward = [(i, i + 1) for i in range(count - 1)]
        backward = [(target, source) for source, target in forward]
        low = lax.ppermute(
            lax.slice_in_dim(block, block.shape[dim] - width, None, axis=dim), axis, forward
        )
        high = lax.ppermute(lax.slice_in_dim(block, 0, width, axis=dim), axis, backward)
        block = jnp.concatenate([low, block, high], axis=dim)
    return block


def layer_norm(values):
    centered = values - jnp.mean(values, axis=-1, keepdims=True)
    variance = jnp.mean(centered * centered, axis=-1, keepdims=True)
    return centered * lax.rsqrt(variance + EPSILON)


def matmul(left, right):
    return jnp.einsum("...k,kn->...n", left, right, precision=HIGHEST_ACCURACY)


def depthwise(row_padded, kernel, conv_shift):
    row_count = row_padded.shape[1] - 2
    col_count = row_padded.shape[2]
    padded = jnp.pad(row_padded, ((0, 0), (0, 0), (1, 1), (0, 0)))
    total_conv = conv_shift
    for row_off in range(3):
        for col_off in range(3):
            total_conv = (
                total_conv
                + padded[:, row_off : row_off + row_count, col_off : col_off + col_count, :]
                * kernel[row_off, col_off]
            )
    return total_conv


def front(row_padded, kernel, conv_shift, expand_w, expand_b):
    normed = layer_norm(depthwise(row_padded, kernel, conv_shift))
    flat = normed.reshape(normed.shape[0], normed.shape[1] * normed.shape[2], normed.shape[3])
    return jax.nn.gelu(matmul(flat, expand_w) + expand_b, approximate=False)


def response_mlp(activated, totals, resp_gain, resp_bias, reduce_w, reduce_b, residual):
    norms = jnp.sqrt(totals + EPSILON)
    scaled = norms / (jnp.mean(norms, axis=-1, keepdims=True) + EPSILON)
    response = resp_gain * (activated * scaled[:, None, :]) + resp_bias + activated
    return residual + matmul(response, reduce_w) + reduce_b


def modulate(hidden_one, ratio_w, ratio_b, embed):
    modulation = jnp.dot(embed, ratio_w, precision=HIGHEST_ACCURACY) + ratio_b
    chan_count = hidden_one.shape[-1]
    return hidden_one * (1.0 + modulation[:, None, :chan_count]) + modulation[:, None, chan_count:]


def project(hidden_two, tokens, map_w, map_b, attend_w, query_b, value_b):
    chan_count = hidden_two.shape[-1]
    normed = layer_norm(hidden_two)
    mapped = matmul(jax.nn.silu(tokens), map_w) + map_b
    source = jnp.concatenate([normed, mapped], axis=1)
    query_matrix = matmul(normed, attend_w[:, :chan_count]) + query_b
    key_value = matmul(source, attend_w[:, chan_count:])
    return (query_matrix, key_value[..., :chan_count], key_value[..., chan_count:] + value_b)


def divide_into_heads(values):
    return values.reshape(values.shape[:-1] + (HEADS, HEAD_CHANNELS))


def attend_single(triple):
    query_matrix, key_matrix, value_matrix = triple
    attention_scores = jnp.einsum(
        "iuy,ouy->uio",
        divide_into_heads(query_matrix),
        divide_into_heads(key_matrix),
        precision=HIGHEST_ACCURACY,
    ) * HEAD_CHANNELS ** (-0.5)
    top_score = jnp.max(attention_scores, axis=-1, keepdims=True)
    expo_terms = jnp.exp(attention_scores - top_score)
    expo_total = jnp.sum(expo_terms, axis=-1, keepdims=True)
    attention_probabilities = expo_terms / expo_total
    attended_output = jnp.einsum(
        "fvb,bfq->vfq",
        attention_probabilities,
        divide_into_heads(value_matrix),
        precision=HIGHEST_ACCURACY,
    )
    log_total = top_score + jnp.log(expo_total)
    return (attended_output.reshape(query_matrix.shape), log_total)


def attend_back_single(items):
    query_matrix, key_matrix, value_matrix, attended_output, log_total, grad_mix = items
    query_per_head = divide_into_heads(query_matrix)
    key_per_head = divide_into_heads(key_matrix)
    value_per_head = divide_into_heads(value_matrix)
    gradient_per_head = divide_into_heads(grad_mix)
    attention_scores = jnp.einsum(
        "iuy,ouy->uio", query_per_head, key_per_head, precision=HIGHEST_ACCURACY
    ) * HEAD_CHANNELS ** (-0.5)
    attention_probabilities = jnp.exp(attention_scores - log_total)
    probability_gradient = jnp.einsum(
        "iuy,ouy->uio", gradient_per_head, value_per_head, precision=HIGHEST_ACCURACY
    )
    delta_rows = jnp.einsum(
        "phd,phd->hp",
        gradient_per_head,
        divide_into_heads(attended_output),
        precision=HIGHEST_ACCURACY,
    )
    score_gradient = (
        attention_probabilities
        * (probability_gradient - delta_rows[..., None])
        * HEAD_CHANNELS ** (-0.5)
    )
    query_gradient = jnp.einsum(
        "fvb,bfq->vfq", score_gradient, key_per_head, precision=HIGHEST_ACCURACY
    )
    key_gradient = jnp.einsum(
        "gyu,ygx->ugx", score_gradient, query_per_head, precision=HIGHEST_ACCURACY
    )
    value_gradient = jnp.einsum(
        "gyu,ygx->ugx", attention_probabilities, gradient_per_head, precision=HIGHEST_ACCURACY
    )
    return (
        query_gradient.reshape(query_matrix.shape),
        key_gradient.reshape(key_matrix.shape),
        value_gradient.reshape(value_matrix.shape),
    )


def body(
    latents,
    ratio_embed,
    clip_tokens,
    cotangent,
    conv_kernel,
    conv_bias,
    expand_weight,
    expand_bias,
    response_gain,
    response_bias,
    reduce_weight,
    reduce_bias,
    ratio_weight,
    ratio_bias,
    text_weight,
    text_bias,
    attend_weight,
    query_bias,
    value_bias,
    output_weight,
    output_bias,
):
    gathered = (
        lax.all_gather(conv_kernel, "dp", axis=2, tiled=True),
        lax.all_gather(conv_bias, "dp", axis=0, tiled=True),
        lax.all_gather(expand_weight, "dp", axis=0, tiled=True),
        lax.all_gather(expand_bias, "dp", axis=0, tiled=True),
        lax.all_gather(response_gain, "dp", axis=0, tiled=True),
        lax.all_gather(response_bias, "dp", axis=0, tiled=True),
        lax.all_gather(reduce_weight, "dp", axis=0, tiled=True),
        lax.all_gather(reduce_bias, "dp", axis=0, tiled=True),
        lax.all_gather(ratio_weight, "dp", axis=0, tiled=True),
        lax.all_gather(ratio_bias, "dp", axis=0, tiled=True),
        lax.all_gather(text_weight, "dp", axis=0, tiled=True),
        lax.all_gather(text_bias, "dp", axis=0, tiled=True),
        lax.all_gather(attend_weight, "dp", axis=0, tiled=True),
        lax.all_gather(query_bias, "dp", axis=0, tiled=True),
        lax.all_gather(value_bias, "dp", axis=0, tiled=True),
        lax.all_gather(output_weight, "dp", axis=0, tiled=True),
        lax.all_gather(output_bias, "dp", axis=0, tiled=True),
    )
    (
        kernel,
        conv_shift,
        expand_w,
        expand_b,
        resp_gain,
        resp_bias,
        reduce_w,
        reduce_b,
        ratio_w,
        ratio_b,
        map_w,
        map_b,
        attend_w,
        query_b,
        value_b,
        out_w,
        out_b,
    ) = gathered
    lat_count, row_count, col_count, chan_count = latents.shape
    pixel_count = row_count * col_count
    row_padded = extended(latents, (("pair", 1),), 1)
    activated, front_pull = jax.vjp(front, row_padded, kernel, conv_shift, expand_w, expand_b)
    totals = lax.psum(jnp.sum(activated * activated, axis=1), "pair")
    residual = latents.reshape(lat_count, pixel_count, chan_count)
    hidden_one, mlp_pull = jax.vjp(
        response_mlp, activated, totals, resp_gain, resp_bias, reduce_w, reduce_b, residual
    )
    hidden_two, mod_pull = jax.vjp(
        functools.partial(modulate, embed=ratio_embed), hidden_one, ratio_w, ratio_b
    )
    (query_matrix, key_local, value_local), proj_pull = jax.vjp(
        project, hidden_two, clip_tokens, map_w, map_b, attend_w, query_b, value_b
    )
    key_matrix, value_matrix = (
        lax.all_gather(key_local, "pair", axis=1, tiled=True),
        lax.all_gather(value_local, "pair", axis=1, tiled=True),
    )
    attended_output, log_total = lax.map(attend_single, (query_matrix, key_matrix, value_matrix))
    result = hidden_two + matmul(attended_output, out_w) + out_b
    layer_output = result.reshape(latents.shape)
    grad_out = cotangent.reshape(lat_count, pixel_count, chan_count)
    out_w_grad = jnp.einsum("lpc,lpn->cn", attended_output, grad_out, precision=HIGHEST_ACCURACY)
    out_b_grad = jnp.sum(grad_out, axis=(0, 1))
    grad_mix = jnp.einsum("lpn,cn->lpc", grad_out, out_w, precision=HIGHEST_ACCURACY)
    query_gradient, key_gradient, value_gradient = lax.map(
        attend_back_single,
        (query_matrix, key_matrix, value_matrix, attended_output, log_total, grad_mix),
    )
    key_share, value_share = (
        lax.psum_scatter(key_gradient, "pair", scatter_dimension=1, tiled=True),
        lax.psum_scatter(value_gradient, "pair", scatter_dimension=1, tiled=True),
    )
    grad_two, tokens_grad, map_w_grad, map_b_grad, attend_w_grad, query_b_grad, value_b_grad = (
        proj_pull((query_gradient, key_share, value_share))
    )
    grad_two = grad_two + grad_out
    attend_shards = (
        lax.psum_scatter(map_w_grad, "dp", scatter_dimension=0, tiled=True),
        lax.psum_scatter(map_b_grad, "dp", scatter_dimension=0, tiled=True),
        lax.psum_scatter(attend_w_grad, "dp", scatter_dimension=0, tiled=True),
        lax.psum_scatter(query_b_grad, "dp", scatter_dimension=0, tiled=True),
        lax.psum_scatter(value_b_grad, "dp", scatter_dimension=0, tiled=True),
        lax.psum_scatter(out_w_grad, "dp", scatter_dimension=0, tiled=True),
        lax.psum_scatter(out_b_grad, "dp", scatter_dimension=0, tiled=True),
    )
    grad_one, ratio_w_grad, ratio_b_grad = mod_pull(grad_two)
    grad_act, grad_totals, gain_grad, respb_grad, reduce_w_grad, reduce_b_grad, grad_res = mlp_pull(
        grad_one
    )
    grad_totals = lax.psum(grad_totals, "pair")
    grad_act = grad_act + 2.0 * activated * grad_totals[:, None, :]
    grad_padded, kernel_grad, shift_grad, expand_w_grad, expand_b_grad = front_pull(grad_act)
    rim_rows = jnp.concatenate([grad_padded[:, :1], grad_padded[:, -1:]], axis=1)
    arrived = extended(rim_rows, (("pair", 1),), 1)
    inner_rows = grad_padded[:, 1:-1]
    inner_rows = inner_rows.at[:, 0].add(arrived[:, 0]).at[:, -1].add(arrived[:, 3])
    latent_grad = inner_rows + grad_res.reshape(latents.shape)
    block_shards = (
        lax.psum_scatter(kernel_grad, "dp", scatter_dimension=2, tiled=True),
        lax.psum_scatter(shift_grad, "dp", scatter_dimension=0, tiled=True),
        lax.psum_scatter(expand_w_grad, "dp", scatter_dimension=0, tiled=True),
        lax.psum_scatter(expand_b_grad, "dp", scatter_dimension=0, tiled=True),
        lax.psum_scatter(gain_grad, "dp", scatter_dimension=0, tiled=True),
        lax.psum_scatter(respb_grad, "dp", scatter_dimension=0, tiled=True),
        lax.psum_scatter(reduce_w_grad, "dp", scatter_dimension=0, tiled=True),
        lax.psum_scatter(reduce_b_grad, "dp", scatter_dimension=0, tiled=True),
        lax.psum_scatter(ratio_w_grad, "dp", scatter_dimension=0, tiled=True),
        lax.psum_scatter(ratio_b_grad, "dp", scatter_dimension=0, tiled=True),
    )
    shards = tuple(block_shards) + tuple(attend_shards)
    summed = lax.psum(shards, ("cond", "pair"))
    return (layer_output, latent_grad, tokens_grad) + tuple(summed)

FAST = lax.Precision.HIGH


def dot(left, right):
    return jnp.dot(left, right, precision=FAST)


def dot_t(left, right):
    return lax.dot_general(left, right, (((1,), (1,)), ((), ())), precision=FAST)


def t_dot(left, right):
    return lax.dot_general(left, right, (((0,), (0,)), ((), ())), precision=FAST)


def norm_stats(values):
    centered = values - jnp.mean(values, axis=-1, keepdims=True)
    variance = jnp.mean(centered * centered, axis=-1, keepdims=True)
    inverse = lax.rsqrt(variance + EPSILON)
    return centered * inverse, inverse


def norm_back(grad, normed, inverse):
    return inverse * (
        grad
        - jnp.mean(grad, axis=-1, keepdims=True)
        - normed * jnp.mean(grad * normed, axis=-1, keepdims=True)
    )


def heads_of(values):
    return values.reshape(values.shape[0], -1, HEAD_CHANNELS)


CHUNK = 32
MESH = pl.DeviceIdType.MESH
DMA = pltpu.SemaphoreType.DMA
ANY = pl.BlockSpec(memory_space=pl.ANY)


def near_of(me, step):
    across = lax.rem(lax.rem(me, 2) + lax.rem(step, 2), 2)
    along = lax.rem(lax.div(me, 2) + lax.div(step, 2), 2)
    return along * 2 + across


def remote(src, dst, send, recv, device):
    return pltpu.make_async_remote_copy(
        src_ref=src, dst_ref=dst, send_sem=send, recv_sem=recv, device_id=device,
        device_id_type=MESH,
    )


def greet(device):
    barrier = pltpu.get_barrier_semaphore()
    pl.semaphore_signal(barrier, inc=1, device_id=device, device_id_type=MESH)


def relay_begin(full, sems):
    cross_out, cross_in, mate_out, mate_in = sems
    core = lax.axis_index("cond")
    level = lax.axis_index("pair")
    me = lax.axis_index("dp")
    unit = full.shape[1] // 4
    side = lax.rem(level, 2)
    across = (core, level + 1 - 2 * side, me)
    mate = (1 - core, level, me)

    def spot(u, step):
        rows = pl.ds(pl.multiple_of((core * 2 + u) * unit, 8), unit)
        return full.at[near_of(me, step), rows]

    steps = (1, 2, 3)
    crosses = [
        remote(
            spot(side, step), spot(side, step), cross_out.at[step - 1], cross_in.at[step - 1], across
        )
        for step in steps
    ]
    mates = [
        [
            remote(
                spot(u, step), spot(u, step), mate_out.at[i, step - 1], mate_in.at[i, step - 1], mate
            )
            for step in steps
        ]
        for i, u in enumerate((side, 1 - side))
    ]

    def begin():
        for copy in crosses + mates[0]:
            copy.start()

    def end():
        for cross, far in zip(crosses, mates[1]):
            cross.wait_recv()
            far.start()
        for copy in crosses:
            copy.wait_send()
        for copy in mates[0] + mates[1]:
            copy.wait()

    return begin, end


def exchange_body(gather_count, scatter_count, swap_count, relays, *refs):
    near_count = gather_count + scatter_count
    count = near_count + swap_count
    ins = refs[:count]
    refs = refs[count + relays :]
    outs = refs[:count]
    full = refs[count] if relays else None
    refs = refs[count + relays :]
    passing, refs = refs[:swap_count], refs[swap_count:]
    holds = refs[: gather_count + swap_count]
    send, recv, keep = refs[gather_count + swap_count :][:3]
    sems = refs[gather_count + swap_count + 3 :]
    core = lax.axis_index("cond")
    level = lax.axis_index("pair")
    me = lax.axis_index("dp")
    goal = near_of(me, rev(level))
    quarter = rev(near_of(level, me))
    shifts = level != 0
    rises = goal != level
    final = me == level
    expected = 3
    for step in (1, 2, 3):
        greet((core, level, near_of(me, step)))
    if relays:
        greet((1 - core, level, me))
        greet((core, level + 1 - 2 * lax.rem(level, 2), me))
        expected = expected + 2
    if swap_count:
        pl.when(rises)(lambda: greet((core, quarter, me)))
        expected = expected + jnp.where(rises, 1, 0)
    pl.semaphore_wait(pltpu.get_barrier_semaphore(), expected)

    def shift(i, goals):
        return remote(
            ins[near_count + i], goals[i], send.at[near_count + i, 0], recv.at[near_count + i, 0],
            (core, level, goal),
        )

    def rise(i, sources):
        return remote(
            sources[i], outs[near_count + i], send.at[near_count + i, 1],
            recv.at[near_count + i, 1], (core, goal, me),
        )

    swap_ins = ins[near_count:]
    swap_outs = outs[near_count:]
    near_copies = []
    if relays:
        relay_start, relay_end = relay_begin(full, sems)
        relay_start()
    for i in range(swap_count):
        pl.when(jnp.logical_and(shifts, final))(shift(i, swap_outs).start)
        pl.when(jnp.logical_and(shifts, jnp.logical_not(final)))(shift(i, passing).start)
        pl.when(jnp.logical_and(jnp.logical_not(shifts), rises))(rise(i, swap_ins).start)
    for step in (3, 1, 2):
        for i in range(near_count):
            if i < gather_count:
                src, dst = ins[i], outs[i].at[step]
            else:
                src, dst = ins[i].at[step], outs[i].at[step - 1]
            copy = remote(
                src, dst, send.at[i, step - 1], recv.at[i, step - 1],
                (core, level, near_of(me, step)),
            )
            copy.start()
            near_copies.append(copy)

    def through(src, hold, dst, sem):
        load = pltpu.make_async_copy(src, hold, sem)
        load.start()
        load.wait()
        store = pltpu.make_async_copy(hold, dst, sem)
        store.start()
        store.wait()

    for i in range(gather_count):
        through(ins[i], holds[i], outs[i].at[0], keep.at[i])
    for i in range(swap_count):
        pl.when(jnp.logical_and(jnp.logical_not(shifts), jnp.logical_not(rises)))(
            lambda i=i: through(
                swap_ins[i], holds[gather_count + i], swap_outs[i], keep.at[gather_count + i]
            )
        )
        pl.when(shifts)(shift(i, passing).wait_recv)
        pl.when(jnp.logical_and(shifts, rises))(rise(i, passing).start)
    if relays:
        relay_end()
    for copy in near_copies:
        copy.wait()
    for i in range(swap_count):
        pl.when(shifts)(shift(i, passing).wait_send)
        pl.when(rises)(rise(i, swap_ins).wait_send)
        pl.when(quarter != level)(rise(i, swap_ins).wait_recv)


def exchange(collective, gathers=(), scatters=(), swaps=(), relay=()):
    f32 = jnp.float32
    shapes = [(4,) + item.shape for item in gathers]
    shapes += [(3,) + item.shape[1:] for item in scatters]
    shapes += [item.shape for item in swaps]
    count = len(shapes)
    shapes += [item.shape for item in relay]
    shapes += [item.shape for item in swaps]
    staged = len(gathers) + len(swaps)
    scratch = [pltpu.VMEM(item.shape, f32) for item in tuple(gathers) + tuple(swaps)]
    scratch += [DMA((count, 3)), DMA((count, 3)), DMA((max(staged, 1),))]
    if relay:
        scratch += [DMA((3,)), DMA((3,)), DMA((2, 3)), DMA((2, 3))]
    outs = pl.pallas_call(
        functools.partial(exchange_body, len(gathers), len(scatters), len(swaps), len(relay)),
        out_shape=[jax.ShapeDtypeStruct(shape, f32) for shape in shapes],
        in_specs=[ANY] * (count + len(relay)),
        out_specs=[ANY] * len(shapes),
        scratch_shapes=scratch,
        input_output_aliases={count: count} if relay else {},
        compiler_params=pltpu.CompilerParams(
            collective_id=collective, has_side_effects=True, vmem_limit_bytes=16 * 2**20
        ),
        name="exchange",
    )(*gathers, *scatters, *swaps, *relay)
    return outs[: count + len(relay)]


PARTS = 4


def open_body(image_in, packed_in, tokens_in, embed_in, weight_in, attend_in, *refs):
    image, packed, tokens, embed, weight, attend = refs[:6]
    passing = refs[6:9]
    hold, send, recv, keep, cross_out, cross_in, pass_out, pass_in, own_out, own_in, block_out, block_in = refs[9:]
    core = lax.axis_index("cond")
    level = lax.axis_index("pair")
    me = lax.axis_index("dp")
    mate = (1 - core, level, me)
    side = lax.rem(level, 2)
    across = (core, level + 1 - 2 * side, me)
    rows = image_in.shape[0]
    wide = weight.shape[3]
    unit = weight.shape[2]
    turn = rev(level)
    goal = near_of(me, turn)
    quarter = rev(near_of(level, me))
    shifts = level != 0
    rises = goal != level
    turned = jnp.logical_and(level == 1, me == 1)
    raises = jnp.logical_and(level > 0, jnp.logical_not(turned))
    falls = level < 3
    taken = jnp.logical_and(quarter < 3, jnp.logical_not(turned))
    greet(mate)
    greet(across)
    for step in (1, 2, 3):
        greet((core, level, near_of(me, step)))
    pl.when(rises)(lambda: greet((core, quarter, me)))
    pl.when(quarter > 0)(lambda: greet((core, quarter - 1, level)))
    pl.when(taken)(lambda: greet((core, quarter + 1, level)))
    expected = (
        5 + jnp.where(rises, 1, 0) + jnp.where(raises, 1, 0) + jnp.where(falls, 1, 0)
    )
    pl.semaphore_wait(pltpu.get_barrier_semaphore(), expected)

    body = image.at[pl.ds(1, rows)]
    ins = (image_in, tokens_in, embed_in)
    ends = (body, tokens, embed)

    def shift(goals):
        return [
            remote(src, dst, send.at[i], recv.at[i], (core, level, goal))
            for i, (src, dst) in enumerate(zip(ins, goals))
        ]

    def rise(sources):
        return [
            remote(src, dst, send.at[3 + i], recv.at[3 + i], (core, goal, me))
            for i, (src, dst) in enumerate(zip(sources, ends))
        ]

    def stay():
        image_load = pltpu.make_async_copy(image_in, hold, keep.at[0])
        image_load.start()
        rest = [
            pltpu.make_async_copy(src, dst, keep.at[i])
            for i, (src, dst) in ((1, (tokens_in, tokens)), (2, (embed_in, embed)))
        ]
        run("start", *rest)
        image_load.wait()
        image_store = pltpu.make_async_copy(hold, body, keep.at[0])
        image_store.start()
        run("wait", image_store, *rest)

    lower = remote(
        image_in.at[pl.ds(rows - 1, 1)], image.at[pl.ds(0, 1)], send.at[6], recv.at[6],
        (core, me, near_of(me, rev(jnp.minimum(level + 1, 3)))),
    )
    upper = remote(
        image_in.at[pl.ds(0, 1)], image.at[pl.ds(rows + 1, 1)], send.at[7], recv.at[7],
        (core, me, near_of(me, rev(jnp.maximum(level - 1, 0)))),
    )
    around = pltpu.make_async_copy(
        image_in.at[pl.ds(0, 1)], image.at[pl.ds(rows + 1, 1)], keep.at[4]
    )

    def vectors(step):
        return remote(
            packed_in, packed.at[me], send.at[7 + step], recv.at[7 + step],
            (core, level, near_of(me, step)),
        )

    mine = core * 2 + side
    other = core * 2 + 1 - side

    size = unit // PARTS

    def block(step, h):
        to = near_of(me, step)
        src = weight_in.at[
            pl.ds(pl.multiple_of(mine * unit + h * size, 8), size),
            pl.ds(pl.multiple_of(to * wide, wide), wide),
        ]
        dst = weight.at[me, mine, pl.ds(h * size, size)]
        return remote(
            src, dst, block_out.at[h, step - 1], block_in.at[h, step - 1], (core, level, to)
        )

    piece = attend.shape[2] // 3

    def thirds(step):
        to = near_of(me, step)
        found = []
        for p in range(3):
            src = attend_in.at[
                pl.ds(pl.multiple_of(mine * unit, 8), unit),
                pl.ds(pl.multiple_of((p * 4 + to) * piece, piece), piece),
            ]
            dst = attend.at[
                me, pl.ds(pl.multiple_of(mine * unit, 8), unit), pl.ds(p * piece, piece)
            ]
            spot = 11 + step * 3 + p
            found.append(remote(src, dst, send.at[spot], recv.at[spot], (core, level, to)))
        return found

    def crossed(step, u, h):
        spot = weight.at[near_of(me, step), u, pl.ds(h * size, size)]
        return remote(spot, spot, cross_out.at[h, step - 1], cross_in.at[h, step - 1], across)

    def passed(step, u, turn, h):
        spot = weight.at[near_of(me, step), u, pl.ds(h * size, size)]
        k = turn * PARTS + h
        return remote(spot, spot, pass_out.at[k, step - 1], pass_in.at[k, step - 1], mate)

    def run(method, *copies):
        for copy in copies:
            getattr(copy, method)()

    final = me == level
    pl.when(jnp.logical_and(shifts, final))(lambda: run("start", *shift(ends)))
    pl.when(jnp.logical_and(shifts, jnp.logical_not(final)))(lambda: run("start", *shift(passing)))
    pl.when(jnp.logical_and(jnp.logical_not(shifts), rises))(lambda: run("start", *rise(ins)))
    pl.when(falls)(lower.start)
    pl.when(raises)(upper.start)
    pl.when(turned)(around.start)
    own = [pltpu.make_async_copy(packed_in, packed.at[me], keep.at[3])]
    own_blocks = [
        remote(
            weight_in.at[pl.ds(u * unit, unit), pl.ds(pl.multiple_of(me * wide, wide), wide)],
            weight.at[me, u],
            own_out.at[u],
            own_in.at[u],
            mate,
        )
        for u in range(4)
    ] + [
        remote(
            attend_in.at[:, pl.ds(pl.multiple_of((p * 4 + me) * piece, piece), piece)],
            attend.at[me, :, pl.ds(p * piece, piece)],
            own_out.at[4 + p],
            own_in.at[4 + p],
            mate,
        )
        for p in range(3)
    ]
    for step in (3, 1, 2):
        vectors(step).start()
    for h in range(2):
        for step in (3, 1, 2):
            block(step, h).start()
    run("start", *own, *own_blocks)
    pl.when(jnp.logical_and(jnp.logical_not(shifts), jnp.logical_not(rises)))(stay)

    @pl.when(shifts)
    def _():
        run("wait_recv", *shift(passing))
        pl.when(rises)(lambda: run("start", *rise(passing)))

    for h in range(PARTS):
        for step in (2, 1, 3):
            block(step, h).wait_recv()
            if h + 2 < PARTS:
                block(step, h + 2).start()
            crossed(step, mine, h).start()
            passed(step, mine, 0, h).start()
    for step in (3, 1, 2):
        run("start", *thirds(step))
    for h in range(PARTS):
        for step in (2, 1, 3):
            crossed(step, other, h).wait_recv()
            passed(step, other, 1, h).start()
    pl.when(shifts)(lambda: run("wait_send", *shift(passing)))
    pl.when(rises)(lambda: run("wait_send", *rise(ins)))
    pl.when(quarter != level)(lambda: run("wait_recv", *rise(ins)))
    pl.when(falls)(lower.wait_send)
    pl.when(raises)(upper.wait_send)
    pl.when(quarter > 0)(lower.wait_recv)
    pl.when(taken)(upper.wait_recv)
    pl.when(turned)(around.wait)
    for step in (1, 2, 3):
        vectors(step).wait()
        run("wait", *thirds(step))
        for h in range(PARTS):
            block(step, h).wait_send()
            crossed(step, mine, h).wait_send()
            for u, turn_of in ((mine, 0), (other, 1)):
                passed(step, u, turn_of, h).wait()
    run("wait", *own, *own_blocks)


def open_exchange(collective, image, packed, tokens, embed, weight, attend):
    rows, cols, chan = image.shape
    unit = weight.shape[0] // 4
    shapes = [
        (rows + 2, cols, chan),
        (4,) + packed.shape,
        tokens.shape,
        embed.shape,
        (4, 4, unit, weight.shape[1] // 4),
        (4, attend.shape[0], attend.shape[1] // 4),
        image.shape,
        tokens.shape,
        embed.shape,
    ]
    return pl.pallas_call(
        open_body,
        out_shape=[jax.ShapeDtypeStruct(shape, jnp.float32) for shape in shapes],
        in_specs=[ANY] * 6,
        out_specs=[ANY] * 9,
        scratch_shapes=[
            pltpu.VMEM(image.shape, jnp.float32),
            DMA((23,)),
            DMA((23,)),
            DMA((5,)),
            DMA((PARTS, 3)),
            DMA((PARTS, 3)),
            DMA((2 * PARTS, 3)),
            DMA((2 * PARTS, 3)),
            DMA((7,)),
            DMA((7,)),
            DMA((PARTS, 3)),
            DMA((PARTS, 3)),
        ],
        compiler_params=pltpu.CompilerParams(collective_id=collective, has_side_effects=True),
        name="open_exchange",
    )(image, packed, tokens, embed, weight, attend)


def rev(z):
    return 2 * lax.rem(z, 2) + lax.div(z, 2)


def plane_spot(level, me):
    return me, near_of(me, rev(level))


def home_spot(level, me):
    return rev(near_of(level, me)), level


def stream_setup(homeward=False):
    core = lax.axis_index("cond")
    level = lax.axis_index("pair")
    me = lax.axis_index("dp")
    greet((1 - core, level, me))
    for step in (1, 2, 3):
        greet((core, level, near_of(me, step)))
    pl.when(level > 0)(lambda: greet((core, level - 1, me)))
    pl.when(level < 3)(lambda: greet((core, level + 1, me)))
    ends = jnp.where(level == 0, 1, 0) + jnp.where(level == 3, 1, 0)
    expected = 6 - ends
    if homeward:
        moves = jnp.logical_or(level != 0, me != 0)
        back_up, back_over = plane_spot(level, me)
        pl.when(moves)(lambda: greet((core, back_up, back_over)))
        expected = expected + jnp.where(moves, 1, 0)
    pl.semaphore_wait(pltpu.get_barrier_semaphore(), expected)


def sum_stream(sections, scratch, hooks):
    (
        data,
        stage,
        first,
        second,
        own,
        load_sem,
        core_out,
        core_in,
        plane_out,
        plane_in,
        first_in,
        second_in,
        hop_out,
        cast_out,
        cast_low,
        final_in,
        keep_sem,
        pair_out,
        pair_in,
    ) = scratch
    ranges = []
    total = 0
    for kind, src, dst in sections:
        if kind == "plain":
            count, width = src.shape[1] // CHUNK, src.shape[2]
        else:
            count, width = 4 * (src.shape[2] // CHUNK), src.shape[3]
        ranges.append((total, total + count, kind, src, dst, width))
        total += count
    core = lax.axis_index("cond")
    level = lax.axis_index("pair")
    me = lax.axis_index("dp")
    mate = (1 - core, level, me)
    ring = data.shape[0]
    full = data.shape[2]

    def rank_of(j):
        return jnp.where(lax.rem(j, 2) == 0, level, 3 - level)

    def at_rank(j, rank):
        return (core, jnp.where(lax.rem(j, 2) == 0, rank, 3 - rank), me)

    def inside(j, low, high):
        return jnp.logical_and(j >= low, j < high)

    def swap_place(j):
        inner = False
        k = 0
        for low, high, kind, src, dst, width in ranges:
            if kind == "swap":
                here = inside(j, low, high)
                inner = jnp.logical_or(inner, here)
                k = jnp.where(here, j - low, k)
        return inner, k

    def moved(j):
        inner, k = swap_place(j)
        return jnp.logical_and(inner, lax.rem(k, 4) != 0)

    def kinds(j, action):
        narrow = False
        for low, high, kind, src, dst, width in ranges:
            if width != full:
                here = inside(j, low, high)
                narrow = jnp.logical_or(narrow, here)
                pl.when(here)(lambda width=width: action(width))
        pl.when(jnp.logical_not(narrow))(lambda: action(full))

    def cut(ref, width):
        return ref if ref.shape[-1] == width else ref.at[:, pl.ds(0, width)]

    def each_source(j, action):
        target = data.at[lax.rem(j, ring)]
        mine = own.at[lax.rem(j, 4)]
        for low, high, kind, src, dst, width in ranges:

            @pl.when(inside(j, low, high))
            def _(low=low, kind=kind, src=src, width=width):
                k = j - low
                if kind == "plain":
                    rows = pl.ds(pl.multiple_of(k * CHUNK, CHUNK), CHUNK)
                    action(lambda half: src.at[half, rows], target, mine)
                else:
                    rows = pl.ds(pl.multiple_of(lax.div(k, 4) * CHUNK, CHUNK), CHUNK)
                    spot = near_of(me, lax.rem(k, 4))
                    action(
                        lambda half: src.at[spot, half, rows], cut(target, width), cut(mine, width)
                    )

    def each_final(j, action):
        for low, high, kind, src, dst, width in ranges:

            @pl.when(inside(j, low, high))
            def _(low=low, kind=kind, dst=dst, width=width):
                k = j - low
                if kind == "plain":
                    rows = pl.ds(pl.multiple_of(k * CHUNK, CHUNK), CHUNK)
                    action(
                        lambda half: [(dst.at[half, rows], lambda x: x, 0)],
                        first.at[lax.rem(j, ring)],
                    )
                else:
                    rows = pl.ds(pl.multiple_of(lax.div(k, 4) * CHUNK, CHUNK), CHUNK)
                    spot = near_of(me, lax.rem(k, 4))
                    pieces = 1 if width == full else 3
                    piece = width // pieces

                    def targets(half):
                        found = []
                        for p in range(pieces):
                            columns = pl.ds(
                                pl.multiple_of(p * 4 * piece + spot * piece, piece), piece
                            )
                            found.append(
                                (
                                    dst.at[half, rows, columns],
                                    lambda x, p=p: x
                                    if x.shape[-1] == piece
                                    else x.at[:, pl.ds(p * piece, piece)],
                                    p,
                                )
                            )
                        return found

                    action(targets, stage.at[k])

    def core_copy(j, src, dst):
        return remote(src, dst, core_out.at[j], core_in.at[j], mate)

    def plane_copy(j, width):
        inner, k = swap_place(j)
        return remote(
            cut(first.at[lax.rem(j, ring)], width),
            cut(stage.at[k], width),
            plane_out.at[j],
            plane_in.at[j],
            (core, level, near_of(me, lax.rem(k, 4))),
        )

    def hop_first(j, src, rank, width):
        return remote(
            cut(src, width), cut(first.at[lax.rem(j, ring)], width), hop_out.at[j], first_in.at[j], at_rank(j, rank)
        )

    def hop_second(j, width):
        k = lax.div(j, 2)
        return remote(
            cut(data.at[lax.rem(j, ring)], width), cut(second.at[lax.rem(k, ring // 2)], width), hop_out.at[j], second_in.at[k],
            at_rank(j, 2),
        )

    def start(j):
        def go(source, target, mine):
            core_copy(j, source(1 - core), target).start()
            pltpu.make_async_copy(source(core), mine, load_sem.at[lax.rem(j, 4)]).start()

        each_source(j, go)

    def combine(j):
        def go(source, target, mine):
            pltpu.make_async_copy(source(core), mine, load_sem.at[lax.rem(j, 4)]).wait()
            core_copy(j, source(1 - core), target).wait_recv()
            target[...] += mine[...]

        each_source(j, go)

    def depart(j):
        rank = rank_of(j)

        def go(width):
            pl.when(rank == 0)(lambda: hop_first(j, data.at[lax.rem(j, ring)], 1, width).start())
            pl.when(rank == 3)(lambda: hop_second(j, width).start())

        kinds(j, go)

    def relay(j):
        def go(width):
            hop_first(j, data.at[lax.rem(j, ring)], 1, width).wait_recv()
            spot = lax.rem(j, ring)
            first[spot, :, :width] += data[spot, :, :width]
            hop_first(j, first.at[lax.rem(j, ring)], 2, width).start()

        pl.when(rank_of(j) == 1)(lambda: kinds(j, go))

    def casts(j, rank, half_targets, source, sems):
        return [
            remote(
                cut_of(source) if source is not None else ref, ref, sems.at[j, p], final_in.at[j, p],
                at_rank(j, rank),
            )
            for ref, cut_of, p in half_targets
        ]

    def pairs(j, half_targets, source):
        return [
            remote(
                cut_of(source) if source is not None else ref, ref, pair_out.at[j, p],
                pair_in.at[j, p], mate,
            )
            for ref, cut_of, p in half_targets
        ]

    def keeps(j, half_targets, source):
        return [
            pltpu.make_async_copy(cut_of(source), ref, keep_sem.at[j, p])
            for ref, cut_of, p in half_targets
        ]

    def root(j):
        def add(width):
            hop_first(j, first.at[lax.rem(j, ring)], 2, width).wait_recv()
            hop_second(j, width).wait_recv()
            spot = lax.rem(j, ring)
            first[spot, :, :width] += (
                data[spot, :, :width] + second[lax.rem(lax.div(j, 2), ring // 2), :, :width]
            )

        @pl.when(rank_of(j) == 2)
        def _():
            kinds(j, add)

            @pl.when(moved(j))
            def _():
                kinds(j, lambda width: plane_copy(j, width).start())

            inner, k = swap_place(j)

            @pl.when(jnp.logical_and(inner, jnp.logical_not(moved(j))))
            def _():
                stage[k] = first[lax.rem(j, ring)]

    def spread(j):
        def send(targets, source):
            goals = targets(core)
            for copy in (
                casts(j, 1, goals, source, cast_out)
                + casts(j, 3, goals, source, cast_low)
                + keeps(j, goals, source)
                + pairs(j, goals, source)
            ):
                copy.start()

        @pl.when(rank_of(j) == 2)
        def _():
            @pl.when(moved(j))
            def _():
                kinds(j, lambda width: plane_copy(j, width).wait_recv())

            each_final(j, send)

    def landed(j):
        rank = rank_of(j)

        def go(targets, source):
            goals = targets(core)
            for copy in casts(j, 1, goals, None, cast_out):
                copy.wait_recv()
            pl.when(rank == 1)(
                lambda: [copy.start() for copy in casts(j, 0, goals, None, cast_out)] and None
            )
            for copy in pairs(j, goals, None):
                copy.start()

        @pl.when(jnp.logical_or(rank == 1, rank == 3))
        def _():
            each_final(j, go)

    def arrived(j):
        def go(targets, source):
            goals = targets(core)
            for copy in casts(j, 0, goals, None, cast_out):
                copy.wait_recv()
            for copy in pairs(j, goals, None):
                copy.start()

        @pl.when(rank_of(j) == 0)
        def _():
            each_final(j, go)

    def finish(j):
        rank = rank_of(j)

        def sent(source, target, mine):
            core_copy(j, source(1 - core), target).wait_send()

        each_source(j, sent)

        @pl.when(jnp.logical_and(moved(j), rank == 2))
        def _():
            kinds(j, lambda width: plane_copy(j, width).wait_send())

        @pl.when(rank != 2)
        def _():
            kinds(j, lambda width: hop_first(j, data.at[lax.rem(j, ring)], 1, width).wait_send())

        def go(targets, source):
            goals = targets(core)

            @pl.when(jnp.logical_or(rank == 1, rank == 2))
            def _():
                for copy in casts(j, 1, goals, None, cast_out):
                    copy.wait_send()

            @pl.when(rank == 2)
            def _():
                for copy in casts(j, 3, goals, None, cast_low):
                    copy.wait_send()
                for copy in keeps(j, goals, source):
                    copy.wait()

            for copy in pairs(j, goals, None):
                copy.wait()

        each_final(j, go)

    stages = (
        (0, start),
        (3, combine),
        (5, depart),
        (8, relay),
        (11, root),
        (14, spread),
        (17, landed),
        (20, arrived),
        (23, finish),
    )

    def step(t, carry):
        for lag, stage_of in stages:
            j = t - lag

            @pl.when(jnp.logical_and(j >= 0, j < total))
            def _(j=j, stage_of=stage_of):
                stage_of(j)

        for low, high, hook in hooks:
            pl.when(jnp.logical_and(t >= low, t < high))(lambda hook=hook, low=low: hook(t - low))
        return carry

    lax.fori_loop(0, total + 23, step, 0)


def stream_scratch(total, most, width):
    ring = 32
    return [
        pltpu.VMEM((ring, CHUNK, width), jnp.float32),
        pltpu.VMEM((most, CHUNK, width), jnp.float32),
        pltpu.VMEM((ring, CHUNK, width), jnp.float32),
        pltpu.VMEM((ring // 2, CHUNK, width), jnp.float32),
        pltpu.VMEM((4, CHUNK, width), jnp.float32),
        DMA((4,)),
        DMA((total,)),
        DMA((total,)),
        DMA((total,)),
        DMA((total,)),
        DMA((total,)),
        DMA(((total + 1) // 2,)),
        DMA((total,)),
        DMA((total, 3)),
        DMA((total, 3)),
        DMA((total, 3)),
        DMA((total, 3)),
        DMA((total, 3)),
        DMA((total, 3)),
    ]


SCRATCH = 19


def near_slots(shares, arrived, send, recv, base):
    core = lax.axis_index("cond")
    level = lax.axis_index("pair")
    me = lax.axis_index("dp")
    return [
        remote(
            shares.at[step], arrived.at[step - 1], send.at[base + step - 1],
            recv.at[base + step - 1], (core, level, near_of(me, step)),
        )
        for step in (3, 1, 2)
    ]


def near_blocks(block, everyone, send, recv, base):
    core = lax.axis_index("cond")
    level = lax.axis_index("pair")
    me = lax.axis_index("dp")
    return [
        remote(
            block, everyone.at[step], send.at[base + step - 1], recv.at[base + step - 1],
            (core, level, near_of(me, step)),
        )
        for step in (3, 1, 2)
    ]


def row_stats(rows):
    centered = rows - jnp.mean(rows, axis=-1, keepdims=True)
    inverse = lax.rsqrt(jnp.mean(centered * centered, axis=-1, keepdims=True) + EPSILON)
    return centered * inverse, inverse


def halves(value):
    high = value.astype(jnp.bfloat16)
    return high, (value - high.astype(jnp.float32)).astype(jnp.bfloat16)


def three_pass(left, right, dims):
    def one(x, y):
        return lax.dot_general(x, y, (dims, ((), ())), preferred_element_type=jnp.float32)

    return one(left[0], right[1]) + one(left[1], right[0]) + one(left[0], right[0])


TILE = 256


def backward_body(
    output_ref, qkv_ref, two_ref, text_ref, cot_ref, one_ref, response_ref, reduce_w_ref,
    act_ref, slope_ref, normed_ref, expand_w_ref, conv_ref, out_ref, base_ref, small_ref,
    normed_two_ref, rows_ref, embed_ref, silu_ref, mapped_ref, text_kv_ref,
    output_out, attend_out, mapper_out, reduce_out, small_out, expand_out,
    attend_part, mapper_part, reduce_part, expand_part, one_out, text_out, grad_out, layer_out,
    *scratch
):
    (
        front_got, front_own, conv, grad, one, out_got, out_own, base, small, wide, high, low,
        weights, acts, slopes, columns, product, front, sums, spread_own, spread_got,
        text_got, text_own, text_all, ratio, mapped,
    ) = scratch[SCRATCH : SCRATCH + 26]
    (
        send, recv, keep, tile_out, tile_in, load, front_out, front_in, spread_out, spread_in,
        piece_out, piece_in, text_out_sem, text_in_sem,
    ) = scratch[SCRATCH + 26 :]
    stream_setup(True)
    core = lax.axis_index("cond")
    level = lax.axis_index("pair")
    me = lax.axis_index("dp")
    moves = jnp.logical_or(level != 0, me != 0)
    up, over = home_spot(level, me)
    pixels, chan = conv.shape
    spots = wide.shape[0]
    texts = text_own.shape[0]
    count = chan // TILE
    scatters = near_slots(two_ref, front_got, send, recv, 0)
    scatters += near_slots(text_ref, text_got, send, recv, 6)
    start_loads = [
        pltpu.make_async_copy(src, dst, keep.at[6 + i])
        for i, (src, dst) in enumerate(
            ((two_ref.at[0], front_own), (text_ref.at[0], text_own), (cot_ref, conv), (one_ref, one))
        )
    ]

    def near_tile(i):
        rows = pl.ds(pl.multiple_of(i * 16, 16), 16)
        return [
            remote(
                grad.at[rows],
                wide.at[pl.ds(pl.multiple_of(step * pixels + i * 16, 16), 16)],
                piece_out.at[i, step - 1],
                piece_in.at[i, step - 1],
                (core, level, near_of(me, step)),
            )
            for step in (3, 1, 2)
        ]

    def late():
        found = []
        for step in (3, 1, 2):
            device = (core, level, near_of(me, step))
            found.append(
                remote(
                    text_all.at[0], text_all.at[step], text_out_sem.at[step - 1],
                    text_in_sem.at[step - 1], device,
                )
            )
            found.append(
                remote(
                    ratio.at[0], ratio.at[step], text_out_sem.at[2 + step],
                    text_in_sem.at[2 + step], device,
                )
            )
        return found

    one_kept = pltpu.make_async_copy(grad, one_out, keep.at[10])
    text_kept = pltpu.make_async_copy(text_all, text_out, keep.at[11])

    def early_loads():
        homes = [(acts, 0), (acts, 1), (slopes, 0), (slopes, 1), (front, 0)]
        found = []
        for i, (buffer, slot) in enumerate(homes):
            width = min(TILE, qkv_ref.shape[1] - i * TILE)
            dst = buffer.at[slot] if width == TILE else buffer.at[slot, :, pl.ds(0, width)]
            found.append(
                pltpu.make_async_copy(
                    qkv_ref.at[:, pl.ds(i * TILE, width)], dst, load.at[2 + i if i < 4 else 0]
                )
            )
        return found, homes

    def early_column(i):
        return pltpu.make_async_copy(
            normed_two_ref.at[:, pl.ds(pl.multiple_of(i * part, part), part)],
            columns.at[lax.rem(i, 2)],
            load.at[6 + lax.rem(i, 2)],
        )

    def attend_stores(i):
        half = part // 2
        return [
            pltpu.make_async_copy(
                product.at[pl.ds(c * half, half), pl.ds(0, 3 * part)],
                attend_part.at[i, c],
                load.at[8 + c],
            )
            for c in (0, 1)
        ]

    def prepare(t):
        copies, homes = early_loads()
        for i, (copy, (buffer, slot)) in enumerate(zip(copies, homes)):
            copy.wait()
            width = min(TILE, qkv_ref.shape[1] - i * TILE)

            def strip(k, carry, i=i, buffer=buffer, slot=slot, width=width):
                rows = pl.ds(pl.multiple_of(k * 48, 48), 48)
                cols = pl.ds(i * TILE, width)
                high[rows, cols], low[rows, cols] = halves(buffer[slot, rows, 0:width])
                return carry

            lax.fori_loop(0, spots // 48, strip, 0)

    def attend_outer(i):
        early_column(i).wait()

        @pl.when(i > 0)
        def _():
            for copy in attend_stores(jnp.maximum(i - 1, 0)):
                copy.wait()

        left = halves(columns[lax.rem(i, 2)])
        text_left = halves(mapped_ref[:, pl.ds(pl.multiple_of(i * part, part), part)])
        for k in range(3):
            cols = pl.ds(k * part, part)
            value = three_pass(left, (high[:, cols], low[:, cols]), ((0,), (0,)))
            if k > 0:
                right = halves(text_kv_ref[:, (k - 1) * part : k * part])
                value = value + three_pass(text_left, right, ((0,), (0,)))
            product[:, cols] = value
        for copy in attend_stores(i):
            copy.start()
        pl.when(i + 2 < 4)(lambda: early_column(jnp.minimum(i + 2, 3)).start())

    def settle_attend(t):
        for copy in attend_stores(3):
            copy.wait()

    def arrive(t):
        for copy in start_loads + scatters:
            copy.wait()
        ratio[0] = jnp.zeros_like(ratio[0])
        text_all[0] = jnp.zeros_like(text_all[0])
        text_all[0, 0:texts] = text_own[...] + text_got[0] + text_got[1] + text_got[2]

    def normalize(t):
        scale = rows_ref[6:7]
        shift = rows_ref[7:8]
        for half in range(2):
            rows = pl.ds(pl.multiple_of(t * 16 + half * 8, 8), 8)
            back = front_own[rows] + front_got[0, rows] + front_got[1, rows] + front_got[2, rows]
            hidden = one[rows]
            normed, inverse = row_stats(hidden * scale + shift)
            two = conv[rows] + inverse * (
                back
                - jnp.mean(back, axis=-1, keepdims=True)
                - normed * jnp.mean(back * normed, axis=-1, keepdims=True)
            )
            grad[rows] = two * scale
            ratio[0, 0:8] += two * hidden
            ratio[0, 8:16] += two
        for copy in near_tile(t):
            copy.start()

    def give_late(t):
        for copy in late():
            copy.start()
        one_kept.start()
        wide[0:pixels] = grad[...]

    def gathered(t):
        def wait(i, carry):
            for copy in near_tile(i):
                copy.wait()
            return carry

        lax.fori_loop(0, pixels // 16, wait, 0)
        for copy in late():
            copy.wait()
        one_kept.wait()
        text_kept.start()

        def piece(i, carry):
            rows = pl.ds(pl.multiple_of(i * 16, 16), 16)
            high[rows], low[rows] = halves(wide[rows])
            return carry

        lax.fori_loop(0, spots // 16, piece, 0)

    def mapper_stores():
        half = mapper_part.shape[1]
        return [
            pltpu.make_async_copy(
                mapped.at[pl.ds(c * half, half)], mapper_part.at[c], load.at[10 + c]
            )
            for c in (0, 1)
        ]

    def text_products(t):
        left = halves(silu_ref[...])

        def strip(k, carry):
            cols = pl.ds(pl.multiple_of(k * TILE, TILE), TILE)
            right = halves(text_all[:, :, cols].reshape(-1, TILE))
            mapped[:, cols] = three_pass(left, right, ((0,), (0,)))
            return carry

        lax.fori_loop(0, count, strip, 0)
        for copy in mapper_stores():
            copy.start()
        column_pair(0)[0].start()
        column_pair(0)[1].start()
        first_loads[0].wait()
        total = ratio[0] + ratio[1] + ratio[2] + ratio[3]
        scale_sum = jnp.sum(total[0:8], axis=0, keepdims=True)
        shift_sum = jnp.sum(total[8:16], axis=0, keepdims=True)
        odd = lax.rem(lax.broadcasted_iota(jnp.int32, (CHUNK, chan), 0), 2) == 1
        both = jnp.where(odd, shift_sum, scale_sum)
        small[0] = both * embed_ref[:, 0:1]
        sums[4:5] = scale_sum
        sums[5:6] = shift_sum
        sums[6:7] = jnp.sum(wide[...], axis=0, keepdims=True)
        sums[7:8] = jnp.sum(text_all[...].reshape(-1, chan), axis=0, keepdims=True)
        width = chan // 4
        place = pl.ds(pl.multiple_of(me * width, width), width)
        small[1, 3:4, 0:width] = sums[6:7, place]
        small[1, 3:4, width : 2 * width] = sums[7:8, place]
        pair_place = pl.ds(pl.multiple_of(lax.rem(me, 2) * 2 * width, width), 2 * width)
        small[1, 4:5, width : 3 * width] = jnp.where(
            me < 2, sums[4:5, pair_place], sums[5:6, pair_place]
        )

    def column_pair(i):
        return [
            pltpu.make_async_copy(
                response_ref.at[
                    :, pl.ds(pl.multiple_of(c * (chan // 2) + i * 128, 128), 128)
                ],
                columns.at[lax.rem(i, 2), :, pl.ds(c * 128, 128)],
                load.at[6 + lax.rem(i, 2) if c == 0 else 12 + lax.rem(i, 2)],
            )
            for c in (0, 1)
        ]

    def reduce_stores(i):
        return [
            pltpu.make_async_copy(
                product.at[pl.ds(c * 128, 128)],
                reduce_part.at[c, pl.ds(pl.multiple_of(i * 128, 128), 128)],
                load.at[8 + c],
            )
            for c in (0, 1)
        ]

    def reduce_outer(i):
        for copy in column_pair(i):
            copy.wait()

        @pl.when(i + 1 < count)
        def _():
            for copy in column_pair(jnp.minimum(i + 1, count - 1)):
                copy.start()

        @pl.when(i + 1 == count)
        def _():
            weight_load(reduce_w_ref, 0).start()
            act_load(0).start()

        @pl.when(i > 0)
        def _():
            for copy in reduce_stores(jnp.maximum(i - 1, 0)):
                copy.wait()

        @pl.when(i == 0)
        def _():
            for copy in mapper_stores():
                copy.wait()

        left = halves(columns[lax.rem(i, 2), :, 0:TILE])

        def strip(k, carry):
            cols = pl.ds(pl.multiple_of(k * TILE, TILE), TILE)
            product[0:TILE, cols] = three_pass(left, (high[:, cols], low[:, cols]), ((0,), (0,)))
            return carry

        lax.fori_loop(0, count, strip, 0)
        for copy in reduce_stores(i):
            copy.start()

    def settle_reduce(t):
        for copy in reduce_stores(count - 1):
            copy.wait()
        text_kept.wait()
        for copy in loads:
            copy.start()
        sums[0:4] = jnp.zeros((4, chan), jnp.float32)

    outward = near_slots(out_ref, out_got, send, recv, 3)

    def away(i):
        rows = pl.ds(pl.multiple_of(i * 8, 8), 8)
        return remote(
            base.at[rows], layer_out.at[rows], tile_out.at[i], tile_in.at[i], (core, up, over)
        )

    def here(i):
        rows = pl.ds(pl.multiple_of(i * 8, 8), 8)
        return pltpu.make_async_copy(base.at[rows], layer_out.at[rows], tile_out.at[i])

    first_loads = [pltpu.make_async_copy(small_ref, small, keep.at[1])]
    loads = [
        pltpu.make_async_copy(conv_ref, conv, keep.at[2]),
        pltpu.make_async_copy(out_ref.at[0], out_own, keep.at[3]),
        pltpu.make_async_copy(base_ref, base, keep.at[4]),
    ]
    kept = pltpu.make_async_copy(one, grad_out, keep.at[5])

    def tile_rows(i):
        return pl.ds(pl.multiple_of(i * TILE, TILE), TILE)

    def weight_load(ref, i):
        return pltpu.make_async_copy(
            ref.at[tile_rows(i)], weights.at[lax.rem(i, 2)], load.at[lax.rem(i, 2)]
        )

    def act_load(i):
        return pltpu.make_async_copy(
            act_ref.at[:, tile_rows(i)], acts.at[lax.rem(i, 2)], load.at[2 + lax.rem(i, 2)]
        )

    def slope_load(i):
        return pltpu.make_async_copy(
            slope_ref.at[:, tile_rows(i)], slopes.at[lax.rem(i, 2)], load.at[4 + lax.rem(i, 2)]
        )

    part = columns.shape[2]

    def column_load(i):
        return pltpu.make_async_copy(
            normed_ref.at[:, pl.ds(pl.multiple_of(i * part, part), part)],
            columns.at[lax.rem(i, 2)],
            load.at[6 + lax.rem(i, 2)],
        )

    def product_stores(i):
        half = part // 2
        return [
            pltpu.make_async_copy(
                product.at[pl.ds(c * half, half)], expand_part.at[i, c], load.at[8 + c]
            )
            for c in (0, 1)
        ]

    def front_sends(i):
        found = []
        for step in (3, 1, 2):
            found.append(
                remote(
                    front.at[lax.rem(i, 2), pl.ds(step * pixels, pixels)],
                    front_got.at[step - 1, :, tile_rows(i)],
                    front_out.at[i, step - 1],
                    front_in.at[i, step - 1],
                    (core, level, near_of(me, step)),
                )
            )
        return found

    for copy in early_loads()[0] + [early_column(0), early_column(1)]:
        copy.start()
    for copy in scatters + start_loads + first_loads:
        copy.start()

    def respond(i):
        weight_load(reduce_w_ref, i).wait()
        act_load(i).wait()

        @pl.when(i + 1 < count)
        def _():
            weight_load(reduce_w_ref, i + 1).start()
            act_load(i + 1).start()

        @pl.when(i + 1 == count)
        def _():
            act_load(0).start()
            slope_load(0).start()

        right = halves(weights[lax.rem(i, 2)])
        cols = tile_rows(i)

        def strip(k, carry):
            rows = pl.ds(pl.multiple_of(k * pixels, pixels), pixels)
            value = three_pass((high[rows], low[rows]), right, ((1,), (1,)))
            wide[rows, cols] = value
            sums[0:1, cols] += jnp.sum(value * acts[lax.rem(i, 2), rows], axis=0, keepdims=True)
            sums[1:2, cols] += jnp.sum(value, axis=0, keepdims=True)
            return carry

        lax.fori_loop(0, 4, strip, 0)

    def spreads():
        return [
            remote(
                spread_own, spread_got.at[step - 1], spread_out.at[step - 1],
                spread_in.at[step - 1], (core, level, near_of(me, step)),
            )
            for step in (3, 1, 2)
        ]

    def send_out(t):
        for copy in outward:
            copy.start()

    def share(t):
        total = jnp.sum(sums[0:1] * rows_ref[0:1] * rows_ref[1:2], axis=1, keepdims=True)
        spread_own[...] = jnp.broadcast_to(total, spread_own.shape)
        for copy in spreads():
            copy.start()

    def agree(t):
        for copy in spreads():
            copy.wait()
        total = spread_own[...] + spread_got[0] + spread_got[1] + spread_got[2]
        total = jnp.max(total[0:1], axis=1, keepdims=True)
        inverse = rows_ref[3:4]
        norms = rows_ref[1:2]
        grad_norms = (
            sums[0:1] * rows_ref[0:1] * inverse - total * rows_ref[4:5] * inverse * inverse
        )
        sums[2:3] = grad_norms / norms
        small[1, 1:2] = sums[0:1] * rows_ref[5:6]
        small[1, 2:3] = sums[1:2]

    def bend(i):
        act_load(i).wait()
        slope_load(i).wait()

        @pl.when(i + 1 < count)
        def _():
            act_load(i + 1).start()
            slope_load(i + 1).start()

        @pl.when(i + 1 == count)
        def _():
            column_load(0).start()
            weight_load(expand_w_ref, 0).start()

        cols = tile_rows(i)
        factor = rows_ref[2:3, cols]
        twice = sums[2:3, cols]

        def strip(k, carry):
            rows = pl.ds(pl.multiple_of(k * 48, 48), 48)
            value = (
                wide[rows, cols] * factor + acts[lax.rem(i, 2), rows] * twice
            ) * slopes[lax.rem(i, 2), rows]
            high[rows, cols], low[rows, cols] = halves(value)
            sums[3:4, cols] += jnp.sum(value, axis=0, keepdims=True)
            return carry

        lax.fori_loop(0, spots // 48, strip, 0)

    def outer(i):
        column_load(i).wait()
        pl.when(i + 1 < 4)(lambda: column_load(jnp.minimum(i + 1, 3)).start())
        pl.when(i > 0)(lambda: [copy.wait() for copy in product_stores(jnp.maximum(i - 1, 0))] and None)
        left = halves(columns[lax.rem(i, 2)])

        def strip(k, carry):
            cols = pl.ds(pl.multiple_of(k * TILE, TILE), TILE)
            product[:, cols] = three_pass(left, (high[:, cols], low[:, cols]), ((0,), (0,)))
            return carry

        lax.fori_loop(0, count, strip, 0)
        for copy in product_stores(i):
            copy.start()

    def settle_outer(t):
        for copy in product_stores(3):
            copy.wait()
        small[1, 0:1] = sums[3:4]

    def backward(i):
        weight_load(expand_w_ref, i).wait()
        pl.when(i + 1 < count)(lambda: weight_load(expand_w_ref, jnp.minimum(i + 1, count - 1)).start())

        @pl.when(i > 1)
        def _():
            for copy in front_sends(jnp.maximum(i - 2, 0)):
                copy.wait_send()

        right = halves(weights[lax.rem(i, 2)])

        def strip(k, carry):
            rows = pl.ds(pl.multiple_of(k * pixels, pixels), pixels)
            front[lax.rem(i, 2), rows] = three_pass((high[rows], low[rows]), right, ((1,), (1,)))
            return carry

        lax.fori_loop(0, 4, strip, 0)
        front_own[:, tile_rows(i)] = front[lax.rem(i, 2), 0:pixels]
        for copy in front_sends(i):
            copy.start()

    def middle(t):
        loads[0].wait()
        for i in range(count):
            for copy in front_sends(i):
                copy.wait_recv()
                if i >= count - 2:
                    copy.wait_send()

    def tiles(t):
        def tile(i, carry):
            rows = pl.ds(pl.multiple_of(i * 8, 8), 8)
            back = front_own[rows] + front_got[0, rows] + front_got[1, rows] + front_got[2, rows]
            normed, inverse = row_stats(conv[rows])
            one[rows] = inverse * (
                back
                - jnp.mean(back, axis=-1, keepdims=True)
                - normed * jnp.mean(back * normed, axis=-1, keepdims=True)
            )
            return carry

        size = pixels // 48
        lax.fori_loop(t * size, (t + 1) * size, tile, 0)

    def give(t):
        kept.start()

    def outlet(t):
        pl.when(t == 0)(lambda: [copy.wait() for copy in loads[1:] + outward] and None)
        rows = pl.ds(pl.multiple_of(t * 8, 8), 8)
        base[rows] += out_own[rows] + out_got[0, rows] + out_got[1, rows] + out_got[2, rows]
        pl.when(moves)(away(t).start)
        pl.when(jnp.logical_not(moves))(here(t).start)

    sum_stream(
        [
            ("plain", output_ref, output_out),
            ("swap", attend_part, attend_out),
            ("plain", mapper_part, mapper_out),
            ("plain", reduce_part, reduce_out),
            ("plain", small, small_out),
            ("swap", expand_part, expand_out),
        ],
        scratch[:SCRATCH],
        [
            (0, 1, prepare),
            (1, 5, attend_outer),
            (5, 6, settle_attend),
            (12, 13, arrive),
            (12, 21, normalize),
            (21, 22, give_late),
            (24, 25, gathered),
            (25, 26, text_products),
            (26, 32, reduce_outer),
            (32, 33, settle_reduce),
            (33, 39, respond),
            (39, 40, share),
            (40, 41, agree),
            (41, 47, bend),
            (47, 51, outer),
            (51, 52, settle_outer),
            (52, 58, backward),
            (68, 69, middle),
            (68, 74, tiles),
            (74, 75, give),
            (60, 78, outlet),
            (43, 44, send_out),
        ],
    )
    kept.wait()

    def settle(i, carry):
        pl.when(moves)(away(i).wait)
        pl.when(jnp.logical_not(moves))(here(i).wait)
        return carry

    lax.fori_loop(0, base.shape[0] // 8, settle, 0)


def backward_sums(
    collective, output_part, qkv, two_share, text_share, cot, one, response, reduce_w, act, slope,
    normed_all, expand_w, conv, out_share, base, small, normed_two, rows, embed, silu, mapped,
    text_kv, mapper_half
):
    pixels, chan = conv.shape
    spots = normed_all.shape[0]
    texts = text_share.shape[1]
    slots = silu.shape[0] // 4
    f32, bf16 = jnp.float32, jnp.bfloat16
    half = chan // 8
    count = chan // TILE

    def shape(*dims):
        return jax.ShapeDtypeStruct(dims, f32)

    total = (half + 8 * half // 2 + mapper_half + chan // 2 + CHUNK + 8 * half // 2) // CHUNK
    block = (pixels, chan)
    return pl.pallas_call(
        backward_body,
        out_shape=[
            shape(2, half, chan),
            shape(2, half, 3 * chan),
            shape(2, mapper_half, chan),
            shape(2, chan // 2, chan),
            shape(2, CHUNK, chan),
            shape(2, half, 4 * chan),
            shape(4, 2, half, 3 * chan // 4),
            shape(2, mapper_half, chan),
            shape(2, chan // 2, chan),
            shape(4, 2, half, chan),
            shape(*block),
            shape(4, slots, chan),
            shape(*block),
            shape(*block),
        ],
        in_specs=[ANY] * 17 + [pl.BlockSpec(memory_space=pltpu.VMEM)] * 5,
        out_specs=[ANY] * 14,
        scratch_shapes=stream_scratch(total, 4 * half // CHUNK, chan)
        + [
            pltpu.VMEM((3,) + block, f32),
            pltpu.VMEM(block, f32),
            pltpu.VMEM(block, f32),
            pltpu.VMEM(block, f32),
            pltpu.VMEM(block, f32),
            pltpu.VMEM((3,) + block, f32),
            pltpu.VMEM(block, f32),
            pltpu.VMEM(block, f32),
            pltpu.VMEM(small.shape, f32),
            pltpu.VMEM((spots, chan), f32),
            pltpu.VMEM((spots, chan), bf16),
            pltpu.VMEM((spots, chan), bf16),
            pltpu.VMEM((2, TILE, chan), f32),
            pltpu.VMEM((2, spots, TILE), f32),
            pltpu.VMEM((2, spots, TILE), f32),
            pltpu.VMEM((2, spots, chan // 4), f32),
            pltpu.VMEM((chan // 4, chan), f32),
            pltpu.VMEM((2, spots, TILE), f32),
            pltpu.VMEM((8, chan), f32),
            pltpu.VMEM((8, 128), f32),
            pltpu.VMEM((3, 8, 128), f32),
            pltpu.VMEM((3, texts, chan), f32),
            pltpu.VMEM((texts, chan), f32),
            pltpu.VMEM((4, slots, chan), f32),
            pltpu.VMEM((4, 16, chan), f32),
            pltpu.VMEM((silu.shape[1], chan), f32),
            DMA((9,)),
            DMA((9,)),
            DMA((12,)),
            DMA((pixels // 8,)),
            DMA((pixels // 8,)),
            DMA((14,)),
            DMA((count, 3)),
            DMA((count, 3)),
            DMA((3,)),
            DMA((3,)),
            DMA((pixels // 16, 3)),
            DMA((pixels // 16, 3)),
            DMA((6,)),
            DMA((6,)),
        ],
        compiler_params=pltpu.CompilerParams(
            collective_id=collective, has_side_effects=True, vmem_limit_bytes=62 * 2**20
        ),
        name="backward_sums",
    )(
        output_part, qkv, two_share, text_share, cot, one, response, reduce_w, act, slope,
        normed_all, expand_w, conv, out_share, base, small, normed_two, rows, embed, silu, mapped,
        text_kv,
    )


def close_body(
    grad_in, token_in, conv_in, up_in, down_in,
    grad_home, token_home, conv_all, below, above,
    hold, send, recv, keep
):
    core = lax.axis_index("cond")
    level = lax.axis_index("pair")
    me = lax.axis_index("dp")
    up, over = home_spot(level, me)
    back_up, back_over = plane_spot(level, me)
    moves = jnp.logical_or(level != 0, me != 0)
    others = [(c, s) for c in (0, 1) for s in (0, 1, 2, 3) if (c, s) != (0, 0)]

    def other(c, s):
        return (lax.rem(core + c, 2), lax.rem(level + s, 4), me)

    for c, s in others:
        greet(other(c, s))
    pl.when(moves)(lambda: greet((core, back_up, back_over)))
    turned = jnp.logical_and(level == 1, me == 1)
    quarter = up
    lifts = quarter > 0
    drops = jnp.logical_and(quarter < 3, jnp.logical_not(turned))
    lifted = level < 3
    dropped = jnp.logical_and(level > 0, jnp.logical_not(turned))
    pl.when(lifted)(lambda: greet((core, me, near_of(me, rev(jnp.minimum(level + 1, 3))))))
    pl.when(dropped)(lambda: greet((core, me, near_of(me, rev(jnp.maximum(level - 1, 0))))))
    pl.semaphore_wait(
        pltpu.get_barrier_semaphore(),
        7 + jnp.where(moves, 1, 0) + jnp.where(lifts, 1, 0) + jnp.where(drops, 1, 0),
    )
    lift = remote(up_in, below, send.at[9], recv.at[9], (core, jnp.maximum(quarter - 1, 0), level))
    drop = remote(down_in, above, send.at[10], recv.at[10], (core, jnp.minimum(quarter + 1, 3), level))
    around = pltpu.make_async_copy(down_in, above, keep.at[3])
    pl.when(lifts)(lift.start)
    pl.when(drops)(drop.start)
    pl.when(turned)(around.start)
    swaps = ((grad_in, grad_home), (token_in, token_home))
    aways = [remote(src, dst, send.at[i], recv.at[i], (core, up, over)) for i, (src, dst) in enumerate(swaps)]
    spreads = [
        remote(conv_in, conv_all.at[1 + i], send.at[2 + i], recv.at[2 + i], other(c, s))
        for i, (c, s) in enumerate(others)
    ]
    mine = pltpu.make_async_copy(conv_in, conv_all.at[0], keep.at[2])
    for copy in spreads + [mine]:
        copy.start()
    for away in aways:
        pl.when(moves)(away.start)

    @pl.when(jnp.logical_not(moves))
    def _():
        load = pltpu.make_async_copy(grad_in, hold, keep.at[0])
        store = pltpu.make_async_copy(hold, grad_home, keep.at[0])
        small = pltpu.make_async_copy(token_in, token_home, keep.at[1])
        small.start()
        load.start()
        load.wait()
        store.start()
        store.wait()
        small.wait()

    for copy in spreads + [mine]:
        copy.wait()
    for away in aways:
        pl.when(moves)(away.wait)
    pl.when(lifts)(lift.wait_send)
    pl.when(drops)(drop.wait_send)
    pl.when(lifted)(lift.wait_recv)
    pl.when(dropped)(drop.wait_recv)
    pl.when(turned)(around.wait)


def close_exchange(collective, grad, tokens, conv, up, down):
    shapes = [grad.shape, tokens.shape, (8,) + conv.shape, up.shape, down.shape]
    return pl.pallas_call(
        close_body,
        out_shape=[jax.ShapeDtypeStruct(shape, jnp.float32) for shape in shapes],
        in_specs=[ANY] * 5,
        out_specs=[ANY] * 5,
        scratch_shapes=[pltpu.VMEM(grad.shape, jnp.float32), DMA((11,)), DMA((11,)), DMA((4,))],
        compiler_params=pltpu.CompilerParams(collective_id=collective, has_side_effects=True),
        name="close_exchange",
    )(grad, tokens, conv, up, down)


def plane_body(
    latents,
    ratio_embed,
    clip_tokens,
    cotangent,
    conv_kernel,
    conv_bias,
    expand_weight,
    expand_bias,
    response_gain,
    response_bias,
    reduce_weight,
    reduce_bias,
    ratio_weight,
    ratio_bias,
    text_weight,
    text_bias,
    attend_weight,
    query_bias,
    value_bias,
    output_weight,
    output_bias,
):
    size = lax.axis_size("dp")
    core = lax.axis_index("cond")
    me = lax.axis_index("dp")
    level = lax.axis_index("pair")
    quarter = home_spot(level, me)[0]
    order = jnp.bitwise_xor(jnp.arange(4), me)
    _, rows, cols, chan = latents.shape
    pixels = rows * cols
    part = chan // size
    hid = size * expand_bias.shape[0]
    texts = clip_tokens.shape[1]
    packed = jnp.concatenate(
        [
            conv_kernel.reshape(9, part),
            conv_bias[None],
            reduce_bias[None],
            text_bias[None],
            output_bias[None],
            ratio_bias.reshape(2, part),
        ],
        axis=0,
    )
    row_padded, every, tokens, embed, expand_w, attend_units = open_exchange(
        3, latents[0], packed, clip_tokens[0], ratio_embed, expand_weight, attend_weight
    )[:6]
    row_padded = row_padded.at[:1].set(jnp.where(quarter > 0, row_padded[:1], 0.0))
    row_padded = row_padded.at[-1:].set(jnp.where(quarter < size - 1, row_padded[-1:], 0.0))
    image = row_padded[1:-1]
    expand_w = expand_w.reshape(chan, -1)
    channel_rows = every[:, :13].transpose(1, 0, 2).reshape(13, chan)
    kernel = channel_rows[:9].reshape(3, 3, chan)
    conv_shift, reduce_b, text_b, out_b = (channel_rows[9 + i] for i in range(4))
    ratio_b = every[:, 13:].reshape(2 * chan)

    half = part // 2
    wide = hid // size
    text_part = text_weight.shape[0]
    token_cols = [
        lax.dynamic_slice(tokens, (0, near_of(me, step) * text_part), (texts, text_part))
        for step in range(4)
    ]
    ratio_part = ratio_weight.shape[0]
    embed_part = lax.dynamic_slice(embed, (0, me * ratio_part), (1, ratio_part))
    mod_part = jnp.dot(embed_part, ratio_weight, precision=HIGHEST_ACCURACY)

    padded = jnp.pad(row_padded, ((0, 0), (1, 1), (0, 0)))
    total_conv = conv_shift
    for i in range(3):
        for j in range(3):
            total_conv = total_conv + padded[i : i + rows, j : j + cols] * kernel[i, j]
    normed, inverse = norm_stats(total_conv.reshape(pixels, chan))
    normed_all, mod_near, near_tokens, attend_w = exchange(
        4,
        gathers=(normed, mod_part),
        scatters=(jnp.stack(token_cols),),
        relay=(attend_units,),
    )
    attend_w = attend_w.reshape(chan, 3 * part)
    modulation = jnp.sum(mod_near[:, 0], axis=0) + ratio_b
    mod_scale = 1.0 + modulation[:chan]
    mod_shift = modulation[chan:]
    normed_all = normed_all.reshape(size * pixels, chan)
    cot, normed_all = lax.optimization_barrier((cotangent[0].reshape(pixels, chan), normed_all))
    turns = (0, 2, 1, 3)
    grid = [(z, d) for z in range(size) for d in range(size)]
    cot = lax.ppermute(
        cot, ("pair", "dp"), [(z * size + d, z * size + (d ^ turns[z])) for z, d in grid]
    )
    near_tokens = jnp.concatenate([token_cols[0], near_tokens.reshape(-1, text_part)], axis=0)
    silu_near = jax.nn.silu(near_tokens)
    mapped_share = dot(silu_near, text_weight).reshape(4, texts, chan)
    hidden = dot(normed_all, expand_w) + expand_bias
    bell = 0.5 * (1.0 + lax.erf(hidden * 0.5**0.5))
    activated = hidden * bell
    density = jnp.exp(-0.5 * hidden * hidden) * (2.0 * jnp.pi) ** -0.5
    slope = bell + hidden * density
    totals = jnp.sum(activated * activated, axis=0)
    norms = jnp.sqrt(totals + EPSILON)
    norm_sums = exchange(5, gathers=(jnp.full((8, 128), jnp.sum(norms)),))[0]
    middle = jnp.sum(norm_sums[:, 0, 0]) / hid + EPSILON
    scaled = norms / middle
    factor = 1.0 + response_gain * scaled
    response = activated * factor + response_bias
    one_share = dot(response, reduce_weight).reshape(4, pixels, chan)
    cot, one_share = lax.optimization_barrier((cot, one_share))
    cot = lax.ppermute(
        cot, ("pair", "dp"), [(z * size + d, (d ^ turns[z]) * size + d) for z, d in grid]
    )
    one_arrived, mapped_arrived = exchange(6, scatters=(one_share, mapped_share))
    mapped = mapped_share[0] + jnp.sum(mapped_arrived, axis=0) + text_b
    hidden_one = one_share[0] + jnp.sum(one_arrived, axis=0) + image.reshape(pixels, chan) + reduce_b
    hidden_two = hidden_one * mod_scale + mod_shift
    normed_two, inverse_two = norm_stats(hidden_two)
    cot, normed_two = lax.optimization_barrier((cot, normed_two))
    normed_two_all, mapped_all = exchange(7, gathers=(normed_two, mapped))
    cot, normed_two_all = lax.optimization_barrier((cot, normed_two_all))
    cot_all = jnp.concatenate(
        [cot]
        + [lax.ppermute(cot, "dp", [(i, i ^ step) for i in range(size)]) for step in (1, 2, 3)],
        axis=0,
    )
    normed_two_all = normed_two_all.reshape(size * pixels, chan)
    mapped_all = mapped_all.reshape(size * texts, chan)

    source = jnp.concatenate([normed_two_all, mapped_all], axis=0)
    query = dot(normed_two_all, attend_w[:, :part]) + query_bias
    key_value = dot(source, attend_w[:, part:])
    key = key_value[:, :part]
    value = key_value[:, part:] + value_bias
    query_h, key_h, value_h = heads_of(query), heads_of(key), heads_of(value)
    scores = jnp.einsum("iuy,ouy->uio", query_h, key_h, precision=FAST) * HEAD_CHANNELS ** (-0.5)
    expo = jnp.exp(scores - jnp.max(scores, axis=-1, keepdims=True))
    probs = expo / jnp.sum(expo, axis=-1, keepdims=True)
    mixture_h = jnp.einsum("uio,ouy->iuy", probs, value_h, precision=FAST)
    mixture = mixture_h.reshape(query.shape)
    out_share = dot(mixture, output_weight).reshape(4, pixels, chan)
    out_base = hidden_two + out_b

    output_grad = t_dot(mixture, cot_all)
    grad_mix_h = heads_of(dot_t(cot_all, output_weight))
    grad_probs = jnp.einsum("iuy,ouy->uio", grad_mix_h, value_h, precision=FAST)
    delta = jnp.sum(grad_mix_h * mixture_h, axis=-1).T
    grad_scores = probs * (grad_probs - delta[..., None]) * HEAD_CHANNELS ** (-0.5)
    grad_query = jnp.einsum("uio,ouy->iuy", grad_scores, key_h, precision=FAST).reshape(query.shape)
    grad_key = jnp.einsum("uio,iuy->ouy", grad_scores, query_h, precision=FAST).reshape(key.shape)
    grad_value = jnp.einsum("uio,iuy->ouy", probs, grad_mix_h, precision=FAST).reshape(key.shape)
    spots = size * pixels
    grad_kv = jnp.concatenate([grad_key, grad_value], axis=1)
    grad_qkv = jnp.concatenate([grad_query, grad_kv[:spots]], axis=1)
    two_share = dot_t(grad_qkv, attend_w).reshape(4, pixels, chan)
    text_share = dot_t(grad_kv[spots:], attend_w[:, part:]).reshape(4, texts, chan)
    def row(value):
        return jnp.sum(value, axis=0, keepdims=True)

    def mine(value):
        width = value.shape[1] // size
        return lax.dynamic_slice(value, (0, me * width), (value.shape[0], width))

    gap = jnp.zeros((1, part), jnp.float32)
    small_rows = jnp.concatenate(
        [
            jnp.zeros((3, chan), jnp.float32),
            jnp.concatenate([gap, gap, row(grad_query), row(grad_value)], axis=1),
            jnp.concatenate([row(mine(cot_all)), gap, gap, gap], axis=1),
            jnp.zeros((CHUNK - 5, chan), jnp.float32),
        ],
        axis=0,
    )
    one_row = jnp.full((1, chan), 1.0, jnp.float32)
    back_rows = jnp.concatenate(
        [
            response_gain[None],
            norms[None],
            factor[None],
            one_row / middle,
            one_row / hid,
            scaled[None],
            mod_scale[None],
            mod_shift[None],
        ],
        axis=0,
    )
    slots = (texts + 7) // 8 * 8

    def padded_rows(value):
        value = value.reshape(4, texts, -1)
        return jnp.pad(value, ((0, 0), (0, slots - texts), (0, 0))).reshape(4 * slots, -1)

    silu_padded = jnp.pad(
        silu_near.reshape(4, texts, text_part), ((0, 0), (0, slots - texts), (0, -text_part % 128))
    ).reshape(4 * slots, -1)
    embed_rows = jnp.broadcast_to(
        embed_part.reshape(ratio_part, 1, 1), (ratio_part, 2, 128)
    ).reshape(2 * ratio_part, 128)
    (
        output_sum, attend_sum, mapper_sum, reduce_sum, small, expand_sum, _, _, _, _,
        grad_one, grad_mapped_all, grad_conv, layer_output,
    ) = backward_sums(
        1,
        output_grad.reshape(2, half, chan),
        grad_qkv,
        two_share,
        text_share,
        cot,
        hidden_one,
        response,
        reduce_weight,
        activated,
        slope,
        normed_all,
        expand_w,
        total_conv.reshape(pixels, chan),
        out_share,
        out_base,
        jnp.stack([jnp.zeros((CHUNK, chan), jnp.float32), small_rows]),
        normed_two_all,
        back_rows,
        embed_rows,
        silu_padded,
        padded_rows(mapped_all),
        padded_rows(grad_kv[spots:]),
        text_part // 2,
    )
    output_sum = output_sum.reshape(part, chan)
    attend_sum = attend_sum.reshape(part, 3 * chan)
    mapper_sum = mapper_sum.reshape(text_part, chan)
    reduce_sum = reduce_sum.reshape(wide, chan)
    expand_sum = expand_sum.reshape(part, hid)
    layer_output = layer_output.reshape(latents.shape)
    grad_mapped_all = grad_mapped_all[:, :texts].reshape(size * texts, chan)
    gate = 1.0 / (1.0 + jnp.exp(-near_tokens))
    tokens_near = dot_t(grad_mapped_all, text_weight) * (
        gate * (1.0 + near_tokens * (1.0 - gate))
    )
    tokens_near = tokens_near.reshape(4, texts, text_part)
    grad_conv = grad_conv.reshape(rows, cols, chan)
    kernel_grad = jnp.stack(
        [
            jnp.sum(padded[i : i + rows, j : j + cols] * grad_conv, axis=(0, 1))
            for i in range(3)
            for j in range(3)
        ]
    )
    spread_conv = jnp.pad(grad_conv, ((2, 2), (1, 1), (0, 0)))
    latent_rows = jnp.zeros((rows + 2, cols, chan), jnp.float32)
    for i in range(3):
        for j in range(3):
            latent_rows = (
                latent_rows
                + spread_conv[2 - i : 2 - i + rows + 2, 2 - j : 2 - j + cols] * kernel[i, j]
            )
    conv_part = jnp.concatenate([kernel_grad, jnp.sum(grad_conv, axis=(0, 1))[None]], axis=0)
    conv_blocks = jnp.stack(
        [
            lax.dynamic_slice(conv_part, (0, near_of(me, step) * part), (10, part))
            for step in range(4)
        ]
    )
    conv_arrived, token_arrived = exchange(13, scatters=(conv_blocks, tokens_near))
    token_blocks = jnp.take(
        jnp.concatenate([tokens_near[:1], token_arrived], axis=0), order, axis=0
    )
    inner = latent_rows[1:-1] + grad_one.reshape(rows, cols, chan)
    latent_grad, tokens_grad, conv_all, from_below, from_above = close_exchange(
        14,
        inner.reshape(pixels, chan),
        token_blocks.transpose(1, 0, 2).reshape(texts, size * text_part),
        conv_blocks[0] + jnp.sum(conv_arrived, axis=0),
        latent_rows[0],
        latent_rows[-1],
    )
    from_above = jnp.where(level > 0, from_above, 0.0)[None]
    from_below = jnp.where(level < size - 1, from_below, 0.0)[None]
    still = jnp.zeros((rows - 2, cols, chan), jnp.float32)
    latent_grad = latent_grad.reshape(rows, cols, chan) + jnp.concatenate(
        [from_above, still, from_below], axis=0
    )
    latent_grad = latent_grad[None]
    tokens_grad = tokens_grad[None]
    conv_mine = jnp.sum(conv_all, axis=0)
    ratio = small[0]
    expb, gain, respb = (small[1, i] for i in range(3))
    redb, mapb, queryb, valueb = (small[1, 3, i * part : (i + 1) * part] for i in range(4))
    outb = small[1, 4, :part]
    ratiob = small[1, 4, part : 3 * part]
    return (
        layer_output,
        latent_grad,
        tokens_grad,
        conv_mine[:9].reshape(3, 3, part),
        conv_mine[9],
        expand_sum,
        expb,
        gain,
        respb,
        reduce_sum,
        redb,
        ratio.reshape(ratio_part, 2 * chan),
        ratiob,
        mapper_sum,
        mapb,
        attend_sum,
        queryb,
        valueb,
        output_sum,
        outb,
    )


def solution(mesh):
    square = mesh.shape["cond"] == 2 and mesh.shape["pair"] == 4 and mesh.shape["dp"] == 4
    return jax.shard_map(
        plane_body if square else body,
        mesh=mesh,
        in_specs=(
            P(("cond", "dp"), "pair", None, None),
            P(("cond", "dp"), None),
            P(("cond", "dp"), "pair", None),
            P(("cond", "dp"), "pair", None, None),
            P(None, None, "dp"),
            P("dp"),
            P("dp", None),
            P("dp"),
            P("dp"),
            P("dp"),
            P("dp", None),
            P("dp"),
            P("dp", None),
            P("dp"),
            P("dp", None),
            P("dp"),
            P("dp", None),
            P("dp"),
            P("dp"),
            P("dp", None),
            P("dp"),
        ),
        out_specs=(
            P(("cond", "dp"), "pair", None, None),
            P(("cond", "dp"), "pair", None, None),
            P(("cond", "dp"), "pair", None),
            P(None, None, "dp"),
            P("dp"),
            P("dp", None),
            P("dp"),
            P("dp"),
            P("dp"),
            P("dp", None),
            P("dp"),
            P("dp", None),
            P("dp"),
            P("dp", None),
            P("dp"),
            P("dp", None),
            P("dp"),
            P("dp"),
            P("dp", None),
            P("dp"),
        ),
        check_vma=False,
    )
```

```python
import functools

import jax
import jax.numpy as jnp
from jax import lax
from jax.experimental import pallas as pl
from jax.experimental.pallas import tpu as pltpu
from jax.sharding import PartitionSpec as P

HEADS = 24
HEAD_CHANNELS = 64


HIGHEST_ACCURACY = lax.Precision.HIGHEST
EPSILON = 1e-06


def extended(block, sides, width):
    for axis, dim in sides:
        count = lax.axis_size(axis)
        forward = [(i, i + 1) for i in range(count - 1)]
        backward = [(target, source) for source, target in forward]
        low = lax.ppermute(
            lax.slice_in_dim(block, block.shape[dim] - width, None, axis=dim), axis, forward
        )
        high = lax.ppermute(lax.slice_in_dim(block, 0, width, axis=dim), axis, backward)
        block = jnp.concatenate([low, block, high], axis=dim)
    return block


def layer_norm(values):
    centered = values - jnp.mean(values, axis=-1, keepdims=True)
    variance = jnp.mean(centered * centered, axis=-1, keepdims=True)
    return centered * lax.rsqrt(variance + EPSILON)


def matmul(left, right):
    return jnp.einsum("...k,kn->...n", left, right, precision=HIGHEST_ACCURACY)


def depthwise(row_padded, kernel, conv_shift):
    row_count = row_padded.shape[1] - 2
    col_count = row_padded.shape[2]
    padded = jnp.pad(row_padded, ((0, 0), (0, 0), (1, 1), (0, 0)))
    total_conv = conv_shift
    for row_off in range(3):
        for col_off in range(3):
            total_conv = (
                total_conv
                + padded[:, row_off : row_off + row_count, col_off : col_off + col_count, :]
                * kernel[row_off, col_off]
            )
    return total_conv


def front(row_padded, kernel, conv_shift, expand_w, expand_b):
    normed = layer_norm(depthwise(row_padded, kernel, conv_shift))
    flat = normed.reshape(normed.shape[0], normed.shape[1] * normed.shape[2], normed.shape[3])
    return jax.nn.gelu(matmul(flat, expand_w) + expand_b, approximate=False)


def response_mlp(activated, totals, resp_gain, resp_bias, reduce_w, reduce_b, residual):
    norms = jnp.sqrt(totals + EPSILON)
    scaled = norms / (jnp.mean(norms, axis=-1, keepdims=True) + EPSILON)
    response = resp_gain * (activated * scaled[:, None, :]) + resp_bias + activated
    return residual + matmul(response, reduce_w) + reduce_b


def modulate(hidden_one, ratio_w, ratio_b, embed):
    modulation = jnp.dot(embed, ratio_w, precision=HIGHEST_ACCURACY) + ratio_b
    chan_count = hidden_one.shape[-1]
    return hidden_one * (1.0 + modulation[:, None, :chan_count]) + modulation[:, None, chan_count:]


def project(hidden_two, tokens, map_w, map_b, attend_w, query_b, value_b):
    chan_count = hidden_two.shape[-1]
    normed = layer_norm(hidden_two)
    mapped = matmul(jax.nn.silu(tokens), map_w) + map_b
    source = jnp.concatenate([normed, mapped], axis=1)
    query_matrix = matmul(normed, attend_w[:, :chan_count]) + query_b
    key_value = matmul(source, attend_w[:, chan_count:])
    return (query_matrix, key_value[..., :chan_count], key_value[..., chan_count:] + value_b)


def divide_into_heads(values):
    return values.reshape(values.shape[:-1] + (HEADS, HEAD_CHANNELS))


def attend_single(triple):
    query_matrix, key_matrix, value_matrix = triple
    attention_scores = jnp.einsum(
        "iuy,ouy->uio",
        divide_into_heads(query_matrix),
        divide_into_heads(key_matrix),
        precision=HIGHEST_ACCURACY,
    ) * HEAD_CHANNELS ** (-0.5)
    top_score = jnp.max(attention_scores, axis=-1, keepdims=True)
    expo_terms = jnp.exp(attention_scores - top_score)
    expo_total = jnp.sum(expo_terms, axis=-1, keepdims=True)
    attention_probabilities = expo_terms / expo_total
    attended_output = jnp.einsum(
        "fvb,bfq->vfq",
        attention_probabilities,
        divide_into_heads(value_matrix),
        precision=HIGHEST_ACCURACY,
    )
    log_total = top_score + jnp.log(expo_total)
    return (attended_output.reshape(query_matrix.shape), log_total)


def attend_back_single(items):
    query_matrix, key_matrix, value_matrix, attended_output, log_total, grad_mix = items
    query_per_head = divide_into_heads(query_matrix)
    key_per_head = divide_into_heads(key_matrix)
    value_per_head = divide_into_heads(value_matrix)
    gradient_per_head = divide_into_heads(grad_mix)
    attention_scores = jnp.einsum(
        "iuy,ouy->uio", query_per_head, key_per_head, precision=HIGHEST_ACCURACY
    ) * HEAD_CHANNELS ** (-0.5)
    attention_probabilities = jnp.exp(attention_scores - log_total)
    probability_gradient = jnp.einsum(
        "iuy,ouy->uio", gradient_per_head, value_per_head, precision=HIGHEST_ACCURACY
    )
    delta_rows = jnp.einsum(
        "phd,phd->hp",
        gradient_per_head,
        divide_into_heads(attended_output),
        precision=HIGHEST_ACCURACY,
    )
    score_gradient = (
        attention_probabilities
        * (probability_gradient - delta_rows[..., None])
        * HEAD_CHANNELS ** (-0.5)
    )
    query_gradient = jnp.einsum(
        "fvb,bfq->vfq", score_gradient, key_per_head, precision=HIGHEST_ACCURACY
    )
    key_gradient = jnp.einsum(
        "gyu,ygx->ugx", score_gradient, query_per_head, precision=HIGHEST_ACCURACY
    )
    value_gradient = jnp.einsum(
        "gyu,ygx->ugx", attention_probabilities, gradient_per_head, precision=HIGHEST_ACCURACY
    )
    return (
        query_gradient.reshape(query_matrix.shape),
        key_gradient.reshape(key_matrix.shape),
        value_gradient.reshape(value_matrix.shape),
    )


def body(
    latents,
    ratio_embed,
    clip_tokens,
    cotangent,
    conv_kernel,
    conv_bias,
    expand_weight,
    expand_bias,
    response_gain,
    response_bias,
    reduce_weight,
    reduce_bias,
    ratio_weight,
    ratio_bias,
    text_weight,
    text_bias,
    attend_weight,
    query_bias,
    value_bias,
    output_weight,
    output_bias,
):
    gathered = (
        lax.all_gather(conv_kernel, "dp", axis=2, tiled=True),
        lax.all_gather(conv_bias, "dp", axis=0, tiled=True),
        lax.all_gather(expand_weight, "dp", axis=0, tiled=True),
        lax.all_gather(expand_bias, "dp", axis=0, tiled=True),
        lax.all_gather(response_gain, "dp", axis=0, tiled=True),
        lax.all_gather(response_bias, "dp", axis=0, tiled=True),
        lax.all_gather(reduce_weight, "dp", axis=0, tiled=True),
        lax.all_gather(reduce_bias, "dp", axis=0, tiled=True),
        lax.all_gather(ratio_weight, "dp", axis=0, tiled=True),
        lax.all_gather(ratio_bias, "dp", axis=0, tiled=True),
        lax.all_gather(text_weight, "dp", axis=0, tiled=True),
        lax.all_gather(text_bias, "dp", axis=0, tiled=True),
        lax.all_gather(attend_weight, "dp", axis=0, tiled=True),
        lax.all_gather(query_bias, "dp", axis=0, tiled=True),
        lax.all_gather(value_bias, "dp", axis=0, tiled=True),
        lax.all_gather(output_weight, "dp", axis=0, tiled=True),
        lax.all_gather(output_bias, "dp", axis=0, tiled=True),
    )
    (
        kernel,
        conv_shift,
        expand_w,
        expand_b,
        resp_gain,
        resp_bias,
        reduce_w,
        reduce_b,
        ratio_w,
        ratio_b,
        map_w,
        map_b,
        attend_w,
        query_b,
        value_b,
        out_w,
        out_b,
    ) = gathered
    lat_count, row_count, col_count, chan_count = latents.shape
    pixel_count = row_count * col_count
    row_padded = extended(latents, (("pair", 1),), 1)
    activated, front_pull = jax.vjp(front, row_padded, kernel, conv_shift, expand_w, expand_b)
    totals = lax.psum(jnp.sum(activated * activated, axis=1), "pair")
    residual = latents.reshape(lat_count, pixel_count, chan_count)
    hidden_one, mlp_pull = jax.vjp(
        response_mlp, activated, totals, resp_gain, resp_bias, reduce_w, reduce_b, residual
    )
    hidden_two, mod_pull = jax.vjp(
        functools.partial(modulate, embed=ratio_embed), hidden_one, ratio_w, ratio_b
    )
    (query_matrix, key_local, value_local), proj_pull = jax.vjp(
        project, hidden_two, clip_tokens, map_w, map_b, attend_w, query_b, value_b
    )
    key_matrix, value_matrix = (
        lax.all_gather(key_local, "pair", axis=1, tiled=True),
        lax.all_gather(value_local, "pair", axis=1, tiled=True),
    )
    attended_output, log_total = lax.map(attend_single, (query_matrix, key_matrix, value_matrix))
    result = hidden_two + matmul(attended_output, out_w) + out_b
    layer_output = result.reshape(latents.shape)
    grad_out = cotangent.reshape(lat_count, pixel_count, chan_count)
    out_w_grad = jnp.einsum("lpc,lpn->cn", attended_output, grad_out, precision=HIGHEST_ACCURACY)
    out_b_grad = jnp.sum(grad_out, axis=(0, 1))
    grad_mix = jnp.einsum("lpn,cn->lpc", grad_out, out_w, precision=HIGHEST_ACCURACY)
    query_gradient, key_gradient, value_gradient = lax.map(
        attend_back_single,
        (query_matrix, key_matrix, value_matrix, attended_output, log_total, grad_mix),
    )
    key_share, value_share = (
        lax.psum_scatter(key_gradient, "pair", scatter_dimension=1, tiled=True),
        lax.psum_scatter(value_gradient, "pair", scatter_dimension=1, tiled=True),
    )
    grad_two, tokens_grad, map_w_grad, map_b_grad, attend_w_grad, query_b_grad, value_b_grad = (
        proj_pull((query_gradient, key_share, value_share))
    )
    grad_two = grad_two + grad_out
    attend_shards = (
        lax.psum_scatter(map_w_grad, "dp", scatter_dimension=0, tiled=True),
        lax.psum_scatter(map_b_grad, "dp", scatter_dimension=0, tiled=True),
        lax.psum_scatter(attend_w_grad, "dp", scatter_dimension=0, tiled=True),
        lax.psum_scatter(query_b_grad, "dp", scatter_dimension=0, tiled=True),
        lax.psum_scatter(value_b_grad, "dp", scatter_dimension=0, tiled=True),
        lax.psum_scatter(out_w_grad, "dp", scatter_dimension=0, tiled=True),
        lax.psum_scatter(out_b_grad, "dp", scatter_dimension=0, tiled=True),
    )
    grad_one, ratio_w_grad, ratio_b_grad = mod_pull(grad_two)
    grad_act, grad_totals, gain_grad, respb_grad, reduce_w_grad, reduce_b_grad, grad_res = mlp_pull(
        grad_one
    )
    grad_totals = lax.psum(grad_totals, "pair")
    grad_act = grad_act + 2.0 * activated * grad_totals[:, None, :]
    grad_padded, kernel_grad, shift_grad, expand_w_grad, expand_b_grad = front_pull(grad_act)
    rim_rows = jnp.concatenate([grad_padded[:, :1], grad_padded[:, -1:]], axis=1)
    arrived = extended(rim_rows, (("pair", 1),), 1)
    inner_rows = grad_padded[:, 1:-1]
    inner_rows = inner_rows.at[:, 0].add(arrived[:, 0]).at[:, -1].add(arrived[:, 3])
    latent_grad = inner_rows + grad_res.reshape(latents.shape)
    block_shards = (
        lax.psum_scatter(kernel_grad, "dp", scatter_dimension=2, tiled=True),
        lax.psum_scatter(shift_grad, "dp", scatter_dimension=0, tiled=True),
        lax.psum_scatter(expand_w_grad, "dp", scatter_dimension=0, tiled=True),
        lax.psum_scatter(expand_b_grad, "dp", scatter_dimension=0, tiled=True),
        lax.psum_scatter(gain_grad, "dp", scatter_dimension=0, tiled=True),
        lax.psum_scatter(respb_grad, "dp", scatter_dimension=0, tiled=True),
        lax.psum_scatter(reduce_w_grad, "dp", scatter_dimension=0, tiled=True),
        lax.psum_scatter(reduce_b_grad, "dp", scatter_dimension=0, tiled=True),
        lax.psum_scatter(ratio_w_grad, "dp", scatter_dimension=0, tiled=True),
        lax.psum_scatter(ratio_b_grad, "dp", scatter_dimension=0, tiled=True),
    )
    shards = tuple(block_shards) + tuple(attend_shards)
    summed = lax.psum(shards, ("cond", "pair"))
    return (layer_output, latent_grad, tokens_grad) + tuple(summed)

FAST = lax.Precision.HIGH


def dot(left, right):
    return jnp.dot(left, right, precision=FAST)


def dot_t(left, right):
    return lax.dot_general(left, right, (((1,), (1,)), ((), ())), precision=FAST)


def t_dot(left, right):
    return lax.dot_general(left, right, (((0,), (0,)), ((), ())), precision=FAST)


def norm_stats(values):
    centered = values - jnp.mean(values, axis=-1, keepdims=True)
    variance = jnp.mean(centered * centered, axis=-1, keepdims=True)
    inverse = lax.rsqrt(variance + EPSILON)
    return centered * inverse, inverse


def norm_back(grad, normed, inverse):
    return inverse * (
        grad
        - jnp.mean(grad, axis=-1, keepdims=True)
        - normed * jnp.mean(grad * normed, axis=-1, keepdims=True)
    )


def heads_of(values):
    return values.reshape(values.shape[0], -1, HEAD_CHANNELS)


CHUNK = 32
MESH = pl.DeviceIdType.MESH
DMA = pltpu.SemaphoreType.DMA
ANY = pl.BlockSpec(memory_space=pl.ANY)


def near_of(me, step):
    across = lax.rem(lax.rem(me, 2) + lax.rem(step, 2), 2)
    along = lax.rem(lax.div(me, 2) + lax.div(step, 2), 2)
    return along * 2 + across


def remote(src, dst, send, recv, device):
    return pltpu.make_async_remote_copy(
        src_ref=src, dst_ref=dst, send_sem=send, recv_sem=recv, device_id=device,
        device_id_type=MESH,
    )


def greet(device):
    barrier = pltpu.get_barrier_semaphore()
    pl.semaphore_signal(barrier, inc=1, device_id=device, device_id_type=MESH)


def relay_begin(full, sems):
    cross_out, cross_in, mate_out, mate_in = sems
    core = lax.axis_index("cond")
    level = lax.axis_index("pair")
    me = lax.axis_index("dp")
    unit = full.shape[1] // 4
    side = lax.rem(level, 2)
    across = (core, level + 1 - 2 * side, me)
    mate = (1 - core, level, me)

    def spot(u, step):
        rows = pl.ds(pl.multiple_of((core * 2 + u) * unit, 8), unit)
        return full.at[near_of(me, step), rows]

    steps = (1, 2, 3)
    crosses = [
        remote(
            spot(side, step), spot(side, step), cross_out.at[step - 1], cross_in.at[step - 1], across
        )
        for step in steps
    ]
    mates = [
        [
            remote(
                spot(u, step), spot(u, step), mate_out.at[i, step - 1], mate_in.at[i, step - 1], mate
            )
            for step in steps
        ]
        for i, u in enumerate((side, 1 - side))
    ]

    def begin():
        for copy in crosses + mates[0]:
            copy.start()

    def end():
        for cross, far in zip(crosses, mates[1]):
            cross.wait_recv()
            far.start()
        for copy in crosses:
            copy.wait_send()
        for copy in mates[0] + mates[1]:
            copy.wait()

    return begin, end


def exchange_body(gather_count, scatter_count, swap_count, relays, *refs):
    near_count = gather_count + scatter_count
    count = near_count + swap_count
    ins = refs[:count]
    refs = refs[count + relays :]
    outs = refs[:count]
    full = refs[count] if relays else None
    refs = refs[count + relays :]
    passing, refs = refs[:swap_count], refs[swap_count:]
    holds = refs[: gather_count + swap_count]
    send, recv, keep, diag_out, diag_in = refs[gather_count + swap_count :][:5]
    sems = refs[gather_count + swap_count + 5 :]
    core = lax.axis_index("cond")
    level = lax.axis_index("pair")
    me = lax.axis_index("dp")
    goal = near_of(me, rev(level))
    quarter = rev(near_of(level, me))
    shifts = level != 0
    rises = goal != level
    final = me == level
    expected = 3
    for step in (1, 2, 3):
        greet((core, level, near_of(me, step)))
    if relays:
        greet((1 - core, level, me))
        greet((core, level + 1 - 2 * lax.rem(level, 2), me))
        expected = expected + 2
    if swap_count:
        pl.when(rises)(lambda: greet((core, quarter, me)))
        expected = expected + jnp.where(rises, 1, 0)
    pl.semaphore_wait(pltpu.get_barrier_semaphore(), expected)

    def shift(i, goals):
        return remote(
            ins[near_count + i], goals[i], send.at[near_count + i, 0], recv.at[near_count + i, 0],
            (core, level, goal),
        )

    def rise(i, sources):
        return remote(
            sources[i], outs[near_count + i], send.at[near_count + i, 1],
            recv.at[near_count + i, 1], (core, goal, me),
        )

    swap_ins = ins[near_count:]
    swap_outs = outs[near_count:]
    near_copies = []
    if relays:
        relay_start, relay_end = relay_begin(full, sems)
        relay_start()
    for i in range(swap_count):
        pl.when(jnp.logical_and(shifts, final))(shift(i, swap_outs).start)
        pl.when(jnp.logical_and(shifts, jnp.logical_not(final)))(shift(i, passing).start)
        pl.when(jnp.logical_and(jnp.logical_not(shifts), rises))(rise(i, swap_ins).start)
    tall = [i for i in range(gather_count) if ins[i].shape[0] % 16 == 0]
    for step in (3, 1, 2):
        for i in range(near_count):
            if step == 3 and i in tall:
                continue
            if i < gather_count:
                src, dst = ins[i], outs[i].at[step]
            else:
                src, dst = ins[i].at[step], outs[i].at[step - 1]
            copy = remote(
                src, dst, send.at[i, step - 1], recv.at[i, step - 1],
                (core, level, near_of(me, step)),
            )
            copy.start()
            if i not in tall:
                near_copies.append(copy)

    def direct(i, step):
        return remote(
            ins[i], outs[i].at[step], send.at[i, step - 1], recv.at[i, step - 1],
            (core, level, near_of(me, step)),
        )

    def onward(i, step):
        half = ins[i].shape[0] // 2
        rows = pl.ds(half * (step - 1), half)
        return remote(
            outs[i].at[step, rows], outs[i].at[3, rows], diag_out.at[i, step - 1],
            diag_in.at[i, step - 1], (core, level, near_of(me, 3 - step)),
        )

    def through(src, hold, dst, sem):
        load = pltpu.make_async_copy(src, hold, sem)
        load.start()
        load.wait()
        store = pltpu.make_async_copy(hold, dst, sem)
        store.start()
        store.wait()

    for i in range(gather_count):
        through(ins[i], holds[i], outs[i].at[0], keep.at[i])
    for i in range(swap_count):
        pl.when(jnp.logical_and(jnp.logical_not(shifts), jnp.logical_not(rises)))(
            lambda i=i: through(
                swap_ins[i], holds[gather_count + i], swap_outs[i], keep.at[gather_count + i]
            )
        )
        pl.when(shifts)(shift(i, passing).wait_recv)
        pl.when(jnp.logical_and(shifts, rises))(rise(i, passing).start)
    for i in tall:
        for step in (1, 2):
            direct(i, step).wait_recv()
            onward(i, step).start()
    if relays:
        relay_end()
    for i in tall:
        for step in (1, 2):
            direct(i, step).wait_send()
            onward(i, step).wait()
    for copy in near_copies:
        copy.wait()
    for i in range(swap_count):
        pl.when(shifts)(shift(i, passing).wait_send)
        pl.when(rises)(rise(i, swap_ins).wait_send)
        pl.when(quarter != level)(rise(i, swap_ins).wait_recv)


def exchange(collective, gathers=(), scatters=(), swaps=(), relay=()):
    f32 = jnp.float32
    shapes = [(4,) + item.shape for item in gathers]
    shapes += [(3,) + item.shape[1:] for item in scatters]
    shapes += [item.shape for item in swaps]
    count = len(shapes)
    shapes += [item.shape for item in relay]
    shapes += [item.shape for item in swaps]
    staged = len(gathers) + len(swaps)
    scratch = [pltpu.VMEM(item.shape, f32) for item in tuple(gathers) + tuple(swaps)]
    scratch += [DMA((count, 3)), DMA((count, 3)), DMA((max(staged, 1),))]
    scratch += [DMA((count, 2)), DMA((count, 2))]
    if relay:
        scratch += [DMA((3,)), DMA((3,)), DMA((2, 3)), DMA((2, 3))]
    outs = pl.pallas_call(
        functools.partial(exchange_body, len(gathers), len(scatters), len(swaps), len(relay)),
        out_shape=[jax.ShapeDtypeStruct(shape, f32) for shape in shapes],
        in_specs=[ANY] * (count + len(relay)),
        out_specs=[ANY] * len(shapes),
        scratch_shapes=scratch,
        input_output_aliases={count: count} if relay else {},
        compiler_params=pltpu.CompilerParams(
            collective_id=collective, has_side_effects=True, vmem_limit_bytes=16 * 2**20
        ),
        name="exchange",
    )(*gathers, *scatters, *swaps, *relay)
    return outs[: count + len(relay)]


PARTS = 4


def open_body(image_in, packed_in, tokens_in, embed_in, weight_in, attend_in, *refs):
    image, packed, tokens, embed, weight, attend = refs[:6]
    passing = refs[6:9]
    hold, send, recv, keep, cross_out, cross_in, pass_out, pass_in, own_out, own_in, block_out, block_in = refs[9:]
    core = lax.axis_index("cond")
    level = lax.axis_index("pair")
    me = lax.axis_index("dp")
    mate = (1 - core, level, me)
    side = lax.rem(level, 2)
    across = (core, level + 1 - 2 * side, me)
    rows = image_in.shape[0]
    wide = weight.shape[3]
    unit = weight.shape[2]
    turn = rev(level)
    goal = near_of(me, turn)
    quarter = rev(near_of(level, me))
    shifts = level != 0
    rises = goal != level
    turned = jnp.logical_and(level == 1, me == 1)
    raises = jnp.logical_and(level > 0, jnp.logical_not(turned))
    falls = level < 3
    taken = jnp.logical_and(quarter < 3, jnp.logical_not(turned))
    greet(mate)
    greet(across)
    for step in (1, 2, 3):
        greet((core, level, near_of(me, step)))
    pl.when(rises)(lambda: greet((core, quarter, me)))
    pl.when(quarter > 0)(lambda: greet((core, quarter - 1, level)))
    pl.when(taken)(lambda: greet((core, quarter + 1, level)))
    expected = (
        5 + jnp.where(rises, 1, 0) + jnp.where(raises, 1, 0) + jnp.where(falls, 1, 0)
    )
    pl.semaphore_wait(pltpu.get_barrier_semaphore(), expected)

    body = image.at[pl.ds(1, rows)]
    ins = (image_in, tokens_in, embed_in)
    ends = (body, tokens, embed)

    def shift(goals):
        return [
            remote(src, dst, send.at[i], recv.at[i], (core, level, goal))
            for i, (src, dst) in enumerate(zip(ins, goals))
        ]

    def rise(sources):
        return [
            remote(src, dst, send.at[3 + i], recv.at[3 + i], (core, goal, me))
            for i, (src, dst) in enumerate(zip(sources, ends))
        ]

    def stay():
        image_load = pltpu.make_async_copy(image_in, hold, keep.at[0])
        image_load.start()
        rest = [
            pltpu.make_async_copy(src, dst, keep.at[i])
            for i, (src, dst) in ((1, (tokens_in, tokens)), (2, (embed_in, embed)))
        ]
        run("start", *rest)
        image_load.wait()
        image_store = pltpu.make_async_copy(hold, body, keep.at[0])
        image_store.start()
        run("wait", image_store, *rest)

    lower = remote(
        image_in.at[pl.ds(rows - 1, 1)], image.at[pl.ds(0, 1)], send.at[6], recv.at[6],
        (core, me, near_of(me, rev(jnp.minimum(level + 1, 3)))),
    )
    upper = remote(
        image_in.at[pl.ds(0, 1)], image.at[pl.ds(rows + 1, 1)], send.at[7], recv.at[7],
        (core, me, near_of(me, rev(jnp.maximum(level - 1, 0)))),
    )
    around = pltpu.make_async_copy(
        image_in.at[pl.ds(0, 1)], image.at[pl.ds(rows + 1, 1)], keep.at[4]
    )

    def vectors(step):
        return remote(
            packed_in, packed.at[me], send.at[7 + step], recv.at[7 + step],
            (core, level, near_of(me, step)),
        )

    mine = core * 2 + side
    other = core * 2 + 1 - side

    size = unit // PARTS

    def block(step, h):
        to = near_of(me, step)
        src = weight_in.at[
            pl.ds(pl.multiple_of(mine * unit + h * size, 8), size),
            pl.ds(pl.multiple_of(to * wide, wide), wide),
        ]
        dst = weight.at[me, mine, pl.ds(h * size, size)]
        return remote(
            src, dst, block_out.at[h, step - 1], block_in.at[h, step - 1], (core, level, to)
        )

    piece = attend.shape[2] // 3

    def thirds(step):
        to = near_of(me, step)
        found = []
        for p in range(3):
            src = attend_in.at[
                pl.ds(pl.multiple_of(mine * unit, 8), unit),
                pl.ds(pl.multiple_of((p * 4 + to) * piece, piece), piece),
            ]
            dst = attend.at[
                me, pl.ds(pl.multiple_of(mine * unit, 8), unit), pl.ds(p * piece, piece)
            ]
            spot = 11 + step * 3 + p
            found.append(remote(src, dst, send.at[spot], recv.at[spot], (core, level, to)))
        return found

    def crossed(step, u, h):
        spot = weight.at[near_of(me, step), u, pl.ds(h * size, size)]
        return remote(spot, spot, cross_out.at[h, step - 1], cross_in.at[h, step - 1], across)

    def passed(step, u, turn, h):
        spot = weight.at[near_of(me, step), u, pl.ds(h * size, size)]
        k = turn * PARTS + h
        return remote(spot, spot, pass_out.at[k, step - 1], pass_in.at[k, step - 1], mate)

    def run(method, *copies):
        for copy in copies:
            getattr(copy, method)()

    final = me == level
    pl.when(jnp.logical_and(shifts, final))(lambda: run("start", *shift(ends)))
    pl.when(jnp.logical_and(shifts, jnp.logical_not(final)))(lambda: run("start", *shift(passing)))
    pl.when(jnp.logical_and(jnp.logical_not(shifts), rises))(lambda: run("start", *rise(ins)))
    pl.when(falls)(lower.start)
    pl.when(raises)(upper.start)
    pl.when(turned)(around.start)
    own = [pltpu.make_async_copy(packed_in, packed.at[me], keep.at[3])]
    own_blocks = [
        remote(
            weight_in.at[pl.ds(u * unit, unit), pl.ds(pl.multiple_of(me * wide, wide), wide)],
            weight.at[me, u],
            own_out.at[u],
            own_in.at[u],
            mate,
        )
        for u in range(4)
    ] + [
        remote(
            attend_in.at[:, pl.ds(pl.multiple_of((p * 4 + me) * piece, piece), piece)],
            attend.at[me, :, pl.ds(p * piece, piece)],
            own_out.at[4 + p],
            own_in.at[4 + p],
            mate,
        )
        for p in range(3)
    ]
    for step in (3, 1, 2):
        vectors(step).start()
    for h in range(2):
        for step in (3, 1, 2):
            block(step, h).start()
    run("start", *own, *own_blocks)
    pl.when(jnp.logical_and(jnp.logical_not(shifts), jnp.logical_not(rises)))(stay)

    @pl.when(shifts)
    def _():
        run("wait_recv", *shift(passing))
        pl.when(rises)(lambda: run("start", *rise(passing)))

    for h in range(PARTS):
        for step in (2, 1, 3):
            block(step, h).wait_recv()
            if h + 2 < PARTS:
                block(step, h + 2).start()
            crossed(step, mine, h).start()
            passed(step, mine, 0, h).start()
    for step in (3, 1, 2):
        run("start", *thirds(step))
    for h in range(PARTS):
        for step in (2, 1, 3):
            crossed(step, other, h).wait_recv()
            passed(step, other, 1, h).start()
    pl.when(shifts)(lambda: run("wait_send", *shift(passing)))
    pl.when(rises)(lambda: run("wait_send", *rise(ins)))
    pl.when(quarter != level)(lambda: run("wait_recv", *rise(ins)))
    pl.when(falls)(lower.wait_send)
    pl.when(raises)(upper.wait_send)
    pl.when(quarter > 0)(lower.wait_recv)
    pl.when(taken)(upper.wait_recv)
    pl.when(turned)(around.wait)
    for step in (1, 2, 3):
        vectors(step).wait()
        run("wait", *thirds(step))
        for h in range(PARTS):
            block(step, h).wait_send()
            crossed(step, mine, h).wait_send()
            for u, turn_of in ((mine, 0), (other, 1)):
                passed(step, u, turn_of, h).wait()
    run("wait", *own, *own_blocks)


def open_exchange(collective, image, packed, tokens, embed, weight, attend):
    rows, cols, chan = image.shape
    unit = weight.shape[0] // 4
    shapes = [
        (rows + 2, cols, chan),
        (4,) + packed.shape,
        tokens.shape,
        embed.shape,
        (4, 4, unit, weight.shape[1] // 4),
        (4, attend.shape[0], attend.shape[1] // 4),
        image.shape,
        tokens.shape,
        embed.shape,
    ]
    return pl.pallas_call(
        open_body,
        out_shape=[jax.ShapeDtypeStruct(shape, jnp.float32) for shape in shapes],
        in_specs=[ANY] * 6,
        out_specs=[ANY] * 9,
        scratch_shapes=[
            pltpu.VMEM(image.shape, jnp.float32),
            DMA((23,)),
            DMA((23,)),
            DMA((5,)),
            DMA((PARTS, 3)),
            DMA((PARTS, 3)),
            DMA((2 * PARTS, 3)),
            DMA((2 * PARTS, 3)),
            DMA((7,)),
            DMA((7,)),
            DMA((PARTS, 3)),
            DMA((PARTS, 3)),
        ],
        compiler_params=pltpu.CompilerParams(collective_id=collective, has_side_effects=True),
        name="open_exchange",
    )(image, packed, tokens, embed, weight, attend)


def rev(z):
    return 2 * lax.rem(z, 2) + lax.div(z, 2)


def plane_spot(level, me):
    return me, near_of(me, rev(level))


def home_spot(level, me):
    return rev(near_of(level, me)), level


def stream_setup(homeward=False):
    core = lax.axis_index("cond")
    level = lax.axis_index("pair")
    me = lax.axis_index("dp")
    greet((1 - core, level, me))
    for step in (1, 2, 3):
        greet((core, level, near_of(me, step)))
    pl.when(level > 0)(lambda: greet((core, level - 1, me)))
    pl.when(level < 3)(lambda: greet((core, level + 1, me)))
    ends = jnp.where(level == 0, 1, 0) + jnp.where(level == 3, 1, 0)
    expected = 6 - ends
    if homeward:
        moves = jnp.logical_or(level != 0, me != 0)
        back_up, back_over = plane_spot(level, me)
        pl.when(moves)(lambda: greet((core, back_up, back_over)))
        expected = expected + jnp.where(moves, 1, 0)
    pl.semaphore_wait(pltpu.get_barrier_semaphore(), expected)


def sum_stream(sections, scratch, hooks):
    (
        data,
        stage,
        first,
        second,
        own,
        load_sem,
        core_out,
        core_in,
        plane_out,
        plane_in,
        first_in,
        second_in,
        hop_out,
        cast_out,
        cast_low,
        final_in,
        keep_sem,
        pair_out,
        pair_in,
    ) = scratch
    ranges = []
    total = 0
    for kind, src, dst in sections:
        if kind == "plain":
            count, width = src.shape[1] // CHUNK, src.shape[2]
        else:
            count, width = 4 * (src.shape[2] // CHUNK), src.shape[3]
        ranges.append((total, total + count, kind, src, dst, width))
        total += count
    core = lax.axis_index("cond")
    level = lax.axis_index("pair")
    me = lax.axis_index("dp")
    mate = (1 - core, level, me)
    ring = data.shape[0]
    full = data.shape[2]

    def rank_of(j):
        return jnp.where(lax.rem(j, 2) == 0, level, 3 - level)

    def at_rank(j, rank):
        return (core, jnp.where(lax.rem(j, 2) == 0, rank, 3 - rank), me)

    def inside(j, low, high):
        return jnp.logical_and(j >= low, j < high)

    def swap_place(j):
        inner = False
        k = 0
        for low, high, kind, src, dst, width in ranges:
            if kind == "swap":
                here = inside(j, low, high)
                inner = jnp.logical_or(inner, here)
                k = jnp.where(here, j - low, k)
        return inner, k

    def moved(j):
        inner, k = swap_place(j)
        return jnp.logical_and(inner, lax.rem(k, 4) != 0)

    def kinds(j, action):
        narrow = False
        for low, high, kind, src, dst, width in ranges:
            if width != full:
                here = inside(j, low, high)
                narrow = jnp.logical_or(narrow, here)
                pl.when(here)(lambda width=width: action(width))
        pl.when(jnp.logical_not(narrow))(lambda: action(full))

    def cut(ref, width):
        return ref if ref.shape[-1] == width else ref.at[:, pl.ds(0, width)]

    def each_source(j, action):
        target = data.at[lax.rem(j, ring)]
        mine = own.at[lax.rem(j, 4)]
        for low, high, kind, src, dst, width in ranges:

            @pl.when(inside(j, low, high))
            def _(low=low, kind=kind, src=src, width=width):
                k = j - low
                if kind == "plain":
                    rows = pl.ds(pl.multiple_of(k * CHUNK, CHUNK), CHUNK)
                    action(lambda half: src.at[half, rows], target, mine)
                else:
                    rows = pl.ds(pl.multiple_of(lax.div(k, 4) * CHUNK, CHUNK), CHUNK)
                    spot = near_of(me, lax.rem(k, 4))
                    action(
                        lambda half: src.at[spot, half, rows], cut(target, width), cut(mine, width)
                    )

    def each_final(j, action):
        for low, high, kind, src, dst, width in ranges:

            @pl.when(inside(j, low, high))
            def _(low=low, kind=kind, dst=dst, width=width):
                k = j - low
                if kind == "plain":
                    rows = pl.ds(pl.multiple_of(k * CHUNK, CHUNK), CHUNK)
                    action(
                        lambda half: [(dst.at[half, rows], lambda x: x, 0)],
                        first.at[lax.rem(j, ring)],
                    )
                else:
                    rows = pl.ds(pl.multiple_of(lax.div(k, 4) * CHUNK, CHUNK), CHUNK)
                    spot = near_of(me, lax.rem(k, 4))
                    pieces = 1 if width == full else 3
                    piece = width // pieces

                    def targets(half):
                        found = []
                        for p in range(pieces):
                            columns = pl.ds(
                                pl.multiple_of(p * 4 * piece + spot * piece, piece), piece
                            )
                            found.append(
                                (
                                    dst.at[half, rows, columns],
                                    lambda x, p=p: x
                                    if x.shape[-1] == piece
                                    else x.at[:, pl.ds(p * piece, piece)],
                                    p,
                                )
                            )
                        return found

                    action(targets, stage.at[k])

    def core_copy(j, src, dst):
        return remote(src, dst, core_out.at[j], core_in.at[j], mate)

    def plane_copy(j, width):
        inner, k = swap_place(j)
        return remote(
            cut(first.at[lax.rem(j, ring)], width),
            cut(stage.at[k], width),
            plane_out.at[j],
            plane_in.at[j],
            (core, level, near_of(me, lax.rem(k, 4))),
        )

    def hop_first(j, src, rank, width):
        return remote(
            cut(src, width), cut(first.at[lax.rem(j, ring)], width), hop_out.at[j], first_in.at[j], at_rank(j, rank)
        )

    def hop_second(j, width):
        k = lax.div(j, 2)
        return remote(
            cut(data.at[lax.rem(j, ring)], width), cut(second.at[lax.rem(k, ring // 2)], width), hop_out.at[j], second_in.at[k],
            at_rank(j, 2),
        )

    def start(j):
        def go(source, target, mine):
            core_copy(j, source(1 - core), target).start()
            pltpu.make_async_copy(source(core), mine, load_sem.at[lax.rem(j, 4)]).start()

        each_source(j, go)

    def combine(j):
        def go(source, target, mine):
            pltpu.make_async_copy(source(core), mine, load_sem.at[lax.rem(j, 4)]).wait()
            core_copy(j, source(1 - core), target).wait_recv()
            target[...] += mine[...]

        each_source(j, go)

    def depart(j):
        rank = rank_of(j)

        def go(width):
            pl.when(rank == 0)(lambda: hop_first(j, data.at[lax.rem(j, ring)], 1, width).start())
            pl.when(rank == 3)(lambda: hop_second(j, width).start())

        kinds(j, go)

    def relay(j):
        def go(width):
            hop_first(j, data.at[lax.rem(j, ring)], 1, width).wait_recv()
            spot = lax.rem(j, ring)
            first[spot, :, :width] += data[spot, :, :width]
            hop_first(j, first.at[lax.rem(j, ring)], 2, width).start()

        pl.when(rank_of(j) == 1)(lambda: kinds(j, go))

    def casts(j, rank, half_targets, source, sems):
        return [
            remote(
                cut_of(source) if source is not None else ref, ref, sems.at[j, p], final_in.at[j, p],
                at_rank(j, rank),
            )
            for ref, cut_of, p in half_targets
        ]

    def pairs(j, half_targets, source):
        return [
            remote(
                cut_of(source) if source is not None else ref, ref, pair_out.at[j, p],
                pair_in.at[j, p], mate,
            )
            for ref, cut_of, p in half_targets
        ]

    def keeps(j, half_targets, source):
        return [
            pltpu.make_async_copy(cut_of(source), ref, keep_sem.at[j, p])
            for ref, cut_of, p in half_targets
        ]

    def root(j):
        def add(width):
            hop_first(j, first.at[lax.rem(j, ring)], 2, width).wait_recv()
            hop_second(j, width).wait_recv()
            spot = lax.rem(j, ring)
            first[spot, :, :width] += (
                data[spot, :, :width] + second[lax.rem(lax.div(j, 2), ring // 2), :, :width]
            )

        @pl.when(rank_of(j) == 2)
        def _():
            kinds(j, add)

            @pl.when(moved(j))
            def _():
                kinds(j, lambda width: plane_copy(j, width).start())

            inner, k = swap_place(j)

            @pl.when(jnp.logical_and(inner, jnp.logical_not(moved(j))))
            def _():
                stage[k] = first[lax.rem(j, ring)]

    def spread(j):
        def send(targets, source):
            goals = targets(core)
            for copy in (
                casts(j, 1, goals, source, cast_out)
                + casts(j, 3, goals, source, cast_low)
                + keeps(j, goals, source)
                + pairs(j, goals, source)
            ):
                copy.start()

        @pl.when(rank_of(j) == 2)
        def _():
            @pl.when(moved(j))
            def _():
                kinds(j, lambda width: plane_copy(j, width).wait_recv())

            each_final(j, send)

    def landed(j):
        rank = rank_of(j)

        def go(targets, source):
            goals = targets(core)
            for copy in casts(j, 1, goals, None, cast_out):
                copy.wait_recv()
            pl.when(rank == 1)(
                lambda: [copy.start() for copy in casts(j, 0, goals, None, cast_out)] and None
            )
            for copy in pairs(j, goals, None):
                copy.start()

        @pl.when(jnp.logical_or(rank == 1, rank == 3))
        def _():
            each_final(j, go)

    def arrived(j):
        def go(targets, source):
            goals = targets(core)
            for copy in casts(j, 0, goals, None, cast_out):
                copy.wait_recv()
            for copy in pairs(j, goals, None):
                copy.start()

        @pl.when(rank_of(j) == 0)
        def _():
            each_final(j, go)

    def finish(j):
        rank = rank_of(j)

        def sent(source, target, mine):
            core_copy(j, source(1 - core), target).wait_send()

        each_source(j, sent)

        @pl.when(jnp.logical_and(moved(j), rank == 2))
        def _():
            kinds(j, lambda width: plane_copy(j, width).wait_send())

        @pl.when(rank != 2)
        def _():
            kinds(j, lambda width: hop_first(j, data.at[lax.rem(j, ring)], 1, width).wait_send())

        def go(targets, source):
            goals = targets(core)

            @pl.when(jnp.logical_or(rank == 1, rank == 2))
            def _():
                for copy in casts(j, 1, goals, None, cast_out):
                    copy.wait_send()

            @pl.when(rank == 2)
            def _():
                for copy in casts(j, 3, goals, None, cast_low):
                    copy.wait_send()
                for copy in keeps(j, goals, source):
                    copy.wait()

            for copy in pairs(j, goals, None):
                copy.wait()

        each_final(j, go)

    stages = (
        (0, start),
        (3, combine),
        (5, depart),
        (8, relay),
        (11, root),
        (14, spread),
        (17, landed),
        (20, arrived),
        (23, finish),
    )

    def step(t, carry):
        for lag, stage_of in stages:
            j = t - lag

            @pl.when(jnp.logical_and(j >= 0, j < total))
            def _(j=j, stage_of=stage_of):
                stage_of(j)

        for low, high, hook in hooks:
            pl.when(jnp.logical_and(t >= low, t < high))(lambda hook=hook, low=low: hook(t - low))
        return carry

    lax.fori_loop(0, total + 23, step, 0)


def stream_scratch(total, most, width):
    ring = 32
    return [
        pltpu.VMEM((ring, CHUNK, width), jnp.float32),
        pltpu.VMEM((most, CHUNK, width), jnp.float32),
        pltpu.VMEM((ring, CHUNK, width), jnp.float32),
        pltpu.VMEM((ring // 2, CHUNK, width), jnp.float32),
        pltpu.VMEM((4, CHUNK, width), jnp.float32),
        DMA((4,)),
        DMA((total,)),
        DMA((total,)),
        DMA((total,)),
        DMA((total,)),
        DMA((total,)),
        DMA(((total + 1) // 2,)),
        DMA((total,)),
        DMA((total, 3)),
        DMA((total, 3)),
        DMA((total, 3)),
        DMA((total, 3)),
        DMA((total, 3)),
        DMA((total, 3)),
    ]


SCRATCH = 19


def near_slots(shares, arrived, send, recv, base):
    core = lax.axis_index("cond")
    level = lax.axis_index("pair")
    me = lax.axis_index("dp")
    return [
        remote(
            shares.at[step], arrived.at[step - 1], send.at[base + step - 1],
            recv.at[base + step - 1], (core, level, near_of(me, step)),
        )
        for step in (3, 1, 2)
    ]


def near_blocks(block, everyone, send, recv, base):
    core = lax.axis_index("cond")
    level = lax.axis_index("pair")
    me = lax.axis_index("dp")
    return [
        remote(
            block, everyone.at[step], send.at[base + step - 1], recv.at[base + step - 1],
            (core, level, near_of(me, step)),
        )
        for step in (3, 1, 2)
    ]


def row_stats(rows):
    centered = rows - jnp.mean(rows, axis=-1, keepdims=True)
    inverse = lax.rsqrt(jnp.mean(centered * centered, axis=-1, keepdims=True) + EPSILON)
    return centered * inverse, inverse


def halves(value):
    high = value.astype(jnp.bfloat16)
    return high, (value - high.astype(jnp.float32)).astype(jnp.bfloat16)


def three_pass(left, right, dims):
    def one(x, y):
        return lax.dot_general(x, y, (dims, ((), ())), preferred_element_type=jnp.float32)

    return one(left[0], right[1]) + one(left[1], right[0]) + one(left[0], right[0])


TILE = 256


def backward_body(
    output_ref, qkv_ref, two_ref, text_ref, cot_ref, one_ref, response_ref, reduce_w_ref,
    act_ref, slope_ref, normed_ref, expand_w_ref, conv_ref, mixture_ref, out_w_ref, base_ref,
    small_ref,
    normed_two_ref, rows_ref, embed_ref, silu_ref, mapped_ref, text_kv_ref,
    output_out, attend_out, mapper_out, reduce_out, small_out, expand_out,
    attend_part, mapper_part, reduce_part, expand_part, one_out, text_out, grad_out, layer_out,
    *scratch
):
    (
        front_got, front_own, conv, grad, one, out_got, out_own, base, small, wide, high, low,
        weights, acts, slopes, columns, product, front, sums, spread_own, spread_got,
        text_got, text_own, text_all, ratio, mapped,
    ) = scratch[SCRATCH : SCRATCH + 26]
    (
        send, recv, keep, tile_out, tile_in, load, front_out, front_in, spread_out, spread_in,
        piece_out, piece_in, text_out_sem, text_in_sem,
    ) = scratch[SCRATCH + 26 :]
    stream_setup(True)
    core = lax.axis_index("cond")
    level = lax.axis_index("pair")
    me = lax.axis_index("dp")
    moves = jnp.logical_or(level != 0, me != 0)
    up, over = home_spot(level, me)
    pixels, chan = conv.shape
    spots = wide.shape[0]
    texts = text_own.shape[0]
    count = chan // TILE
    scatters = near_slots(two_ref, front_got, send, recv, 0)
    scatters += near_slots(text_ref, text_got, send, recv, 6)
    start_loads = [
        pltpu.make_async_copy(src, dst, keep.at[6 + i])
        for i, (src, dst) in enumerate(
            ((two_ref.at[0], front_own), (text_ref.at[0], text_own), (cot_ref, conv), (one_ref, one))
        )
    ]

    def near_tile(i):
        rows = pl.ds(pl.multiple_of(i * 16, 16), 16)
        return [
            remote(
                grad.at[rows],
                wide.at[pl.ds(pl.multiple_of(step * pixels + i * 16, 16), 16)],
                piece_out.at[i, step - 1],
                piece_in.at[i, step - 1],
                (core, level, near_of(me, step)),
            )
            for step in (3, 1, 2)
        ]

    def late():
        found = []
        for step in (3, 1, 2):
            device = (core, level, near_of(me, step))
            found.append(
                remote(
                    text_all.at[0], text_all.at[step], text_out_sem.at[step - 1],
                    text_in_sem.at[step - 1], device,
                )
            )
            found.append(
                remote(
                    ratio.at[0], ratio.at[step], text_out_sem.at[2 + step],
                    text_in_sem.at[2 + step], device,
                )
            )
        return found

    one_kept = pltpu.make_async_copy(grad, one_out, keep.at[10])
    text_kept = pltpu.make_async_copy(text_all, text_out, keep.at[11])

    def early_loads():
        homes = [(acts, 0), (acts, 1), (slopes, 0), (slopes, 1), (front, 0)]
        found = []
        for i, (buffer, slot) in enumerate(homes):
            width = min(TILE, qkv_ref.shape[1] - i * TILE)
            dst = buffer.at[slot] if width == TILE else buffer.at[slot, :, pl.ds(0, width)]
            found.append(
                pltpu.make_async_copy(
                    qkv_ref.at[:, pl.ds(i * TILE, width)], dst, load.at[2 + i if i < 4 else 0]
                )
            )
        return found, homes

    def early_column(i):
        return pltpu.make_async_copy(
            normed_two_ref.at[:, pl.ds(pl.multiple_of(i * part, part), part)],
            columns.at[lax.rem(i, 2)],
            load.at[6 + lax.rem(i, 2)],
        )

    def attend_stores(i):
        half = part // 2
        return [
            pltpu.make_async_copy(
                product.at[pl.ds(c * half, half), pl.ds(0, 3 * part)],
                attend_part.at[i, c],
                load.at[8 + c],
            )
            for c in (0, 1)
        ]

    def prepare(t):
        copies, homes = early_loads()
        for i, (copy, (buffer, slot)) in enumerate(zip(copies, homes)):
            copy.wait()
            width = min(TILE, qkv_ref.shape[1] - i * TILE)

            def strip(k, carry, i=i, buffer=buffer, slot=slot, width=width):
                rows = pl.ds(pl.multiple_of(k * 48, 48), 48)
                cols = pl.ds(i * TILE, width)
                high[rows, cols], low[rows, cols] = halves(buffer[slot, rows, 0:width])
                return carry

            lax.fori_loop(0, spots // 48, strip, 0)

    def attend_outer(i):
        early_column(i).wait()

        @pl.when(i > 0)
        def _():
            for copy in attend_stores(jnp.maximum(i - 1, 0)):
                copy.wait()

        left = halves(columns[lax.rem(i, 2)])
        text_left = halves(mapped_ref[:, pl.ds(pl.multiple_of(i * part, part), part)])
        for k in range(3):
            cols = pl.ds(k * part, part)
            value = three_pass(left, (high[:, cols], low[:, cols]), ((0,), (0,)))
            if k > 0:
                right = halves(text_kv_ref[:, (k - 1) * part : k * part])
                value = value + three_pass(text_left, right, ((0,), (0,)))
            product[:, cols] = value
        for copy in attend_stores(i):
            copy.start()
        pl.when(i + 2 < 4)(lambda: early_column(jnp.minimum(i + 2, 3)).start())

    def settle_attend(t):
        for copy in attend_stores(3):
            copy.wait()

    def arrive(t):
        for copy in start_loads + scatters:
            copy.wait()
        ratio[0] = jnp.zeros_like(ratio[0])
        text_all[0] = jnp.zeros_like(text_all[0])
        text_all[0, 0:texts] = text_own[...] + text_got[0] + text_got[1] + text_got[2]

    def normalize(t):
        scale = rows_ref[6:7]
        shift = rows_ref[7:8]
        for half in range(2):
            rows = pl.ds(pl.multiple_of(t * 16 + half * 8, 8), 8)
            back = front_own[rows] + front_got[0, rows] + front_got[1, rows] + front_got[2, rows]
            hidden = one[rows]
            normed, inverse = row_stats(hidden * scale + shift)
            two = conv[rows] + inverse * (
                back
                - jnp.mean(back, axis=-1, keepdims=True)
                - normed * jnp.mean(back * normed, axis=-1, keepdims=True)
            )
            grad[rows] = two * scale
            ratio[0, 0:8] += two * hidden
            ratio[0, 8:16] += two
        for copy in near_tile(t):
            copy.start()

    def give_late(t):
        for copy in late():
            copy.start()
        one_kept.start()
        wide[0:pixels] = grad[...]

    def gathered(t):
        def wait(i, carry):
            for copy in near_tile(i):
                copy.wait()
            return carry

        lax.fori_loop(0, pixels // 16, wait, 0)
        for copy in late():
            copy.wait()
        one_kept.wait()
        text_kept.start()

        def piece(i, carry):
            rows = pl.ds(pl.multiple_of(i * 16, 16), 16)
            high[rows], low[rows] = halves(wide[rows])
            return carry

        lax.fori_loop(0, spots // 16, piece, 0)

    def mapper_stores():
        half = mapper_part.shape[1]
        return [
            pltpu.make_async_copy(
                mapped.at[pl.ds(c * half, half)], mapper_part.at[c], load.at[10 + c]
            )
            for c in (0, 1)
        ]

    def text_products(t):
        left = halves(silu_ref[...])

        def strip(k, carry):
            cols = pl.ds(pl.multiple_of(k * TILE, TILE), TILE)
            right = halves(text_all[:, :, cols].reshape(-1, TILE))
            mapped[:, cols] = three_pass(left, right, ((0,), (0,)))
            return carry

        lax.fori_loop(0, count, strip, 0)
        for copy in mapper_stores():
            copy.start()
        column_pair(0)[0].start()
        column_pair(0)[1].start()
        first_loads[0].wait()
        total = ratio[0] + ratio[1] + ratio[2] + ratio[3]
        scale_sum = jnp.sum(total[0:8], axis=0, keepdims=True)
        shift_sum = jnp.sum(total[8:16], axis=0, keepdims=True)
        odd = lax.rem(lax.broadcasted_iota(jnp.int32, (CHUNK, chan), 0), 2) == 1
        both = jnp.where(odd, shift_sum, scale_sum)
        small[0] = both * embed_ref[:, 0:1]
        sums[4:5] = scale_sum
        sums[5:6] = shift_sum
        sums[6:7] = jnp.sum(wide[...], axis=0, keepdims=True)
        sums[7:8] = jnp.sum(text_all[...].reshape(-1, chan), axis=0, keepdims=True)
        width = chan // 4
        place = pl.ds(pl.multiple_of(me * width, width), width)
        small[1, 3:4, 0:width] = sums[6:7, place]
        small[1, 3:4, width : 2 * width] = sums[7:8, place]
        pair_place = pl.ds(pl.multiple_of(lax.rem(me, 2) * 2 * width, width), 2 * width)
        small[1, 4:5, width : 3 * width] = jnp.where(
            me < 2, sums[4:5, pair_place], sums[5:6, pair_place]
        )

    def column_pair(i):
        return [
            pltpu.make_async_copy(
                response_ref.at[
                    :, pl.ds(pl.multiple_of(c * (chan // 2) + i * 128, 128), 128)
                ],
                columns.at[lax.rem(i, 2), :, pl.ds(c * 128, 128)],
                load.at[6 + lax.rem(i, 2) if c == 0 else 12 + lax.rem(i, 2)],
            )
            for c in (0, 1)
        ]

    def reduce_stores(i):
        return [
            pltpu.make_async_copy(
                product.at[pl.ds(c * 128, 128)],
                reduce_part.at[c, pl.ds(pl.multiple_of(i * 128, 128), 128)],
                load.at[8 + c],
            )
            for c in (0, 1)
        ]

    def reduce_outer(i):
        for copy in column_pair(i):
            copy.wait()

        @pl.when(i + 1 < count)
        def _():
            for copy in column_pair(jnp.minimum(i + 1, count - 1)):
                copy.start()

        @pl.when(i + 1 == count)
        def _():
            weight_load(reduce_w_ref, 0).start()
            act_load(0).start()

        @pl.when(i > 0)
        def _():
            for copy in reduce_stores(jnp.maximum(i - 1, 0)):
                copy.wait()

        @pl.when(i == 0)
        def _():
            for copy in mapper_stores():
                copy.wait()

        left = halves(columns[lax.rem(i, 2), :, 0:TILE])

        def strip(k, carry):
            cols = pl.ds(pl.multiple_of(k * TILE, TILE), TILE)
            product[0:TILE, cols] = three_pass(left, (high[:, cols], low[:, cols]), ((0,), (0,)))
            return carry

        lax.fori_loop(0, count, strip, 0)
        for copy in reduce_stores(i):
            copy.start()

    def settle_reduce(t):
        for copy in reduce_stores(count - 1):
            copy.wait()
        text_kept.wait()
        for copy in loads + out_loads():
            copy.start()
        sums[0:4] = jnp.zeros((4, chan), jnp.float32)

    outward = near_slots(out_own, out_got, send, recv, 3)

    def away(i):
        rows = pl.ds(pl.multiple_of(i * 8, 8), 8)
        return remote(
            base.at[rows], layer_out.at[rows], tile_out.at[i], tile_in.at[i], (core, up, over)
        )

    def here(i):
        rows = pl.ds(pl.multiple_of(i * 8, 8), 8)
        return pltpu.make_async_copy(base.at[rows], layer_out.at[rows], tile_out.at[i])

    first_loads = [pltpu.make_async_copy(small_ref, small, keep.at[1])]
    loads = [
        pltpu.make_async_copy(conv_ref, conv, keep.at[2]),
        pltpu.make_async_copy(base_ref, base, keep.at[4]),
    ]
    kept = pltpu.make_async_copy(one, grad_out, keep.at[5])

    def tile_rows(i):
        return pl.ds(pl.multiple_of(i * TILE, TILE), TILE)

    def weight_load(ref, i):
        return pltpu.make_async_copy(
            ref.at[tile_rows(i)], weights.at[lax.rem(i, 2)], load.at[lax.rem(i, 2)]
        )

    def act_load(i):
        return pltpu.make_async_copy(
            act_ref.at[:, tile_rows(i)], acts.at[lax.rem(i, 2)], load.at[2 + lax.rem(i, 2)]
        )

    def slope_load(i):
        return pltpu.make_async_copy(
            slope_ref.at[:, tile_rows(i)], slopes.at[lax.rem(i, 2)], load.at[4 + lax.rem(i, 2)]
        )

    part = columns.shape[2]

    def column_load(i):
        return pltpu.make_async_copy(
            normed_ref.at[:, pl.ds(pl.multiple_of(i * part, part), part)],
            columns.at[lax.rem(i, 2)],
            load.at[6 + lax.rem(i, 2)],
        )

    def product_stores(i):
        half = part // 2
        return [
            pltpu.make_async_copy(
                product.at[pl.ds(c * half, half)], expand_part.at[i, c], load.at[8 + c]
            )
            for c in (0, 1)
        ]

    def front_sends(i):
        found = []
        for step in (3, 1, 2):
            found.append(
                remote(
                    front.at[lax.rem(i, 2), pl.ds(step * pixels, pixels)],
                    front_got.at[step - 1, :, tile_rows(i)],
                    front_out.at[i, step - 1],
                    front_in.at[i, step - 1],
                    (core, level, near_of(me, step)),
                )
            )
        return found

    for copy in early_loads()[0] + [early_column(0), early_column(1)]:
        copy.start()
    for copy in scatters + start_loads + first_loads:
        copy.start()

    def respond(i):
        weight_load(reduce_w_ref, i).wait()
        act_load(i).wait()

        @pl.when(i + 1 < count)
        def _():
            weight_load(reduce_w_ref, i + 1).start()
            act_load(i + 1).start()

        @pl.when(i + 1 == count)
        def _():
            act_load(0).start()
            slope_load(0).start()

        right = halves(weights[lax.rem(i, 2)])
        cols = tile_rows(i)

        def strip(k, carry):
            rows = pl.ds(pl.multiple_of(k * pixels, pixels), pixels)
            value = three_pass((high[rows], low[rows]), right, ((1,), (1,)))
            wide[rows, cols] = value
            sums[0:1, cols] += jnp.sum(value * acts[lax.rem(i, 2), rows], axis=0, keepdims=True)
            sums[1:2, cols] += jnp.sum(value, axis=0, keepdims=True)
            return carry

        lax.fori_loop(0, 4, strip, 0)

    def spreads():
        return [
            remote(
                spread_own, spread_got.at[step - 1], spread_out.at[step - 1],
                spread_in.at[step - 1], (core, level, near_of(me, step)),
            )
            for step in (3, 1, 2)
        ]

    def out_loads():
        return [
            pltpu.make_async_copy(mixture_ref, columns.at[0], load.at[6]),
            pltpu.make_async_copy(out_w_ref, product, load.at[7]),
        ]

    def out_product(i):
        pl.when(i == 0)(lambda: [copy.wait() for copy in out_loads()] and None)
        rows = pl.ds(pl.multiple_of(i * pixels, pixels), pixels)
        left = halves(columns[0, rows])

        def strip(k, carry):
            cols = pl.ds(pl.multiple_of(k * TILE, TILE), TILE)
            out_own[i, :, cols] = three_pass(left, halves(product[:, cols]), ((1,), (0,)))
            return carry

        lax.fori_loop(0, count, strip, 0)

    def send_out(t):
        for copy in outward:
            copy.start()

    def share(t):
        total = jnp.sum(sums[0:1] * rows_ref[0:1] * rows_ref[1:2], axis=1, keepdims=True)
        spread_own[...] = jnp.broadcast_to(total, spread_own.shape)
        for copy in spreads():
            copy.start()

    def agree(t):
        for copy in spreads():
            copy.wait()
        total = spread_own[...] + spread_got[0] + spread_got[1] + spread_got[2]
        total = jnp.max(total[0:1], axis=1, keepdims=True)
        inverse = rows_ref[3:4]
        norms = rows_ref[1:2]
        grad_norms = (
            sums[0:1] * rows_ref[0:1] * inverse - total * rows_ref[4:5] * inverse * inverse
        )
        sums[2:3] = grad_norms / norms
        small[1, 1:2] = sums[0:1] * rows_ref[5:6]
        small[1, 2:3] = sums[1:2]

    def bend(i):
        act_load(i).wait()
        slope_load(i).wait()

        @pl.when(i + 1 < count)
        def _():
            act_load(i + 1).start()
            slope_load(i + 1).start()

        @pl.when(i + 1 == count)
        def _():
            column_load(0).start()
            weight_load(expand_w_ref, 0).start()

        cols = tile_rows(i)
        factor = rows_ref[2:3, cols]
        twice = sums[2:3, cols]

        def strip(k, carry):
            rows = pl.ds(pl.multiple_of(k * 48, 48), 48)
            value = (
                wide[rows, cols] * factor + acts[lax.rem(i, 2), rows] * twice
            ) * slopes[lax.rem(i, 2), rows]
            high[rows, cols], low[rows, cols] = halves(value)
            sums[3:4, cols] += jnp.sum(value, axis=0, keepdims=True)
            return carry

        lax.fori_loop(0, spots // 48, strip, 0)

    def outer(i):
        column_load(i).wait()
        pl.when(i + 1 < 4)(lambda: column_load(jnp.minimum(i + 1, 3)).start())
        pl.when(i > 0)(lambda: [copy.wait() for copy in product_stores(jnp.maximum(i - 1, 0))] and None)
        left = halves(columns[lax.rem(i, 2)])

        def strip(k, carry):
            cols = pl.ds(pl.multiple_of(k * TILE, TILE), TILE)
            product[:, cols] = three_pass(left, (high[:, cols], low[:, cols]), ((0,), (0,)))
            return carry

        lax.fori_loop(0, count, strip, 0)
        for copy in product_stores(i):
            copy.start()

    def settle_outer(t):
        for copy in product_stores(3):
            copy.wait()
        small[1, 0:1] = sums[3:4]

    def backward(i):
        weight_load(expand_w_ref, i).wait()
        pl.when(i + 1 < count)(lambda: weight_load(expand_w_ref, jnp.minimum(i + 1, count - 1)).start())

        @pl.when(i > 1)
        def _():
            for copy in front_sends(jnp.maximum(i - 2, 0)):
                copy.wait_send()

        right = halves(weights[lax.rem(i, 2)])

        def strip(k, carry):
            rows = pl.ds(pl.multiple_of(k * pixels, pixels), pixels)
            front[lax.rem(i, 2), rows] = three_pass((high[rows], low[rows]), right, ((1,), (1,)))
            return carry

        lax.fori_loop(0, 4, strip, 0)
        front_own[:, tile_rows(i)] = front[lax.rem(i, 2), 0:pixels]
        for copy in front_sends(i):
            copy.start()

    def middle(t):
        loads[0].wait()
        for i in range(count):
            for copy in front_sends(i):
                copy.wait_recv()
                if i >= count - 2:
                    copy.wait_send()

    def tiles(t):
        def tile(i, carry):
            rows = pl.ds(pl.multiple_of(i * 8, 8), 8)
            back = front_own[rows] + front_got[0, rows] + front_got[1, rows] + front_got[2, rows]
            normed, inverse = row_stats(conv[rows])
            one[rows] = inverse * (
                back
                - jnp.mean(back, axis=-1, keepdims=True)
                - normed * jnp.mean(back * normed, axis=-1, keepdims=True)
            )
            return carry

        size = pixels // 48
        lax.fori_loop(t * size, (t + 1) * size, tile, 0)

    def give(t):
        kept.start()

    def outlet(t):
        pl.when(t == 0)(lambda: [copy.wait() for copy in loads[1:] + outward] and None)
        rows = pl.ds(pl.multiple_of(t * 8, 8), 8)
        base[rows] += out_own[0, rows] + out_got[0, rows] + out_got[1, rows] + out_got[2, rows]
        pl.when(moves)(away(t).start)
        pl.when(jnp.logical_not(moves))(here(t).start)

    sum_stream(
        [
            ("plain", output_ref, output_out),
            ("swap", attend_part, attend_out),
            ("plain", mapper_part, mapper_out),
            ("plain", reduce_part, reduce_out),
            ("plain", small, small_out),
            ("swap", expand_part, expand_out),
        ],
        scratch[:SCRATCH],
        [
            (0, 1, prepare),
            (1, 5, attend_outer),
            (5, 6, settle_attend),
            (12, 13, arrive),
            (12, 21, normalize),
            (21, 22, give_late),
            (24, 25, gathered),
            (25, 26, text_products),
            (26, 32, reduce_outer),
            (32, 33, settle_reduce),
            (33, 39, respond),
            (39, 40, share),
            (40, 41, agree),
            (41, 47, bend),
            (47, 51, outer),
            (51, 52, settle_outer),
            (52, 58, backward),
            (68, 69, middle),
            (68, 74, tiles),
            (74, 75, give),
            (60, 78, outlet),
            (39, 43, out_product),
            (43, 44, send_out),
        ],
    )
    kept.wait()

    def settle(i, carry):
        pl.when(moves)(away(i).wait)
        pl.when(jnp.logical_not(moves))(here(i).wait)
        return carry

    lax.fori_loop(0, base.shape[0] // 8, settle, 0)


def backward_sums(
    collective, output_part, qkv, two_share, text_share, cot, one, response, reduce_w, act, slope,
    normed_all, expand_w, conv, mixture, out_w, base, small, normed_two, rows, embed, silu,
    mapped, text_kv, mapper_half
):
    pixels, chan = conv.shape
    spots = normed_all.shape[0]
    texts = text_share.shape[1]
    slots = silu.shape[0] // 4
    f32, bf16 = jnp.float32, jnp.bfloat16
    half = chan // 8
    count = chan // TILE

    def shape(*dims):
        return jax.ShapeDtypeStruct(dims, f32)

    total = (half + 8 * half // 2 + mapper_half + chan // 2 + CHUNK + 8 * half // 2) // CHUNK
    block = (pixels, chan)
    return pl.pallas_call(
        backward_body,
        out_shape=[
            shape(2, half, chan),
            shape(2, half, 3 * chan),
            shape(2, mapper_half, chan),
            shape(2, chan // 2, chan),
            shape(2, CHUNK, chan),
            shape(2, half, 4 * chan),
            shape(4, 2, half, 3 * chan // 4),
            shape(2, mapper_half, chan),
            shape(2, chan // 2, chan),
            shape(4, 2, half, chan),
            shape(*block),
            shape(4, slots, chan),
            shape(*block),
            shape(*block),
        ],
        in_specs=[ANY] * 18 + [pl.BlockSpec(memory_space=pltpu.VMEM)] * 5,
        out_specs=[ANY] * 14,
        scratch_shapes=stream_scratch(total, 4 * half // CHUNK, chan)
        + [
            pltpu.VMEM((3,) + block, f32),
            pltpu.VMEM(block, f32),
            pltpu.VMEM(block, f32),
            pltpu.VMEM(block, f32),
            pltpu.VMEM(block, f32),
            pltpu.VMEM((3,) + block, f32),
            pltpu.VMEM((4,) + block, f32),
            pltpu.VMEM(block, f32),
            pltpu.VMEM(small.shape, f32),
            pltpu.VMEM((spots, chan), f32),
            pltpu.VMEM((spots, chan), bf16),
            pltpu.VMEM((spots, chan), bf16),
            pltpu.VMEM((2, TILE, chan), f32),
            pltpu.VMEM((2, spots, TILE), f32),
            pltpu.VMEM((2, spots, TILE), f32),
            pltpu.VMEM((2, spots, chan // 4), f32),
            pltpu.VMEM((chan // 4, chan), f32),
            pltpu.VMEM((2, spots, TILE), f32),
            pltpu.VMEM((8, chan), f32),
            pltpu.VMEM((8, 128), f32),
            pltpu.VMEM((3, 8, 128), f32),
            pltpu.VMEM((3, texts, chan), f32),
            pltpu.VMEM((texts, chan), f32),
            pltpu.VMEM((4, slots, chan), f32),
            pltpu.VMEM((4, 16, chan), f32),
            pltpu.VMEM((silu.shape[1], chan), f32),
            DMA((9,)),
            DMA((9,)),
            DMA((12,)),
            DMA((pixels // 8,)),
            DMA((pixels // 8,)),
            DMA((14,)),
            DMA((count, 3)),
            DMA((count, 3)),
            DMA((3,)),
            DMA((3,)),
            DMA((pixels // 16, 3)),
            DMA((pixels // 16, 3)),
            DMA((6,)),
            DMA((6,)),
        ],
        compiler_params=pltpu.CompilerParams(
            collective_id=collective, has_side_effects=True, vmem_limit_bytes=62 * 2**20
        ),
        name="backward_sums",
    )(
        output_part, qkv, two_share, text_share, cot, one, response, reduce_w, act, slope,
        normed_all, expand_w, conv, mixture, out_w, base, small, normed_two, rows, embed, silu,
        mapped, text_kv,
    )


def close_body(
    grad_in, token_in, conv_in, up_in, down_in,
    grad_home, token_home, conv_all, below, above,
    hold, send, recv, keep
):
    core = lax.axis_index("cond")
    level = lax.axis_index("pair")
    me = lax.axis_index("dp")
    up, over = home_spot(level, me)
    back_up, back_over = plane_spot(level, me)
    moves = jnp.logical_or(level != 0, me != 0)
    others = [(c, s) for c in (0, 1) for s in (0, 1, 2, 3) if (c, s) != (0, 0)]

    def other(c, s):
        return (lax.rem(core + c, 2), lax.rem(level + s, 4), me)

    for c, s in others:
        greet(other(c, s))
    pl.when(moves)(lambda: greet((core, back_up, back_over)))
    turned = jnp.logical_and(level == 1, me == 1)
    quarter = up
    lifts = quarter > 0
    drops = jnp.logical_and(quarter < 3, jnp.logical_not(turned))
    lifted = level < 3
    dropped = jnp.logical_and(level > 0, jnp.logical_not(turned))
    pl.when(lifted)(lambda: greet((core, me, near_of(me, rev(jnp.minimum(level + 1, 3))))))
    pl.when(dropped)(lambda: greet((core, me, near_of(me, rev(jnp.maximum(level - 1, 0))))))
    pl.semaphore_wait(
        pltpu.get_barrier_semaphore(),
        7 + jnp.where(moves, 1, 0) + jnp.where(lifts, 1, 0) + jnp.where(drops, 1, 0),
    )
    lift = remote(up_in, below, send.at[9], recv.at[9], (core, jnp.maximum(quarter - 1, 0), level))
    drop = remote(down_in, above, send.at[10], recv.at[10], (core, jnp.minimum(quarter + 1, 3), level))
    around = pltpu.make_async_copy(down_in, above, keep.at[3])
    pl.when(lifts)(lift.start)
    pl.when(drops)(drop.start)
    pl.when(turned)(around.start)
    swaps = ((grad_in, grad_home), (token_in, token_home))
    aways = [remote(src, dst, send.at[i], recv.at[i], (core, up, over)) for i, (src, dst) in enumerate(swaps)]
    spreads = [
        remote(conv_in, conv_all.at[1 + i], send.at[2 + i], recv.at[2 + i], other(c, s))
        for i, (c, s) in enumerate(others)
    ]
    mine = pltpu.make_async_copy(conv_in, conv_all.at[0], keep.at[2])
    for copy in spreads + [mine]:
        copy.start()
    for away in aways:
        pl.when(moves)(away.start)

    @pl.when(jnp.logical_not(moves))
    def _():
        load = pltpu.make_async_copy(grad_in, hold, keep.at[0])
        store = pltpu.make_async_copy(hold, grad_home, keep.at[0])
        small = pltpu.make_async_copy(token_in, token_home, keep.at[1])
        small.start()
        load.start()
        load.wait()
        store.start()
        store.wait()
        small.wait()

    for copy in spreads + [mine]:
        copy.wait()
    for away in aways:
        pl.when(moves)(away.wait)
    pl.when(lifts)(lift.wait_send)
    pl.when(drops)(drop.wait_send)
    pl.when(lifted)(lift.wait_recv)
    pl.when(dropped)(drop.wait_recv)
    pl.when(turned)(around.wait)


def close_exchange(collective, grad, tokens, conv, up, down):
    shapes = [grad.shape, tokens.shape, (8,) + conv.shape, up.shape, down.shape]
    return pl.pallas_call(
        close_body,
        out_shape=[jax.ShapeDtypeStruct(shape, jnp.float32) for shape in shapes],
        in_specs=[ANY] * 5,
        out_specs=[ANY] * 5,
        scratch_shapes=[pltpu.VMEM(grad.shape, jnp.float32), DMA((11,)), DMA((11,)), DMA((4,))],
        compiler_params=pltpu.CompilerParams(collective_id=collective, has_side_effects=True),
        name="close_exchange",
    )(grad, tokens, conv, up, down)


def plane_body(
    latents,
    ratio_embed,
    clip_tokens,
    cotangent,
    conv_kernel,
    conv_bias,
    expand_weight,
    expand_bias,
    response_gain,
    response_bias,
    reduce_weight,
    reduce_bias,
    ratio_weight,
    ratio_bias,
    text_weight,
    text_bias,
    attend_weight,
    query_bias,
    value_bias,
    output_weight,
    output_bias,
):
    size = lax.axis_size("dp")
    core = lax.axis_index("cond")
    me = lax.axis_index("dp")
    level = lax.axis_index("pair")
    quarter = home_spot(level, me)[0]
    order = jnp.bitwise_xor(jnp.arange(4), me)
    _, rows, cols, chan = latents.shape
    pixels = rows * cols
    part = chan // size
    hid = size * expand_bias.shape[0]
    texts = clip_tokens.shape[1]
    packed = jnp.concatenate(
        [
            conv_kernel.reshape(9, part),
            conv_bias[None],
            reduce_bias[None],
            text_bias[None],
            output_bias[None],
            ratio_bias.reshape(2, part),
        ],
        axis=0,
    )
    row_padded, every, tokens, embed, expand_w, attend_units = open_exchange(
        3, latents[0], packed, clip_tokens[0], ratio_embed, expand_weight, attend_weight
    )[:6]
    row_padded = row_padded.at[:1].set(jnp.where(quarter > 0, row_padded[:1], 0.0))
    row_padded = row_padded.at[-1:].set(jnp.where(quarter < size - 1, row_padded[-1:], 0.0))
    image = row_padded[1:-1]
    expand_w = expand_w.reshape(chan, -1)
    channel_rows = every[:, :13].transpose(1, 0, 2).reshape(13, chan)
    kernel = channel_rows[:9].reshape(3, 3, chan)
    conv_shift, reduce_b, text_b, out_b = (channel_rows[9 + i] for i in range(4))
    ratio_b = every[:, 13:].reshape(2 * chan)

    half = part // 2
    wide = hid // size
    text_part = text_weight.shape[0]
    token_cols = [
        lax.dynamic_slice(tokens, (0, near_of(me, step) * text_part), (texts, text_part))
        for step in range(4)
    ]
    ratio_part = ratio_weight.shape[0]
    embed_part = lax.dynamic_slice(embed, (0, me * ratio_part), (1, ratio_part))
    mod_part = jnp.dot(embed_part, ratio_weight, precision=HIGHEST_ACCURACY)

    padded = jnp.pad(row_padded, ((0, 0), (1, 1), (0, 0)))
    total_conv = conv_shift
    for i in range(3):
        for j in range(3):
            total_conv = total_conv + padded[i : i + rows, j : j + cols] * kernel[i, j]
    normed, inverse = norm_stats(total_conv.reshape(pixels, chan))
    normed_all, mod_near, near_tokens, attend_w = exchange(
        4,
        gathers=(normed, mod_part),
        scatters=(jnp.stack(token_cols),),
        relay=(attend_units,),
    )
    attend_w = attend_w.reshape(chan, 3 * part)
    modulation = jnp.sum(mod_near[:, 0], axis=0) + ratio_b
    mod_scale = 1.0 + modulation[:chan]
    mod_shift = modulation[chan:]
    normed_all = normed_all.reshape(size * pixels, chan)
    cot, normed_all = lax.optimization_barrier((cotangent[0].reshape(pixels, chan), normed_all))
    turns = (0, 2, 1, 3)
    grid = [(z, d) for z in range(size) for d in range(size)]
    cot = lax.ppermute(
        cot, ("pair", "dp"), [(z * size + d, z * size + (d ^ turns[z])) for z, d in grid]
    )
    near_tokens = jnp.concatenate([token_cols[0], near_tokens.reshape(-1, text_part)], axis=0)
    silu_near = jax.nn.silu(near_tokens)
    mapped_share = dot(silu_near, text_weight).reshape(4, texts, chan)
    hidden = dot(normed_all, expand_w) + expand_bias
    bell = 0.5 * (1.0 + lax.erf(hidden * 0.5**0.5))
    activated = hidden * bell
    density = jnp.exp(-0.5 * hidden * hidden) * (2.0 * jnp.pi) ** -0.5
    slope = bell + hidden * density
    totals = jnp.sum(activated * activated, axis=0)
    norms = jnp.sqrt(totals + EPSILON)
    norm_sums = exchange(5, gathers=(jnp.full((8, 128), jnp.sum(norms)),))[0]
    middle = jnp.sum(norm_sums[:, 0, 0]) / hid + EPSILON
    scaled = norms / middle
    factor = 1.0 + response_gain * scaled
    response = activated * factor + response_bias
    one_share = dot(response, reduce_weight).reshape(4, pixels, chan)
    cot, one_share = lax.optimization_barrier((cot, one_share))
    cot = lax.ppermute(
        cot, ("pair", "dp"), [(z * size + d, (d ^ turns[z]) * size + d) for z, d in grid]
    )
    one_arrived, mapped_arrived = exchange(6, scatters=(one_share, mapped_share))
    mapped = mapped_share[0] + jnp.sum(mapped_arrived, axis=0) + text_b
    hidden_one = one_share[0] + jnp.sum(one_arrived, axis=0) + image.reshape(pixels, chan) + reduce_b
    hidden_two = hidden_one * mod_scale + mod_shift
    normed_two, inverse_two = norm_stats(hidden_two)
    cot, normed_two = lax.optimization_barrier((cot, normed_two))
    normed_two_all, mapped_all = exchange(7, gathers=(normed_two, mapped))
    cot, normed_two_all = lax.optimization_barrier((cot, normed_two_all))
    cot_all = jnp.concatenate(
        [cot]
        + [lax.ppermute(cot, "dp", [(i, i ^ step) for i in range(size)]) for step in (1, 2, 3)],
        axis=0,
    )
    normed_two_all = normed_two_all.reshape(size * pixels, chan)
    mapped_all = mapped_all.reshape(size * texts, chan)

    source = jnp.concatenate([normed_two_all, mapped_all], axis=0)
    query = dot(normed_two_all, attend_w[:, :part]) + query_bias
    key_value = dot(source, attend_w[:, part:])
    key = key_value[:, :part]
    value = key_value[:, part:] + value_bias
    query_h, key_h, value_h = heads_of(query), heads_of(key), heads_of(value)
    scores = jnp.einsum("iuy,ouy->uio", query_h, key_h, precision=FAST) * HEAD_CHANNELS ** (-0.5)
    expo = jnp.exp(scores - jnp.max(scores, axis=-1, keepdims=True))
    probs = expo / jnp.sum(expo, axis=-1, keepdims=True)
    mixture_h = jnp.einsum("uio,ouy->iuy", probs, value_h, precision=FAST)
    mixture = mixture_h.reshape(query.shape)
    out_base = hidden_two + out_b

    output_grad = t_dot(mixture, cot_all)
    grad_mix_h = heads_of(dot_t(cot_all, output_weight))
    grad_probs = jnp.einsum("iuy,ouy->uio", grad_mix_h, value_h, precision=FAST)
    delta = jnp.sum(grad_mix_h * mixture_h, axis=-1).T
    grad_scores = probs * (grad_probs - delta[..., None]) * HEAD_CHANNELS ** (-0.5)
    grad_query = jnp.einsum("uio,ouy->iuy", grad_scores, key_h, precision=FAST).reshape(query.shape)
    grad_key = jnp.einsum("uio,iuy->ouy", grad_scores, query_h, precision=FAST).reshape(key.shape)
    grad_value = jnp.einsum("uio,iuy->ouy", probs, grad_mix_h, precision=FAST).reshape(key.shape)
    spots = size * pixels
    grad_kv = jnp.concatenate([grad_key, grad_value], axis=1)
    grad_qkv = jnp.concatenate([grad_query, grad_kv[:spots]], axis=1)
    two_share = dot_t(grad_qkv, attend_w).reshape(4, pixels, chan)
    text_share = dot_t(grad_kv[spots:], attend_w[:, part:]).reshape(4, texts, chan)
    def row(value):
        return jnp.sum(value, axis=0, keepdims=True)

    def mine(value):
        width = value.shape[1] // size
        return lax.dynamic_slice(value, (0, me * width), (value.shape[0], width))

    gap = jnp.zeros((1, part), jnp.float32)
    small_rows = jnp.concatenate(
        [
            jnp.zeros((3, chan), jnp.float32),
            jnp.concatenate([gap, gap, row(grad_query), row(grad_value)], axis=1),
            jnp.concatenate([row(mine(cot_all)), gap, gap, gap], axis=1),
            jnp.zeros((CHUNK - 5, chan), jnp.float32),
        ],
        axis=0,
    )
    one_row = jnp.full((1, chan), 1.0, jnp.float32)
    back_rows = jnp.concatenate(
        [
            response_gain[None],
            norms[None],
            factor[None],
            one_row / middle,
            one_row / hid,
            scaled[None],
            mod_scale[None],
            mod_shift[None],
        ],
        axis=0,
    )
    slots = (texts + 7) // 8 * 8

    def padded_rows(value):
        value = value.reshape(4, texts, -1)
        return jnp.pad(value, ((0, 0), (0, slots - texts), (0, 0))).reshape(4 * slots, -1)

    silu_padded = jnp.pad(
        silu_near.reshape(4, texts, text_part), ((0, 0), (0, slots - texts), (0, -text_part % 128))
    ).reshape(4 * slots, -1)
    embed_rows = jnp.broadcast_to(
        embed_part.reshape(ratio_part, 1, 1), (ratio_part, 2, 128)
    ).reshape(2 * ratio_part, 128)
    (
        output_sum, attend_sum, mapper_sum, reduce_sum, small, expand_sum, _, _, _, _,
        grad_one, grad_mapped_all, grad_conv, layer_output,
    ) = backward_sums(
        1,
        output_grad.reshape(2, half, chan),
        grad_qkv,
        two_share,
        text_share,
        cot,
        hidden_one,
        response,
        reduce_weight,
        activated,
        slope,
        normed_all,
        expand_w,
        total_conv.reshape(pixels, chan),
        mixture,
        output_weight,
        out_base,
        jnp.stack([jnp.zeros((CHUNK, chan), jnp.float32), small_rows]),
        normed_two_all,
        back_rows,
        embed_rows,
        silu_padded,
        padded_rows(mapped_all),
        padded_rows(grad_kv[spots:]),
        text_part // 2,
    )
    output_sum = output_sum.reshape(part, chan)
    attend_sum = attend_sum.reshape(part, 3 * chan)
    mapper_sum = mapper_sum.reshape(text_part, chan)
    reduce_sum = reduce_sum.reshape(wide, chan)
    expand_sum = expand_sum.reshape(part, hid)
    layer_output = layer_output.reshape(latents.shape)
    grad_mapped_all = grad_mapped_all[:, :texts].reshape(size * texts, chan)
    gate = 1.0 / (1.0 + jnp.exp(-near_tokens))
    tokens_near = dot_t(grad_mapped_all, text_weight) * (
        gate * (1.0 + near_tokens * (1.0 - gate))
    )
    tokens_near = tokens_near.reshape(4, texts, text_part)
    grad_conv = grad_conv.reshape(rows, cols, chan)
    kernel_grad = jnp.stack(
        [
            jnp.sum(padded[i : i + rows, j : j + cols] * grad_conv, axis=(0, 1))
            for i in range(3)
            for j in range(3)
        ]
    )
    spread_conv = jnp.pad(grad_conv, ((2, 2), (1, 1), (0, 0)))
    latent_rows = jnp.zeros((rows + 2, cols, chan), jnp.float32)
    for i in range(3):
        for j in range(3):
            latent_rows = (
                latent_rows
                + spread_conv[2 - i : 2 - i + rows + 2, 2 - j : 2 - j + cols] * kernel[i, j]
            )
    conv_part = jnp.concatenate([kernel_grad, jnp.sum(grad_conv, axis=(0, 1))[None]], axis=0)
    conv_blocks = jnp.stack(
        [
            lax.dynamic_slice(conv_part, (0, near_of(me, step) * part), (10, part))
            for step in range(4)
        ]
    )
    conv_arrived, token_arrived = exchange(13, scatters=(conv_blocks, tokens_near))
    token_blocks = jnp.take(
        jnp.concatenate([tokens_near[:1], token_arrived], axis=0), order, axis=0
    )
    inner = latent_rows[1:-1] + grad_one.reshape(rows, cols, chan)
    latent_grad, tokens_grad, conv_all, from_below, from_above = close_exchange(
        14,
        inner.reshape(pixels, chan),
        token_blocks.transpose(1, 0, 2).reshape(texts, size * text_part),
        conv_blocks[0] + jnp.sum(conv_arrived, axis=0),
        latent_rows[0],
        latent_rows[-1],
    )
    from_above = jnp.where(level > 0, from_above, 0.0)[None]
    from_below = jnp.where(level < size - 1, from_below, 0.0)[None]
    still = jnp.zeros((rows - 2, cols, chan), jnp.float32)
    latent_grad = latent_grad.reshape(rows, cols, chan) + jnp.concatenate(
        [from_above, still, from_below], axis=0
    )
    latent_grad = latent_grad[None]
    tokens_grad = tokens_grad[None]
    conv_mine = jnp.sum(conv_all, axis=0)
    ratio = small[0]
    expb, gain, respb = (small[1, i] for i in range(3))
    redb, mapb, queryb, valueb = (small[1, 3, i * part : (i + 1) * part] for i in range(4))
    outb = small[1, 4, :part]
    ratiob = small[1, 4, part : 3 * part]
    return (
        layer_output,
        latent_grad,
        tokens_grad,
        conv_mine[:9].reshape(3, 3, part),
        conv_mine[9],
        expand_sum,
        expb,
        gain,
        respb,
        reduce_sum,
        redb,
        ratio.reshape(ratio_part, 2 * chan),
        ratiob,
        mapper_sum,
        mapb,
        attend_sum,
        queryb,
        valueb,
        output_sum,
        outb,
    )


def solution(mesh):
    square = mesh.shape["cond"] == 2 and mesh.shape["pair"] == 4 and mesh.shape["dp"] == 4
    return jax.shard_map(
        plane_body if square else body,
        mesh=mesh,
        in_specs=(
            P(("cond", "dp"), "pair", None, None),
            P(("cond", "dp"), None),
            P(("cond", "dp"), "pair", None),
            P(("cond", "dp"), "pair", None, None),
            P(None, None, "dp"),
            P("dp"),
            P("dp", None),
            P("dp"),
            P("dp"),
            P("dp"),
            P("dp", None),
            P("dp"),
            P("dp", None),
            P("dp"),
            P("dp", None),
            P("dp"),
            P("dp", None),
            P("dp"),
            P("dp"),
            P("dp", None),
            P("dp"),
        ),
        out_specs=(
            P(("cond", "dp"), "pair", None, None),
            P(("cond", "dp"), "pair", None, None),
            P(("cond", "dp"), "pair", None),
            P(None, None, "dp"),
            P("dp"),
            P("dp", None),
            P("dp"),
            P("dp"),
            P("dp"),
            P("dp", None),
            P("dp"),
            P("dp", None),
            P("dp"),
            P("dp", None),
            P("dp"),
            P("dp", None),
            P("dp"),
            P("dp"),
            P("dp", None),
            P("dp"),
        ),
        check_vma=False,
    )
```

```python
import functools

import jax
import jax.numpy as jnp
from jax import lax
from jax.experimental import pallas as pl
from jax.experimental.pallas import tpu as pltpu
from jax.sharding import PartitionSpec as P

HEADS = 24
HEAD_CHANNELS = 64


HIGHEST_ACCURACY = lax.Precision.HIGHEST
EPSILON = 1e-06


def extended(block, sides, width):
    for axis, dim in sides:
        count = lax.axis_size(axis)
        forward = [(i, i + 1) for i in range(count - 1)]
        backward = [(target, source) for source, target in forward]
        low = lax.ppermute(
            lax.slice_in_dim(block, block.shape[dim] - width, None, axis=dim), axis, forward
        )
        high = lax.ppermute(lax.slice_in_dim(block, 0, width, axis=dim), axis, backward)
        block = jnp.concatenate([low, block, high], axis=dim)
    return block


def layer_norm(values):
    centered = values - jnp.mean(values, axis=-1, keepdims=True)
    variance = jnp.mean(centered * centered, axis=-1, keepdims=True)
    return centered * lax.rsqrt(variance + EPSILON)


def matmul(left, right):
    return jnp.einsum("...k,kn->...n", left, right, precision=HIGHEST_ACCURACY)


def depthwise(row_padded, kernel, conv_shift):
    row_count = row_padded.shape[1] - 2
    col_count = row_padded.shape[2]
    padded = jnp.pad(row_padded, ((0, 0), (0, 0), (1, 1), (0, 0)))
    total_conv = conv_shift
    for row_off in range(3):
        for col_off in range(3):
            total_conv = (
                total_conv
                + padded[:, row_off : row_off + row_count, col_off : col_off + col_count, :]
                * kernel[row_off, col_off]
            )
    return total_conv


def front(row_padded, kernel, conv_shift, expand_w, expand_b):
    normed = layer_norm(depthwise(row_padded, kernel, conv_shift))
    flat = normed.reshape(normed.shape[0], normed.shape[1] * normed.shape[2], normed.shape[3])
    return jax.nn.gelu(matmul(flat, expand_w) + expand_b, approximate=False)


def response_mlp(activated, totals, resp_gain, resp_bias, reduce_w, reduce_b, residual):
    norms = jnp.sqrt(totals + EPSILON)
    scaled = norms / (jnp.mean(norms, axis=-1, keepdims=True) + EPSILON)
    response = resp_gain * (activated * scaled[:, None, :]) + resp_bias + activated
    return residual + matmul(response, reduce_w) + reduce_b


def modulate(hidden_one, ratio_w, ratio_b, embed):
    modulation = jnp.dot(embed, ratio_w, precision=HIGHEST_ACCURACY) + ratio_b
    chan_count = hidden_one.shape[-1]
    return hidden_one * (1.0 + modulation[:, None, :chan_count]) + modulation[:, None, chan_count:]


def project(hidden_two, tokens, map_w, map_b, attend_w, query_b, value_b):
    chan_count = hidden_two.shape[-1]
    normed = layer_norm(hidden_two)
    mapped = matmul(jax.nn.silu(tokens), map_w) + map_b
    source = jnp.concatenate([normed, mapped], axis=1)
    query_matrix = matmul(normed, attend_w[:, :chan_count]) + query_b
    key_value = matmul(source, attend_w[:, chan_count:])
    return (query_matrix, key_value[..., :chan_count], key_value[..., chan_count:] + value_b)


def divide_into_heads(values):
    return values.reshape(values.shape[:-1] + (HEADS, HEAD_CHANNELS))


def attend_single(triple):
    query_matrix, key_matrix, value_matrix = triple
    attention_scores = jnp.einsum(
        "iuy,ouy->uio",
        divide_into_heads(query_matrix),
        divide_into_heads(key_matrix),
        precision=HIGHEST_ACCURACY,
    ) * HEAD_CHANNELS ** (-0.5)
    top_score = jnp.max(attention_scores, axis=-1, keepdims=True)
    expo_terms = jnp.exp(attention_scores - top_score)
    expo_total = jnp.sum(expo_terms, axis=-1, keepdims=True)
    attention_probabilities = expo_terms / expo_total
    attended_output = jnp.einsum(
        "fvb,bfq->vfq",
        attention_probabilities,
        divide_into_heads(value_matrix),
        precision=HIGHEST_ACCURACY,
    )
    log_total = top_score + jnp.log(expo_total)
    return (attended_output.reshape(query_matrix.shape), log_total)


def attend_back_single(items):
    query_matrix, key_matrix, value_matrix, attended_output, log_total, grad_mix = items
    query_per_head = divide_into_heads(query_matrix)
    key_per_head = divide_into_heads(key_matrix)
    value_per_head = divide_into_heads(value_matrix)
    gradient_per_head = divide_into_heads(grad_mix)
    attention_scores = jnp.einsum(
        "iuy,ouy->uio", query_per_head, key_per_head, precision=HIGHEST_ACCURACY
    ) * HEAD_CHANNELS ** (-0.5)
    attention_probabilities = jnp.exp(attention_scores - log_total)
    probability_gradient = jnp.einsum(
        "iuy,ouy->uio", gradient_per_head, value_per_head, precision=HIGHEST_ACCURACY
    )
    delta_rows = jnp.einsum(
        "phd,phd->hp",
        gradient_per_head,
        divide_into_heads(attended_output),
        precision=HIGHEST_ACCURACY,
    )
    score_gradient = (
        attention_probabilities
        * (probability_gradient - delta_rows[..., None])
        * HEAD_CHANNELS ** (-0.5)
    )
    query_gradient = jnp.einsum(
        "fvb,bfq->vfq", score_gradient, key_per_head, precision=HIGHEST_ACCURACY
    )
    key_gradient = jnp.einsum(
        "gyu,ygx->ugx", score_gradient, query_per_head, precision=HIGHEST_ACCURACY
    )
    value_gradient = jnp.einsum(
        "gyu,ygx->ugx", attention_probabilities, gradient_per_head, precision=HIGHEST_ACCURACY
    )
    return (
        query_gradient.reshape(query_matrix.shape),
        key_gradient.reshape(key_matrix.shape),
        value_gradient.reshape(value_matrix.shape),
    )


def body(
    latents,
    ratio_embed,
    clip_tokens,
    cotangent,
    conv_kernel,
    conv_bias,
    expand_weight,
    expand_bias,
    response_gain,
    response_bias,
    reduce_weight,
    reduce_bias,
    ratio_weight,
    ratio_bias,
    text_weight,
    text_bias,
    attend_weight,
    query_bias,
    value_bias,
    output_weight,
    output_bias,
):
    gathered = (
        lax.all_gather(conv_kernel, "dp", axis=2, tiled=True),
        lax.all_gather(conv_bias, "dp", axis=0, tiled=True),
        lax.all_gather(expand_weight, "dp", axis=0, tiled=True),
        lax.all_gather(expand_bias, "dp", axis=0, tiled=True),
        lax.all_gather(response_gain, "dp", axis=0, tiled=True),
        lax.all_gather(response_bias, "dp", axis=0, tiled=True),
        lax.all_gather(reduce_weight, "dp", axis=0, tiled=True),
        lax.all_gather(reduce_bias, "dp", axis=0, tiled=True),
        lax.all_gather(ratio_weight, "dp", axis=0, tiled=True),
        lax.all_gather(ratio_bias, "dp", axis=0, tiled=True),
        lax.all_gather(text_weight, "dp", axis=0, tiled=True),
        lax.all_gather(text_bias, "dp", axis=0, tiled=True),
        lax.all_gather(attend_weight, "dp", axis=0, tiled=True),
        lax.all_gather(query_bias, "dp", axis=0, tiled=True),
        lax.all_gather(value_bias, "dp", axis=0, tiled=True),
        lax.all_gather(output_weight, "dp", axis=0, tiled=True),
        lax.all_gather(output_bias, "dp", axis=0, tiled=True),
    )
    (
        kernel,
        conv_shift,
        expand_w,
        expand_b,
        resp_gain,
        resp_bias,
        reduce_w,
        reduce_b,
        ratio_w,
        ratio_b,
        map_w,
        map_b,
        attend_w,
        query_b,
        value_b,
        out_w,
        out_b,
    ) = gathered
    lat_count, row_count, col_count, chan_count = latents.shape
    pixel_count = row_count * col_count
    row_padded = extended(latents, (("pair", 1),), 1)
    activated, front_pull = jax.vjp(front, row_padded, kernel, conv_shift, expand_w, expand_b)
    totals = lax.psum(jnp.sum(activated * activated, axis=1), "pair")
    residual = latents.reshape(lat_count, pixel_count, chan_count)
    hidden_one, mlp_pull = jax.vjp(
        response_mlp, activated, totals, resp_gain, resp_bias, reduce_w, reduce_b, residual
    )
    hidden_two, mod_pull = jax.vjp(
        functools.partial(modulate, embed=ratio_embed), hidden_one, ratio_w, ratio_b
    )
    (query_matrix, key_local, value_local), proj_pull = jax.vjp(
        project, hidden_two, clip_tokens, map_w, map_b, attend_w, query_b, value_b
    )
    key_matrix, value_matrix = (
        lax.all_gather(key_local, "pair", axis=1, tiled=True),
        lax.all_gather(value_local, "pair", axis=1, tiled=True),
    )
    attended_output, log_total = lax.map(attend_single, (query_matrix, key_matrix, value_matrix))
    result = hidden_two + matmul(attended_output, out_w) + out_b
    layer_output = result.reshape(latents.shape)
    grad_out = cotangent.reshape(lat_count, pixel_count, chan_count)
    out_w_grad = jnp.einsum("lpc,lpn->cn", attended_output, grad_out, precision=HIGHEST_ACCURACY)
    out_b_grad = jnp.sum(grad_out, axis=(0, 1))
    grad_mix = jnp.einsum("lpn,cn->lpc", grad_out, out_w, precision=HIGHEST_ACCURACY)
    query_gradient, key_gradient, value_gradient = lax.map(
        attend_back_single,
        (query_matrix, key_matrix, value_matrix, attended_output, log_total, grad_mix),
    )
    key_share, value_share = (
        lax.psum_scatter(key_gradient, "pair", scatter_dimension=1, tiled=True),
        lax.psum_scatter(value_gradient, "pair", scatter_dimension=1, tiled=True),
    )
    grad_two, tokens_grad, map_w_grad, map_b_grad, attend_w_grad, query_b_grad, value_b_grad = (
        proj_pull((query_gradient, key_share, value_share))
    )
    grad_two = grad_two + grad_out
    attend_shards = (
        lax.psum_scatter(map_w_grad, "dp", scatter_dimension=0, tiled=True),
        lax.psum_scatter(map_b_grad, "dp", scatter_dimension=0, tiled=True),
        lax.psum_scatter(attend_w_grad, "dp", scatter_dimension=0, tiled=True),
        lax.psum_scatter(query_b_grad, "dp", scatter_dimension=0, tiled=True),
        lax.psum_scatter(value_b_grad, "dp", scatter_dimension=0, tiled=True),
        lax.psum_scatter(out_w_grad, "dp", scatter_dimension=0, tiled=True),
        lax.psum_scatter(out_b_grad, "dp", scatter_dimension=0, tiled=True),
    )
    grad_one, ratio_w_grad, ratio_b_grad = mod_pull(grad_two)
    grad_act, grad_totals, gain_grad, respb_grad, reduce_w_grad, reduce_b_grad, grad_res = mlp_pull(
        grad_one
    )
    grad_totals = lax.psum(grad_totals, "pair")
    grad_act = grad_act + 2.0 * activated * grad_totals[:, None, :]
    grad_padded, kernel_grad, shift_grad, expand_w_grad, expand_b_grad = front_pull(grad_act)
    rim_rows = jnp.concatenate([grad_padded[:, :1], grad_padded[:, -1:]], axis=1)
    arrived = extended(rim_rows, (("pair", 1),), 1)
    inner_rows = grad_padded[:, 1:-1]
    inner_rows = inner_rows.at[:, 0].add(arrived[:, 0]).at[:, -1].add(arrived[:, 3])
    latent_grad = inner_rows + grad_res.reshape(latents.shape)
    block_shards = (
        lax.psum_scatter(kernel_grad, "dp", scatter_dimension=2, tiled=True),
        lax.psum_scatter(shift_grad, "dp", scatter_dimension=0, tiled=True),
        lax.psum_scatter(expand_w_grad, "dp", scatter_dimension=0, tiled=True),
        lax.psum_scatter(expand_b_grad, "dp", scatter_dimension=0, tiled=True),
        lax.psum_scatter(gain_grad, "dp", scatter_dimension=0, tiled=True),
        lax.psum_scatter(respb_grad, "dp", scatter_dimension=0, tiled=True),
        lax.psum_scatter(reduce_w_grad, "dp", scatter_dimension=0, tiled=True),
        lax.psum_scatter(reduce_b_grad, "dp", scatter_dimension=0, tiled=True),
        lax.psum_scatter(ratio_w_grad, "dp", scatter_dimension=0, tiled=True),
        lax.psum_scatter(ratio_b_grad, "dp", scatter_dimension=0, tiled=True),
    )
    shards = tuple(block_shards) + tuple(attend_shards)
    summed = lax.psum(shards, ("cond", "pair"))
    return (layer_output, latent_grad, tokens_grad) + tuple(summed)

FAST = lax.Precision.HIGH


def dot(left, right):
    return jnp.dot(left, right, precision=FAST)


def dot_t(left, right):
    return lax.dot_general(left, right, (((1,), (1,)), ((), ())), precision=FAST)


def t_dot(left, right):
    return lax.dot_general(left, right, (((0,), (0,)), ((), ())), precision=FAST)


def norm_stats(values):
    centered = values - jnp.mean(values, axis=-1, keepdims=True)
    variance = jnp.mean(centered * centered, axis=-1, keepdims=True)
    inverse = lax.rsqrt(variance + EPSILON)
    return centered * inverse, inverse


def norm_back(grad, normed, inverse):
    return inverse * (
        grad
        - jnp.mean(grad, axis=-1, keepdims=True)
        - normed * jnp.mean(grad * normed, axis=-1, keepdims=True)
    )


def heads_of(values):
    return values.reshape(values.shape[0], -1, HEAD_CHANNELS)


CHUNK = 32
MESH = pl.DeviceIdType.MESH
DMA = pltpu.SemaphoreType.DMA
ANY = pl.BlockSpec(memory_space=pl.ANY)


def near_of(me, step):
    across = lax.rem(lax.rem(me, 2) + lax.rem(step, 2), 2)
    along = lax.rem(lax.div(me, 2) + lax.div(step, 2), 2)
    return along * 2 + across


def remote(src, dst, send, recv, device):
    return pltpu.make_async_remote_copy(
        src_ref=src, dst_ref=dst, send_sem=send, recv_sem=recv, device_id=device,
        device_id_type=MESH,
    )


def greet(device):
    barrier = pltpu.get_barrier_semaphore()
    pl.semaphore_signal(barrier, inc=1, device_id=device, device_id_type=MESH)


def relay_begin(full, sems):
    cross_out, cross_in, mate_out, mate_in = sems
    core = lax.axis_index("cond")
    level = lax.axis_index("pair")
    me = lax.axis_index("dp")
    unit = full.shape[1] // 4
    side = lax.rem(level, 2)
    across = (core, level + 1 - 2 * side, me)
    mate = (1 - core, level, me)

    def spot(u, step):
        rows = pl.ds(pl.multiple_of((core * 2 + u) * unit, 8), unit)
        return full.at[near_of(me, step), rows]

    steps = (1, 2, 3)
    crosses = [
        remote(
            spot(side, step), spot(side, step), cross_out.at[step - 1], cross_in.at[step - 1], across
        )
        for step in steps
    ]
    mates = [
        [
            remote(
                spot(u, step), spot(u, step), mate_out.at[i, step - 1], mate_in.at[i, step - 1], mate
            )
            for step in steps
        ]
        for i, u in enumerate((side, 1 - side))
    ]

    def begin():
        for copy in crosses + mates[0]:
            copy.start()

    def end():
        for cross, far in zip(crosses, mates[1]):
            cross.wait_recv()
            far.start()
        for copy in crosses:
            copy.wait_send()
        for copy in mates[0] + mates[1]:
            copy.wait()

    return begin, end


def exchange_body(gather_count, scatter_count, swap_count, relays, *refs):
    near_count = gather_count + scatter_count
    count = near_count + swap_count
    ins = refs[:count]
    refs = refs[count + relays :]
    outs = refs[:count]
    full = refs[count] if relays else None
    refs = refs[count + relays :]
    passing, refs = refs[:swap_count], refs[swap_count:]
    holds = refs[: gather_count + swap_count]
    refs = refs[gather_count + swap_count :]
    joined = [i for i in range(gather_count, near_count) if ins[i].shape[1] % 16 == 0]
    sums = dict(zip(joined, zip(refs[: 2 * len(joined) : 2], refs[1 : 2 * len(joined) : 2])))
    refs = refs[2 * len(joined) :]
    send, recv, keep, diag_out, diag_in, join_out, join_in, join_load = refs[:8]
    sems = refs[8:]
    core = lax.axis_index("cond")
    level = lax.axis_index("pair")
    me = lax.axis_index("dp")
    goal = near_of(me, rev(level))
    quarter = rev(near_of(level, me))
    shifts = level != 0
    rises = goal != level
    final = me == level
    expected = 3
    for step in (1, 2, 3):
        greet((core, level, near_of(me, step)))
    if relays:
        greet((1 - core, level, me))
        greet((core, level + 1 - 2 * lax.rem(level, 2), me))
        expected = expected + 2
    if swap_count:
        pl.when(rises)(lambda: greet((core, quarter, me)))
        expected = expected + jnp.where(rises, 1, 0)
    pl.semaphore_wait(pltpu.get_barrier_semaphore(), expected)

    def shift(i, goals):
        return remote(
            ins[near_count + i], goals[i], send.at[near_count + i, 0], recv.at[near_count + i, 0],
            (core, level, goal),
        )

    def rise(i, sources):
        return remote(
            sources[i], outs[near_count + i], send.at[near_count + i, 1],
            recv.at[near_count + i, 1], (core, goal, me),
        )

    def part_rows(i, k):
        half = ins[i].shape[1] // 2
        return pl.ds(half * k, half)

    def early(i, step):
        return remote(
            ins[i].at[3, part_rows(i, step - 1)], sums[i][1].at[step - 1],
            diag_out.at[i, step - 1], diag_in.at[i, step - 1], (core, level, near_of(me, step)),
        )

    def alone(i, step):
        rows = part_rows(i, step - 1)
        return remote(
            ins[i].at[step, rows], outs[i].at[step - 1, rows], send.at[i, step - 1],
            recv.at[i, step - 1], (core, level, near_of(me, step)),
        )

    def join(i, step):
        rows = part_rows(i, 2 - step)
        return remote(
            sums[i][0].at[step - 1], outs[i].at[step - 1, rows], join_out.at[i, step - 1],
            join_in.at[i, step - 1], (core, level, near_of(me, step)),
        )

    def join_own(i, step):
        return pltpu.make_async_copy(
            ins[i].at[step, part_rows(i, 2 - step)], sums[i][0].at[step - 1], join_load.at[i, step - 1]
        )

    for i in joined:
        for step in (1, 2):
            early(i, step).start()
            alone(i, step).start()
            join_own(i, step).start()
    swap_ins = ins[near_count:]
    swap_outs = outs[near_count:]
    near_copies = []
    if relays:
        relay_start, relay_end = relay_begin(full, sems)
        relay_start()
    for i in range(swap_count):
        pl.when(jnp.logical_and(shifts, final))(shift(i, swap_outs).start)
        pl.when(jnp.logical_and(shifts, jnp.logical_not(final)))(shift(i, passing).start)
        pl.when(jnp.logical_and(jnp.logical_not(shifts), rises))(rise(i, swap_ins).start)
    tall = [i for i in range(gather_count) if ins[i].shape[0] % 16 == 0]
    for step in (3, 1, 2):
        for i in range(near_count):
            if (step == 3 and i in tall) or i in joined:
                continue
            if i < gather_count:
                src, dst = ins[i], outs[i].at[step]
            else:
                src, dst = ins[i].at[step], outs[i].at[step - 1]
            copy = remote(
                src, dst, send.at[i, step - 1], recv.at[i, step - 1],
                (core, level, near_of(me, step)),
            )
            copy.start()
            if i not in tall:
                near_copies.append(copy)

    def direct(i, step):
        return remote(
            ins[i], outs[i].at[step], send.at[i, step - 1], recv.at[i, step - 1],
            (core, level, near_of(me, step)),
        )

    def onward(i, step):
        half = ins[i].shape[0] // 2
        rows = pl.ds(half * (step - 1), half)
        return remote(
            outs[i].at[step, rows], outs[i].at[3, rows], diag_out.at[i, step - 1],
            diag_in.at[i, step - 1], (core, level, near_of(me, 3 - step)),
        )

    def through(src, hold, dst, sem):
        load = pltpu.make_async_copy(src, hold, sem)
        load.start()
        load.wait()
        store = pltpu.make_async_copy(hold, dst, sem)
        store.start()
        store.wait()

    for i in range(gather_count):
        through(ins[i], holds[i], outs[i].at[0], keep.at[i])
    for i in range(swap_count):
        pl.when(jnp.logical_and(jnp.logical_not(shifts), jnp.logical_not(rises)))(
            lambda i=i: through(
                swap_ins[i], holds[gather_count + i], swap_outs[i], keep.at[gather_count + i]
            )
        )
        pl.when(shifts)(shift(i, passing).wait_recv)
        pl.when(jnp.logical_and(shifts, rises))(rise(i, passing).start)
    for i in joined:
        for step in (1, 2):
            early(i, 3 - step).wait_recv()
            join_own(i, step).wait()
            sums[i][0][step - 1] += sums[i][1][2 - step]
            join(i, step).start()
        for step in (1, 2):
            early(i, step).wait_send()
            alone(i, step).wait()
            join(i, step).wait()
    for i in tall:
        for step in (1, 2):
            direct(i, step).wait_recv()
            onward(i, step).start()
    if relays:
        relay_end()
    for i in tall:
        for step in (1, 2):
            direct(i, step).wait_send()
            onward(i, step).wait()
    for copy in near_copies:
        copy.wait()
    for i in range(swap_count):
        pl.when(shifts)(shift(i, passing).wait_send)
        pl.when(rises)(rise(i, swap_ins).wait_send)
        pl.when(quarter != level)(rise(i, swap_ins).wait_recv)


def exchange(collective, gathers=(), scatters=(), swaps=(), relay=()):
    f32 = jnp.float32
    shapes = [(4,) + item.shape for item in gathers]
    joined = [item for item in scatters if item.shape[1] % 16 == 0]
    shapes += [(2 if item.shape[1] % 16 == 0 else 3,) + item.shape[1:] for item in scatters]
    shapes += [item.shape for item in swaps]
    count = len(shapes)
    shapes += [item.shape for item in relay]
    shapes += [item.shape for item in swaps]
    staged = len(gathers) + len(swaps)
    scratch = [pltpu.VMEM(item.shape, f32) for item in tuple(gathers) + tuple(swaps)]
    for item in joined:
        half = (2, item.shape[1] // 2) + item.shape[2:]
        scratch += [pltpu.VMEM(half, f32), pltpu.VMEM(half, f32)]
    scratch += [DMA((count, 3)), DMA((count, 3)), DMA((max(staged, 1),))]
    scratch += [DMA((count, 2))] * 5
    if relay:
        scratch += [DMA((3,)), DMA((3,)), DMA((2, 3)), DMA((2, 3))]
    outs = pl.pallas_call(
        functools.partial(exchange_body, len(gathers), len(scatters), len(swaps), len(relay)),
        out_shape=[jax.ShapeDtypeStruct(shape, f32) for shape in shapes],
        in_specs=[ANY] * (count + len(relay)),
        out_specs=[ANY] * len(shapes),
        scratch_shapes=scratch,
        input_output_aliases={count: count} if relay else {},
        compiler_params=pltpu.CompilerParams(
            collective_id=collective, has_side_effects=True, vmem_limit_bytes=16 * 2**20
        ),
        name="exchange",
    )(*gathers, *scatters, *swaps, *relay)
    return outs[: count + len(relay)]


PARTS = 4


def open_body(image_in, packed_in, tokens_in, embed_in, weight_in, attend_in, *refs):
    image, packed, tokens, embed, weight, attend = refs[:6]
    passing = refs[6:9]
    hold, send, recv, keep, cross_out, cross_in, pass_out, pass_in, own_out, own_in, block_out, block_in = refs[9:]
    core = lax.axis_index("cond")
    level = lax.axis_index("pair")
    me = lax.axis_index("dp")
    mate = (1 - core, level, me)
    side = lax.rem(level, 2)
    across = (core, level + 1 - 2 * side, me)
    rows = image_in.shape[0]
    wide = weight.shape[3]
    unit = weight.shape[2]
    turn = rev(level)
    goal = near_of(me, turn)
    quarter = rev(near_of(level, me))
    shifts = level != 0
    rises = goal != level
    turned = jnp.logical_and(level == 1, me == 1)
    raises = jnp.logical_and(level > 0, jnp.logical_not(turned))
    falls = level < 3
    taken = jnp.logical_and(quarter < 3, jnp.logical_not(turned))
    greet(mate)
    greet(across)
    for step in (1, 2, 3):
        greet((core, level, near_of(me, step)))
    pl.when(rises)(lambda: greet((core, quarter, me)))
    pl.when(quarter > 0)(lambda: greet((core, quarter - 1, level)))
    pl.when(taken)(lambda: greet((core, quarter + 1, level)))
    expected = (
        5 + jnp.where(rises, 1, 0) + jnp.where(raises, 1, 0) + jnp.where(falls, 1, 0)
    )
    pl.semaphore_wait(pltpu.get_barrier_semaphore(), expected)

    body = image.at[pl.ds(1, rows)]
    ins = (image_in, tokens_in, embed_in)
    ends = (body, tokens, embed)

    def shift(goals):
        return [
            remote(src, dst, send.at[i], recv.at[i], (core, level, goal))
            for i, (src, dst) in enumerate(zip(ins, goals))
        ]

    def rise(sources):
        return [
            remote(src, dst, send.at[3 + i], recv.at[3 + i], (core, goal, me))
            for i, (src, dst) in enumerate(zip(sources, ends))
        ]

    def stay():
        image_load = pltpu.make_async_copy(image_in, hold, keep.at[0])
        image_load.start()
        rest = [
            pltpu.make_async_copy(src, dst, keep.at[i])
            for i, (src, dst) in ((1, (tokens_in, tokens)), (2, (embed_in, embed)))
        ]
        run("start", *rest)
        image_load.wait()
        image_store = pltpu.make_async_copy(hold, body, keep.at[0])
        image_store.start()
        run("wait", image_store, *rest)

    lower = remote(
        image_in.at[pl.ds(rows - 1, 1)], image.at[pl.ds(0, 1)], send.at[6], recv.at[6],
        (core, me, near_of(me, rev(jnp.minimum(level + 1, 3)))),
    )
    upper = remote(
        image_in.at[pl.ds(0, 1)], image.at[pl.ds(rows + 1, 1)], send.at[7], recv.at[7],
        (core, me, near_of(me, rev(jnp.maximum(level - 1, 0)))),
    )
    around = pltpu.make_async_copy(
        image_in.at[pl.ds(0, 1)], image.at[pl.ds(rows + 1, 1)], keep.at[4]
    )

    def vectors(step):
        return remote(
            packed_in, packed.at[me], send.at[7 + step], recv.at[7 + step],
            (core, level, near_of(me, step)),
        )

    mine = core * 2 + side
    other = core * 2 + 1 - side

    size = unit // PARTS

    def block(step, h):
        to = near_of(me, step)
        src = weight_in.at[
            pl.ds(pl.multiple_of(mine * unit + h * size, 8), size),
            pl.ds(pl.multiple_of(to * wide, wide), wide),
        ]
        dst = weight.at[me, mine, pl.ds(h * size, size)]
        return remote(
            src, dst, block_out.at[h, step - 1], block_in.at[h, step - 1], (core, level, to)
        )

    piece = attend.shape[2] // 3

    def thirds(step):
        to = near_of(me, step)
        found = []
        for p in range(3):
            src = attend_in.at[
                pl.ds(pl.multiple_of(mine * unit, 8), unit),
                pl.ds(pl.multiple_of((p * 4 + to) * piece, piece), piece),
            ]
            dst = attend.at[
                me, pl.ds(pl.multiple_of(mine * unit, 8), unit), pl.ds(p * piece, piece)
            ]
            spot = 11 + step * 3 + p
            found.append(remote(src, dst, send.at[spot], recv.at[spot], (core, level, to)))
        return found

    def crossed(step, u, h):
        spot = weight.at[near_of(me, step), u, pl.ds(h * size, size)]
        return remote(spot, spot, cross_out.at[h, step - 1], cross_in.at[h, step - 1], across)

    def passed(step, u, turn, h):
        spot = weight.at[near_of(me, step), u, pl.ds(h * size, size)]
        k = turn * PARTS + h
        return remote(spot, spot, pass_out.at[k, step - 1], pass_in.at[k, step - 1], mate)

    def run(method, *copies):
        for copy in copies:
            getattr(copy, method)()

    final = me == level
    pl.when(jnp.logical_and(shifts, final))(lambda: run("start", *shift(ends)))
    pl.when(jnp.logical_and(shifts, jnp.logical_not(final)))(lambda: run("start", *shift(passing)))
    pl.when(jnp.logical_and(jnp.logical_not(shifts), rises))(lambda: run("start", *rise(ins)))
    pl.when(falls)(lower.start)
    pl.when(raises)(upper.start)
    pl.when(turned)(around.start)
    own = [pltpu.make_async_copy(packed_in, packed.at[me], keep.at[3])]
    own_blocks = [
        remote(
            weight_in.at[pl.ds(u * unit, unit), pl.ds(pl.multiple_of(me * wide, wide), wide)],
            weight.at[me, u],
            own_out.at[u],
            own_in.at[u],
            mate,
        )
        for u in range(4)
    ] + [
        remote(
            attend_in.at[:, pl.ds(pl.multiple_of((p * 4 + me) * piece, piece), piece)],
            attend.at[me, :, pl.ds(p * piece, piece)],
            own_out.at[4 + p],
            own_in.at[4 + p],
            mate,
        )
        for p in range(3)
    ]
    for step in (3, 1, 2):
        vectors(step).start()
    for h in range(2):
        for step in (3, 1, 2):
            block(step, h).start()
    run("start", *own, *own_blocks)
    pl.when(jnp.logical_and(jnp.logical_not(shifts), jnp.logical_not(rises)))(stay)

    @pl.when(shifts)
    def _():
        run("wait_recv", *shift(passing))
        pl.when(rises)(lambda: run("start", *rise(passing)))

    for h in range(PARTS):
        for step in (2, 1, 3):
            block(step, h).wait_recv()
            if h + 2 < PARTS:
                block(step, h + 2).start()
            crossed(step, mine, h).start()
            passed(step, mine, 0, h).start()
    for step in (3, 1, 2):
        run("start", *thirds(step))
    for h in range(PARTS):
        for step in (2, 1, 3):
            crossed(step, other, h).wait_recv()
            passed(step, other, 1, h).start()
    pl.when(shifts)(lambda: run("wait_send", *shift(passing)))
    pl.when(rises)(lambda: run("wait_send", *rise(ins)))
    pl.when(quarter != level)(lambda: run("wait_recv", *rise(ins)))
    pl.when(falls)(lower.wait_send)
    pl.when(raises)(upper.wait_send)
    pl.when(quarter > 0)(lower.wait_recv)
    pl.when(taken)(upper.wait_recv)
    pl.when(turned)(around.wait)
    for step in (1, 2, 3):
        vectors(step).wait()
        run("wait", *thirds(step))
        for h in range(PARTS):
            block(step, h).wait_send()
            crossed(step, mine, h).wait_send()
            for u, turn_of in ((mine, 0), (other, 1)):
                passed(step, u, turn_of, h).wait()
    run("wait", *own, *own_blocks)


def open_exchange(collective, image, packed, tokens, embed, weight, attend):
    rows, cols, chan = image.shape
    unit = weight.shape[0] // 4
    shapes = [
        (rows + 2, cols, chan),
        (4,) + packed.shape,
        tokens.shape,
        embed.shape,
        (4, 4, unit, weight.shape[1] // 4),
        (4, attend.shape[0], attend.shape[1] // 4),
        image.shape,
        tokens.shape,
        embed.shape,
    ]
    return pl.pallas_call(
        open_body,
        out_shape=[jax.ShapeDtypeStruct(shape, jnp.float32) for shape in shapes],
        in_specs=[ANY] * 6,
        out_specs=[ANY] * 9,
        scratch_shapes=[
            pltpu.VMEM(image.shape, jnp.float32),
            DMA((23,)),
            DMA((23,)),
            DMA((5,)),
            DMA((PARTS, 3)),
            DMA((PARTS, 3)),
            DMA((2 * PARTS, 3)),
            DMA((2 * PARTS, 3)),
            DMA((7,)),
            DMA((7,)),
            DMA((PARTS, 3)),
            DMA((PARTS, 3)),
        ],
        compiler_params=pltpu.CompilerParams(collective_id=collective, has_side_effects=True),
        name="open_exchange",
    )(image, packed, tokens, embed, weight, attend)


def rev(z):
    return 2 * lax.rem(z, 2) + lax.div(z, 2)


def plane_spot(level, me):
    return me, near_of(me, rev(level))


def home_spot(level, me):
    return rev(near_of(level, me)), level


def stream_setup(homeward=False):
    core = lax.axis_index("cond")
    level = lax.axis_index("pair")
    me = lax.axis_index("dp")
    greet((1 - core, level, me))
    for step in (1, 2, 3):
        greet((core, level, near_of(me, step)))
    pl.when(level > 0)(lambda: greet((core, level - 1, me)))
    pl.when(level < 3)(lambda: greet((core, level + 1, me)))
    ends = jnp.where(level == 0, 1, 0) + jnp.where(level == 3, 1, 0)
    expected = 6 - ends
    if homeward:
        moves = jnp.logical_or(level != 0, me != 0)
        back_up, back_over = plane_spot(level, me)
        pl.when(moves)(lambda: greet((core, back_up, back_over)))
        expected = expected + jnp.where(moves, 1, 0)
    pl.semaphore_wait(pltpu.get_barrier_semaphore(), expected)


def sum_stream(sections, scratch, hooks):
    (
        data,
        stage,
        first,
        second,
        own,
        load_sem,
        core_out,
        core_in,
        plane_out,
        plane_in,
        first_in,
        second_in,
        hop_out,
        cast_out,
        cast_low,
        final_in,
        keep_sem,
        pair_out,
        pair_in,
    ) = scratch
    ranges = []
    total = 0
    for kind, src, dst in sections:
        if kind == "plain":
            count, width = src.shape[1] // CHUNK, src.shape[2]
        else:
            count, width = 4 * (src.shape[2] // CHUNK), src.shape[3]
        ranges.append((total, total + count, kind, src, dst, width))
        total += count
    core = lax.axis_index("cond")
    level = lax.axis_index("pair")
    me = lax.axis_index("dp")
    mate = (1 - core, level, me)
    ring = data.shape[0]
    full = data.shape[2]

    def rank_of(j):
        return jnp.where(lax.rem(j, 2) == 0, level, 3 - level)

    def at_rank(j, rank):
        return (core, jnp.where(lax.rem(j, 2) == 0, rank, 3 - rank), me)

    def inside(j, low, high):
        return jnp.logical_and(j >= low, j < high)

    def swap_place(j):
        inner = False
        k = 0
        for low, high, kind, src, dst, width in ranges:
            if kind == "swap":
                here = inside(j, low, high)
                inner = jnp.logical_or(inner, here)
                k = jnp.where(here, j - low, k)
        return inner, k

    def moved(j):
        inner, k = swap_place(j)
        return jnp.logical_and(inner, lax.rem(k, 4) != 0)

    def kinds(j, action):
        narrow = False
        for low, high, kind, src, dst, width in ranges:
            if width != full:
                here = inside(j, low, high)
                narrow = jnp.logical_or(narrow, here)
                pl.when(here)(lambda width=width: action(width))
        pl.when(jnp.logical_not(narrow))(lambda: action(full))

    def cut(ref, width):
        return ref if ref.shape[-1] == width else ref.at[:, pl.ds(0, width)]

    def each_source(j, action):
        target = data.at[lax.rem(j, ring)]
        mine = own.at[lax.rem(j, 4)]
        for low, high, kind, src, dst, width in ranges:

            @pl.when(inside(j, low, high))
            def _(low=low, kind=kind, src=src, width=width):
                k = j - low
                if kind == "plain":
                    rows = pl.ds(pl.multiple_of(k * CHUNK, CHUNK), CHUNK)
                    action(lambda half: src.at[half, rows], target, mine)
                else:
                    rows = pl.ds(pl.multiple_of(lax.div(k, 4) * CHUNK, CHUNK), CHUNK)
                    spot = near_of(me, lax.rem(k, 4))
                    action(
                        lambda half: src.at[spot, half, rows], cut(target, width), cut(mine, width)
                    )

    def each_final(j, action):
        for low, high, kind, src, dst, width in ranges:

            @pl.when(inside(j, low, high))
            def _(low=low, kind=kind, dst=dst, width=width):
                k = j - low
                if kind == "plain":
                    rows = pl.ds(pl.multiple_of(k * CHUNK, CHUNK), CHUNK)
                    action(
                        lambda half: [(dst.at[half, rows], lambda x: x, 0)],
                        first.at[lax.rem(j, ring)],
                    )
                else:
                    rows = pl.ds(pl.multiple_of(lax.div(k, 4) * CHUNK, CHUNK), CHUNK)
                    spot = near_of(me, lax.rem(k, 4))
                    pieces = 1 if width == full else 3
                    piece = width // pieces

                    def targets(half):
                        found = []
                        for p in range(pieces):
                            columns = pl.ds(
                                pl.multiple_of(p * 4 * piece + spot * piece, piece), piece
                            )
                            found.append(
                                (
                                    dst.at[half, rows, columns],
                                    lambda x, p=p: x
                                    if x.shape[-1] == piece
                                    else x.at[:, pl.ds(p * piece, piece)],
                                    p,
                                )
                            )
                        return found

                    action(targets, stage.at[k])

    def core_copy(j, src, dst):
        return remote(src, dst, core_out.at[j], core_in.at[j], mate)

    def plane_copy(j, width):
        inner, k = swap_place(j)
        return remote(
            cut(first.at[lax.rem(j, ring)], width),
            cut(stage.at[k], width),
            plane_out.at[j],
            plane_in.at[j],
            (core, level, near_of(me, lax.rem(k, 4))),
        )

    def hop_first(j, src, rank, width):
        return remote(
            cut(src, width), cut(first.at[lax.rem(j, ring)], width), hop_out.at[j], first_in.at[j], at_rank(j, rank)
        )

    def hop_second(j, width):
        k = lax.div(j, 2)
        return remote(
            cut(data.at[lax.rem(j, ring)], width), cut(second.at[lax.rem(k, ring // 2)], width), hop_out.at[j], second_in.at[k],
            at_rank(j, 2),
        )

    def start(j):
        def go(source, target, mine):
            core_copy(j, source(1 - core), target).start()
            pltpu.make_async_copy(source(core), mine, load_sem.at[lax.rem(j, 4)]).start()

        each_source(j, go)

    def combine(j):
        def go(source, target, mine):
            pltpu.make_async_copy(source(core), mine, load_sem.at[lax.rem(j, 4)]).wait()
            core_copy(j, source(1 - core), target).wait_recv()
            target[...] += mine[...]

        each_source(j, go)

    def depart(j):
        rank = rank_of(j)

        def go(width):
            pl.when(rank == 0)(lambda: hop_first(j, data.at[lax.rem(j, ring)], 1, width).start())
            pl.when(rank == 3)(lambda: hop_second(j, width).start())

        kinds(j, go)

    def relay(j):
        def go(width):
            hop_first(j, data.at[lax.rem(j, ring)], 1, width).wait_recv()
            spot = lax.rem(j, ring)
            first[spot, :, :width] += data[spot, :, :width]
            hop_first(j, first.at[lax.rem(j, ring)], 2, width).start()

        pl.when(rank_of(j) == 1)(lambda: kinds(j, go))

    def casts(j, rank, half_targets, source, sems):
        return [
            remote(
                cut_of(source) if source is not None else ref, ref, sems.at[j, p], final_in.at[j, p],
                at_rank(j, rank),
            )
            for ref, cut_of, p in half_targets
        ]

    def pairs(j, half_targets, source):
        return [
            remote(
                cut_of(source) if source is not None else ref, ref, pair_out.at[j, p],
                pair_in.at[j, p], mate,
            )
            for ref, cut_of, p in half_targets
        ]

    def keeps(j, half_targets, source):
        return [
            pltpu.make_async_copy(cut_of(source), ref, keep_sem.at[j, p])
            for ref, cut_of, p in half_targets
        ]

    def root(j):
        def add(width):
            hop_first(j, first.at[lax.rem(j, ring)], 2, width).wait_recv()
            hop_second(j, width).wait_recv()
            spot = lax.rem(j, ring)
            first[spot, :, :width] += (
                data[spot, :, :width] + second[lax.rem(lax.div(j, 2), ring // 2), :, :width]
            )

        @pl.when(rank_of(j) == 2)
        def _():
            kinds(j, add)

            @pl.when(moved(j))
            def _():
                kinds(j, lambda width: plane_copy(j, width).start())

            inner, k = swap_place(j)

            @pl.when(jnp.logical_and(inner, jnp.logical_not(moved(j))))
            def _():
                stage[k] = first[lax.rem(j, ring)]

    def spread(j):
        def send(targets, source):
            goals = targets(core)
            for copy in (
                casts(j, 1, goals, source, cast_out)
                + casts(j, 3, goals, source, cast_low)
                + keeps(j, goals, source)
                + pairs(j, goals, source)
            ):
                copy.start()

        @pl.when(rank_of(j) == 2)
        def _():
            @pl.when(moved(j))
            def _():
                kinds(j, lambda width: plane_copy(j, width).wait_recv())

            each_final(j, send)

    def landed(j):
        rank = rank_of(j)

        def go(targets, source):
            goals = targets(core)
            for copy in casts(j, 1, goals, None, cast_out):
                copy.wait_recv()
            pl.when(rank == 1)(
                lambda: [copy.start() for copy in casts(j, 0, goals, None, cast_out)] and None
            )
            for copy in pairs(j, goals, None):
                copy.start()

        @pl.when(jnp.logical_or(rank == 1, rank == 3))
        def _():
            each_final(j, go)

    def arrived(j):
        def go(targets, source):
            goals = targets(core)
            for copy in casts(j, 0, goals, None, cast_out):
                copy.wait_recv()
            for copy in pairs(j, goals, None):
                copy.start()

        @pl.when(rank_of(j) == 0)
        def _():
            each_final(j, go)

    def finish(j):
        rank = rank_of(j)

        def sent(source, target, mine):
            core_copy(j, source(1 - core), target).wait_send()

        each_source(j, sent)

        @pl.when(jnp.logical_and(moved(j), rank == 2))
        def _():
            kinds(j, lambda width: plane_copy(j, width).wait_send())

        @pl.when(rank != 2)
        def _():
            kinds(j, lambda width: hop_first(j, data.at[lax.rem(j, ring)], 1, width).wait_send())

        def go(targets, source):
            goals = targets(core)

            @pl.when(jnp.logical_or(rank == 1, rank == 2))
            def _():
                for copy in casts(j, 1, goals, None, cast_out):
                    copy.wait_send()

            @pl.when(rank == 2)
            def _():
                for copy in casts(j, 3, goals, None, cast_low):
                    copy.wait_send()
                for copy in keeps(j, goals, source):
                    copy.wait()

            for copy in pairs(j, goals, None):
                copy.wait()

        each_final(j, go)

    stages = (
        (0, start),
        (3, combine),
        (5, depart),
        (8, relay),
        (11, root),
        (14, spread),
        (17, landed),
        (20, arrived),
        (23, finish),
    )

    def step(t, carry):
        for lag, stage_of in stages:
            j = t - lag

            @pl.when(jnp.logical_and(j >= 0, j < total))
            def _(j=j, stage_of=stage_of):
                stage_of(j)

        for low, high, hook in hooks:
            pl.when(jnp.logical_and(t >= low, t < high))(lambda hook=hook, low=low: hook(t - low))
        return carry

    lax.fori_loop(0, total + 23, step, 0)


def stream_scratch(total, most, width):
    ring = 32
    return [
        pltpu.VMEM((ring, CHUNK, width), jnp.float32),
        pltpu.VMEM((most, CHUNK, width), jnp.float32),
        pltpu.VMEM((ring, CHUNK, width), jnp.float32),
        pltpu.VMEM((ring // 2, CHUNK, width), jnp.float32),
        pltpu.VMEM((4, CHUNK, width), jnp.float32),
        DMA((4,)),
        DMA((total,)),
        DMA((total,)),
        DMA((total,)),
        DMA((total,)),
        DMA((total,)),
        DMA(((total + 1) // 2,)),
        DMA((total,)),
        DMA((total, 3)),
        DMA((total, 3)),
        DMA((total, 3)),
        DMA((total, 3)),
        DMA((total, 3)),
        DMA((total, 3)),
    ]


SCRATCH = 19


def near_slots(shares, arrived, send, recv, base):
    core = lax.axis_index("cond")
    level = lax.axis_index("pair")
    me = lax.axis_index("dp")
    return [
        remote(
            shares.at[step], arrived.at[step - 1], send.at[base + step - 1],
            recv.at[base + step - 1], (core, level, near_of(me, step)),
        )
        for step in (3, 1, 2)
    ]


def near_blocks(block, everyone, send, recv, base):
    core = lax.axis_index("cond")
    level = lax.axis_index("pair")
    me = lax.axis_index("dp")
    return [
        remote(
            block, everyone.at[step], send.at[base + step - 1], recv.at[base + step - 1],
            (core, level, near_of(me, step)),
        )
        for step in (3, 1, 2)
    ]


def row_stats(rows):
    centered = rows - jnp.mean(rows, axis=-1, keepdims=True)
    inverse = lax.rsqrt(jnp.mean(centered * centered, axis=-1, keepdims=True) + EPSILON)
    return centered * inverse, inverse


def halves(value):
    high = value.astype(jnp.bfloat16)
    return high, (value - high.astype(jnp.float32)).astype(jnp.bfloat16)


def three_pass(left, right, dims):
    def one(x, y):
        return lax.dot_general(x, y, (dims, ((), ())), preferred_element_type=jnp.float32)

    return one(left[0], right[1]) + one(left[1], right[0]) + one(left[0], right[0])


TILE = 256


def backward_body(
    output_ref, qkv_ref, two_ref, text_ref, cot_ref, one_ref, response_ref, reduce_w_ref,
    act_ref, slope_ref, normed_ref, expand_w_ref, conv_ref, mixture_ref, out_w_ref, base_ref,
    small_ref,
    normed_two_ref, rows_ref, embed_ref, silu_ref, mapped_ref, text_kv_ref,
    output_out, attend_out, mapper_out, reduce_out, small_out, expand_out,
    attend_part, mapper_part, reduce_part, expand_part, one_out, text_out, grad_out, layer_out,
    *scratch
):
    (
        front_got, front_own, conv, grad, one, out_got, out_own, base, small, wide, high, low,
        weights, acts, slopes, columns, product, front, sums, spread_own, spread_got,
        text_got, text_own, text_all, ratio, mapped,
    ) = scratch[SCRATCH : SCRATCH + 26]
    (
        send, recv, keep, tile_out, tile_in, load, front_out, front_in, spread_out, spread_in,
        piece_out, piece_in, text_out_sem, text_in_sem,
    ) = scratch[SCRATCH + 26 :]
    stream_setup(True)
    core = lax.axis_index("cond")
    level = lax.axis_index("pair")
    me = lax.axis_index("dp")
    moves = jnp.logical_or(level != 0, me != 0)
    up, over = home_spot(level, me)
    pixels, chan = conv.shape
    spots = wide.shape[0]
    texts = text_own.shape[0]
    count = chan // TILE
    scatters = near_slots(two_ref, front_got, send, recv, 0)
    scatters += near_slots(text_ref, text_got, send, recv, 6)
    start_loads = [
        pltpu.make_async_copy(src, dst, keep.at[6 + i])
        for i, (src, dst) in enumerate(
            ((two_ref.at[0], front_own), (text_ref.at[0], text_own), (cot_ref, conv), (one_ref, one))
        )
    ]

    def near_tile(i):
        rows = pl.ds(pl.multiple_of(i * 16, 16), 16)
        return [
            remote(
                grad.at[rows],
                wide.at[pl.ds(pl.multiple_of(step * pixels + i * 16, 16), 16)],
                piece_out.at[i, step - 1],
                piece_in.at[i, step - 1],
                (core, level, near_of(me, step)),
            )
            for step in (3, 1, 2)
        ]

    def late():
        found = []
        for step in (3, 1, 2):
            device = (core, level, near_of(me, step))
            found.append(
                remote(
                    text_all.at[0], text_all.at[step], text_out_sem.at[step - 1],
                    text_in_sem.at[step - 1], device,
                )
            )
            found.append(
                remote(
                    ratio.at[0], ratio.at[step], text_out_sem.at[2 + step],
                    text_in_sem.at[2 + step], device,
                )
            )
        return found

    one_kept = pltpu.make_async_copy(grad, one_out, keep.at[10])
    text_kept = pltpu.make_async_copy(text_all, text_out, keep.at[11])

    def early_loads():
        homes = [(acts, 0), (acts, 1), (slopes, 0), (slopes, 1), (front, 0)]
        found = []
        for i, (buffer, slot) in enumerate(homes):
            width = min(TILE, qkv_ref.shape[1] - i * TILE)
            dst = buffer.at[slot] if width == TILE else buffer.at[slot, :, pl.ds(0, width)]
            found.append(
                pltpu.make_async_copy(
                    qkv_ref.at[:, pl.ds(i * TILE, width)], dst, load.at[2 + i if i < 4 else 0]
                )
            )
        return found, homes

    def early_column(i):
        return pltpu.make_async_copy(
            normed_two_ref.at[:, pl.ds(pl.multiple_of(i * part, part), part)],
            columns.at[lax.rem(i, 2)],
            load.at[6 + lax.rem(i, 2)],
        )

    def attend_stores(i):
        half = part // 2
        return [
            pltpu.make_async_copy(
                product.at[pl.ds(c * half, half), pl.ds(0, 3 * part)],
                attend_part.at[i, c],
                load.at[8 + c],
            )
            for c in (0, 1)
        ]

    def prepare(t):
        copies, homes = early_loads()
        for i, (copy, (buffer, slot)) in enumerate(zip(copies, homes)):
            copy.wait()
            width = min(TILE, qkv_ref.shape[1] - i * TILE)

            def strip(k, carry, i=i, buffer=buffer, slot=slot, width=width):
                rows = pl.ds(pl.multiple_of(k * 48, 48), 48)
                cols = pl.ds(i * TILE, width)
                high[rows, cols], low[rows, cols] = halves(buffer[slot, rows, 0:width])
                return carry

            lax.fori_loop(0, spots // 48, strip, 0)

    def attend_outer(i):
        early_column(i).wait()

        @pl.when(i > 0)
        def _():
            for copy in attend_stores(jnp.maximum(i - 1, 0)):
                copy.wait()

        left = halves(columns[lax.rem(i, 2)])
        text_left = halves(mapped_ref[:, pl.ds(pl.multiple_of(i * part, part), part)])
        for k in range(3):
            cols = pl.ds(k * part, part)
            value = three_pass(left, (high[:, cols], low[:, cols]), ((0,), (0,)))
            if k > 0:
                right = halves(text_kv_ref[:, (k - 1) * part : k * part])
                value = value + three_pass(text_left, right, ((0,), (0,)))
            product[:, cols] = value
        for copy in attend_stores(i):
            copy.start()
        pl.when(i + 2 < 4)(lambda: early_column(jnp.minimum(i + 2, 3)).start())

    def settle_attend(t):
        for copy in attend_stores(3):
            copy.wait()

    def arrive(t):
        for copy in start_loads + scatters:
            copy.wait()
        ratio[0] = jnp.zeros_like(ratio[0])
        text_all[0] = jnp.zeros_like(text_all[0])
        text_all[0, 0:texts] = text_own[...] + text_got[0] + text_got[1] + text_got[2]

    def normalize(t):
        scale = rows_ref[6:7]
        shift = rows_ref[7:8]
        for half in range(2):
            rows = pl.ds(pl.multiple_of(t * 16 + half * 8, 8), 8)
            back = front_own[rows] + front_got[0, rows] + front_got[1, rows] + front_got[2, rows]
            hidden = one[rows]
            normed, inverse = row_stats(hidden * scale + shift)
            two = conv[rows] + inverse * (
                back
                - jnp.mean(back, axis=-1, keepdims=True)
                - normed * jnp.mean(back * normed, axis=-1, keepdims=True)
            )
            grad[rows] = two * scale
            ratio[0, 0:8] += two * hidden
            ratio[0, 8:16] += two
        for copy in near_tile(t):
            copy.start()

    def give_late(t):
        for copy in late():
            copy.start()
        one_kept.start()
        wide[0:pixels] = grad[...]

    def gathered(t):
        def wait(i, carry):
            for copy in near_tile(i):
                copy.wait()
            return carry

        lax.fori_loop(0, pixels // 16, wait, 0)
        for copy in late():
            copy.wait()
        one_kept.wait()
        text_kept.start()

        def piece(i, carry):
            rows = pl.ds(pl.multiple_of(i * 16, 16), 16)
            high[rows], low[rows] = halves(wide[rows])
            return carry

        lax.fori_loop(0, spots // 16, piece, 0)

    def mapper_stores():
        half = mapper_part.shape[1]
        return [
            pltpu.make_async_copy(
                mapped.at[pl.ds(c * half, half)], mapper_part.at[c], load.at[10 + c]
            )
            for c in (0, 1)
        ]

    def text_products(t):
        left = halves(silu_ref[...])

        def strip(k, carry):
            cols = pl.ds(pl.multiple_of(k * TILE, TILE), TILE)
            right = halves(text_all[:, :, cols].reshape(-1, TILE))
            mapped[:, cols] = three_pass(left, right, ((0,), (0,)))
            return carry

        lax.fori_loop(0, count, strip, 0)
        for copy in mapper_stores():
            copy.start()
        column_pair(0)[0].start()
        column_pair(0)[1].start()
        first_loads[0].wait()
        total = ratio[0] + ratio[1] + ratio[2] + ratio[3]
        scale_sum = jnp.sum(total[0:8], axis=0, keepdims=True)
        shift_sum = jnp.sum(total[8:16], axis=0, keepdims=True)
        odd = lax.rem(lax.broadcasted_iota(jnp.int32, (CHUNK, chan), 0), 2) == 1
        both = jnp.where(odd, shift_sum, scale_sum)
        small[0] = both * embed_ref[:, 0:1]
        sums[4:5] = scale_sum
        sums[5:6] = shift_sum
        sums[6:7] = jnp.sum(wide[...], axis=0, keepdims=True)
        sums[7:8] = jnp.sum(text_all[...].reshape(-1, chan), axis=0, keepdims=True)
        width = chan // 4
        place = pl.ds(pl.multiple_of(me * width, width), width)
        small[1, 3:4, 0:width] = sums[6:7, place]
        small[1, 3:4, width : 2 * width] = sums[7:8, place]
        pair_place = pl.ds(pl.multiple_of(lax.rem(me, 2) * 2 * width, width), 2 * width)
        small[1, 4:5, width : 3 * width] = jnp.where(
            me < 2, sums[4:5, pair_place], sums[5:6, pair_place]
        )

    def column_pair(i):
        return [
            pltpu.make_async_copy(
                response_ref.at[
                    :, pl.ds(pl.multiple_of(c * (chan // 2) + i * 128, 128), 128)
                ],
                columns.at[lax.rem(i, 2), :, pl.ds(c * 128, 128)],
                load.at[6 + lax.rem(i, 2) if c == 0 else 12 + lax.rem(i, 2)],
            )
            for c in (0, 1)
        ]

    def reduce_stores(i):
        return [
            pltpu.make_async_copy(
                product.at[pl.ds(c * 128, 128)],
                reduce_part.at[c, pl.ds(pl.multiple_of(i * 128, 128), 128)],
                load.at[8 + c],
            )
            for c in (0, 1)
        ]

    def reduce_outer(i):
        for copy in column_pair(i):
            copy.wait()

        @pl.when(i + 1 < count)
        def _():
            for copy in column_pair(jnp.minimum(i + 1, count - 1)):
                copy.start()

        @pl.when(i + 1 == count)
        def _():
            weight_load(reduce_w_ref, 0).start()
            act_load(0).start()

        @pl.when(i > 0)
        def _():
            for copy in reduce_stores(jnp.maximum(i - 1, 0)):
                copy.wait()

        @pl.when(i == 0)
        def _():
            for copy in mapper_stores():
                copy.wait()

        left = halves(columns[lax.rem(i, 2), :, 0:TILE])

        def strip(k, carry):
            cols = pl.ds(pl.multiple_of(k * TILE, TILE), TILE)
            product[0:TILE, cols] = three_pass(left, (high[:, cols], low[:, cols]), ((0,), (0,)))
            return carry

        lax.fori_loop(0, count, strip, 0)
        for copy in reduce_stores(i):
            copy.start()

    def settle_reduce(t):
        for copy in reduce_stores(count - 1):
            copy.wait()
        text_kept.wait()
        for copy in loads + out_loads():
            copy.start()
        sums[0:4] = jnp.zeros((4, chan), jnp.float32)

    outward = near_slots(out_own, out_got, send, recv, 3)

    def away(i):
        rows = pl.ds(pl.multiple_of(i * 8, 8), 8)
        return remote(
            base.at[rows], layer_out.at[rows], tile_out.at[i], tile_in.at[i], (core, up, over)
        )

    def here(i):
        rows = pl.ds(pl.multiple_of(i * 8, 8), 8)
        return pltpu.make_async_copy(base.at[rows], layer_out.at[rows], tile_out.at[i])

    first_loads = [pltpu.make_async_copy(small_ref, small, keep.at[1])]
    loads = [
        pltpu.make_async_copy(conv_ref, conv, keep.at[2]),
        pltpu.make_async_copy(base_ref, base, keep.at[4]),
    ]
    kept = pltpu.make_async_copy(one, grad_out, keep.at[5])

    def tile_rows(i):
        return pl.ds(pl.multiple_of(i * TILE, TILE), TILE)

    def weight_load(ref, i):
        return pltpu.make_async_copy(
            ref.at[tile_rows(i)], weights.at[lax.rem(i, 2)], load.at[lax.rem(i, 2)]
        )

    def act_load(i):
        return pltpu.make_async_copy(
            act_ref.at[:, tile_rows(i)], acts.at[lax.rem(i, 2)], load.at[2 + lax.rem(i, 2)]
        )

    def slope_load(i):
        return pltpu.make_async_copy(
            slope_ref.at[:, tile_rows(i)], slopes.at[lax.rem(i, 2)], load.at[4 + lax.rem(i, 2)]
        )

    part = columns.shape[2]

    def column_load(i):
        return pltpu.make_async_copy(
            normed_ref.at[:, pl.ds(pl.multiple_of(i * part, part), part)],
            columns.at[lax.rem(i, 2)],
            load.at[6 + lax.rem(i, 2)],
        )

    def product_stores(i):
        half = part // 2
        return [
            pltpu.make_async_copy(
                product.at[pl.ds(c * half, half)], expand_part.at[i, c], load.at[8 + c]
            )
            for c in (0, 1)
        ]

    def front_sends(i):
        found = []
        for step in (3, 1, 2):
            found.append(
                remote(
                    front.at[lax.rem(i, 2), pl.ds(step * pixels, pixels)],
                    front_got.at[step - 1, :, tile_rows(i)],
                    front_out.at[i, step - 1],
                    front_in.at[i, step - 1],
                    (core, level, near_of(me, step)),
                )
            )
        return found

    for copy in early_loads()[0] + [early_column(0), early_column(1)]:
        copy.start()
    for copy in scatters + start_loads + first_loads:
        copy.start()

    def respond(i):
        weight_load(reduce_w_ref, i).wait()
        act_load(i).wait()

        @pl.when(i + 1 < count)
        def _():
            weight_load(reduce_w_ref, i + 1).start()
            act_load(i + 1).start()

        @pl.when(i + 1 == count)
        def _():
            act_load(0).start()
            slope_load(0).start()

        right = halves(weights[lax.rem(i, 2)])
        cols = tile_rows(i)

        def strip(k, carry):
            rows = pl.ds(pl.multiple_of(k * pixels, pixels), pixels)
            value = three_pass((high[rows], low[rows]), right, ((1,), (1,)))
            wide[rows, cols] = value
            sums[0:1, cols] += jnp.sum(value * acts[lax.rem(i, 2), rows], axis=0, keepdims=True)
            sums[1:2, cols] += jnp.sum(value, axis=0, keepdims=True)
            return carry

        lax.fori_loop(0, 4, strip, 0)

    def spreads():
        return [
            remote(
                spread_own, spread_got.at[step - 1], spread_out.at[step - 1],
                spread_in.at[step - 1], (core, level, near_of(me, step)),
            )
            for step in (3, 1, 2)
        ]

    def out_loads():
        return [
            pltpu.make_async_copy(mixture_ref, columns.at[0], load.at[6]),
            pltpu.make_async_copy(out_w_ref, product, load.at[7]),
        ]

    def out_product(i):
        pl.when(i == 0)(lambda: [copy.wait() for copy in out_loads()] and None)
        rows = pl.ds(pl.multiple_of(i * pixels, pixels), pixels)
        left = halves(columns[0, rows])

        def strip(k, carry):
            cols = pl.ds(pl.multiple_of(k * TILE, TILE), TILE)
            out_own[i, :, cols] = three_pass(left, halves(product[:, cols]), ((1,), (0,)))
            return carry

        lax.fori_loop(0, count, strip, 0)

    def send_out(t):
        for copy in outward:
            copy.start()

    def share(t):
        total = jnp.sum(sums[0:1] * rows_ref[0:1] * rows_ref[1:2], axis=1, keepdims=True)
        spread_own[...] = jnp.broadcast_to(total, spread_own.shape)
        for copy in spreads():
            copy.start()

    def agree(t):
        for copy in spreads():
            copy.wait()
        total = spread_own[...] + spread_got[0] + spread_got[1] + spread_got[2]
        total = jnp.max(total[0:1], axis=1, keepdims=True)
        inverse = rows_ref[3:4]
        norms = rows_ref[1:2]
        grad_norms = (
            sums[0:1] * rows_ref[0:1] * inverse - total * rows_ref[4:5] * inverse * inverse
        )
        sums[2:3] = grad_norms / norms
        small[1, 1:2] = sums[0:1] * rows_ref[5:6]
        small[1, 2:3] = sums[1:2]

    def bend(i):
        act_load(i).wait()
        slope_load(i).wait()

        @pl.when(i + 1 < count)
        def _():
            act_load(i + 1).start()
            slope_load(i + 1).start()

        @pl.when(i + 1 == count)
        def _():
            column_load(0).start()
            weight_load(expand_w_ref, 0).start()

        cols = tile_rows(i)
        factor = rows_ref[2:3, cols]
        twice = sums[2:3, cols]

        def strip(k, carry):
            rows = pl.ds(pl.multiple_of(k * 48, 48), 48)
            value = (
                wide[rows, cols] * factor + acts[lax.rem(i, 2), rows] * twice
            ) * slopes[lax.rem(i, 2), rows]
            high[rows, cols], low[rows, cols] = halves(value)
            sums[3:4, cols] += jnp.sum(value, axis=0, keepdims=True)
            return carry

        lax.fori_loop(0, spots // 48, strip, 0)

    def outer(i):
        column_load(i).wait()
        pl.when(i + 1 < 4)(lambda: column_load(jnp.minimum(i + 1, 3)).start())
        pl.when(i > 0)(lambda: [copy.wait() for copy in product_stores(jnp.maximum(i - 1, 0))] and None)
        left = halves(columns[lax.rem(i, 2)])

        def strip(k, carry):
            cols = pl.ds(pl.multiple_of(k * TILE, TILE), TILE)
            product[:, cols] = three_pass(left, (high[:, cols], low[:, cols]), ((0,), (0,)))
            return carry

        lax.fori_loop(0, count, strip, 0)
        for copy in product_stores(i):
            copy.start()

    def settle_outer(t):
        for copy in product_stores(3):
            copy.wait()
        small[1, 0:1] = sums[3:4]

    def backward(i):
        weight_load(expand_w_ref, i).wait()
        pl.when(i + 1 < count)(lambda: weight_load(expand_w_ref, jnp.minimum(i + 1, count - 1)).start())

        @pl.when(i > 1)
        def _():
            for copy in front_sends(jnp.maximum(i - 2, 0)):
                copy.wait_send()

        right = halves(weights[lax.rem(i, 2)])

        def strip(k, carry):
            rows = pl.ds(pl.multiple_of(k * pixels, pixels), pixels)
            front[lax.rem(i, 2), rows] = three_pass((high[rows], low[rows]), right, ((1,), (1,)))
            return carry

        lax.fori_loop(0, 4, strip, 0)
        front_own[:, tile_rows(i)] = front[lax.rem(i, 2), 0:pixels]
        for copy in front_sends(i):
            copy.start()

    def middle(t):
        loads[0].wait()
        for i in range(count):
            for copy in front_sends(i):
                copy.wait_recv()
                if i >= count - 2:
                    copy.wait_send()

    def tiles(t):
        def tile(i, carry):
            rows = pl.ds(pl.multiple_of(i * 8, 8), 8)
            back = front_own[rows] + front_got[0, rows] + front_got[1, rows] + front_got[2, rows]
            normed, inverse = row_stats(conv[rows])
            one[rows] = inverse * (
                back
                - jnp.mean(back, axis=-1, keepdims=True)
                - normed * jnp.mean(back * normed, axis=-1, keepdims=True)
            )
            return carry

        size = pixels // 48
        lax.fori_loop(t * size, (t + 1) * size, tile, 0)

    def give(t):
        kept.start()

    def outlet(t):
        pl.when(t == 0)(lambda: [copy.wait() for copy in loads[1:] + outward] and None)
        rows = pl.ds(pl.multiple_of(t * 8, 8), 8)
        base[rows] += out_own[0, rows] + out_got[0, rows] + out_got[1, rows] + out_got[2, rows]
        pl.when(moves)(away(t).start)
        pl.when(jnp.logical_not(moves))(here(t).start)

    sum_stream(
        [
            ("plain", output_ref, output_out),
            ("swap", attend_part, attend_out),
            ("plain", mapper_part, mapper_out),
            ("plain", reduce_part, reduce_out),
            ("plain", small, small_out),
            ("swap", expand_part, expand_out),
        ],
        scratch[:SCRATCH],
        [
            (0, 1, prepare),
            (1, 5, attend_outer),
            (5, 6, settle_attend),
            (12, 13, arrive),
            (12, 21, normalize),
            (21, 22, give_late),
            (24, 25, gathered),
            (25, 26, text_products),
            (26, 32, reduce_outer),
            (32, 33, settle_reduce),
            (33, 39, respond),
            (39, 40, share),
            (40, 41, agree),
            (41, 47, bend),
            (47, 51, outer),
            (51, 52, settle_outer),
            (52, 58, backward),
            (68, 69, middle),
            (68, 74, tiles),
            (74, 75, give),
            (60, 78, outlet),
            (39, 43, out_product),
            (43, 44, send_out),
        ],
    )
    kept.wait()

    def settle(i, carry):
        pl.when(moves)(away(i).wait)
        pl.when(jnp.logical_not(moves))(here(i).wait)
        return carry

    lax.fori_loop(0, base.shape[0] // 8, settle, 0)


def backward_sums(
    collective, output_part, qkv, two_share, text_share, cot, one, response, reduce_w, act, slope,
    normed_all, expand_w, conv, mixture, out_w, base, small, normed_two, rows, embed, silu,
    mapped, text_kv, mapper_half
):
    pixels, chan = conv.shape
    spots = normed_all.shape[0]
    texts = text_share.shape[1]
    slots = silu.shape[0] // 4
    f32, bf16 = jnp.float32, jnp.bfloat16
    half = chan // 8
    count = chan // TILE

    def shape(*dims):
        return jax.ShapeDtypeStruct(dims, f32)

    total = (half + 8 * half // 2 + mapper_half + chan // 2 + CHUNK + 8 * half // 2) // CHUNK
    block = (pixels, chan)
    return pl.pallas_call(
        backward_body,
        out_shape=[
            shape(2, half, chan),
            shape(2, half, 3 * chan),
            shape(2, mapper_half, chan),
            shape(2, chan // 2, chan),
            shape(2, CHUNK, chan),
            shape(2, half, 4 * chan),
            shape(4, 2, half, 3 * chan // 4),
            shape(2, mapper_half, chan),
            shape(2, chan // 2, chan),
            shape(4, 2, half, chan),
            shape(*block),
            shape(4, slots, chan),
            shape(*block),
            shape(*block),
        ],
        in_specs=[ANY] * 18 + [pl.BlockSpec(memory_space=pltpu.VMEM)] * 5,
        out_specs=[ANY] * 14,
        scratch_shapes=stream_scratch(total, 4 * half // CHUNK, chan)
        + [
            pltpu.VMEM((3,) + block, f32),
            pltpu.VMEM(block, f32),
            pltpu.VMEM(block, f32),
            pltpu.VMEM(block, f32),
            pltpu.VMEM(block, f32),
            pltpu.VMEM((3,) + block, f32),
            pltpu.VMEM((4,) + block, f32),
            pltpu.VMEM(block, f32),
            pltpu.VMEM(small.shape, f32),
            pltpu.VMEM((spots, chan), f32),
            pltpu.VMEM((spots, chan), bf16),
            pltpu.VMEM((spots, chan), bf16),
            pltpu.VMEM((2, TILE, chan), f32),
            pltpu.VMEM((2, spots, TILE), f32),
            pltpu.VMEM((2, spots, TILE), f32),
            pltpu.VMEM((2, spots, chan // 4), f32),
            pltpu.VMEM((chan // 4, chan), f32),
            pltpu.VMEM((2, spots, TILE), f32),
            pltpu.VMEM((8, chan), f32),
            pltpu.VMEM((8, 128), f32),
            pltpu.VMEM((3, 8, 128), f32),
            pltpu.VMEM((3, texts, chan), f32),
            pltpu.VMEM((texts, chan), f32),
            pltpu.VMEM((4, slots, chan), f32),
            pltpu.VMEM((4, 16, chan), f32),
            pltpu.VMEM((silu.shape[1], chan), f32),
            DMA((9,)),
            DMA((9,)),
            DMA((12,)),
            DMA((pixels // 8,)),
            DMA((pixels // 8,)),
            DMA((14,)),
            DMA((count, 3)),
            DMA((count, 3)),
            DMA((3,)),
            DMA((3,)),
            DMA((pixels // 16, 3)),
            DMA((pixels // 16, 3)),
            DMA((6,)),
            DMA((6,)),
        ],
        compiler_params=pltpu.CompilerParams(
            collective_id=collective, has_side_effects=True, vmem_limit_bytes=62 * 2**20
        ),
        name="backward_sums",
    )(
        output_part, qkv, two_share, text_share, cot, one, response, reduce_w, act, slope,
        normed_all, expand_w, conv, mixture, out_w, base, small, normed_two, rows, embed, silu,
        mapped, text_kv,
    )


def close_body(
    grad_in, token_in, conv_in, up_in, down_in,
    grad_home, token_home, conv_all, below, above,
    hold, send, recv, keep
):
    core = lax.axis_index("cond")
    level = lax.axis_index("pair")
    me = lax.axis_index("dp")
    up, over = home_spot(level, me)
    back_up, back_over = plane_spot(level, me)
    moves = jnp.logical_or(level != 0, me != 0)
    others = [(c, s) for c in (0, 1) for s in (0, 1, 2, 3) if (c, s) != (0, 0)]

    def other(c, s):
        return (lax.rem(core + c, 2), lax.rem(level + s, 4), me)

    for c, s in others:
        greet(other(c, s))
    pl.when(moves)(lambda: greet((core, back_up, back_over)))
    turned = jnp.logical_and(level == 1, me == 1)
    quarter = up
    lifts = quarter > 0
    drops = jnp.logical_and(quarter < 3, jnp.logical_not(turned))
    lifted = level < 3
    dropped = jnp.logical_and(level > 0, jnp.logical_not(turned))
    pl.when(lifted)(lambda: greet((core, me, near_of(me, rev(jnp.minimum(level + 1, 3))))))
    pl.when(dropped)(lambda: greet((core, me, near_of(me, rev(jnp.maximum(level - 1, 0))))))
    pl.semaphore_wait(
        pltpu.get_barrier_semaphore(),
        7 + jnp.where(moves, 1, 0) + jnp.where(lifts, 1, 0) + jnp.where(drops, 1, 0),
    )
    lift = remote(up_in, below, send.at[9], recv.at[9], (core, jnp.maximum(quarter - 1, 0), level))
    drop = remote(down_in, above, send.at[10], recv.at[10], (core, jnp.minimum(quarter + 1, 3), level))
    around = pltpu.make_async_copy(down_in, above, keep.at[3])
    pl.when(lifts)(lift.start)
    pl.when(drops)(drop.start)
    pl.when(turned)(around.start)
    swaps = ((grad_in, grad_home), (token_in, token_home))
    aways = [remote(src, dst, send.at[i], recv.at[i], (core, up, over)) for i, (src, dst) in enumerate(swaps)]
    spreads = [
        remote(conv_in, conv_all.at[1 + i], send.at[2 + i], recv.at[2 + i], other(c, s))
        for i, (c, s) in enumerate(others)
    ]
    mine = pltpu.make_async_copy(conv_in, conv_all.at[0], keep.at[2])
    for copy in spreads + [mine]:
        copy.start()
    for away in aways:
        pl.when(moves)(away.start)

    @pl.when(jnp.logical_not(moves))
    def _():
        load = pltpu.make_async_copy(grad_in, hold, keep.at[0])
        store = pltpu.make_async_copy(hold, grad_home, keep.at[0])
        small = pltpu.make_async_copy(token_in, token_home, keep.at[1])
        small.start()
        load.start()
        load.wait()
        store.start()
        store.wait()
        small.wait()

    for copy in spreads + [mine]:
        copy.wait()
    for away in aways:
        pl.when(moves)(away.wait)
    pl.when(lifts)(lift.wait_send)
    pl.when(drops)(drop.wait_send)
    pl.when(lifted)(lift.wait_recv)
    pl.when(dropped)(drop.wait_recv)
    pl.when(turned)(around.wait)


def close_exchange(collective, grad, tokens, conv, up, down):
    shapes = [grad.shape, tokens.shape, (8,) + conv.shape, up.shape, down.shape]
    return pl.pallas_call(
        close_body,
        out_shape=[jax.ShapeDtypeStruct(shape, jnp.float32) for shape in shapes],
        in_specs=[ANY] * 5,
        out_specs=[ANY] * 5,
        scratch_shapes=[pltpu.VMEM(grad.shape, jnp.float32), DMA((11,)), DMA((11,)), DMA((4,))],
        compiler_params=pltpu.CompilerParams(collective_id=collective, has_side_effects=True),
        name="close_exchange",
    )(grad, tokens, conv, up, down)


def plane_body(
    latents,
    ratio_embed,
    clip_tokens,
    cotangent,
    conv_kernel,
    conv_bias,
    expand_weight,
    expand_bias,
    response_gain,
    response_bias,
    reduce_weight,
    reduce_bias,
    ratio_weight,
    ratio_bias,
    text_weight,
    text_bias,
    attend_weight,
    query_bias,
    value_bias,
    output_weight,
    output_bias,
):
    size = lax.axis_size("dp")
    core = lax.axis_index("cond")
    me = lax.axis_index("dp")
    level = lax.axis_index("pair")
    quarter = home_spot(level, me)[0]
    order = jnp.bitwise_xor(jnp.arange(4), me)
    _, rows, cols, chan = latents.shape
    pixels = rows * cols
    part = chan // size
    hid = size * expand_bias.shape[0]
    texts = clip_tokens.shape[1]
    packed = jnp.concatenate(
        [
            conv_kernel.reshape(9, part),
            conv_bias[None],
            reduce_bias[None],
            text_bias[None],
            output_bias[None],
            ratio_bias.reshape(2, part),
        ],
        axis=0,
    )
    row_padded, every, tokens, embed, expand_w, attend_units = open_exchange(
        3, latents[0], packed, clip_tokens[0], ratio_embed, expand_weight, attend_weight
    )[:6]
    row_padded = row_padded.at[:1].set(jnp.where(quarter > 0, row_padded[:1], 0.0))
    row_padded = row_padded.at[-1:].set(jnp.where(quarter < size - 1, row_padded[-1:], 0.0))
    image = row_padded[1:-1]
    expand_w = expand_w.reshape(chan, -1)
    channel_rows = every[:, :13].transpose(1, 0, 2).reshape(13, chan)
    kernel = channel_rows[:9].reshape(3, 3, chan)
    conv_shift, reduce_b, text_b, out_b = (channel_rows[9 + i] for i in range(4))
    ratio_b = every[:, 13:].reshape(2 * chan)

    half = part // 2
    wide = hid // size
    text_part = text_weight.shape[0]
    token_cols = [
        lax.dynamic_slice(tokens, (0, near_of(me, step) * text_part), (texts, text_part))
        for step in range(4)
    ]
    ratio_part = ratio_weight.shape[0]
    embed_part = lax.dynamic_slice(embed, (0, me * ratio_part), (1, ratio_part))
    mod_part = jnp.dot(embed_part, ratio_weight, precision=HIGHEST_ACCURACY)

    padded = jnp.pad(row_padded, ((0, 0), (1, 1), (0, 0)))
    total_conv = conv_shift
    for i in range(3):
        for j in range(3):
            total_conv = total_conv + padded[i : i + rows, j : j + cols] * kernel[i, j]
    normed, inverse = norm_stats(total_conv.reshape(pixels, chan))
    normed_all, mod_near, near_tokens, attend_w = exchange(
        4,
        gathers=(normed, mod_part),
        scatters=(jnp.stack(token_cols),),
        relay=(attend_units,),
    )
    attend_w = attend_w.reshape(chan, 3 * part)
    modulation = jnp.sum(mod_near[:, 0], axis=0) + ratio_b
    mod_scale = 1.0 + modulation[:chan]
    mod_shift = modulation[chan:]
    normed_all = normed_all.reshape(size * pixels, chan)
    cot, normed_all = lax.optimization_barrier((cotangent[0].reshape(pixels, chan), normed_all))
    turns = (0, 2, 1, 3)
    grid = [(z, d) for z in range(size) for d in range(size)]
    cot = lax.ppermute(
        cot, ("pair", "dp"), [(z * size + d, z * size + (d ^ turns[z])) for z, d in grid]
    )
    near_tokens = jnp.concatenate([token_cols[0], near_tokens.reshape(-1, text_part)], axis=0)
    silu_near = jax.nn.silu(near_tokens)
    mapped_share = dot(silu_near, text_weight).reshape(4, texts, chan)
    hidden = dot(normed_all, expand_w) + expand_bias
    bell = 0.5 * (1.0 + lax.erf(hidden * 0.5**0.5))
    activated = hidden * bell
    density = jnp.exp(-0.5 * hidden * hidden) * (2.0 * jnp.pi) ** -0.5
    slope = bell + hidden * density
    totals = jnp.sum(activated * activated, axis=0)
    norms = jnp.sqrt(totals + EPSILON)
    norm_sums = exchange(5, gathers=(jnp.full((8, 128), jnp.sum(norms)),))[0]
    middle = jnp.sum(norm_sums[:, 0, 0]) / hid + EPSILON
    scaled = norms / middle
    factor = 1.0 + response_gain * scaled
    response = activated * factor + response_bias
    one_share = dot(response, reduce_weight).reshape(4, pixels, chan)
    cot, one_share = lax.optimization_barrier((cot, one_share))
    cot = lax.ppermute(
        cot, ("pair", "dp"), [(z * size + d, (d ^ turns[z]) * size + d) for z, d in grid]
    )
    one_arrived, mapped_arrived = exchange(6, scatters=(one_share, mapped_share))
    mapped = mapped_share[0] + jnp.sum(mapped_arrived, axis=0) + text_b
    hidden_one = one_share[0] + jnp.sum(one_arrived, axis=0) + image.reshape(pixels, chan) + reduce_b
    hidden_two = hidden_one * mod_scale + mod_shift
    normed_two, inverse_two = norm_stats(hidden_two)
    cot, normed_two = lax.optimization_barrier((cot, normed_two))
    normed_two_all, mapped_all = exchange(7, gathers=(normed_two, mapped))
    cot, normed_two_all = lax.optimization_barrier((cot, normed_two_all))
    cot_all = jnp.concatenate(
        [cot]
        + [lax.ppermute(cot, "dp", [(i, i ^ step) for i in range(size)]) for step in (1, 2, 3)],
        axis=0,
    )
    normed_two_all = normed_two_all.reshape(size * pixels, chan)
    mapped_all = mapped_all.reshape(size * texts, chan)

    source = jnp.concatenate([normed_two_all, mapped_all], axis=0)
    query = dot(normed_two_all, attend_w[:, :part]) + query_bias
    key_value = dot(source, attend_w[:, part:])
    key = key_value[:, :part]
    value = key_value[:, part:] + value_bias
    query_h, key_h, value_h = heads_of(query), heads_of(key), heads_of(value)
    scores = jnp.einsum("iuy,ouy->uio", query_h, key_h, precision=FAST) * HEAD_CHANNELS ** (-0.5)
    expo = jnp.exp(scores - jnp.max(scores, axis=-1, keepdims=True))
    probs = expo / jnp.sum(expo, axis=-1, keepdims=True)
    mixture_h = jnp.einsum("uio,ouy->iuy", probs, value_h, precision=FAST)
    mixture = mixture_h.reshape(query.shape)
    out_base = hidden_two + out_b

    output_grad = t_dot(mixture, cot_all)
    grad_mix_h = heads_of(dot_t(cot_all, output_weight))
    grad_probs = jnp.einsum("iuy,ouy->uio", grad_mix_h, value_h, precision=FAST)
    delta = jnp.sum(grad_mix_h * mixture_h, axis=-1).T
    grad_scores = probs * (grad_probs - delta[..., None]) * HEAD_CHANNELS ** (-0.5)
    grad_query = jnp.einsum("uio,ouy->iuy", grad_scores, key_h, precision=FAST).reshape(query.shape)
    grad_key = jnp.einsum("uio,iuy->ouy", grad_scores, query_h, precision=FAST).reshape(key.shape)
    grad_value = jnp.einsum("uio,iuy->ouy", probs, grad_mix_h, precision=FAST).reshape(key.shape)
    spots = size * pixels
    grad_kv = jnp.concatenate([grad_key, grad_value], axis=1)
    grad_qkv = jnp.concatenate([grad_query, grad_kv[:spots]], axis=1)
    two_share = dot_t(grad_qkv, attend_w).reshape(4, pixels, chan)
    text_share = dot_t(grad_kv[spots:], attend_w[:, part:]).reshape(4, texts, chan)
    def row(value):
        return jnp.sum(value, axis=0, keepdims=True)

    def mine(value):
        width = value.shape[1] // size
        return lax.dynamic_slice(value, (0, me * width), (value.shape[0], width))

    gap = jnp.zeros((1, part), jnp.float32)
    small_rows = jnp.concatenate(
        [
            jnp.zeros((3, chan), jnp.float32),
            jnp.concatenate([gap, gap, row(grad_query), row(grad_value)], axis=1),
            jnp.concatenate([row(mine(cot_all)), gap, gap, gap], axis=1),
            jnp.zeros((CHUNK - 5, chan), jnp.float32),
        ],
        axis=0,
    )
    one_row = jnp.full((1, chan), 1.0, jnp.float32)
    back_rows = jnp.concatenate(
        [
            response_gain[None],
            norms[None],
            factor[None],
            one_row / middle,
            one_row / hid,
            scaled[None],
            mod_scale[None],
            mod_shift[None],
        ],
        axis=0,
    )
    slots = (texts + 7) // 8 * 8

    def padded_rows(value):
        value = value.reshape(4, texts, -1)
        return jnp.pad(value, ((0, 0), (0, slots - texts), (0, 0))).reshape(4 * slots, -1)

    silu_padded = jnp.pad(
        silu_near.reshape(4, texts, text_part), ((0, 0), (0, slots - texts), (0, -text_part % 128))
    ).reshape(4 * slots, -1)
    embed_rows = jnp.broadcast_to(
        embed_part.reshape(ratio_part, 1, 1), (ratio_part, 2, 128)
    ).reshape(2 * ratio_part, 128)
    (
        output_sum, attend_sum, mapper_sum, reduce_sum, small, expand_sum, _, _, _, _,
        grad_one, grad_mapped_all, grad_conv, layer_output,
    ) = backward_sums(
        1,
        output_grad.reshape(2, half, chan),
        grad_qkv,
        two_share,
        text_share,
        cot,
        hidden_one,
        response,
        reduce_weight,
        activated,
        slope,
        normed_all,
        expand_w,
        total_conv.reshape(pixels, chan),
        mixture,
        output_weight,
        out_base,
        jnp.stack([jnp.zeros((CHUNK, chan), jnp.float32), small_rows]),
        normed_two_all,
        back_rows,
        embed_rows,
        silu_padded,
        padded_rows(mapped_all),
        padded_rows(grad_kv[spots:]),
        text_part // 2,
    )
    output_sum = output_sum.reshape(part, chan)
    attend_sum = attend_sum.reshape(part, 3 * chan)
    mapper_sum = mapper_sum.reshape(text_part, chan)
    reduce_sum = reduce_sum.reshape(wide, chan)
    expand_sum = expand_sum.reshape(part, hid)
    layer_output = layer_output.reshape(latents.shape)
    grad_mapped_all = grad_mapped_all[:, :texts].reshape(size * texts, chan)
    gate = 1.0 / (1.0 + jnp.exp(-near_tokens))
    tokens_near = dot_t(grad_mapped_all, text_weight) * (
        gate * (1.0 + near_tokens * (1.0 - gate))
    )
    tokens_near = tokens_near.reshape(4, texts, text_part)
    grad_conv = grad_conv.reshape(rows, cols, chan)
    kernel_grad = jnp.stack(
        [
            jnp.sum(padded[i : i + rows, j : j + cols] * grad_conv, axis=(0, 1))
            for i in range(3)
            for j in range(3)
        ]
    )
    spread_conv = jnp.pad(grad_conv, ((2, 2), (1, 1), (0, 0)))
    latent_rows = jnp.zeros((rows + 2, cols, chan), jnp.float32)
    for i in range(3):
        for j in range(3):
            latent_rows = (
                latent_rows
                + spread_conv[2 - i : 2 - i + rows + 2, 2 - j : 2 - j + cols] * kernel[i, j]
            )
    conv_part = jnp.concatenate([kernel_grad, jnp.sum(grad_conv, axis=(0, 1))[None]], axis=0)
    conv_blocks = jnp.stack(
        [
            lax.dynamic_slice(conv_part, (0, near_of(me, step) * part), (10, part))
            for step in range(4)
        ]
    )
    conv_arrived, token_arrived = exchange(13, scatters=(conv_blocks, tokens_near))
    token_blocks = jnp.take(
        jnp.concatenate([tokens_near[:1], token_arrived], axis=0), order, axis=0
    )
    inner = latent_rows[1:-1] + grad_one.reshape(rows, cols, chan)
    latent_grad, tokens_grad, conv_all, from_below, from_above = close_exchange(
        14,
        inner.reshape(pixels, chan),
        token_blocks.transpose(1, 0, 2).reshape(texts, size * text_part),
        conv_blocks[0] + jnp.sum(conv_arrived, axis=0),
        latent_rows[0],
        latent_rows[-1],
    )
    from_above = jnp.where(level > 0, from_above, 0.0)[None]
    from_below = jnp.where(level < size - 1, from_below, 0.0)[None]
    still = jnp.zeros((rows - 2, cols, chan), jnp.float32)
    latent_grad = latent_grad.reshape(rows, cols, chan) + jnp.concatenate(
        [from_above, still, from_below], axis=0
    )
    latent_grad = latent_grad[None]
    tokens_grad = tokens_grad[None]
    conv_mine = jnp.sum(conv_all, axis=0)
    ratio = small[0]
    expb, gain, respb = (small[1, i] for i in range(3))
    redb, mapb, queryb, valueb = (small[1, 3, i * part : (i + 1) * part] for i in range(4))
    outb = small[1, 4, :part]
    ratiob = small[1, 4, part : 3 * part]
    return (
        layer_output,
        latent_grad,
        tokens_grad,
        conv_mine[:9].reshape(3, 3, part),
        conv_mine[9],
        expand_sum,
        expb,
        gain,
        respb,
        reduce_sum,
        redb,
        ratio.reshape(ratio_part, 2 * chan),
        ratiob,
        mapper_sum,
        mapb,
        attend_sum,
        queryb,
        valueb,
        output_sum,
        outb,
    )


def solution(mesh):
    square = mesh.shape["cond"] == 2 and mesh.shape["pair"] == 4 and mesh.shape["dp"] == 4
    return jax.shard_map(
        plane_body if square else body,
        mesh=mesh,
        in_specs=(
            P(("cond", "dp"), "pair", None, None),
            P(("cond", "dp"), None),
            P(("cond", "dp"), "pair", None),
            P(("cond", "dp"), "pair", None, None),
            P(None, None, "dp"),
            P("dp"),
            P("dp", None),
            P("dp"),
            P("dp"),
            P("dp"),
            P("dp", None),
            P("dp"),
            P("dp", None),
            P("dp"),
            P("dp", None),
            P("dp"),
            P("dp", None),
            P("dp"),
            P("dp"),
            P("dp", None),
            P("dp"),
        ),
        out_specs=(
            P(("cond", "dp"), "pair", None, None),
            P(("cond", "dp"), "pair", None, None),
            P(("cond", "dp"), "pair", None),
            P(None, None, "dp"),
            P("dp"),
            P("dp", None),
            P("dp"),
            P("dp"),
            P("dp"),
            P("dp", None),
            P("dp"),
            P("dp", None),
            P("dp"),
            P("dp", None),
            P("dp"),
            P("dp", None),
            P("dp"),
            P("dp"),
            P("dp", None),
            P("dp"),
        ),
        check_vma=False,
    )
```

```python
import functools

import jax
import jax.numpy as jnp
from jax import lax
from jax.experimental import pallas as pl
from jax.experimental.pallas import tpu as pltpu
from jax.sharding import PartitionSpec as P

HEADS = 24
HEAD_CHANNELS = 64


HIGHEST_ACCURACY = lax.Precision.HIGHEST
EPSILON = 1e-06


def extended(block, sides, width):
    for axis, dim in sides:
        count = lax.axis_size(axis)
        forward = [(i, i + 1) for i in range(count - 1)]
        backward = [(target, source) for source, target in forward]
        low = lax.ppermute(
            lax.slice_in_dim(block, block.shape[dim] - width, None, axis=dim), axis, forward
        )
        high = lax.ppermute(lax.slice_in_dim(block, 0, width, axis=dim), axis, backward)
        block = jnp.concatenate([low, block, high], axis=dim)
    return block


def layer_norm(values):
    centered = values - jnp.mean(values, axis=-1, keepdims=True)
    variance = jnp.mean(centered * centered, axis=-1, keepdims=True)
    return centered * lax.rsqrt(variance + EPSILON)


def matmul(left, right):
    return jnp.einsum("...k,kn->...n", left, right, precision=HIGHEST_ACCURACY)


def depthwise(row_padded, kernel, conv_shift):
    row_count = row_padded.shape[1] - 2
    col_count = row_padded.shape[2]
    padded = jnp.pad(row_padded, ((0, 0), (0, 0), (1, 1), (0, 0)))
    total_conv = conv_shift
    for row_off in range(3):
        for col_off in range(3):
            total_conv = (
                total_conv
                + padded[:, row_off : row_off + row_count, col_off : col_off + col_count, :]
                * kernel[row_off, col_off]
            )
    return total_conv


def front(row_padded, kernel, conv_shift, expand_w, expand_b):
    normed = layer_norm(depthwise(row_padded, kernel, conv_shift))
    flat = normed.reshape(normed.shape[0], normed.shape[1] * normed.shape[2], normed.shape[3])
    return jax.nn.gelu(matmul(flat, expand_w) + expand_b, approximate=False)


def response_mlp(activated, totals, resp_gain, resp_bias, reduce_w, reduce_b, residual):
    norms = jnp.sqrt(totals + EPSILON)
    scaled = norms / (jnp.mean(norms, axis=-1, keepdims=True) + EPSILON)
    response = resp_gain * (activated * scaled[:, None, :]) + resp_bias + activated
    return residual + matmul(response, reduce_w) + reduce_b


def modulate(hidden_one, ratio_w, ratio_b, embed):
    modulation = jnp.dot(embed, ratio_w, precision=HIGHEST_ACCURACY) + ratio_b
    chan_count = hidden_one.shape[-1]
    return hidden_one * (1.0 + modulation[:, None, :chan_count]) + modulation[:, None, chan_count:]


def project(hidden_two, tokens, map_w, map_b, attend_w, query_b, value_b):
    chan_count = hidden_two.shape[-1]
    normed = layer_norm(hidden_two)
    mapped = matmul(jax.nn.silu(tokens), map_w) + map_b
    source = jnp.concatenate([normed, mapped], axis=1)
    query_matrix = matmul(normed, attend_w[:, :chan_count]) + query_b
    key_value = matmul(source, attend_w[:, chan_count:])
    return (query_matrix, key_value[..., :chan_count], key_value[..., chan_count:] + value_b)


def divide_into_heads(values):
    return values.reshape(values.shape[:-1] + (HEADS, HEAD_CHANNELS))


def attend_single(triple):
    query_matrix, key_matrix, value_matrix = triple
    attention_scores = jnp.einsum(
        "iuy,ouy->uio",
        divide_into_heads(query_matrix),
        divide_into_heads(key_matrix),
        precision=HIGHEST_ACCURACY,
    ) * HEAD_CHANNELS ** (-0.5)
    top_score = jnp.max(attention_scores, axis=-1, keepdims=True)
    expo_terms = jnp.exp(attention_scores - top_score)
    expo_total = jnp.sum(expo_terms, axis=-1, keepdims=True)
    attention_probabilities = expo_terms / expo_total
    attended_output = jnp.einsum(
        "fvb,bfq->vfq",
        attention_probabilities,
        divide_into_heads(value_matrix),
        precision=HIGHEST_ACCURACY,
    )
    log_total = top_score + jnp.log(expo_total)
    return (attended_output.reshape(query_matrix.shape), log_total)


def attend_back_single(items):
    query_matrix, key_matrix, value_matrix, attended_output, log_total, grad_mix = items
    query_per_head = divide_into_heads(query_matrix)
    key_per_head = divide_into_heads(key_matrix)
    value_per_head = divide_into_heads(value_matrix)
    gradient_per_head = divide_into_heads(grad_mix)
    attention_scores = jnp.einsum(
        "iuy,ouy->uio", query_per_head, key_per_head, precision=HIGHEST_ACCURACY
    ) * HEAD_CHANNELS ** (-0.5)
    attention_probabilities = jnp.exp(attention_scores - log_total)
    probability_gradient = jnp.einsum(
        "iuy,ouy->uio", gradient_per_head, value_per_head, precision=HIGHEST_ACCURACY
    )
    delta_rows = jnp.einsum(
        "phd,phd->hp",
        gradient_per_head,
        divide_into_heads(attended_output),
        precision=HIGHEST_ACCURACY,
    )
    score_gradient = (
        attention_probabilities
        * (probability_gradient - delta_rows[..., None])
        * HEAD_CHANNELS ** (-0.5)
    )
    query_gradient = jnp.einsum(
        "fvb,bfq->vfq", score_gradient, key_per_head, precision=HIGHEST_ACCURACY
    )
    key_gradient = jnp.einsum(
        "gyu,ygx->ugx", score_gradient, query_per_head, precision=HIGHEST_ACCURACY
    )
    value_gradient = jnp.einsum(
        "gyu,ygx->ugx", attention_probabilities, gradient_per_head, precision=HIGHEST_ACCURACY
    )
    return (
        query_gradient.reshape(query_matrix.shape),
        key_gradient.reshape(key_matrix.shape),
        value_gradient.reshape(value_matrix.shape),
    )


def body(
    latents,
    ratio_embed,
    clip_tokens,
    cotangent,
    conv_kernel,
    conv_bias,
    expand_weight,
    expand_bias,
    response_gain,
    response_bias,
    reduce_weight,
    reduce_bias,
    ratio_weight,
    ratio_bias,
    text_weight,
    text_bias,
    attend_weight,
    query_bias,
    value_bias,
    output_weight,
    output_bias,
):
    gathered = (
        lax.all_gather(conv_kernel, "dp", axis=2, tiled=True),
        lax.all_gather(conv_bias, "dp", axis=0, tiled=True),
        lax.all_gather(expand_weight, "dp", axis=0, tiled=True),
        lax.all_gather(expand_bias, "dp", axis=0, tiled=True),
        lax.all_gather(response_gain, "dp", axis=0, tiled=True),
        lax.all_gather(response_bias, "dp", axis=0, tiled=True),
        lax.all_gather(reduce_weight, "dp", axis=0, tiled=True),
        lax.all_gather(reduce_bias, "dp", axis=0, tiled=True),
        lax.all_gather(ratio_weight, "dp", axis=0, tiled=True),
        lax.all_gather(ratio_bias, "dp", axis=0, tiled=True),
        lax.all_gather(text_weight, "dp", axis=0, tiled=True),
        lax.all_gather(text_bias, "dp", axis=0, tiled=True),
        lax.all_gather(attend_weight, "dp", axis=0, tiled=True),
        lax.all_gather(query_bias, "dp", axis=0, tiled=True),
        lax.all_gather(value_bias, "dp", axis=0, tiled=True),
        lax.all_gather(output_weight, "dp", axis=0, tiled=True),
        lax.all_gather(output_bias, "dp", axis=0, tiled=True),
    )
    (
        kernel,
        conv_shift,
        expand_w,
        expand_b,
        resp_gain,
        resp_bias,
        reduce_w,
        reduce_b,
        ratio_w,
        ratio_b,
        map_w,
        map_b,
        attend_w,
        query_b,
        value_b,
        out_w,
        out_b,
    ) = gathered
    lat_count, row_count, col_count, chan_count = latents.shape
    pixel_count = row_count * col_count
    row_padded = extended(latents, (("pair", 1),), 1)
    activated, front_pull = jax.vjp(front, row_padded, kernel, conv_shift, expand_w, expand_b)
    totals = lax.psum(jnp.sum(activated * activated, axis=1), "pair")
    residual = latents.reshape(lat_count, pixel_count, chan_count)
    hidden_one, mlp_pull = jax.vjp(
        response_mlp, activated, totals, resp_gain, resp_bias, reduce_w, reduce_b, residual
    )
    hidden_two, mod_pull = jax.vjp(
        functools.partial(modulate, embed=ratio_embed), hidden_one, ratio_w, ratio_b
    )
    (query_matrix, key_local, value_local), proj_pull = jax.vjp(
        project, hidden_two, clip_tokens, map_w, map_b, attend_w, query_b, value_b
    )
    key_matrix, value_matrix = (
        lax.all_gather(key_local, "pair", axis=1, tiled=True),
        lax.all_gather(value_local, "pair", axis=1, tiled=True),
    )
    attended_output, log_total = lax.map(attend_single, (query_matrix, key_matrix, value_matrix))
    result = hidden_two + matmul(attended_output, out_w) + out_b
    layer_output = result.reshape(latents.shape)
    grad_out = cotangent.reshape(lat_count, pixel_count, chan_count)
    out_w_grad = jnp.einsum("lpc,lpn->cn", attended_output, grad_out, precision=HIGHEST_ACCURACY)
    out_b_grad = jnp.sum(grad_out, axis=(0, 1))
    grad_mix = jnp.einsum("lpn,cn->lpc", grad_out, out_w, precision=HIGHEST_ACCURACY)
    query_gradient, key_gradient, value_gradient = lax.map(
        attend_back_single,
        (query_matrix, key_matrix, value_matrix, attended_output, log_total, grad_mix),
    )
    key_share, value_share = (
        lax.psum_scatter(key_gradient, "pair", scatter_dimension=1, tiled=True),
        lax.psum_scatter(value_gradient, "pair", scatter_dimension=1, tiled=True),
    )
    grad_two, tokens_grad, map_w_grad, map_b_grad, attend_w_grad, query_b_grad, value_b_grad = (
        proj_pull((query_gradient, key_share, value_share))
    )
    grad_two = grad_two + grad_out
    attend_shards = (
        lax.psum_scatter(map_w_grad, "dp", scatter_dimension=0, tiled=True),
        lax.psum_scatter(map_b_grad, "dp", scatter_dimension=0, tiled=True),
        lax.psum_scatter(attend_w_grad, "dp", scatter_dimension=0, tiled=True),
        lax.psum_scatter(query_b_grad, "dp", scatter_dimension=0, tiled=True),
        lax.psum_scatter(value_b_grad, "dp", scatter_dimension=0, tiled=True),
        lax.psum_scatter(out_w_grad, "dp", scatter_dimension=0, tiled=True),
        lax.psum_scatter(out_b_grad, "dp", scatter_dimension=0, tiled=True),
    )
    grad_one, ratio_w_grad, ratio_b_grad = mod_pull(grad_two)
    grad_act, grad_totals, gain_grad, respb_grad, reduce_w_grad, reduce_b_grad, grad_res = mlp_pull(
        grad_one
    )
    grad_totals = lax.psum(grad_totals, "pair")
    grad_act = grad_act + 2.0 * activated * grad_totals[:, None, :]
    grad_padded, kernel_grad, shift_grad, expand_w_grad, expand_b_grad = front_pull(grad_act)
    rim_rows = jnp.concatenate([grad_padded[:, :1], grad_padded[:, -1:]], axis=1)
    arrived = extended(rim_rows, (("pair", 1),), 1)
    inner_rows = grad_padded[:, 1:-1]
    inner_rows = inner_rows.at[:, 0].add(arrived[:, 0]).at[:, -1].add(arrived[:, 3])
    latent_grad = inner_rows + grad_res.reshape(latents.shape)
    block_shards = (
        lax.psum_scatter(kernel_grad, "dp", scatter_dimension=2, tiled=True),
        lax.psum_scatter(shift_grad, "dp", scatter_dimension=0, tiled=True),
        lax.psum_scatter(expand_w_grad, "dp", scatter_dimension=0, tiled=True),
        lax.psum_scatter(expand_b_grad, "dp", scatter_dimension=0, tiled=True),
        lax.psum_scatter(gain_grad, "dp", scatter_dimension=0, tiled=True),
        lax.psum_scatter(respb_grad, "dp", scatter_dimension=0, tiled=True),
        lax.psum_scatter(reduce_w_grad, "dp", scatter_dimension=0, tiled=True),
        lax.psum_scatter(reduce_b_grad, "dp", scatter_dimension=0, tiled=True),
        lax.psum_scatter(ratio_w_grad, "dp", scatter_dimension=0, tiled=True),
        lax.psum_scatter(ratio_b_grad, "dp", scatter_dimension=0, tiled=True),
    )
    shards = tuple(block_shards) + tuple(attend_shards)
    summed = lax.psum(shards, ("cond", "pair"))
    return (layer_output, latent_grad, tokens_grad) + tuple(summed)

FAST = lax.Precision.HIGH


def dot(left, right):
    return jnp.dot(left, right, precision=FAST)


def dot_t(left, right):
    return lax.dot_general(left, right, (((1,), (1,)), ((), ())), precision=FAST)


def t_dot(left, right):
    return lax.dot_general(left, right, (((0,), (0,)), ((), ())), precision=FAST)


def norm_stats(values):
    centered = values - jnp.mean(values, axis=-1, keepdims=True)
    variance = jnp.mean(centered * centered, axis=-1, keepdims=True)
    inverse = lax.rsqrt(variance + EPSILON)
    return centered * inverse, inverse


def norm_back(grad, normed, inverse):
    return inverse * (
        grad
        - jnp.mean(grad, axis=-1, keepdims=True)
        - normed * jnp.mean(grad * normed, axis=-1, keepdims=True)
    )


def heads_of(values):
    return values.reshape(values.shape[0], -1, HEAD_CHANNELS)


CHUNK = 32
MESH = pl.DeviceIdType.MESH
DMA = pltpu.SemaphoreType.DMA
ANY = pl.BlockSpec(memory_space=pl.ANY)


def near_of(me, step):
    across = lax.rem(lax.rem(me, 2) + lax.rem(step, 2), 2)
    along = lax.rem(lax.div(me, 2) + lax.div(step, 2), 2)
    return along * 2 + across


def remote(src, dst, send, recv, device):
    return pltpu.make_async_remote_copy(
        src_ref=src, dst_ref=dst, send_sem=send, recv_sem=recv, device_id=device,
        device_id_type=MESH,
    )


def greet(device):
    barrier = pltpu.get_barrier_semaphore()
    pl.semaphore_signal(barrier, inc=1, device_id=device, device_id_type=MESH)


def relay_begin(full, sems):
    cross_out, cross_in, mate_out, mate_in = sems
    core = lax.axis_index("cond")
    level = lax.axis_index("pair")
    me = lax.axis_index("dp")
    unit = full.shape[1] // 4
    side = lax.rem(level, 2)
    across = (core, level + 1 - 2 * side, me)
    mate = (1 - core, level, me)

    def spot(u, step):
        rows = pl.ds(pl.multiple_of((core * 2 + u) * unit, 8), unit)
        return full.at[near_of(me, step), rows]

    steps = (1, 2, 3)
    crosses = [
        remote(
            spot(side, step), spot(side, step), cross_out.at[step - 1], cross_in.at[step - 1], across
        )
        for step in steps
    ]
    mates = [
        [
            remote(
                spot(u, step), spot(u, step), mate_out.at[i, step - 1], mate_in.at[i, step - 1], mate
            )
            for step in steps
        ]
        for i, u in enumerate((side, 1 - side))
    ]

    def begin():
        for copy in crosses + mates[0]:
            copy.start()

    def end():
        for cross, far in zip(crosses, mates[1]):
            cross.wait_recv()
            far.start()
        for copy in crosses:
            copy.wait_send()
        for copy in mates[0] + mates[1]:
            copy.wait()

    return begin, end


def exchange_body(gather_count, scatter_count, swap_count, relays, *refs):
    near_count = gather_count + scatter_count
    count = near_count + swap_count
    ins = refs[:count]
    refs = refs[count + relays :]
    outs = refs[:count]
    full = refs[count] if relays else None
    refs = refs[count + relays :]
    passing, refs = refs[:swap_count], refs[swap_count:]
    holds = refs[: gather_count + swap_count]
    refs = refs[gather_count + swap_count :]
    joined = [i for i in range(gather_count, near_count) if ins[i].shape[1] % 16 == 0]
    sums = dict(zip(joined, zip(refs[: 2 * len(joined) : 2], refs[1 : 2 * len(joined) : 2])))
    refs = refs[2 * len(joined) :]
    send, recv, keep, diag_out, diag_in, join_out, join_in, join_load = refs[:8]
    sems = refs[8:]
    core = lax.axis_index("cond")
    level = lax.axis_index("pair")
    me = lax.axis_index("dp")
    goal = near_of(me, rev(level))
    quarter = rev(near_of(level, me))
    shifts = level != 0
    rises = goal != level
    final = me == level
    expected = 3
    for step in (1, 2, 3):
        greet((core, level, near_of(me, step)))
    if relays:
        greet((1 - core, level, me))
        greet((core, level + 1 - 2 * lax.rem(level, 2), me))
        expected = expected + 2
    if swap_count:
        pl.when(rises)(lambda: greet((core, quarter, me)))
        expected = expected + jnp.where(rises, 1, 0)
    pl.semaphore_wait(pltpu.get_barrier_semaphore(), expected)

    def shift(i, goals):
        return remote(
            ins[near_count + i], goals[i], send.at[near_count + i, 0], recv.at[near_count + i, 0],
            (core, level, goal),
        )

    def rise(i, sources):
        return remote(
            sources[i], outs[near_count + i], send.at[near_count + i, 1],
            recv.at[near_count + i, 1], (core, goal, me),
        )

    def part_rows(i, k):
        half = ins[i].shape[1] // 2
        return pl.ds(half * k, half)

    def early(i, step):
        return remote(
            ins[i].at[3, part_rows(i, step - 1)], sums[i][1].at[step - 1],
            diag_out.at[i, step - 1], diag_in.at[i, step - 1], (core, level, near_of(me, step)),
        )

    def alone(i, step):
        rows = part_rows(i, step - 1)
        return remote(
            ins[i].at[step, rows], outs[i].at[step - 1, rows], send.at[i, step - 1],
            recv.at[i, step - 1], (core, level, near_of(me, step)),
        )

    def join(i, step):
        rows = part_rows(i, 2 - step)
        return remote(
            sums[i][0].at[step - 1], outs[i].at[step - 1, rows], join_out.at[i, step - 1],
            join_in.at[i, step - 1], (core, level, near_of(me, step)),
        )

    def join_own(i, step):
        return pltpu.make_async_copy(
            ins[i].at[step, part_rows(i, 2 - step)], sums[i][0].at[step - 1], join_load.at[i, step - 1]
        )

    for i in joined:
        for step in (1, 2):
            early(i, step).start()
            alone(i, step).start()
            join_own(i, step).start()
    swap_ins = ins[near_count:]
    swap_outs = outs[near_count:]
    near_copies = []
    if relays:
        relay_start, relay_end = relay_begin(full, sems)
        relay_start()
    for i in range(swap_count):
        pl.when(jnp.logical_and(shifts, final))(shift(i, swap_outs).start)
        pl.when(jnp.logical_and(shifts, jnp.logical_not(final)))(shift(i, passing).start)
        pl.when(jnp.logical_and(jnp.logical_not(shifts), rises))(rise(i, swap_ins).start)
    tall = [i for i in range(gather_count) if ins[i].shape[0] % 16 == 0]
    for step in (3, 1, 2):
        for i in range(near_count):
            if (step == 3 and i in tall) or i in joined:
                continue
            if i < gather_count:
                src, dst = ins[i], outs[i].at[step]
            else:
                src, dst = ins[i].at[step], outs[i].at[step - 1]
            copy = remote(
                src, dst, send.at[i, step - 1], recv.at[i, step - 1],
                (core, level, near_of(me, step)),
            )
            copy.start()
            if i not in tall:
                near_copies.append(copy)

    def direct(i, step):
        return remote(
            ins[i], outs[i].at[step], send.at[i, step - 1], recv.at[i, step - 1],
            (core, level, near_of(me, step)),
        )

    def onward(i, step):
        half = ins[i].shape[0] // 2
        rows = pl.ds(half * (step - 1), half)
        return remote(
            outs[i].at[step, rows], outs[i].at[3, rows], diag_out.at[i, step - 1],
            diag_in.at[i, step - 1], (core, level, near_of(me, 3 - step)),
        )

    def through(src, hold, dst, sem):
        load = pltpu.make_async_copy(src, hold, sem)
        load.start()
        load.wait()
        store = pltpu.make_async_copy(hold, dst, sem)
        store.start()
        store.wait()

    for i in range(gather_count):
        through(ins[i], holds[i], outs[i].at[0], keep.at[i])
    for i in range(swap_count):
        pl.when(jnp.logical_and(jnp.logical_not(shifts), jnp.logical_not(rises)))(
            lambda i=i: through(
                swap_ins[i], holds[gather_count + i], swap_outs[i], keep.at[gather_count + i]
            )
        )
        pl.when(shifts)(shift(i, passing).wait_recv)
        pl.when(jnp.logical_and(shifts, rises))(rise(i, passing).start)
    for i in joined:
        for step in (1, 2):
            early(i, 3 - step).wait_recv()
            join_own(i, step).wait()
            sums[i][0][step - 1] += sums[i][1][2 - step]
            join(i, step).start()
        for step in (1, 2):
            early(i, step).wait_send()
            alone(i, step).wait()
            join(i, step).wait()
    for i in tall:
        for step in (1, 2):
            direct(i, step).wait_recv()
            onward(i, step).start()
    if relays:
        relay_end()
    for i in tall:
        for step in (1, 2):
            direct(i, step).wait_send()
            onward(i, step).wait()
    for copy in near_copies:
        copy.wait()
    for i in range(swap_count):
        pl.when(shifts)(shift(i, passing).wait_send)
        pl.when(rises)(rise(i, swap_ins).wait_send)
        pl.when(quarter != level)(rise(i, swap_ins).wait_recv)


def exchange(collective, gathers=(), scatters=(), swaps=(), relay=()):
    f32 = jnp.float32
    shapes = [(4,) + item.shape for item in gathers]
    joined = [item for item in scatters if item.shape[1] % 16 == 0]
    shapes += [(2 if item.shape[1] % 16 == 0 else 3,) + item.shape[1:] for item in scatters]
    shapes += [item.shape for item in swaps]
    count = len(shapes)
    shapes += [item.shape for item in relay]
    shapes += [item.shape for item in swaps]
    staged = len(gathers) + len(swaps)
    scratch = [pltpu.VMEM(item.shape, f32) for item in tuple(gathers) + tuple(swaps)]
    for item in joined:
        half = (2, item.shape[1] // 2) + item.shape[2:]
        scratch += [pltpu.VMEM(half, f32), pltpu.VMEM(half, f32)]
    scratch += [DMA((count, 3)), DMA((count, 3)), DMA((max(staged, 1),))]
    scratch += [DMA((count, 2))] * 5
    if relay:
        scratch += [DMA((3,)), DMA((3,)), DMA((2, 3)), DMA((2, 3))]
    outs = pl.pallas_call(
        functools.partial(exchange_body, len(gathers), len(scatters), len(swaps), len(relay)),
        out_shape=[jax.ShapeDtypeStruct(shape, f32) for shape in shapes],
        in_specs=[ANY] * (count + len(relay)),
        out_specs=[ANY] * len(shapes),
        scratch_shapes=scratch,
        input_output_aliases={count: count} if relay else {},
        compiler_params=pltpu.CompilerParams(
            collective_id=collective, has_side_effects=True, vmem_limit_bytes=16 * 2**20
        ),
        name="exchange",
    )(*gathers, *scatters, *swaps, *relay)
    return outs[: count + len(relay)]


PARTS = 4


def open_body(image_in, packed_in, tokens_in, embed_in, weight_in, attend_in, *refs):
    image, packed, tokens, embed, weight, attend = refs[:6]
    passing = refs[6:9]
    hold, send, recv, keep, cross_out, cross_in, pass_out, pass_in, own_out, own_in, block_out, block_in = refs[9:]
    core = lax.axis_index("cond")
    level = lax.axis_index("pair")
    me = lax.axis_index("dp")
    mate = (1 - core, level, me)
    side = lax.rem(level, 2)
    across = (core, level + 1 - 2 * side, me)
    rows = image_in.shape[0]
    wide = weight.shape[3]
    unit = weight.shape[2]
    turn = rev(level)
    goal = near_of(me, turn)
    quarter = rev(near_of(level, me))
    shifts = level != 0
    rises = goal != level
    turned = jnp.logical_and(level == 1, me == 1)
    raises = jnp.logical_and(level > 0, jnp.logical_not(turned))
    falls = level < 3
    taken = jnp.logical_and(quarter < 3, jnp.logical_not(turned))
    greet(mate)
    greet(across)
    for step in (1, 2, 3):
        greet((core, level, near_of(me, step)))
    pl.when(rises)(lambda: greet((core, quarter, me)))
    pl.when(quarter > 0)(lambda: greet((core, quarter - 1, level)))
    pl.when(taken)(lambda: greet((core, quarter + 1, level)))
    expected = (
        5 + jnp.where(rises, 1, 0) + jnp.where(raises, 1, 0) + jnp.where(falls, 1, 0)
    )
    pl.semaphore_wait(pltpu.get_barrier_semaphore(), expected)

    body = image.at[pl.ds(1, rows)]
    ins = (image_in, tokens_in, embed_in)
    ends = (body, tokens, embed)

    def shift(goals):
        return [
            remote(src, dst, send.at[i], recv.at[i], (core, level, goal))
            for i, (src, dst) in enumerate(zip(ins, goals))
        ]

    def rise(sources):
        return [
            remote(src, dst, send.at[3 + i], recv.at[3 + i], (core, goal, me))
            for i, (src, dst) in enumerate(zip(sources, ends))
        ]

    def stay():
        image_load = pltpu.make_async_copy(image_in, hold, keep.at[0])
        image_load.start()
        rest = [
            pltpu.make_async_copy(src, dst, keep.at[i])
            for i, (src, dst) in ((1, (tokens_in, tokens)), (2, (embed_in, embed)))
        ]
        run("start", *rest)
        image_load.wait()
        image_store = pltpu.make_async_copy(hold, body, keep.at[0])
        image_store.start()
        run("wait", image_store, *rest)

    lower = remote(
        image_in.at[pl.ds(rows - 1, 1)], image.at[pl.ds(0, 1)], send.at[6], recv.at[6],
        (core, me, near_of(me, rev(jnp.minimum(level + 1, 3)))),
    )
    upper = remote(
        image_in.at[pl.ds(0, 1)], image.at[pl.ds(rows + 1, 1)], send.at[7], recv.at[7],
        (core, me, near_of(me, rev(jnp.maximum(level - 1, 0)))),
    )
    around = pltpu.make_async_copy(
        image_in.at[pl.ds(0, 1)], image.at[pl.ds(rows + 1, 1)], keep.at[4]
    )

    def vectors(step):
        return remote(
            packed_in, packed.at[me], send.at[7 + step], recv.at[7 + step],
            (core, level, near_of(me, step)),
        )

    mine = core * 2 + side
    other = core * 2 + 1 - side

    size = unit // PARTS

    def block(step, h):
        to = near_of(me, step)
        src = weight_in.at[
            pl.ds(pl.multiple_of(mine * unit + h * size, 8), size),
            pl.ds(pl.multiple_of(to * wide, wide), wide),
        ]
        dst = weight.at[me, mine, pl.ds(h * size, size)]
        return remote(
            src, dst, block_out.at[h, step - 1], block_in.at[h, step - 1], (core, level, to)
        )

    piece = attend.shape[2] // 3

    def thirds(step):
        to = near_of(me, step)
        found = []
        for p in range(3):
            src = attend_in.at[
                pl.ds(pl.multiple_of(mine * unit, 8), unit),
                pl.ds(pl.multiple_of((p * 4 + to) * piece, piece), piece),
            ]
            dst = attend.at[
                me, pl.ds(pl.multiple_of(mine * unit, 8), unit), pl.ds(p * piece, piece)
            ]
            spot = 11 + step * 3 + p
            found.append(remote(src, dst, send.at[spot], recv.at[spot], (core, level, to)))
        return found

    def crossed(step, u, h):
        spot = weight.at[near_of(me, step), u, pl.ds(h * size, size)]
        return remote(spot, spot, cross_out.at[h, step - 1], cross_in.at[h, step - 1], across)

    def passed(step, u, turn, h):
        spot = weight.at[near_of(me, step), u, pl.ds(h * size, size)]
        k = turn * PARTS + h
        return remote(spot, spot, pass_out.at[k, step - 1], pass_in.at[k, step - 1], mate)

    def run(method, *copies):
        for copy in copies:
            getattr(copy, method)()

    final = me == level
    pl.when(jnp.logical_and(shifts, final))(lambda: run("start", *shift(ends)))
    pl.when(jnp.logical_and(shifts, jnp.logical_not(final)))(lambda: run("start", *shift(passing)))
    pl.when(jnp.logical_and(jnp.logical_not(shifts), rises))(lambda: run("start", *rise(ins)))
    pl.when(falls)(lower.start)
    pl.when(raises)(upper.start)
    pl.when(turned)(around.start)
    own = [pltpu.make_async_copy(packed_in, packed.at[me], keep.at[3])]
    own_blocks = [
        remote(
            weight_in.at[pl.ds(u * unit, unit), pl.ds(pl.multiple_of(me * wide, wide), wide)],
            weight.at[me, u],
            own_out.at[u],
            own_in.at[u],
            mate,
        )
        for u in range(4)
    ] + [
        remote(
            attend_in.at[:, pl.ds(pl.multiple_of((p * 4 + me) * piece, piece), piece)],
            attend.at[me, :, pl.ds(p * piece, piece)],
            own_out.at[4 + p],
            own_in.at[4 + p],
            mate,
        )
        for p in range(3)
    ]
    for step in (3, 1, 2):
        vectors(step).start()
    for h in range(2):
        for step in (3, 1, 2):
            block(step, h).start()
    run("start", *own, *own_blocks)
    pl.when(jnp.logical_and(jnp.logical_not(shifts), jnp.logical_not(rises)))(stay)

    @pl.when(shifts)
    def _():
        run("wait_recv", *shift(passing))
        pl.when(rises)(lambda: run("start", *rise(passing)))

    for h in range(PARTS):
        for step in (2, 1, 3):
            block(step, h).wait_recv()
            if h + 2 < PARTS:
                block(step, h + 2).start()
            crossed(step, mine, h).start()
            passed(step, mine, 0, h).start()
    for step in (3, 1, 2):
        run("start", *thirds(step))
    for h in range(PARTS):
        for step in (2, 1, 3):
            crossed(step, other, h).wait_recv()
            passed(step, other, 1, h).start()
    pl.when(shifts)(lambda: run("wait_send", *shift(passing)))
    pl.when(rises)(lambda: run("wait_send", *rise(ins)))
    pl.when(quarter != level)(lambda: run("wait_recv", *rise(ins)))
    pl.when(falls)(lower.wait_send)
    pl.when(raises)(upper.wait_send)
    pl.when(quarter > 0)(lower.wait_recv)
    pl.when(taken)(upper.wait_recv)
    pl.when(turned)(around.wait)
    for step in (1, 2, 3):
        vectors(step).wait()
        run("wait", *thirds(step))
        for h in range(PARTS):
            block(step, h).wait_send()
            crossed(step, mine, h).wait_send()
            for u, turn_of in ((mine, 0), (other, 1)):
                passed(step, u, turn_of, h).wait()
    run("wait", *own, *own_blocks)


def open_exchange(collective, image, packed, tokens, embed, weight, attend):
    rows, cols, chan = image.shape
    unit = weight.shape[0] // 4
    shapes = [
        (rows + 2, cols, chan),
        (4,) + packed.shape,
        tokens.shape,
        embed.shape,
        (4, 4, unit, weight.shape[1] // 4),
        (4, attend.shape[0], attend.shape[1] // 4),
        image.shape,
        tokens.shape,
        embed.shape,
    ]
    return pl.pallas_call(
        open_body,
        out_shape=[jax.ShapeDtypeStruct(shape, jnp.float32) for shape in shapes],
        in_specs=[ANY] * 6,
        out_specs=[ANY] * 9,
        scratch_shapes=[
            pltpu.VMEM(image.shape, jnp.float32),
            DMA((23,)),
            DMA((23,)),
            DMA((5,)),
            DMA((PARTS, 3)),
            DMA((PARTS, 3)),
            DMA((2 * PARTS, 3)),
            DMA((2 * PARTS, 3)),
            DMA((7,)),
            DMA((7,)),
            DMA((PARTS, 3)),
            DMA((PARTS, 3)),
        ],
        compiler_params=pltpu.CompilerParams(collective_id=collective, has_side_effects=True),
        name="open_exchange",
    )(image, packed, tokens, embed, weight, attend)


def rev(z):
    return 2 * lax.rem(z, 2) + lax.div(z, 2)


def plane_spot(level, me):
    return me, near_of(me, rev(level))


def home_spot(level, me):
    return rev(near_of(level, me)), level


def stream_setup(homeward=False):
    core = lax.axis_index("cond")
    level = lax.axis_index("pair")
    me = lax.axis_index("dp")
    greet((1 - core, level, me))
    for step in (1, 2, 3):
        greet((core, level, near_of(me, step)))
    pl.when(level > 0)(lambda: greet((core, level - 1, me)))
    pl.when(level < 3)(lambda: greet((core, level + 1, me)))
    ends = jnp.where(level == 0, 1, 0) + jnp.where(level == 3, 1, 0)
    expected = 6 - ends
    if homeward:
        moves = jnp.logical_or(level != 0, me != 0)
        back_up, back_over = plane_spot(level, me)
        pl.when(moves)(lambda: greet((core, back_up, back_over)))
        expected = expected + jnp.where(moves, 1, 0)
    pl.semaphore_wait(pltpu.get_barrier_semaphore(), expected)


def sum_stream(sections, scratch, hooks):
    (
        data,
        stage,
        first,
        second,
        own,
        load_sem,
        core_out,
        core_in,
        plane_out,
        plane_in,
        first_in,
        second_in,
        hop_out,
        cast_out,
        cast_low,
        final_in,
        keep_sem,
        pair_out,
        pair_in,
    ) = scratch
    ranges = []
    total = 0
    for kind, src, dst in sections:
        if kind == "plain":
            count, width = src.shape[1] // CHUNK, src.shape[2]
        else:
            count, width = 4 * (src.shape[2] // CHUNK), src.shape[3]
        ranges.append((total, total + count, kind, src, dst, width))
        total += count
    core = lax.axis_index("cond")
    level = lax.axis_index("pair")
    me = lax.axis_index("dp")
    mate = (1 - core, level, me)
    ring = data.shape[0]
    full = data.shape[2]

    def rank_of(j):
        return jnp.where(lax.rem(j, 2) == 0, level, 3 - level)

    def at_rank(j, rank):
        return (core, jnp.where(lax.rem(j, 2) == 0, rank, 3 - rank), me)

    def inside(j, low, high):
        return jnp.logical_and(j >= low, j < high)

    def swap_place(j):
        inner = False
        k = 0
        for low, high, kind, src, dst, width in ranges:
            if kind == "swap":
                here = inside(j, low, high)
                inner = jnp.logical_or(inner, here)
                k = jnp.where(here, j - low, k)
        return inner, k

    def moved(j):
        inner, k = swap_place(j)
        return jnp.logical_and(inner, lax.rem(k, 4) != 0)

    def kinds(j, action):
        narrow = False
        for low, high, kind, src, dst, width in ranges:
            if width != full:
                here = inside(j, low, high)
                narrow = jnp.logical_or(narrow, here)
                pl.when(here)(lambda width=width: action(width))
        pl.when(jnp.logical_not(narrow))(lambda: action(full))

    def cut(ref, width):
        return ref if ref.shape[-1] == width else ref.at[:, pl.ds(0, width)]

    def each_source(j, action):
        target = data.at[lax.rem(j, ring)]
        mine = own.at[lax.rem(j, 4)]
        for low, high, kind, src, dst, width in ranges:

            @pl.when(inside(j, low, high))
            def _(low=low, kind=kind, src=src, width=width):
                k = j - low
                if kind == "plain":
                    rows = pl.ds(pl.multiple_of(k * CHUNK, CHUNK), CHUNK)
                    action(lambda half: src.at[half, rows], target, mine)
                else:
                    rows = pl.ds(pl.multiple_of(lax.div(k, 4) * CHUNK, CHUNK), CHUNK)
                    spot = near_of(me, lax.rem(k, 4))
                    action(
                        lambda half: src.at[spot, half, rows], cut(target, width), cut(mine, width)
                    )

    def each_final(j, action):
        for low, high, kind, src, dst, width in ranges:

            @pl.when(inside(j, low, high))
            def _(low=low, kind=kind, dst=dst, width=width):
                k = j - low
                if kind == "plain":
                    rows = pl.ds(pl.multiple_of(k * CHUNK, CHUNK), CHUNK)
                    action(
                        lambda half: [(dst.at[half, rows], lambda x: x, 0)],
                        first.at[lax.rem(j, ring)],
                    )
                else:
                    rows = pl.ds(pl.multiple_of(lax.div(k, 4) * CHUNK, CHUNK), CHUNK)
                    spot = near_of(me, lax.rem(k, 4))
                    pieces = 1 if width == full else 3
                    piece = width // pieces

                    def targets(half):
                        found = []
                        for p in range(pieces):
                            columns = pl.ds(
                                pl.multiple_of(p * 4 * piece + spot * piece, piece), piece
                            )
                            found.append(
                                (
                                    dst.at[half, rows, columns],
                                    lambda x, p=p: x
                                    if x.shape[-1] == piece
                                    else x.at[:, pl.ds(p * piece, piece)],
                                    p,
                                )
                            )
                        return found

                    action(targets, stage.at[k])

    def core_copy(j, src, dst):
        return remote(src, dst, core_out.at[j], core_in.at[j], mate)

    def plane_copy(j, width):
        inner, k = swap_place(j)
        return remote(
            cut(first.at[lax.rem(j, ring)], width),
            cut(stage.at[k], width),
            plane_out.at[j],
            plane_in.at[j],
            (core, level, near_of(me, lax.rem(k, 4))),
        )

    def hop_first(j, src, rank, width):
        return remote(
            cut(src, width), cut(first.at[lax.rem(j, ring)], width), hop_out.at[j], first_in.at[j], at_rank(j, rank)
        )

    def hop_second(j, width):
        k = lax.div(j, 2)
        return remote(
            cut(data.at[lax.rem(j, ring)], width), cut(second.at[lax.rem(k, ring // 2)], width), hop_out.at[j], second_in.at[k],
            at_rank(j, 2),
        )

    def start(j):
        def go(source, target, mine):
            core_copy(j, source(1 - core), target).start()
            pltpu.make_async_copy(source(core), mine, load_sem.at[lax.rem(j, 4)]).start()

        each_source(j, go)

    def combine(j):
        def go(source, target, mine):
            pltpu.make_async_copy(source(core), mine, load_sem.at[lax.rem(j, 4)]).wait()
            core_copy(j, source(1 - core), target).wait_recv()
            target[...] += mine[...]

        each_source(j, go)

    def depart(j):
        rank = rank_of(j)

        def go(width):
            pl.when(rank == 0)(lambda: hop_first(j, data.at[lax.rem(j, ring)], 1, width).start())
            pl.when(rank == 3)(lambda: hop_second(j, width).start())

        kinds(j, go)

    def relay(j):
        def go(width):
            hop_first(j, data.at[lax.rem(j, ring)], 1, width).wait_recv()
            spot = lax.rem(j, ring)
            first[spot, :, :width] += data[spot, :, :width]
            hop_first(j, first.at[lax.rem(j, ring)], 2, width).start()

        pl.when(rank_of(j) == 1)(lambda: kinds(j, go))

    def casts(j, rank, half_targets, source, sems):
        return [
            remote(
                cut_of(source) if source is not None else ref, ref, sems.at[j, p], final_in.at[j, p],
                at_rank(j, rank),
            )
            for ref, cut_of, p in half_targets
        ]

    def pairs(j, half_targets, source):
        return [
            remote(
                cut_of(source) if source is not None else ref, ref, pair_out.at[j, p],
                pair_in.at[j, p], mate,
            )
            for ref, cut_of, p in half_targets
        ]

    def keeps(j, half_targets, source):
        return [
            pltpu.make_async_copy(cut_of(source), ref, keep_sem.at[j, p])
            for ref, cut_of, p in half_targets
        ]

    def root(j):
        def add(width):
            hop_first(j, first.at[lax.rem(j, ring)], 2, width).wait_recv()
            hop_second(j, width).wait_recv()
            spot = lax.rem(j, ring)
            first[spot, :, :width] += (
                data[spot, :, :width] + second[lax.rem(lax.div(j, 2), ring // 2), :, :width]
            )

        @pl.when(rank_of(j) == 2)
        def _():
            kinds(j, add)

            @pl.when(moved(j))
            def _():
                kinds(j, lambda width: plane_copy(j, width).start())

            inner, k = swap_place(j)

            @pl.when(jnp.logical_and(inner, jnp.logical_not(moved(j))))
            def _():
                stage[k] = first[lax.rem(j, ring)]

    def spread(j):
        def send(targets, source):
            goals = targets(core)
            for copy in (
                casts(j, 1, goals, source, cast_out)
                + casts(j, 3, goals, source, cast_low)
                + keeps(j, goals, source)
                + pairs(j, goals, source)
            ):
                copy.start()

        @pl.when(rank_of(j) == 2)
        def _():
            @pl.when(moved(j))
            def _():
                kinds(j, lambda width: plane_copy(j, width).wait_recv())

            each_final(j, send)

    def landed(j):
        rank = rank_of(j)

        def go(targets, source):
            goals = targets(core)
            for copy in casts(j, 1, goals, None, cast_out):
                copy.wait_recv()
            pl.when(rank == 1)(
                lambda: [copy.start() for copy in casts(j, 0, goals, None, cast_out)] and None
            )
            for copy in pairs(j, goals, None):
                copy.start()

        @pl.when(jnp.logical_or(rank == 1, rank == 3))
        def _():
            each_final(j, go)

    def arrived(j):
        def go(targets, source):
            goals = targets(core)
            for copy in casts(j, 0, goals, None, cast_out):
                copy.wait_recv()
            for copy in pairs(j, goals, None):
                copy.start()

        @pl.when(rank_of(j) == 0)
        def _():
            each_final(j, go)

    def finish(j):
        rank = rank_of(j)

        def sent(source, target, mine):
            core_copy(j, source(1 - core), target).wait_send()

        each_source(j, sent)

        @pl.when(jnp.logical_and(moved(j), rank == 2))
        def _():
            kinds(j, lambda width: plane_copy(j, width).wait_send())

        @pl.when(rank != 2)
        def _():
            kinds(j, lambda width: hop_first(j, data.at[lax.rem(j, ring)], 1, width).wait_send())

        def go(targets, source):
            goals = targets(core)

            @pl.when(jnp.logical_or(rank == 1, rank == 2))
            def _():
                for copy in casts(j, 1, goals, None, cast_out):
                    copy.wait_send()

            @pl.when(rank == 2)
            def _():
                for copy in casts(j, 3, goals, None, cast_low):
                    copy.wait_send()
                for copy in keeps(j, goals, source):
                    copy.wait()

            for copy in pairs(j, goals, None):
                copy.wait()

        each_final(j, go)

    stages = (
        (0, start),
        (2, combine),
        (3, depart),
        (6, relay),
        (9, root),
        (12, spread),
        (15, landed),
        (18, arrived),
        (21, finish),
    )

    def step(t, carry):
        for lag, stage_of in stages:
            j = t - lag

            @pl.when(jnp.logical_and(j >= 0, j < total))
            def _(j=j, stage_of=stage_of):
                stage_of(j)

        for low, high, hook in hooks:
            pl.when(jnp.logical_and(t >= low, t < high))(lambda hook=hook, low=low: hook(t - low))
        return carry

    lax.fori_loop(0, total + 21, step, 0)


def stream_scratch(total, most, width):
    ring = 32
    return [
        pltpu.VMEM((ring, CHUNK, width), jnp.float32),
        pltpu.VMEM((most, CHUNK, width), jnp.float32),
        pltpu.VMEM((ring, CHUNK, width), jnp.float32),
        pltpu.VMEM((ring // 2, CHUNK, width), jnp.float32),
        pltpu.VMEM((4, CHUNK, width), jnp.float32),
        DMA((4,)),
        DMA((total,)),
        DMA((total,)),
        DMA((total,)),
        DMA((total,)),
        DMA((total,)),
        DMA(((total + 1) // 2,)),
        DMA((total,)),
        DMA((total, 3)),
        DMA((total, 3)),
        DMA((total, 3)),
        DMA((total, 3)),
        DMA((total, 3)),
        DMA((total, 3)),
    ]


SCRATCH = 19


def near_slots(shares, arrived, send, recv, base):
    core = lax.axis_index("cond")
    level = lax.axis_index("pair")
    me = lax.axis_index("dp")
    return [
        remote(
            shares.at[step], arrived.at[step - 1], send.at[base + step - 1],
            recv.at[base + step - 1], (core, level, near_of(me, step)),
        )
        for step in (3, 1, 2)
    ]


def near_blocks(block, everyone, send, recv, base):
    core = lax.axis_index("cond")
    level = lax.axis_index("pair")
    me = lax.axis_index("dp")
    return [
        remote(
            block, everyone.at[step], send.at[base + step - 1], recv.at[base + step - 1],
            (core, level, near_of(me, step)),
        )
        for step in (3, 1, 2)
    ]


def row_stats(rows):
    centered = rows - jnp.mean(rows, axis=-1, keepdims=True)
    inverse = lax.rsqrt(jnp.mean(centered * centered, axis=-1, keepdims=True) + EPSILON)
    return centered * inverse, inverse


def halves(value):
    high = value.astype(jnp.bfloat16)
    return high, (value - high.astype(jnp.float32)).astype(jnp.bfloat16)


def three_pass(left, right, dims):
    def one(x, y):
        return lax.dot_general(x, y, (dims, ((), ())), preferred_element_type=jnp.float32)

    return one(left[0], right[1]) + one(left[1], right[0]) + one(left[0], right[0])


TILE = 256


def backward_body(
    output_ref, qkv_ref, two_ref, text_ref, cot_ref, one_ref, response_ref, reduce_w_ref,
    act_ref, slope_ref, normed_ref, expand_w_ref, conv_ref, mixture_ref, out_w_ref, base_ref,
    small_ref,
    normed_two_ref, rows_ref, embed_ref, silu_ref, mapped_ref, text_kv_ref,
    output_out, attend_out, mapper_out, reduce_out, small_out, expand_out,
    attend_part, mapper_part, reduce_part, expand_part, one_out, text_out, grad_out, layer_out,
    *scratch
):
    (
        front_got, front_own, conv, grad, one, out_got, out_own, base, small, wide, high, low,
        weights, acts, slopes, columns, product, front, sums, spread_own, spread_got,
        text_got, text_own, text_all, ratio, mapped,
    ) = scratch[SCRATCH : SCRATCH + 26]
    (
        send, recv, keep, tile_out, tile_in, load, front_out, front_in, spread_out, spread_in,
        piece_out, piece_in, text_out_sem, text_in_sem,
    ) = scratch[SCRATCH + 26 :]
    stream_setup(True)
    core = lax.axis_index("cond")
    level = lax.axis_index("pair")
    me = lax.axis_index("dp")
    moves = jnp.logical_or(level != 0, me != 0)
    up, over = home_spot(level, me)
    pixels, chan = conv.shape
    spots = wide.shape[0]
    texts = text_own.shape[0]
    count = chan // TILE
    scatters = near_slots(two_ref, front_got, send, recv, 0)
    scatters += near_slots(text_ref, text_got, send, recv, 6)
    start_loads = [
        pltpu.make_async_copy(src, dst, keep.at[6 + i])
        for i, (src, dst) in enumerate(
            ((two_ref.at[0], front_own), (text_ref.at[0], text_own), (cot_ref, conv), (one_ref, one))
        )
    ]

    def near_tile(i):
        rows = pl.ds(pl.multiple_of(i * 16, 16), 16)
        return [
            remote(
                grad.at[rows],
                wide.at[pl.ds(pl.multiple_of(step * pixels + i * 16, 16), 16)],
                piece_out.at[i, step - 1],
                piece_in.at[i, step - 1],
                (core, level, near_of(me, step)),
            )
            for step in (3, 1, 2)
        ]

    def late():
        found = []
        for step in (3, 1, 2):
            device = (core, level, near_of(me, step))
            found.append(
                remote(
                    text_all.at[0], text_all.at[step], text_out_sem.at[step - 1],
                    text_in_sem.at[step - 1], device,
                )
            )
            found.append(
                remote(
                    ratio.at[0], ratio.at[step], text_out_sem.at[2 + step],
                    text_in_sem.at[2 + step], device,
                )
            )
        return found

    one_kept = pltpu.make_async_copy(grad, one_out, keep.at[10])
    text_kept = pltpu.make_async_copy(text_all, text_out, keep.at[11])

    def early_loads():
        homes = [(acts, 0), (acts, 1), (slopes, 0), (slopes, 1), (front, 0)]
        found = []
        for i, (buffer, slot) in enumerate(homes):
            width = min(TILE, qkv_ref.shape[1] - i * TILE)
            dst = buffer.at[slot] if width == TILE else buffer.at[slot, :, pl.ds(0, width)]
            found.append(
                pltpu.make_async_copy(
                    qkv_ref.at[:, pl.ds(i * TILE, width)], dst, load.at[2 + i if i < 4 else 0]
                )
            )
        return found, homes

    def early_column(i):
        return pltpu.make_async_copy(
            normed_two_ref.at[:, pl.ds(pl.multiple_of(i * part, part), part)],
            columns.at[lax.rem(i, 2)],
            load.at[6 + lax.rem(i, 2)],
        )

    def attend_stores(i):
        half = part // 2
        return [
            pltpu.make_async_copy(
                product.at[pl.ds(c * half, half), pl.ds(0, 3 * part)],
                attend_part.at[i, c],
                load.at[8 + c],
            )
            for c in (0, 1)
        ]

    def prepare(t):
        copies, homes = early_loads()
        for i, (copy, (buffer, slot)) in enumerate(zip(copies, homes)):
            copy.wait()
            width = min(TILE, qkv_ref.shape[1] - i * TILE)

            def strip(k, carry, i=i, buffer=buffer, slot=slot, width=width):
                rows = pl.ds(pl.multiple_of(k * 48, 48), 48)
                cols = pl.ds(i * TILE, width)
                high[rows, cols], low[rows, cols] = halves(buffer[slot, rows, 0:width])
                return carry

            lax.fori_loop(0, spots // 48, strip, 0)

    def attend_outer(i):
        early_column(i).wait()

        @pl.when(i > 0)
        def _():
            for copy in attend_stores(jnp.maximum(i - 1, 0)):
                copy.wait()

        left = halves(columns[lax.rem(i, 2)])
        text_left = halves(mapped_ref[:, pl.ds(pl.multiple_of(i * part, part), part)])
        for k in range(3):
            cols = pl.ds(k * part, part)
            value = three_pass(left, (high[:, cols], low[:, cols]), ((0,), (0,)))
            if k > 0:
                right = halves(text_kv_ref[:, (k - 1) * part : k * part])
                value = value + three_pass(text_left, right, ((0,), (0,)))
            product[:, cols] = value
        for copy in attend_stores(i):
            copy.start()
        pl.when(i + 2 < 4)(lambda: early_column(jnp.minimum(i + 2, 3)).start())

    def settle_attend(t):
        for copy in attend_stores(3):
            copy.wait()

    def arrive(t):
        for copy in start_loads + scatters:
            copy.wait()
        ratio[0] = jnp.zeros_like(ratio[0])
        text_all[0] = jnp.zeros_like(text_all[0])
        text_all[0, 0:texts] = text_own[...] + text_got[0] + text_got[1] + text_got[2]

    def normalize(t):
        scale = rows_ref[6:7]
        shift = rows_ref[7:8]
        for half in range(2):
            rows = pl.ds(pl.multiple_of(t * 16 + half * 8, 8), 8)
            back = front_own[rows] + front_got[0, rows] + front_got[1, rows] + front_got[2, rows]
            hidden = one[rows]
            normed, inverse = row_stats(hidden * scale + shift)
            two = conv[rows] + inverse * (
                back
                - jnp.mean(back, axis=-1, keepdims=True)
                - normed * jnp.mean(back * normed, axis=-1, keepdims=True)
            )
            grad[rows] = two * scale
            ratio[0, 0:8] += two * hidden
            ratio[0, 8:16] += two
        for copy in near_tile(t):
            copy.start()

    def give_late(t):
        for copy in late():
            copy.start()
        one_kept.start()
        wide[0:pixels] = grad[...]

    def gathered(t):
        def wait(i, carry):
            for copy in near_tile(i):
                copy.wait()
            return carry

        lax.fori_loop(0, pixels // 16, wait, 0)
        for copy in late():
            copy.wait()
        one_kept.wait()
        text_kept.start()

        def piece(i, carry):
            rows = pl.ds(pl.multiple_of(i * 16, 16), 16)
            high[rows], low[rows] = halves(wide[rows])
            return carry

        lax.fori_loop(0, spots // 16, piece, 0)

    def mapper_stores():
        half = mapper_part.shape[1]
        return [
            pltpu.make_async_copy(
                mapped.at[pl.ds(c * half, half)], mapper_part.at[c], load.at[10 + c]
            )
            for c in (0, 1)
        ]

    def text_products(t):
        left = halves(silu_ref[...])

        def strip(k, carry):
            cols = pl.ds(pl.multiple_of(k * TILE, TILE), TILE)
            right = halves(text_all[:, :, cols].reshape(-1, TILE))
            mapped[:, cols] = three_pass(left, right, ((0,), (0,)))
            return carry

        lax.fori_loop(0, count, strip, 0)
        for copy in mapper_stores():
            copy.start()
        column_pair(0)[0].start()
        column_pair(0)[1].start()
        first_loads[0].wait()
        total = ratio[0] + ratio[1] + ratio[2] + ratio[3]
        scale_sum = jnp.sum(total[0:8], axis=0, keepdims=True)
        shift_sum = jnp.sum(total[8:16], axis=0, keepdims=True)
        odd = lax.rem(lax.broadcasted_iota(jnp.int32, (CHUNK, chan), 0), 2) == 1
        both = jnp.where(odd, shift_sum, scale_sum)
        small[0] = both * embed_ref[:, 0:1]
        sums[4:5] = scale_sum
        sums[5:6] = shift_sum
        sums[6:7] = jnp.sum(wide[...], axis=0, keepdims=True)
        sums[7:8] = jnp.sum(text_all[...].reshape(-1, chan), axis=0, keepdims=True)
        width = chan // 4
        place = pl.ds(pl.multiple_of(me * width, width), width)
        small[1, 3:4, 0:width] = sums[6:7, place]
        small[1, 3:4, width : 2 * width] = sums[7:8, place]
        pair_place = pl.ds(pl.multiple_of(lax.rem(me, 2) * 2 * width, width), 2 * width)
        small[1, 4:5, width : 3 * width] = jnp.where(
            me < 2, sums[4:5, pair_place], sums[5:6, pair_place]
        )

    def column_pair(i):
        return [
            pltpu.make_async_copy(
                response_ref.at[
                    :, pl.ds(pl.multiple_of(c * (chan // 2) + i * 128, 128), 128)
                ],
                columns.at[lax.rem(i, 2), :, pl.ds(c * 128, 128)],
                load.at[6 + lax.rem(i, 2) if c == 0 else 12 + lax.rem(i, 2)],
            )
            for c in (0, 1)
        ]

    def reduce_stores(i):
        return [
            pltpu.make_async_copy(
                product.at[pl.ds(c * 128, 128)],
                reduce_part.at[c, pl.ds(pl.multiple_of(i * 128, 128), 128)],
                load.at[8 + c],
            )
            for c in (0, 1)
        ]

    def reduce_outer(i):
        for copy in column_pair(i):
            copy.wait()

        @pl.when(i + 1 < count)
        def _():
            for copy in column_pair(jnp.minimum(i + 1, count - 1)):
                copy.start()

        @pl.when(i + 1 == count)
        def _():
            weight_load(reduce_w_ref, 0).start()
            act_load(0).start()

        @pl.when(i > 0)
        def _():
            for copy in reduce_stores(jnp.maximum(i - 1, 0)):
                copy.wait()

        @pl.when(i == 0)
        def _():
            for copy in mapper_stores():
                copy.wait()

        left = halves(columns[lax.rem(i, 2), :, 0:TILE])

        def strip(k, carry):
            cols = pl.ds(pl.multiple_of(k * TILE, TILE), TILE)
            product[0:TILE, cols] = three_pass(left, (high[:, cols], low[:, cols]), ((0,), (0,)))
            return carry

        lax.fori_loop(0, count, strip, 0)
        for copy in reduce_stores(i):
            copy.start()

    def settle_reduce(t):
        for copy in reduce_stores(count - 1):
            copy.wait()
        text_kept.wait()
        for copy in loads + out_loads():
            copy.start()
        sums[0:4] = jnp.zeros((4, chan), jnp.float32)

    outward = near_slots(out_own, out_got, send, recv, 3)

    def away(i):
        rows = pl.ds(pl.multiple_of(i * 8, 8), 8)
        return remote(
            base.at[rows], layer_out.at[rows], tile_out.at[i], tile_in.at[i], (core, up, over)
        )

    def here(i):
        rows = pl.ds(pl.multiple_of(i * 8, 8), 8)
        return pltpu.make_async_copy(base.at[rows], layer_out.at[rows], tile_out.at[i])

    first_loads = [pltpu.make_async_copy(small_ref, small, keep.at[1])]
    loads = [
        pltpu.make_async_copy(conv_ref, conv, keep.at[2]),
        pltpu.make_async_copy(base_ref, base, keep.at[4]),
    ]
    kept = pltpu.make_async_copy(one, grad_out, keep.at[5])

    def tile_rows(i):
        return pl.ds(pl.multiple_of(i * TILE, TILE), TILE)

    def weight_load(ref, i):
        return pltpu.make_async_copy(
            ref.at[tile_rows(i)], weights.at[lax.rem(i, 2)], load.at[lax.rem(i, 2)]
        )

    def act_load(i):
        return pltpu.make_async_copy(
            act_ref.at[:, tile_rows(i)], acts.at[lax.rem(i, 2)], load.at[2 + lax.rem(i, 2)]
        )

    def slope_load(i):
        return pltpu.make_async_copy(
            slope_ref.at[:, tile_rows(i)], slopes.at[lax.rem(i, 2)], load.at[4 + lax.rem(i, 2)]
        )

    part = columns.shape[2]

    def column_load(i):
        return pltpu.make_async_copy(
            normed_ref.at[:, pl.ds(pl.multiple_of(i * part, part), part)],
            columns.at[lax.rem(i, 2)],
            load.at[6 + lax.rem(i, 2)],
        )

    def product_stores(i):
        half = part // 2
        return [
            pltpu.make_async_copy(
                product.at[pl.ds(c * half, half)], expand_part.at[i, c], load.at[8 + c]
            )
            for c in (0, 1)
        ]

    def front_sends(i):
        found = []
        for step in (3, 1, 2):
            found.append(
                remote(
                    front.at[lax.rem(i, 2), pl.ds(step * pixels, pixels)],
                    front_got.at[step - 1, :, tile_rows(i)],
                    front_out.at[i, step - 1],
                    front_in.at[i, step - 1],
                    (core, level, near_of(me, step)),
                )
            )
        return found

    for copy in early_loads()[0] + [early_column(0), early_column(1)]:
        copy.start()
    for copy in scatters + start_loads + first_loads:
        copy.start()

    def respond(i):
        weight_load(reduce_w_ref, i).wait()
        act_load(i).wait()

        @pl.when(i + 1 < count)
        def _():
            weight_load(reduce_w_ref, i + 1).start()
            act_load(i + 1).start()

        @pl.when(i + 1 == count)
        def _():
            act_load(0).start()
            slope_load(0).start()

        right = halves(weights[lax.rem(i, 2)])
        cols = tile_rows(i)

        def strip(k, carry):
            rows = pl.ds(pl.multiple_of(k * pixels, pixels), pixels)
            value = three_pass((high[rows], low[rows]), right, ((1,), (1,)))
            wide[rows, cols] = value
            sums[0:1, cols] += jnp.sum(value * acts[lax.rem(i, 2), rows], axis=0, keepdims=True)
            sums[1:2, cols] += jnp.sum(value, axis=0, keepdims=True)
            return carry

        lax.fori_loop(0, 4, strip, 0)

    def spreads():
        return [
            remote(
                spread_own, spread_got.at[step - 1], spread_out.at[step - 1],
                spread_in.at[step - 1], (core, level, near_of(me, step)),
            )
            for step in (3, 1, 2)
        ]

    def out_loads():
        return [
            pltpu.make_async_copy(mixture_ref, columns.at[0], load.at[6]),
            pltpu.make_async_copy(out_w_ref, product, load.at[7]),
        ]

    def out_product(i):
        pl.when(i == 0)(lambda: [copy.wait() for copy in out_loads()] and None)
        rows = pl.ds(pl.multiple_of(i * pixels, pixels), pixels)
        left = halves(columns[0, rows])

        def strip(k, carry):
            cols = pl.ds(pl.multiple_of(k * TILE, TILE), TILE)
            out_own[i, :, cols] = three_pass(left, halves(product[:, cols]), ((1,), (0,)))
            return carry

        lax.fori_loop(0, count, strip, 0)

    def send_out(t):
        for copy in outward:
            copy.start()

    def share(t):
        total = jnp.sum(sums[0:1] * rows_ref[0:1] * rows_ref[1:2], axis=1, keepdims=True)
        spread_own[...] = jnp.broadcast_to(total, spread_own.shape)
        for copy in spreads():
            copy.start()

    def agree(t):
        for copy in spreads():
            copy.wait()
        total = spread_own[...] + spread_got[0] + spread_got[1] + spread_got[2]
        total = jnp.max(total[0:1], axis=1, keepdims=True)
        inverse = rows_ref[3:4]
        norms = rows_ref[1:2]
        grad_norms = (
            sums[0:1] * rows_ref[0:1] * inverse - total * rows_ref[4:5] * inverse * inverse
        )
        sums[2:3] = grad_norms / norms
        small[1, 1:2] = sums[0:1] * rows_ref[5:6]
        small[1, 2:3] = sums[1:2]

    def bend(i):
        act_load(i).wait()
        slope_load(i).wait()

        @pl.when(i + 1 < count)
        def _():
            act_load(i + 1).start()
            slope_load(i + 1).start()

        @pl.when(i + 1 == count)
        def _():
            column_load(0).start()
            weight_load(expand_w_ref, 0).start()

        cols = tile_rows(i)
        factor = rows_ref[2:3, cols]
        twice = sums[2:3, cols]

        def strip(k, carry):
            rows = pl.ds(pl.multiple_of(k * 48, 48), 48)
            value = (
                wide[rows, cols] * factor + acts[lax.rem(i, 2), rows] * twice
            ) * slopes[lax.rem(i, 2), rows]
            high[rows, cols], low[rows, cols] = halves(value)
            sums[3:4, cols] += jnp.sum(value, axis=0, keepdims=True)
            return carry

        lax.fori_loop(0, spots // 48, strip, 0)

    def outer(i):
        column_load(i).wait()
        pl.when(i + 1 < 4)(lambda: column_load(jnp.minimum(i + 1, 3)).start())
        pl.when(i > 0)(lambda: [copy.wait() for copy in product_stores(jnp.maximum(i - 1, 0))] and None)
        left = halves(columns[lax.rem(i, 2)])

        def strip(k, carry):
            cols = pl.ds(pl.multiple_of(k * TILE, TILE), TILE)
            product[:, cols] = three_pass(left, (high[:, cols], low[:, cols]), ((0,), (0,)))
            return carry

        lax.fori_loop(0, count, strip, 0)
        for copy in product_stores(i):
            copy.start()

    def settle_outer(t):
        for copy in product_stores(3):
            copy.wait()
        small[1, 0:1] = sums[3:4]

    def backward(i):
        weight_load(expand_w_ref, i).wait()
        pl.when(i + 1 < count)(lambda: weight_load(expand_w_ref, jnp.minimum(i + 1, count - 1)).start())

        @pl.when(i > 1)
        def _():
            for copy in front_sends(jnp.maximum(i - 2, 0)):
                copy.wait_send()

        right = halves(weights[lax.rem(i, 2)])

        def strip(k, carry):
            rows = pl.ds(pl.multiple_of(k * pixels, pixels), pixels)
            front[lax.rem(i, 2), rows] = three_pass((high[rows], low[rows]), right, ((1,), (1,)))
            return carry

        lax.fori_loop(0, 4, strip, 0)
        front_own[:, tile_rows(i)] = front[lax.rem(i, 2), 0:pixels]
        for copy in front_sends(i):
            copy.start()

    def middle(t):
        loads[0].wait()
        for i in range(count):
            for copy in front_sends(i):
                copy.wait_recv()
                if i >= count - 2:
                    copy.wait_send()

    def tiles(t):
        def tile(i, carry):
            rows = pl.ds(pl.multiple_of(i * 8, 8), 8)
            back = front_own[rows] + front_got[0, rows] + front_got[1, rows] + front_got[2, rows]
            normed, inverse = row_stats(conv[rows])
            one[rows] = inverse * (
                back
                - jnp.mean(back, axis=-1, keepdims=True)
                - normed * jnp.mean(back * normed, axis=-1, keepdims=True)
            )
            return carry

        size = pixels // 48
        lax.fori_loop(t * size, (t + 1) * size, tile, 0)

    def give(t):
        kept.start()

    def outlet(t):
        pl.when(t == 0)(lambda: [copy.wait() for copy in loads[1:] + outward] and None)
        rows = pl.ds(pl.multiple_of(t * 8, 8), 8)
        base[rows] += out_own[0, rows] + out_got[0, rows] + out_got[1, rows] + out_got[2, rows]
        pl.when(moves)(away(t).start)
        pl.when(jnp.logical_not(moves))(here(t).start)

    sum_stream(
        [
            ("plain", output_ref, output_out),
            ("swap", attend_part, attend_out),
            ("plain", mapper_part, mapper_out),
            ("plain", reduce_part, reduce_out),
            ("plain", small, small_out),
            ("swap", expand_part, expand_out),
        ],
        scratch[:SCRATCH],
        [
            (0, 1, prepare),
            (1, 5, attend_outer),
            (5, 6, settle_attend),
            (12, 13, arrive),
            (12, 21, normalize),
            (21, 22, give_late),
            (24, 25, gathered),
            (25, 26, text_products),
            (26, 32, reduce_outer),
            (32, 33, settle_reduce),
            (33, 39, respond),
            (39, 40, share),
            (40, 41, agree),
            (41, 47, bend),
            (47, 51, outer),
            (51, 52, settle_outer),
            (52, 58, backward),
            (68, 69, middle),
            (68, 74, tiles),
            (74, 75, give),
            (60, 78, outlet),
            (39, 43, out_product),
            (43, 44, send_out),
        ],
    )
    kept.wait()

    def settle(i, carry):
        pl.when(moves)(away(i).wait)
        pl.when(jnp.logical_not(moves))(here(i).wait)
        return carry

    lax.fori_loop(0, base.shape[0] // 8, settle, 0)


def backward_sums(
    collective, output_part, qkv, two_share, text_share, cot, one, response, reduce_w, act, slope,
    normed_all, expand_w, conv, mixture, out_w, base, small, normed_two, rows, embed, silu,
    mapped, text_kv, mapper_half
):
    pixels, chan = conv.shape
    spots = normed_all.shape[0]
    texts = text_share.shape[1]
    slots = silu.shape[0] // 4
    f32, bf16 = jnp.float32, jnp.bfloat16
    half = chan // 8
    count = chan // TILE

    def shape(*dims):
        return jax.ShapeDtypeStruct(dims, f32)

    total = (half + 8 * half // 2 + mapper_half + chan // 2 + CHUNK + 8 * half // 2) // CHUNK
    block = (pixels, chan)
    return pl.pallas_call(
        backward_body,
        out_shape=[
            shape(2, half, chan),
            shape(2, half, 3 * chan),
            shape(2, mapper_half, chan),
            shape(2, chan // 2, chan),
            shape(2, CHUNK, chan),
            shape(2, half, 4 * chan),
            shape(4, 2, half, 3 * chan // 4),
            shape(2, mapper_half, chan),
            shape(2, chan // 2, chan),
            shape(4, 2, half, chan),
            shape(*block),
            shape(4, slots, chan),
            shape(*block),
            shape(*block),
        ],
        in_specs=[ANY] * 18 + [pl.BlockSpec(memory_space=pltpu.VMEM)] * 5,
        out_specs=[ANY] * 14,
        scratch_shapes=stream_scratch(total, 4 * half // CHUNK, chan)
        + [
            pltpu.VMEM((3,) + block, f32),
            pltpu.VMEM(block, f32),
            pltpu.VMEM(block, f32),
            pltpu.VMEM(block, f32),
            pltpu.VMEM(block, f32),
            pltpu.VMEM((3,) + block, f32),
            pltpu.VMEM((4,) + block, f32),
            pltpu.VMEM(block, f32),
            pltpu.VMEM(small.shape, f32),
            pltpu.VMEM((spots, chan), f32),
            pltpu.VMEM((spots, chan), bf16),
            pltpu.VMEM((spots, chan), bf16),
            pltpu.VMEM((2, TILE, chan), f32),
            pltpu.VMEM((2, spots, TILE), f32),
            pltpu.VMEM((2, spots, TILE), f32),
            pltpu.VMEM((2, spots, chan // 4), f32),
            pltpu.VMEM((chan // 4, chan), f32),
            pltpu.VMEM((2, spots, TILE), f32),
            pltpu.VMEM((8, chan), f32),
            pltpu.VMEM((8, 128), f32),
            pltpu.VMEM((3, 8, 128), f32),
            pltpu.VMEM((3, texts, chan), f32),
            pltpu.VMEM((texts, chan), f32),
            pltpu.VMEM((4, slots, chan), f32),
            pltpu.VMEM((4, 16, chan), f32),
            pltpu.VMEM((silu.shape[1], chan), f32),
            DMA((9,)),
            DMA((9,)),
            DMA((12,)),
            DMA((pixels // 8,)),
            DMA((pixels // 8,)),
            DMA((14,)),
            DMA((count, 3)),
            DMA((count, 3)),
            DMA((3,)),
            DMA((3,)),
            DMA((pixels // 16, 3)),
            DMA((pixels // 16, 3)),
            DMA((6,)),
            DMA((6,)),
        ],
        compiler_params=pltpu.CompilerParams(
            collective_id=collective, has_side_effects=True, vmem_limit_bytes=62 * 2**20
        ),
        name="backward_sums",
    )(
        output_part, qkv, two_share, text_share, cot, one, response, reduce_w, act, slope,
        normed_all, expand_w, conv, mixture, out_w, base, small, normed_two, rows, embed, silu,
        mapped, text_kv,
    )


def close_body(
    grad_in, token_in, conv_in, up_in, down_in,
    grad_home, token_home, conv_all, below, above,
    hold, send, recv, keep
):
    core = lax.axis_index("cond")
    level = lax.axis_index("pair")
    me = lax.axis_index("dp")
    up, over = home_spot(level, me)
    back_up, back_over = plane_spot(level, me)
    moves = jnp.logical_or(level != 0, me != 0)
    others = [(c, s) for c in (0, 1) for s in (0, 1, 2, 3) if (c, s) != (0, 0)]

    def other(c, s):
        return (lax.rem(core + c, 2), lax.rem(level + s, 4), me)

    for c, s in others:
        greet(other(c, s))
    pl.when(moves)(lambda: greet((core, back_up, back_over)))
    turned = jnp.logical_and(level == 1, me == 1)
    quarter = up
    lifts = quarter > 0
    drops = jnp.logical_and(quarter < 3, jnp.logical_not(turned))
    lifted = level < 3
    dropped = jnp.logical_and(level > 0, jnp.logical_not(turned))
    pl.when(lifted)(lambda: greet((core, me, near_of(me, rev(jnp.minimum(level + 1, 3))))))
    pl.when(dropped)(lambda: greet((core, me, near_of(me, rev(jnp.maximum(level - 1, 0))))))
    pl.semaphore_wait(
        pltpu.get_barrier_semaphore(),
        7 + jnp.where(moves, 1, 0) + jnp.where(lifts, 1, 0) + jnp.where(drops, 1, 0),
    )
    lift = remote(up_in, below, send.at[9], recv.at[9], (core, jnp.maximum(quarter - 1, 0), level))
    drop = remote(down_in, above, send.at[10], recv.at[10], (core, jnp.minimum(quarter + 1, 3), level))
    around = pltpu.make_async_copy(down_in, above, keep.at[3])
    pl.when(lifts)(lift.start)
    pl.when(drops)(drop.start)
    pl.when(turned)(around.start)
    swaps = ((grad_in, grad_home), (token_in, token_home))
    aways = [remote(src, dst, send.at[i], recv.at[i], (core, up, over)) for i, (src, dst) in enumerate(swaps)]
    spreads = [
        remote(conv_in, conv_all.at[1 + i], send.at[2 + i], recv.at[2 + i], other(c, s))
        for i, (c, s) in enumerate(others)
    ]
    mine = pltpu.make_async_copy(conv_in, conv_all.at[0], keep.at[2])
    for copy in spreads + [mine]:
        copy.start()
    for away in aways:
        pl.when(moves)(away.start)

    @pl.when(jnp.logical_not(moves))
    def _():
        load = pltpu.make_async_copy(grad_in, hold, keep.at[0])
        store = pltpu.make_async_copy(hold, grad_home, keep.at[0])
        small = pltpu.make_async_copy(token_in, token_home, keep.at[1])
        small.start()
        load.start()
        load.wait()
        store.start()
        store.wait()
        small.wait()

    for copy in spreads + [mine]:
        copy.wait()
    for away in aways:
        pl.when(moves)(away.wait)
    pl.when(lifts)(lift.wait_send)
    pl.when(drops)(drop.wait_send)
    pl.when(lifted)(lift.wait_recv)
    pl.when(dropped)(drop.wait_recv)
    pl.when(turned)(around.wait)


def close_exchange(collective, grad, tokens, conv, up, down):
    shapes = [grad.shape, tokens.shape, (8,) + conv.shape, up.shape, down.shape]
    return pl.pallas_call(
        close_body,
        out_shape=[jax.ShapeDtypeStruct(shape, jnp.float32) for shape in shapes],
        in_specs=[ANY] * 5,
        out_specs=[ANY] * 5,
        scratch_shapes=[pltpu.VMEM(grad.shape, jnp.float32), DMA((11,)), DMA((11,)), DMA((4,))],
        compiler_params=pltpu.CompilerParams(collective_id=collective, has_side_effects=True),
        name="close_exchange",
    )(grad, tokens, conv, up, down)


def deliver_body(count, *refs):
    ins, outs, holds = refs[:count], refs[count : 2 * count], refs[2 * count : 3 * count]
    load, store = refs[3 * count :]
    loads, stores = [], []
    for i in range(count):
        rows = ins[i].shape[0] // 8
        for k in range(8):
            part = pl.ds(k * rows, rows)
            loads.append(pltpu.make_async_copy(ins[i].at[part], holds[i].at[part], load.at[i, k]))
            stores.append(pltpu.make_async_copy(holds[i].at[part], outs[i].at[part], store.at[i, k]))
    for copy in loads:
        copy.start()
    for first, then in zip(loads, stores):
        first.wait()
        then.start()
    for copy in stores:
        copy.wait()


def deliver(*arrays):
    count = len(arrays)
    return pl.pallas_call(
        functools.partial(deliver_body, count),
        out_shape=[jax.ShapeDtypeStruct(item.shape, item.dtype) for item in arrays],
        in_specs=[ANY] * count,
        out_specs=[ANY] * count,
        scratch_shapes=[pltpu.VMEM(item.shape, item.dtype) for item in arrays]
        + [DMA((count, 8)), DMA((count, 8))],
        compiler_params=pltpu.CompilerParams(vmem_limit_bytes=48 * 2**20),
        name="deliver",
    )(*arrays)


def plane_body(
    latents,
    ratio_embed,
    clip_tokens,
    cotangent,
    conv_kernel,
    conv_bias,
    expand_weight,
    expand_bias,
    response_gain,
    response_bias,
    reduce_weight,
    reduce_bias,
    ratio_weight,
    ratio_bias,
    text_weight,
    text_bias,
    attend_weight,
    query_bias,
    value_bias,
    output_weight,
    output_bias,
):
    size = lax.axis_size("dp")
    core = lax.axis_index("cond")
    me = lax.axis_index("dp")
    level = lax.axis_index("pair")
    quarter = home_spot(level, me)[0]
    order = jnp.bitwise_xor(jnp.arange(4), me)
    _, rows, cols, chan = latents.shape
    pixels = rows * cols
    part = chan // size
    hid = size * expand_bias.shape[0]
    texts = clip_tokens.shape[1]
    packed = jnp.concatenate(
        [
            conv_kernel.reshape(9, part),
            conv_bias[None],
            reduce_bias[None],
            text_bias[None],
            output_bias[None],
            ratio_bias.reshape(2, part),
        ],
        axis=0,
    )
    row_padded, every, tokens, embed, expand_w, attend_units = open_exchange(
        3, latents[0], packed, clip_tokens[0], ratio_embed, expand_weight, attend_weight
    )[:6]
    row_padded = row_padded.at[:1].set(jnp.where(quarter > 0, row_padded[:1], 0.0))
    row_padded = row_padded.at[-1:].set(jnp.where(quarter < size - 1, row_padded[-1:], 0.0))
    image = row_padded[1:-1]
    expand_w = expand_w.reshape(chan, -1)
    channel_rows = every[:, :13].transpose(1, 0, 2).reshape(13, chan)
    kernel = channel_rows[:9].reshape(3, 3, chan)
    conv_shift, reduce_b, text_b, out_b = (channel_rows[9 + i] for i in range(4))
    ratio_b = every[:, 13:].reshape(2 * chan)

    half = part // 2
    wide = hid // size
    text_part = text_weight.shape[0]
    token_cols = [
        lax.dynamic_slice(tokens, (0, near_of(me, step) * text_part), (texts, text_part))
        for step in range(4)
    ]
    ratio_part = ratio_weight.shape[0]
    embed_part = lax.dynamic_slice(embed, (0, me * ratio_part), (1, ratio_part))
    mod_part = jnp.dot(embed_part, ratio_weight, precision=HIGHEST_ACCURACY)

    padded = jnp.pad(row_padded, ((0, 0), (1, 1), (0, 0)))
    total_conv = conv_shift
    for i in range(3):
        for j in range(3):
            total_conv = total_conv + padded[i : i + rows, j : j + cols] * kernel[i, j]
    normed, inverse = norm_stats(total_conv.reshape(pixels, chan))
    normed_all, mod_near, near_tokens, attend_w = exchange(
        4,
        gathers=(normed, mod_part),
        scatters=(jnp.stack(token_cols),),
        relay=(attend_units,),
    )
    attend_w = attend_w.reshape(chan, 3 * part)
    modulation = jnp.sum(mod_near[:, 0], axis=0) + ratio_b
    mod_scale = 1.0 + modulation[:chan]
    mod_shift = modulation[chan:]
    normed_all = normed_all.reshape(size * pixels, chan)
    cot, normed_all = lax.optimization_barrier((cotangent[0].reshape(pixels, chan), normed_all))
    turns = (0, 2, 1, 3)
    grid = [(z, d) for z in range(size) for d in range(size)]
    cot = lax.ppermute(
        cot, ("pair", "dp"), [(z * size + d, z * size + (d ^ turns[z])) for z, d in grid]
    )
    near_tokens = jnp.concatenate([token_cols[0], near_tokens.reshape(-1, text_part)], axis=0)
    silu_near = jax.nn.silu(near_tokens)
    mapped_share = dot(silu_near, text_weight).reshape(4, texts, chan)
    hidden = dot(normed_all, expand_w) + expand_bias
    bell = 0.5 * (1.0 + lax.erf(hidden * 0.5**0.5))
    activated = hidden * bell
    density = jnp.exp(-0.5 * hidden * hidden) * (2.0 * jnp.pi) ** -0.5
    slope = bell + hidden * density
    totals = jnp.sum(activated * activated, axis=0)
    norms = jnp.sqrt(totals + EPSILON)
    norm_sums = exchange(5, gathers=(jnp.full((8, 128), jnp.sum(norms)),))[0]
    middle = jnp.sum(norm_sums[:, 0, 0]) / hid + EPSILON
    scaled = norms / middle
    factor = 1.0 + response_gain * scaled
    response = activated * factor + response_bias
    one_share = dot(response, reduce_weight).reshape(4, pixels, chan)
    cot, one_share = lax.optimization_barrier((cot, one_share))
    cot = lax.ppermute(
        cot, ("pair", "dp"), [(z * size + d, (d ^ turns[z]) * size + d) for z, d in grid]
    )
    one_arrived, mapped_arrived = exchange(6, scatters=(one_share, mapped_share))
    mapped = mapped_share[0] + jnp.sum(mapped_arrived, axis=0) + text_b
    hidden_one = one_share[0] + jnp.sum(one_arrived, axis=0) + image.reshape(pixels, chan) + reduce_b
    hidden_two = hidden_one * mod_scale + mod_shift
    normed_two, inverse_two = norm_stats(hidden_two)
    cot, normed_two = lax.optimization_barrier((cot, normed_two))
    normed_two_all, mapped_all = exchange(7, gathers=(normed_two, mapped))
    cot, normed_two_all = lax.optimization_barrier((cot, normed_two_all))
    cot_all = jnp.concatenate(
        [cot]
        + [lax.ppermute(cot, "dp", [(i, i ^ step) for i in range(size)]) for step in (1, 2, 3)],
        axis=0,
    )
    normed_two_all = normed_two_all.reshape(size * pixels, chan)
    mapped_all = mapped_all.reshape(size * texts, chan)

    source = jnp.concatenate([normed_two_all, mapped_all], axis=0)
    query = dot(normed_two_all, attend_w[:, :part]) + query_bias
    key_value = dot(source, attend_w[:, part:])
    key = key_value[:, :part]
    value = key_value[:, part:] + value_bias
    query_h, key_h, value_h = heads_of(query), heads_of(key), heads_of(value)
    scores = jnp.einsum("iuy,ouy->uio", query_h, key_h, precision=FAST) * HEAD_CHANNELS ** (-0.5)
    expo = jnp.exp(scores - jnp.max(scores, axis=-1, keepdims=True))
    probs = expo / jnp.sum(expo, axis=-1, keepdims=True)
    mixture_h = jnp.einsum("uio,ouy->iuy", probs, value_h, precision=FAST)
    mixture = mixture_h.reshape(query.shape)
    out_base = hidden_two + out_b

    output_grad = t_dot(mixture, cot_all)
    grad_mix_h = heads_of(dot_t(cot_all, output_weight))
    grad_probs = jnp.einsum("iuy,ouy->uio", grad_mix_h, value_h, precision=FAST)
    delta = jnp.sum(grad_mix_h * mixture_h, axis=-1).T
    grad_scores = probs * (grad_probs - delta[..., None]) * HEAD_CHANNELS ** (-0.5)
    grad_query = jnp.einsum("uio,ouy->iuy", grad_scores, key_h, precision=FAST).reshape(query.shape)
    grad_key = jnp.einsum("uio,iuy->ouy", grad_scores, query_h, precision=FAST).reshape(key.shape)
    grad_value = jnp.einsum("uio,iuy->ouy", probs, grad_mix_h, precision=FAST).reshape(key.shape)
    spots = size * pixels
    grad_kv = jnp.concatenate([grad_key, grad_value], axis=1)
    grad_qkv = jnp.concatenate([grad_query, grad_kv[:spots]], axis=1)
    two_share = dot_t(grad_qkv, attend_w).reshape(4, pixels, chan)
    text_share = dot_t(grad_kv[spots:], attend_w[:, part:]).reshape(4, texts, chan)
    def row(value):
        return jnp.sum(value, axis=0, keepdims=True)

    def mine(value):
        width = value.shape[1] // size
        return lax.dynamic_slice(value, (0, me * width), (value.shape[0], width))

    gap = jnp.zeros((1, part), jnp.float32)
    small_rows = jnp.concatenate(
        [
            jnp.zeros((3, chan), jnp.float32),
            jnp.concatenate([gap, gap, row(grad_query), row(grad_value)], axis=1),
            jnp.concatenate([row(mine(cot_all)), gap, gap, gap], axis=1),
            jnp.zeros((CHUNK - 5, chan), jnp.float32),
        ],
        axis=0,
    )
    one_row = jnp.full((1, chan), 1.0, jnp.float32)
    back_rows = jnp.concatenate(
        [
            response_gain[None],
            norms[None],
            factor[None],
            one_row / middle,
            one_row / hid,
            scaled[None],
            mod_scale[None],
            mod_shift[None],
        ],
        axis=0,
    )
    slots = (texts + 7) // 8 * 8

    def padded_rows(value):
        value = value.reshape(4, texts, -1)
        return jnp.pad(value, ((0, 0), (0, slots - texts), (0, 0))).reshape(4 * slots, -1)

    silu_padded = jnp.pad(
        silu_near.reshape(4, texts, text_part), ((0, 0), (0, slots - texts), (0, -text_part % 128))
    ).reshape(4 * slots, -1)
    embed_rows = jnp.broadcast_to(
        embed_part.reshape(ratio_part, 1, 1), (ratio_part, 2, 128)
    ).reshape(2 * ratio_part, 128)
    (
        output_sum, attend_sum, mapper_sum, reduce_sum, small, expand_sum, _, _, _, _,
        grad_one, grad_mapped_all, grad_conv, layer_output,
    ) = backward_sums(
        1,
        output_grad.reshape(2, half, chan),
        grad_qkv,
        two_share,
        text_share,
        cot,
        hidden_one,
        response,
        reduce_weight,
        activated,
        slope,
        normed_all,
        expand_w,
        total_conv.reshape(pixels, chan),
        mixture,
        output_weight,
        out_base,
        jnp.stack([jnp.zeros((CHUNK, chan), jnp.float32), small_rows]),
        normed_two_all,
        back_rows,
        embed_rows,
        silu_padded,
        padded_rows(mapped_all),
        padded_rows(grad_kv[spots:]),
        text_part // 2,
    )
    output_sum = output_sum.reshape(part, chan)
    attend_sum = attend_sum.reshape(part, 3 * chan)
    mapper_sum = mapper_sum.reshape(text_part, chan)
    reduce_sum = reduce_sum.reshape(wide, chan)
    expand_sum = expand_sum.reshape(part, hid)
    layer_output = layer_output.reshape(latents.shape)
    mapper_sum, expand_sum = deliver(mapper_sum, expand_sum)
    grad_mapped_all = grad_mapped_all[:, :texts].reshape(size * texts, chan)
    gate = 1.0 / (1.0 + jnp.exp(-near_tokens))
    tokens_near = dot_t(grad_mapped_all, text_weight) * (
        gate * (1.0 + near_tokens * (1.0 - gate))
    )
    tokens_near = tokens_near.reshape(4, texts, text_part)
    grad_conv = grad_conv.reshape(rows, cols, chan)
    kernel_grad = jnp.stack(
        [
            jnp.sum(padded[i : i + rows, j : j + cols] * grad_conv, axis=(0, 1))
            for i in range(3)
            for j in range(3)
        ]
    )
    spread_conv = jnp.pad(grad_conv, ((2, 2), (1, 1), (0, 0)))
    latent_rows = jnp.zeros((rows + 2, cols, chan), jnp.float32)
    for i in range(3):
        for j in range(3):
            latent_rows = (
                latent_rows
                + spread_conv[2 - i : 2 - i + rows + 2, 2 - j : 2 - j + cols] * kernel[i, j]
            )
    conv_part = jnp.concatenate([kernel_grad, jnp.sum(grad_conv, axis=(0, 1))[None]], axis=0)
    conv_blocks = jnp.stack(
        [
            lax.dynamic_slice(conv_part, (0, near_of(me, step) * part), (10, part))
            for step in range(4)
        ]
    )
    conv_arrived, token_arrived = exchange(13, scatters=(conv_blocks, tokens_near))
    token_blocks = jnp.take(
        jnp.concatenate([tokens_near[:1], token_arrived], axis=0), order, axis=0
    )
    inner = latent_rows[1:-1] + grad_one.reshape(rows, cols, chan)
    latent_grad, tokens_grad, conv_all, from_below, from_above = close_exchange(
        14,
        inner.reshape(pixels, chan),
        token_blocks.transpose(1, 0, 2).reshape(texts, size * text_part),
        conv_blocks[0] + jnp.sum(conv_arrived, axis=0),
        latent_rows[0],
        latent_rows[-1],
    )
    from_above = jnp.where(level > 0, from_above, 0.0)[None]
    from_below = jnp.where(level < size - 1, from_below, 0.0)[None]
    still = jnp.zeros((rows - 2, cols, chan), jnp.float32)
    latent_grad = latent_grad.reshape(rows, cols, chan) + jnp.concatenate(
        [from_above, still, from_below], axis=0
    )
    latent_grad = latent_grad[None]
    tokens_grad = tokens_grad[None]
    conv_mine = jnp.sum(conv_all, axis=0)
    ratio = small[0]
    expb, gain, respb = (small[1, i] for i in range(3))
    redb, mapb, queryb, valueb = (small[1, 3, i * part : (i + 1) * part] for i in range(4))
    outb = small[1, 4, :part]
    ratiob = small[1, 4, part : 3 * part]
    return (
        layer_output,
        latent_grad,
        tokens_grad,
        conv_mine[:9].reshape(3, 3, part),
        conv_mine[9],
        expand_sum,
        expb,
        gain,
        respb,
        reduce_sum,
        redb,
        ratio.reshape(ratio_part, 2 * chan),
        ratiob,
        mapper_sum,
        mapb,
        attend_sum,
        queryb,
        valueb,
        output_sum,
        outb,
    )


def solution(mesh):
    square = mesh.shape["cond"] == 2 and mesh.shape["pair"] == 4 and mesh.shape["dp"] == 4
    return jax.shard_map(
        plane_body if square else body,
        mesh=mesh,
        in_specs=(
            P(("cond", "dp"), "pair", None, None),
            P(("cond", "dp"), None),
            P(("cond", "dp"), "pair", None),
            P(("cond", "dp"), "pair", None, None),
            P(None, None, "dp"),
            P("dp"),
            P("dp", None),
            P("dp"),
            P("dp"),
            P("dp"),
            P("dp", None),
            P("dp"),
            P("dp", None),
            P("dp"),
            P("dp", None),
            P("dp"),
            P("dp", None),
            P("dp"),
            P("dp"),
            P("dp", None),
            P("dp"),
        ),
        out_specs=(
            P(("cond", "dp"), "pair", None, None),
            P(("cond", "dp"), "pair", None, None),
            P(("cond", "dp"), "pair", None),
            P(None, None, "dp"),
            P("dp"),
            P("dp", None),
            P("dp"),
            P("dp"),
            P("dp"),
            P("dp", None),
            P("dp"),
            P("dp", None),
            P("dp"),
            P("dp", None),
            P("dp"),
            P("dp", None),
            P("dp"),
            P("dp"),
            P("dp", None),
            P("dp"),
        ),
        check_vma=False,
    )
```
